32 devices in a mesh: fsdp: 8 (over y, x, core), seq: 4 (over z).
Axes of the slice: x: 2, y: 2, z: 4, core: 2. Of those that a mesh axis runs over, the one named last changes fastest.
Arguments:
- inputs: bfloat16 [8, 2048, 1536], P('fsdp', 'seq'), may hold values from -6 to 6
- teacher: bfloat16 [8, 2048, 1536], P('fsdp', 'seq'), may hold values from -6 to 6
- routes: int32 [8, 2048, 8], P('fsdp', 'seq'), may hold values from 0 to 39, all different within a row; in each aligned block of 512 rows (0 to 511, 512 to 1023, ..., all dimensions but the last counted through in order) at most 153 rows name the same one
- valid_mask: int32 [8, 2048], P('fsdp', 'seq'), may hold values from 0 to 1, as said below
- block_lengths: int32 [8, 16], P('fsdp'), may hold values from 1 to 256, 2048 in all within a row
- gain_one: bfloat16 [1536], P('fsdp'), may hold values from 0.5 to 1.5
- w_qkv: bfloat16 [1536, 2560], P('fsdp'), may hold values from -0.5 to 0.5
- w_out: bfloat16 [1536, 1536], P('fsdp'), may hold values from -2.5 to 2.5
- gain_two: bfloat16 [1536], P('fsdp'), may hold values from 0.5 to 1.5
- w_router: bfloat16 [1536, 40], P('fsdp'), may hold values from -0.078125 to 0.078125
- w_gate: bfloat16 [40, 1536, 512], P('seq', 'fsdp'), may hold values from -0.3125 to 0.3125
- w_up: bfloat16 [40, 1536, 512], P('seq', 'fsdp'), may hold values from -0.3125 to 0.3125
- w_down: bfloat16 [40, 512, 1536], P('seq', 'fsdp'), may hold values from -1 to 1
Outputs:
- activations: bfloat16 [8, 2048, 1536], P('fsdp', 'seq')
- loss: float32 [], replicated
- input_grad: float32 [8, 2048, 1536], P('fsdp', 'seq')
- gain_one_grad: float32 [1536], P('fsdp')
- qkv_grad: float32 [1536, 2560], P('fsdp')
- out_grad: float32 [1536, 1536], P('fsdp')
- gain_two_grad: float32 [1536], P('fsdp')
- router_grad: float32 [1536, 40], P('fsdp')
- gate_grad: float32 [40, 1536, 512], P('seq', 'fsdp')
- up_grad: float32 [40, 1536, 512], P('seq', 'fsdp')
- down_grad: float32 [40, 512, 1536], P('seq', 'fsdp')
The draws below stay inside these ranges and needn't reach their ends.
Inputs may be any that keep to these rules, and one draw needn't show every extreme that they name: In each aligned block of 512 rows (one sequence's positions on one index of seq), no expert is named by more than 153 routes; in some block one expert is named by exactly 153; a token's 8 experts differ. `block_lengths`: each row sums to 2048, and its longest block is 256. `valid_mask`: 1 marks a token that the loss counts.
All inputs are finite; a program needn't handle non-finite values.
Results may differ from the reference program's by a relative error of at most 0.019.
Values may be sent and summed in bfloat16 or wider, within the bound.
No kernel may reach another device: no remote copies, remote signals or barrier semaphores. Data moves between devices by JAX's collectives and lax.ppermute only.
A program may use at most 512 MiB of HBM per device.

```python
import math
from functools import partial
import jax
import jax.numpy as jnp
import numpy as np
from jax import lax

D = 1536
HEADS = 24
KV_HEADS = 8
HEAD_DIM = 64
EXPERTS = 40
FF = 512
TOPK = 8
BLOCK = 256
SEQ_LEN = 2048
GROUP = 3
QKV_W = 2560
NBLK = 16
SEQS = 8
SHARD = 512
CAP = 153
TOKENS = 16384
N_SEQ = 4


def draw_valid_mask(key, part):
    key = jax.random.fold_in(key, 7)
    seq_ids = jnp.arange(SEQS, dtype=jnp.int32)[:, None]
    pos_ids = jnp.arange(SEQ_LEN, dtype=jnp.int32)[None, :]
    threshold = 150 + 400 * seq_ids // SEQS + 400 * pos_ids // SEQ_LEN
    rolled = jax.random.randint(key, (SEQS, SEQ_LEN), 0, 1000, dtype=jnp.int32)
    return (rolled < threshold).astype(jnp.int32)


def with_spikes(values, own_key, source, target, parts, factor):
    def block_of(position):
        return (jnp.arange(values.shape[position]) // (values.shape[position] // parts)).reshape((-1,) + (1,) * (values.ndim - 1 - position))

    first = jax.random.permutation(own_key, parts)[block_of(target)]
    other_side = (block_of(target) + parts // 2) % parts
    return jnp.where((block_of(source) == first) | (block_of(source) == other_side), factor * values, values)


def steps_of(key, shape, split, least, top_value):
    level = 1.0
    for dim, blocks in split:
        heights = jax.random.uniform(jax.random.fold_in(jax.random.fold_in(key, 6), dim), (blocks,), jnp.float32, least / len(split), top_value / len(split))
        level = level * jnp.repeat(jnp.exp(heights), shape[dim] // blocks).reshape((-1,) + (1,) * (len(shape) - 1 - dim))
    return level


def length_profile(number_of, total, most, slope):
    portions = [(1 << 20) // math.isqrt(standing ** slope) + 1 for standing in range(2, number_of + 1)]
    rest, counts = total - most - (number_of - 1), [1] * (number_of - 1)
    while rest > 0:
        candidates = [i for i in range(number_of - 1) if counts[i] < most]
        pool, budget = sum([portions[i] for i in candidates]), rest
        for i in candidates:
            addition = min(most - counts[i], max(1, budget * portions[i] // pool), rest)
            counts[i] = counts[i] + addition
            rest = rest - addition
    return np.array([most] + counts)


def ragged_sizes(key, amount, total, most, skew):
    if amount == 2:
        one = jax.random.randint(key, (), max(1, total - most), min(most, total - 1) + 1)
        return jnp.stack([one, total - one])
    tallies = jnp.asarray(length_profile(amount, total, most, skew), jnp.int32)
    pairs = (amount - 1) // 2
    giver, receiver = tallies[1:1 + 2 * pairs:2], tallies[2:2 + 2 * pairs:2]
    slack = jnp.minimum(giver - 1, most - receiver)
    passed = jax.random.randint(jax.random.fold_in(key, 1), (pairs,), 0, 1 << 20) % (slack + 1)
    tallies = tallies.at[1:1 + 2 * pairs:2].set(giver - passed).at[2:2 + 2 * pairs:2].set(receiver + passed)
    return tallies[jax.random.permutation(jax.random.fold_in(key, 2), amount)]


def assign_block(stream_key, own, number, rows, amount, top, limit, lean):
    sequence = jax.random.permutation(stream_key, amount)
    crowded, ordinary = load_shares(amount, rows * top, limit, lean, True), load_shares(amount, rows * top, limit, lean, False)
    places = jnp.arange(amount)

    def named(sizes, turn):
        used = int((sizes > 0).sum())
        fixed = max(1, used // 4)
        moved = fixed + (places - fixed + turn * (used - fixed)) % max(1, amount - fixed)
        return jnp.zeros((amount,), jnp.int32).at[sequence[jnp.where(places < fixed, places, moved)]].set(jnp.asarray(sizes, jnp.int32))

    sizes = jnp.where(number % 4 == 0, named(crowded, number // 4), named(ordinary, number - number // 4 - 1))
    mixed = jax.random.permutation(jax.random.fold_in(own, 3), amount)
    source_of, taker = mixed[0:amount // 2 * 2:2], mixed[1:amount // 2 * 2:2]
    slack = jnp.minimum(sizes[source_of] - 1, limit - sizes[taker]) // 2
    slack = jnp.where((source_of == sequence[0]) | (taker == sequence[0]) | (sizes[taker] == 0), 0, jnp.maximum(slack, 0))
    moved = jax.random.randint(jax.random.fold_in(own, 4), (amount // 2,), 0, 1 << 20) % (slack + 1)
    sizes = sizes.at[source_of].add(-moved).at[taker].add(moved)
    members = jnp.searchsorted(jnp.cumsum(sizes), jnp.arange(rows * top), side="right").astype(jnp.int32)
    grid = members.reshape(top, rows).T
    grid = grid[jax.random.permutation(jax.random.fold_in(own, 1), rows)]
    turn = jax.random.randint(jax.random.fold_in(own, 2), (rows, 1), 0, top)
    return jnp.take_along_axis(grid, (jnp.arange(top)[None, :] + turn) % top, axis=1)


def load_shares(amount, total, reach, lean, full):
    loads = [(1 << 20) // math.isqrt(standing ** lean) + 1 for standing in range(1, amount + 1)]
    largest = reach if full else min(reach, max(-(-total // amount), total * loads[0] // sum(loads)))
    least = 1 if total - largest >= amount - 1 else 0
    holding, surplus = [largest] + [least] * (amount - 1), total - largest - least * (amount - 1)
    while surplus > 0:
        free = [i for i in range(1, amount) if holding[i] < largest] or [i for i in range(1, amount) if holding[i] < reach]
        mass, remaining = sum([loads[i] for i in free]), surplus
        for i in free:
            extra = min(reach - holding[i], max(1, remaining * loads[i] // mass), surplus)
            holding[i] = holding[i] + extra
            surplus = surplus - extra
    return np.array(holding)


def centred(key, dims, spread, limit, split=(), held_as=jnp.bfloat16):
    drawn = spread * jax.random.normal(key, dims, jnp.float32)
    if split:
        drawn = drawn * steps_of(key, dims, split, -0.22, 0.18)
    return jnp.clip(drawn, -limit, limit).astype(held_as)


def noise_with(own_key, shape, spread, bound, shards, heavy, held_as=jnp.bfloat16):
    drawn = spread * jax.random.normal(own_key, shape, jnp.float32)
    if shards:
        drawn = drawn * steps_of(own_key, shape, shards, -0.22, 0.18)
    return jnp.clip(with_spikes(drawn, jax.random.fold_in(own_key, 3), *heavy), -bound, bound).astype(held_as)


def setup_inputs(seed: int = 0) -> dict:
    splits = jax.random.split(jax.random.key(seed), 14)
    inputs = noise_with(splits[0], (SEQS, SEQ_LEN, D), 1.0, 6.0, ((0, 8), (1, 4)), (0, 2, 8, 2.0))
    teacher = centred(splits[1], (SEQS, SEQ_LEN, D), 1.0, 6.0, ((0, 8), (1, 4)))
    routes_keys = jax.random.split(jax.random.fold_in(splits[2], 1), SEQS * SEQ_LEN // SHARD)
    routes_turns = jax.random.permutation(jax.random.fold_in(splits[2], 3), SEQS * SEQ_LEN // SHARD)
    routes = jax.vmap(lambda own, number: assign_block(jax.random.fold_in(splits[2], 2), own, number, SHARD, EXPERTS, TOPK, CAP, 1))(routes_keys, routes_turns).reshape((SEQS, SEQ_LEN, TOPK))
    valid_mask = draw_valid_mask(jax.random.fold_in(splits[13], 71), 0)
    block_lengths = jax.vmap(lambda own: ragged_sizes(own, NBLK, SEQ_LEN, BLOCK, 2))(jax.random.split(splits[4], SEQS)).reshape((SEQS, NBLK)).astype(jnp.int32)
    gain_one = jnp.clip(1.0 + 0.1 * jax.random.normal(splits[5], (D,), jnp.float32), 0.5, 1.5).astype(jnp.bfloat16)
    w_qkv = centred(splits[6], (D, QKV_W), (max(1, D // 12)) ** -0.5, 0.5, ((0, 8),))
    w_out = centred(splits[7], (HEADS * HEAD_DIM, D), (max(1, HEADS * HEAD_DIM // 256)) ** -0.5, 2.5, ((0, 8),))
    gain_two = jnp.clip(1.0 + 0.1 * jax.random.normal(splits[8], (D,), jnp.float32), 0.5, 1.5).astype(jnp.bfloat16)
    w_router = centred(splits[9], (D, EXPERTS), (4 * D) ** -0.5, 0.078125, ((0, 8),))
    w_gate = centred(splits[10], (EXPERTS, D, FF), (max(1, D // 4)) ** -0.5, 0.3125, ((0, 4), (1, 8)))
    w_up = centred(splits[11], (EXPERTS, D, FF), (max(1, D // 4)) ** -0.5, 0.3125, ((0, 4), (1, 8)))
    w_down = centred(splits[12], (EXPERTS, FF, D), (max(1, FF // 16)) ** -0.5, 1.0, ((0, 4), (1, 8)))
    return dict(inputs=inputs, teacher=teacher, routes=routes, valid_mask=valid_mask, block_lengths=block_lengths, gain_one=gain_one, w_qkv=w_qkv, w_out=w_out, gain_two=gain_two, w_router=w_router, w_gate=w_gate, w_up=w_up, w_down=w_down)


epsilon = 1e-06
attn_mult = 0.015625
resid_mult = 0.22
rope_base = 10000.0
masked_score = -1e+30
highest = lax.Precision.HIGHEST

@jax.custom_vjp
def low(v):
    return lax.optimization_barrier(v.astype(jnp.bfloat16)).astype(jnp.float32)

@jax.custom_vjp
def low_back(v):
    return v

def low_keep(v):
    return (low(v), None)

def low_pass(kept, grad):
    return (grad,)

def back_keep(v):
    return (v, None)

def back_low(kept, grad):
    return (low(grad),)
low.defvjp(low_keep, low_pass)
low_back.defvjp(back_keep, back_low)

def rms_norm(values, gain_vec):
    inv_rms = lax.rsqrt(lax.optimization_barrier(jnp.mean(values * values, axis=-1, keepdims=True)) + epsilon)
    return values * inv_rms * gain_vec

def rope_tables(positions, head_dim):
    half_dim = head_dim // 2
    frequency = rope_base ** (-(2.0 * jnp.arange(half_dim, dtype=jnp.float32)) / head_dim)
    angles = positions[:, None] * frequency[None, :]
    return (jnp.cos(angles), jnp.sin(angles))

def rotate(values, cosine, sine_vals):
    half_dim = values.shape[-1] // 2
    front_half = values[..., :half_dim]
    back_half = values[..., half_dim:]
    return jnp.concatenate([front_half * cosine - back_half * sine_vals, back_half * cosine + front_half * sine_vals], axis=-1)

def block_ids(lengths_row, positions):
    block_ends = jnp.cumsum(lengths_row).astype(jnp.int32)
    return lax.optimization_barrier(jnp.sum((positions[:, None] >= block_ends[None, :]).astype(jnp.int32), axis=1)).astype(jnp.int32)

def route_slots(route_block, expert_count):
    flat_ids = route_block.reshape(-1)
    onehot = (flat_ids[:, None] == jnp.arange(expert_count, dtype=jnp.int32)[None, :]).astype(jnp.int32)
    rank_ids = jnp.cumsum(onehot, axis=0).astype(jnp.int32) - 1
    return lax.optimization_barrier(jnp.sum(rank_ids * onehot, axis=1)).astype(jnp.int32).reshape(route_block.shape)

def slot_table(route_block, slot_ids, expert_count, capacity):
    row_total = route_block.shape[0]
    token_ids = jnp.broadcast_to(jnp.arange(row_total, dtype=jnp.int32)[:, None], route_block.shape)
    slot_map = jnp.full((expert_count, capacity), row_total, jnp.int32)
    return slot_map.at[route_block.reshape(-1), slot_ids.reshape(-1)].set(token_ids.reshape(-1))

def forward(params, seq_inputs, seq_routes, seq_lengths):
    gain_one, w_qkv, w_out, gain_two, w_router, w_gate, w_up, w_down = params
    seq_total = seq_inputs.shape[0]
    normed_one = low(rms_norm(seq_inputs, gain_one))
    qkv_rows = low_back(jnp.dot(normed_one, w_qkv, precision=highest))
    qkv_rows = qkv_rows.reshape(seq_total, KV_HEADS, GROUP + 2, HEAD_DIM)
    positions = jnp.arange(seq_total, dtype=jnp.int32)
    cosine, sine_vals = rope_tables(positions.astype(jnp.float32), HEAD_DIM)
    queries = low(low_back(rotate(qkv_rows[:, :, :GROUP], cosine[:, None, None, :], sine_vals[:, None, None, :])))
    key_rows = low(low_back(rotate(qkv_rows[:, :, GROUP], cosine[:, None, :], sine_vals[:, None, :])))
    value_rows = low(low_back(qkv_rows[:, :, GROUP + 1]))
    blocks = block_ids(seq_lengths, positions)
    query_rows = min(512, seq_total)

    def attend(pieces):
        query_blk, query_blocks = pieces
        scores = low_back(jnp.einsum('qghd,kgd->ghqk', query_blk, key_rows, precision=highest) * attn_mult)
        allowed = blocks[None, :] <= query_blocks[:, None]
        scores = jnp.where(allowed[None, None], scores, masked_score)
        prob_rows = low(jax.nn.softmax(scores, axis=-1))
        return jnp.einsum('ghqk,kgd->qghd', prob_rows, value_rows, precision=highest)
    attended = lax.map(jax.checkpoint(attend), (queries.reshape(seq_total // query_rows, query_rows, KV_HEADS, GROUP, HEAD_DIM), blocks.reshape(seq_total // query_rows, query_rows)))
    attended = low(low_back(attended.reshape(seq_total, HEADS * HEAD_DIM)))
    hidden = seq_inputs + resid_mult * low_back(jnp.dot(attended, w_out, precision=highest))
    normed_two = low(rms_norm(hidden, gain_two))
    logits = low_back(jnp.dot(normed_two, w_router, precision=highest))
    gate_vals = jax.nn.softmax(jnp.take_along_axis(logits, seq_routes, axis=1), axis=-1)
    route_blocks = seq_routes.reshape(N_SEQ, SHARD, TOPK)
    slot_ids = jax.vmap(partial(route_slots, expert_count=EXPERTS))(route_blocks)
    tables = jax.vmap(partial(slot_table, expert_count=EXPERTS, capacity=CAP), out_axes=1)(route_blocks, slot_ids)
    tables = tables + (jnp.arange(N_SEQ, dtype=jnp.int32) * (SHARD + 1))[None, :, None]
    padded = jnp.concatenate([normed_two.reshape(N_SEQ, SHARD, D), jnp.zeros((N_SEQ, 1, D), jnp.float32)], axis=1).reshape(N_SEQ * (SHARD + 1), D)
    expert_in = low_back(padded[tables].reshape(EXPERTS, N_SEQ * CAP, D))
    gate_act = low_back(jnp.einsum('erd,edf->erf', expert_in, w_gate, precision=highest))
    up_act = low_back(jnp.einsum('erd,edf->erf', expert_in, w_up, precision=highest))
    act_rows = low(jax.nn.silu(gate_act) * up_act)
    expert_out = low(low_back(jnp.einsum('erf,efd->erd', act_rows, w_down, precision=highest)))
    flat_out = expert_out.reshape(EXPERTS * N_SEQ * CAP, D)
    block_of = (jnp.arange(seq_total, dtype=jnp.int32) // SHARD)[:, None]
    flat_index = seq_routes * (N_SEQ * CAP) + block_of * CAP + slot_ids.reshape(seq_total, TOPK)
    picked = flat_out[flat_index]
    mixture = lax.optimization_barrier(jnp.sum(gate_vals[:, :, None] * picked, axis=1))
    return hidden + resid_mult * mixture

def reference(inputs, teacher, routes, valid_mask, block_lengths, gain_one, w_qkv, w_out, gain_two, w_router, w_gate, w_up, w_down):
    params = (gain_one.astype(jnp.float32), w_qkv.astype(jnp.float32), w_out.astype(jnp.float32), gain_two.astype(jnp.float32), w_router.astype(jnp.float32), w_gate.astype(jnp.float32), w_up.astype(jnp.float32), w_down.astype(jnp.float32))
    valid_f = valid_mask.astype(jnp.float32)
    valid_count = jnp.sum(valid_f)
    grad_scale = TOKENS / valid_count

    def one_sequence(carried, pieces):
        grad_sums, squares = carried
        seq_inputs, seq_teacher, seq_routes, seq_valid, seq_lengths = pieces

        def run_layer(layer_params, layer_inputs):
            return forward(layer_params, layer_inputs, seq_routes, seq_lengths)
        outputs, pullback = jax.vjp(run_layer, params, seq_inputs.astype(jnp.float32))
        error_rows = outputs - seq_teacher.astype(jnp.float32)
        weighted = seq_valid[:, None] * error_rows
        squares = squares + jnp.sum(weighted * error_rows)
        param_grads, input_grad = pullback(weighted * grad_scale)
        grad_sums = jax.tree.map(jnp.add, grad_sums, param_grads)
        return ((grad_sums, squares), (outputs.astype(jnp.bfloat16), input_grad))
    zero_grads = jax.tree.map(jnp.zeros_like, params)
    (grad_sums, squares), (activations, input_grads) = lax.scan(one_sequence, (zero_grads, jnp.zeros((), jnp.float32)), (inputs, teacher, routes, valid_f, block_lengths))
    loss_value = squares / (valid_count * D)
    return (activations, loss_value, input_grads, grad_sums[0], grad_sums[1], grad_sums[2], grad_sums[3], grad_sums[4], grad_sums[5], grad_sums[6], grad_sums[7])
```

```python
import jax
import jax.numpy as jnp
from jax import lax
from jax.sharding import PartitionSpec as P

HEADS = 24
KV_HEADS = 8
HEAD_DIM = 64
BLOCK = 256
GROUP = 3
QKV_W = 2560


epsilon = 1e-06
attn_mult = 0.015625
resid_mult = 0.22
rope_base = 10000.0
masked_score = -1e30

low = jnp.bfloat16
full = jnp.float32


def dot(spec, left, right):
    return jnp.einsum(spec, left, right, preferred_element_type=full)


def rms_norm(values, gain_vec):
    inv_rms = lax.rsqrt(jnp.mean(values * values, axis=-1, keepdims=True) + epsilon)
    return values * inv_rms * gain_vec


def rope_tables(positions, head_dim):
    half_dim = head_dim // 2
    frequency = rope_base ** (-(2.0 * jnp.arange(half_dim, dtype=full)) / head_dim)
    angles = positions[:, None] * frequency[None, :]
    return (jnp.cos(angles), jnp.sin(angles))


def rotate(values, cosine, sine_vals):
    half_dim = values.shape[-1] // 2
    front_half = values[..., :half_dim]
    back_half = values[..., half_dim:]
    return jnp.concatenate(
        [front_half * cosine - back_half * sine_vals, back_half * cosine + front_half * sine_vals],
        axis=-1,
    )


def block_ids(lengths_row, positions):
    block_ends = jnp.cumsum(lengths_row)
    return jnp.sum((positions[:, None] >= block_ends[None, :]).astype(jnp.int32), axis=1)


def swiglu(gate_act, up_act):
    return jax.nn.silu(gate_act) * up_act


def line_gather(block):
    n = lax.axis_size("seq")
    me = lax.axis_index("seq")
    rights, lefts = [block], [block]
    for k in range(1, n):
        rights.append(lax.ppermute(rights[-1], "seq", [(i, i + 1) for i in range(k - 1, n - 1)]))
        lefts.append(lax.ppermute(lefts[-1], "seq", [(i, i - 1) for i in range(1, n - k + 1)]))
    return [block] + [jnp.where(me >= k, rights[k], lefts[n - k]) for k in range(1, n)]


def line_scatter(parts):
    n = lax.axis_size("seq")
    right = left = None
    for k in range(n - 1, 0, -1):
        to_right, to_left = parts[n - k], parts[k]
        if right is not None:
            to_right = to_right + right.astype(full)
            to_left = to_left + left.astype(full)
        right = lax.ppermute(to_right.astype(low), "seq", [(i, i + 1) for i in range(n - k)])
        left = lax.ppermute(to_left.astype(low), "seq", [(i, i - 1) for i in range(k, n)])
    return parts[0] + (right.astype(full) + left.astype(full))


def by_place(blocks):
    n = lax.axis_size("seq")
    me = lax.axis_index("seq")
    return jnp.stack(blocks)[(me - jnp.arange(n)) % n]


def attention_forward(query, key, value, blocks, query_rows):
    seq_len = key.shape[0]
    attended_list = []
    lse_list = []
    for row_start in range(0, seq_len, query_rows):
        row_stop = min(seq_len, row_start + query_rows + BLOCK)
        scores = masked_scores(query, key, blocks, row_start, row_stop, query_rows)
        row_peak = jnp.max(scores, axis=-1, keepdims=True)
        exp_rows = jnp.exp(scores - row_peak)
        exp_sum = jnp.sum(exp_rows, axis=-1, keepdims=True)
        prob_low = (exp_rows / exp_sum).astype(low)
        attended_list.append(dot("ghqk,kgd->qghd", prob_low, value[:row_stop]))
        lse_list.append(row_peak + jnp.log(exp_sum))
    return jnp.concatenate(attended_list, axis=0).astype(low), lse_list


def masked_scores(query, key, blocks, row_start, row_stop, query_rows):
    query_blk = query[row_start : row_start + query_rows]
    scores = dot("qghd,kgd->ghqk", query_blk, key[:row_stop]) * attn_mult
    allowed = blocks[None, :row_stop] <= blocks[row_start : row_start + query_rows, None]
    return jnp.where(allowed, scores, masked_score)


def attention_backward(query, key, value, blocks, lse_list, d_heads, query_rows):
    seq_len, kv_here = key.shape[:2]
    key_grad = jnp.zeros((seq_len, kv_here, HEAD_DIM), full)
    value_grad = jnp.zeros((seq_len, kv_here, HEAD_DIM), full)
    query_grads = []
    for block_number, row_start in enumerate(range(0, seq_len, query_rows)):
        row_stop = min(seq_len, row_start + query_rows + BLOCK)
        scores = masked_scores(query, key, blocks, row_start, row_stop, query_rows)
        prob_rows = jnp.exp(scores - lse_list[block_number])
        d_out_blk = d_heads[row_start : row_start + query_rows]
        d_probs = dot("qghd,kgd->ghqk", d_out_blk, value[:row_stop])
        row_delta = jnp.sum(prob_rows * d_probs, axis=-1, keepdims=True)
        d_scores = (prob_rows * (d_probs - row_delta)).astype(low)
        query_blk = query[row_start : row_start + query_rows]
        query_grads.append(dot("ghqk,kgd->qghd", d_scores, key[:row_stop]) * attn_mult)
        key_grad = key_grad.at[:row_stop].add(
            dot("ghqk,qghd->kgd", d_scores, query_blk) * attn_mult
        )
        value_grad = value_grad.at[:row_stop].add(
            dot("ghqk,qghd->kgd", prob_rows.astype(low), d_out_blk)
        )
    return jnp.concatenate(query_grads, axis=0), key_grad, value_grad


def shards(
    inputs,
    teacher,
    routes,
    valid_mask,
    block_lengths,
    gain_one,
    w_qkv,
    w_out,
    gain_two,
    w_router,
    w_gate,
    w_up,
    w_down,
):
    seq_devs = lax.axis_size("seq")
    me = lax.axis_index("seq")
    seqs_here, shard_len, width = inputs.shape
    assert seqs_here == 1
    seq_len = shard_len * seq_devs
    tokens_all = lax.axis_size("fsdp") * seq_len
    kv_here = KV_HEADS // seq_devs
    heads_w = kv_here * GROUP * HEAD_DIM
    group_w = kv_here * (GROUP + 2) * HEAD_DIM
    experts_here = w_gate.shape[0]
    expert_total = experts_here * seq_devs
    top_count = routes.shape[2]
    capacity = 3 * shard_len * top_count // (2 * expert_total)
    slots = -(-capacity // 16) * 16
    x_low = inputs.reshape(shard_len, width)

    own_qkv = lax.dynamic_slice_in_dim(w_qkv, me * group_w, group_w, 1)
    small = jnp.concatenate(
        [gain_one[:, None], gain_two[:, None], w_router], axis=1
    )
    small = lax.all_gather(small, "fsdp", axis=0, tiled=True)
    full_qkv = lax.all_gather(own_qkv, "fsdp", axis=0, tiled=True)
    full_out = lax.all_gather(w_out, "fsdp", axis=0, tiled=True)
    full_gate = lax.all_gather(w_gate, "fsdp", axis=1, tiled=True)
    full_up = lax.all_gather(w_up, "fsdp", axis=1, tiled=True)
    full_down = lax.all_gather(w_down, "fsdp", axis=1, tiled=True)
    full_g1 = small[:, 0].astype(full)
    full_g2 = small[:, 1].astype(full)
    full_router = small[:, 2:]
    valid_rows = valid_mask.reshape(shard_len).astype(full)
    valid_count = lax.psum(jnp.sum(valid_rows), ("fsdp", "seq"))

    routes_all = lax.all_gather(routes.reshape(shard_len, top_count), "seq", axis=0)
    routes_rel = routes_all[(me - jnp.arange(seq_devs)) % seq_devs]
    expert_ids = jnp.arange(expert_total, dtype=jnp.int32)
    member = jnp.any(routes_rel[:, :, :, None] == expert_ids, axis=2)
    own_member = lax.dynamic_slice_in_dim(member, me * experts_here, experts_here, 2)
    own_member = jnp.transpose(own_member, (2, 0, 1)).astype(low)
    earlier = jnp.arange(shard_len)[:, None] < jnp.arange(shard_len)[None, :]
    slot_of = dot("ent,tu->enu", own_member, earlier.astype(low)).astype(jnp.int32)
    slot_of = jnp.where(own_member > 0, slot_of, -1)
    onehot = slot_of[:, :, None, :] == jnp.arange(slots, dtype=jnp.int32)[None, None, :, None]
    pick = onehot.astype(low)

    x_all = by_place(line_gather(x_low)).reshape(seq_len, width).astype(full)
    normed_one = rms_norm(x_all, full_g1).astype(low)
    qkv_rows = dot("td,dc->tc", normed_one, full_qkv)
    qkv_rows = qkv_rows.reshape(seq_len, kv_here, GROUP + 2, HEAD_DIM)
    positions = jnp.arange(seq_len, dtype=jnp.int32)
    cosine, sine_vals = rope_tables(positions.astype(full), HEAD_DIM)
    cos_rows = cosine[:, None, None, :]
    sin_rows = sine_vals[:, None, None, :]
    turned = rotate(qkv_rows[:, :, : GROUP + 1], cos_rows, sin_rows).astype(low)
    query = turned[:, :, :GROUP]
    key = turned[:, :, GROUP]
    value = qkv_rows[:, :, GROUP + 1].astype(low)
    blocks = block_ids(block_lengths[0], positions)
    query_rows = min(512, seq_len)
    attended, lse_list = attention_forward(query, key, value, blocks, query_rows)
    attended = attended.reshape(seq_devs, shard_len, heads_w)
    attn_rows = lax.all_to_all(attended, "seq", split_axis=0, concat_axis=0, tiled=True)
    out_rows = full_out.reshape(seq_devs, heads_w, width)
    projected = dot("gtk,gkd->td", attn_rows, out_rows)
    hidden = x_low.astype(full) + resid_mult * projected
    normed_two, norm_two_pull = jax.vjp(rms_norm, hidden, full_g2)

    tokens = jnp.stack(line_gather(normed_two.astype(low)))
    logits = dot("ntd,de->nte", tokens, full_router)
    chosen = jnp.where(member, logits, masked_score)
    gate_exp = jnp.where(member, jnp.exp(chosen - jnp.max(chosen, axis=2, keepdims=True)), 0.0)
    gates = gate_exp / jnp.sum(gate_exp, axis=2, keepdims=True)
    own_gates = lax.dynamic_slice_in_dim(gates, me * experts_here, experts_here, 2)
    slot_gates = jnp.sum(
        onehot.astype(full) * jnp.transpose(own_gates, (2, 0, 1))[:, :, None, :], axis=3
    )
    expert_in = dot("enct,ntd->encd", pick, tokens).astype(low)
    expert_in = expert_in.reshape(experts_here, seq_devs * slots, width)
    gate_act = dot("erd,edf->erf", expert_in, full_gate)
    up_act = dot("erd,edf->erf", expert_in, full_up)
    act_out, act_pull = jax.vjp(swiglu, gate_act, up_act)
    act_low = act_out.astype(low)
    expert_out = dot("erf,efd->erd", act_low, full_down).astype(low)
    expert_out = expert_out.reshape(experts_here, seq_devs, slots, width)
    gated_pick = pick * slot_gates.astype(low)[..., None]
    mix_parts = dot("enct,encd->ntd", gated_pick, expert_out)
    mixture = line_scatter([mix_parts[k] for k in range(seq_devs)])
    output_f32 = hidden + resid_mult * mixture
    activations = output_f32.astype(low).reshape(1, shard_len, width)
    error_rows = output_f32 - teacher.astype(full).reshape(shard_len, width)
    weighted = valid_rows[:, None] * error_rows
    squares = lax.psum(jnp.sum(weighted * error_rows), ("fsdp", "seq"))
    loss_value = squares / (valid_count * width)
    d_out = weighted * (tokens_all / valid_count)

    d_mix = resid_mult * d_out
    mix_dot = lax.all_gather(jnp.sum(d_mix * mixture, axis=1), "seq", axis=0)
    mix_dot = mix_dot[(me - jnp.arange(seq_devs)) % seq_devs]
    d_tokens = jnp.stack(line_gather(d_mix.astype(low)))
    d_rows = dot("enct,ntd->encd", pick, d_tokens).astype(low)
    d_rows = d_rows.reshape(experts_here, seq_devs * slots, width)
    d_act_raw = dot("erd,efd->erf", d_rows, full_down)
    row_gates = slot_gates.reshape(experts_here, seq_devs * slots, 1)
    d_slot_gates = jnp.sum(d_act_raw * act_low.astype(full), axis=2)
    down_part = dot("erf,erd->efd", (act_low.astype(full) * row_gates).astype(low), d_rows)
    d_gate_act, d_up_act = act_pull(d_act_raw * row_gates)
    d_gate_low = d_gate_act.astype(low)
    d_up_low = d_up_act.astype(low)
    gate_part = dot("erd,erf->edf", expert_in, d_gate_low)
    up_part = dot("erd,erf->edf", expert_in, d_up_low)
    d_expert_in = dot("erf,edf->erd", d_gate_low, full_gate)
    d_expert_in = (d_expert_in + dot("erf,edf->erd", d_up_low, full_up)).astype(low)
    d_expert_in = d_expert_in.reshape(experts_here, seq_devs, slots, width)
    d_gates = jnp.sum(
        onehot.astype(full)
        * d_slot_gates.reshape(experts_here, seq_devs, slots)[..., None],
        axis=2,
    )
    d_gates = jnp.transpose(d_gates, (1, 2, 0))
    d_logits = (own_gates * (d_gates - mix_dot[:, :, None])).astype(low)
    own_router = lax.dynamic_slice_in_dim(full_router, me * experts_here, experts_here, 1)
    d_normed_parts = dot("enct,encd->ntd", pick, d_expert_in) + dot(
        "nte,de->ntd", d_logits, own_router
    )
    router_part = dot("ntd,nte->de", tokens, d_logits)
    d_normed_two = line_scatter([d_normed_parts[k] for k in range(seq_devs)])

    d_hidden_norm, gain_two_part = norm_two_pull(d_normed_two)
    d_hidden = d_out + d_hidden_norm
    d_proj = (resid_mult * d_hidden).astype(low)
    d_attended = dot("td,gkd->gtk", d_proj, out_rows).astype(low)
    d_heads = lax.all_to_all(d_attended, "seq", split_axis=0, concat_axis=0, tiled=True)
    out_part = dot("gtk,td->gkd", attn_rows, d_proj).astype(low).reshape(HEADS * HEAD_DIM, width)
    d_heads = d_heads.reshape(seq_len, kv_here, GROUP, HEAD_DIM)
    query_grad, key_grad, value_grad = attention_backward(
        query, key, value, blocks, lse_list, d_heads, query_rows
    )
    d_turned = jnp.concatenate([query_grad, key_grad[:, :, None]], axis=2).astype(low).astype(full)
    d_turned = rotate(d_turned, cos_rows, -sin_rows).astype(low)
    d_qkv = jnp.concatenate([d_turned, value_grad[:, :, None].astype(low)], axis=2)
    d_qkv = d_qkv.reshape(seq_len, group_w)
    qkv_part = dot("td,tc->dc", normed_one, d_qkv).astype(low)
    d_normed_parts = dot("tc,dc->td", d_qkv, full_qkv).reshape(seq_devs, shard_len, width)
    d_normed_parts = d_normed_parts[(me - jnp.arange(seq_devs)) % seq_devs]
    d_normed_one = line_scatter([d_normed_parts[k] for k in range(seq_devs)])
    x_rows = x_low.astype(full)
    _, norm_one_pull = jax.vjp(lambda v: rms_norm(v, full_g1), x_rows)
    input_grad = (d_hidden + norm_one_pull(d_normed_one)[0]).reshape(1, shard_len, width)

    def rows_sum(part, dim):
        return lax.psum_scatter(part, "fsdp", scatter_dimension=dim, tiled=True)

    gate_grad = rows_sum(gate_part.astype(low), 1).astype(full)
    up_grad = rows_sum(up_part.astype(low), 1).astype(full)
    down_grad = rows_sum(down_part.astype(low), 1).astype(full)
    own_columns = jnp.zeros((width, expert_total), full)
    own_columns = lax.dynamic_update_slice_in_dim(
        own_columns, router_part, me * experts_here, 1
    )
    dense_part = jnp.concatenate(
        [out_part, own_columns.astype(low), gain_two_part[:, None].astype(low)], axis=1
    )
    dense_part = lax.psum(rows_sum(dense_part, 0), "seq").astype(full)
    out_grad = dense_part[:, :width]
    router_grad = dense_part[:, width : width + expert_total]
    gain_two_grad = dense_part[:, width + expert_total]
    qkv_grad = lax.all_gather(rows_sum(qkv_part, 0), "seq", axis=1, tiled=True).astype(full)
    gain_one_grad = jnp.sum(qkv_grad * w_qkv.astype(full), axis=1) / gain_one.astype(full)
    return (
        activations,
        loss_value,
        input_grad,
        gain_one_grad,
        qkv_grad,
        out_grad,
        gain_two_grad,
        router_grad,
        gate_grad,
        up_grad,
        down_grad,
    )


def solution(mesh):
    return jax.shard_map(
        shards,
        mesh=mesh,
        in_specs=(
            P("fsdp", "seq", None),
            P("fsdp", "seq", None),
            P("fsdp", "seq", None),
            P("fsdp", "seq"),
            P("fsdp", None),
            P("fsdp"),
            P("fsdp", None),
            P("fsdp", None),
            P("fsdp"),
            P("fsdp", None),
            P("seq", "fsdp", None),
            P("seq", "fsdp", None),
            P("seq", "fsdp", None),
        ),
        out_specs=(
            P("fsdp", "seq", None),
            P(),
            P("fsdp", "seq", None),
            P("fsdp"),
            P("fsdp", None),
            P("fsdp", None),
            P("fsdp"),
            P("fsdp", None),
            P("seq", "fsdp", None),
            P("seq", "fsdp", None),
            P("seq", "fsdp", None),
        ),
        check_vma=False,
    )
```

```python
import functools

import jax
import jax.numpy as jnp
from jax import lax
from jax.experimental import pallas as pl
from jax.experimental.pallas import tpu as pltpu
from jax.sharding import PartitionSpec as P

HEADS = 24
KV_HEADS = 8
HEAD_DIM = 64
BLOCK = 256
GROUP = 3
QKV_W = 2560


epsilon = 1e-06
attn_mult = 0.015625
resid_mult = 0.22
rope_base = 10000.0
masked_score = -1e30

low = jnp.bfloat16
full = jnp.float32


def dot(spec, left, right):
    return jnp.einsum(spec, left, right, preferred_element_type=full)


def rms_norm(values, gain_vec):
    inv_rms = lax.rsqrt(jnp.mean(values * values, axis=-1, keepdims=True) + epsilon)
    return values * inv_rms * gain_vec


def rope_tables(positions, head_dim):
    half_dim = head_dim // 2
    frequency = rope_base ** (-(2.0 * jnp.arange(half_dim, dtype=full)) / head_dim)
    angles = frequency[:, None] * positions[None, :]
    return (jnp.cos(angles), jnp.sin(angles))


def rotate(values, cosine, sine_vals):
    half_dim = values.shape[-2] // 2
    front_half = values[..., :half_dim, :]
    back_half = values[..., half_dim:, :]
    return jnp.concatenate(
        [front_half * cosine - back_half * sine_vals, back_half * cosine + front_half * sine_vals],
        axis=-2,
    )


def block_limits(lengths_row, positions):
    block_ends = jnp.cumsum(lengths_row)
    open_ends = jnp.where(block_ends[None, :] > positions[:, None], block_ends[None, :], positions.shape[0])
    return jnp.min(open_ends, axis=1).astype(jnp.int32)


def swiglu(gate_act, up_act):
    return jax.nn.silu(gate_act) * up_act


def line_gather(block):
    n = lax.axis_size("seq")
    me = lax.axis_index("seq")
    rights, lefts = [block], [block]
    for k in range(1, n):
        rights.append(lax.ppermute(rights[-1], "seq", [(i, i + 1) for i in range(k - 1, n - 1)]))
        lefts.append(lax.ppermute(lefts[-1], "seq", [(i, i - 1) for i in range(1, n - k + 1)]))
    return [block] + [jnp.where(me >= k, rights[k], lefts[n - k]) for k in range(1, n)]


def line_scatter(parts):
    n = lax.axis_size("seq")
    right = left = None
    for k in range(n - 1, 0, -1):
        to_right, to_left = parts[n - k], parts[k]
        if right is not None:
            to_right = to_right + right.astype(full)
            to_left = to_left + left.astype(full)
        right = lax.ppermute(to_right.astype(low), "seq", [(i, i + 1) for i in range(n - k)])
        left = lax.ppermute(to_left.astype(low), "seq", [(i, i - 1) for i in range(k, n)])
    return parts[0] + (right.astype(full) + left.astype(full))


def by_place(blocks):
    n = lax.axis_size("seq")
    me = lax.axis_index("seq")
    return jnp.stack(blocks)[(me - jnp.arange(n)) % n]


def nt(a, b):
    return lax.dot_general(a, b, (((1,), (1,)), ((), ())), preferred_element_type=full)

def nn(a, b):
    return lax.dot_general(a, b, (((1,), (0,)), ((), ())), preferred_element_type=full)

def beside(ref):
    return jnp.concatenate([ref[0, h] for h in range(GROUP)], axis=1)

def key_steps(i, seq_len, query_rows, key_rows):
    free = (i * query_rows) // key_rows
    need = ((i + 1) * query_rows + BLOCK - 1 + key_rows - 1) // key_rows
    return free, jnp.minimum(need, seq_len // key_rows)

def forward_kernel(seq_len, query_rows, key_rows, limit_ref, q_ref, k_ref, vt_ref, low_ref, out_ref, lse_ref):
    i = pl.program_id(1)
    qt = beside(q_ref)
    width = GROUP * query_rows
    limit = jnp.concatenate([limit_ref[...]] * GROUP, axis=1)

    def step(masked, j, carry):
        peak, total, acc = carry
        start = pl.multiple_of(j * key_rows, key_rows)
        s = nn(k_ref[0, pl.ds(start, key_rows), :], qt)
        if masked:
            place = start + lax.broadcasted_iota(jnp.int32, (key_rows, 1), 0)
            s = jnp.where(place < limit, s, masked_score)
        new_peak = jnp.maximum(peak, jnp.max(s, axis=0, keepdims=True))
        shrink = jnp.exp(peak - new_peak)
        p = jnp.exp(s - new_peak)
        total = shrink * total + jnp.sum(p, axis=0, keepdims=True)
        acc = shrink * acc + nn(vt_ref[0, :, pl.ds(start, key_rows)], p.astype(low))
        return new_peak, total, acc

    free, need = key_steps(i, seq_len, query_rows, key_rows)
    carry = (
        jnp.full((1, width), masked_score, full),
        jnp.zeros((1, width), full),
        jnp.zeros((HEAD_DIM, width), full),
    )
    carry = lax.fori_loop(0, free, lambda j, c: step(False, j, c), carry)
    peak, total, acc = lax.fori_loop(free, need, lambda j, c: step(True, j, c), carry)
    out = acc / total
    lse = peak + jnp.log(total)
    for h in range(GROUP):
        cols = slice(h * query_rows, (h + 1) * query_rows)
        out_ref[0, h] = out[:, cols]
        low_ref[0, pl.ds(h * HEAD_DIM, HEAD_DIM), :] = out[:, cols].astype(low)
        lse_ref[0, h] = lse[:, cols]

def attention_forward(qt, k_rows, vt, limit, shard_len):
    kv_here, _, _, seq_len = qt.shape
    query_rows = min(256, shard_len)
    key_rows = min(512, seq_len)
    per = shard_len // query_rows
    return pl.pallas_call(
        functools.partial(forward_kernel, seq_len, query_rows, key_rows),
        grid=(kv_here, seq_len // query_rows),
        in_specs=[
            pl.BlockSpec((1, query_rows), lambda g, i: (0, i)),
            pl.BlockSpec((1, GROUP, HEAD_DIM, query_rows), lambda g, i: (g, 0, 0, i)),
            pl.BlockSpec((1, seq_len, HEAD_DIM), lambda g, i: (g, 0, 0)),
            pl.BlockSpec((1, HEAD_DIM, seq_len), lambda g, i: (g, 0, 0)),
        ],
        out_specs=[
            pl.BlockSpec((1, GROUP * HEAD_DIM, query_rows), lambda g, i: (i // per, g, i % per)),
            pl.BlockSpec((1, GROUP, HEAD_DIM, query_rows), lambda g, i: (g, 0, 0, i)),
            pl.BlockSpec((1, GROUP, 1, query_rows), lambda g, i: (g, 0, 0, i)),
        ],
        out_shape=[
            jax.ShapeDtypeStruct((seq_len // shard_len, kv_here * GROUP * HEAD_DIM, shard_len), low),
            jax.ShapeDtypeStruct((kv_here, GROUP, HEAD_DIM, seq_len), full),
            jax.ShapeDtypeStruct((kv_here, GROUP, 1, seq_len), full),
        ],
        compiler_params=pltpu.CompilerParams(vmem_limit_bytes=40 * 2**20),
        name="attention_forward",
    )(limit, qt, k_rows, vt)

def backward_kernel(seq_len, query_rows, key_rows, limit_ref, q_ref, k_ref, v_ref, kt_ref, out_ref, lse_ref, dout_ref, dq_ref, dk_ref, dv_ref, dk_acc, dv_acc):
    i = pl.program_id(1)

    @pl.when(i == 0)
    def _():
        dk_acc[...] = jnp.zeros_like(dk_acc)
        dv_acc[...] = jnp.zeros_like(dv_acc)

    qt = beside(q_ref)
    limit = jnp.concatenate([limit_ref[...]] * GROUP, axis=1)
    dout = jnp.concatenate([dout_ref[0, pl.ds(h * HEAD_DIM, HEAD_DIM), :] for h in range(GROUP)], axis=1)
    delta = jnp.sum(dout.astype(full) * beside(out_ref), axis=0, keepdims=True)
    lse = beside(lse_ref)

    def step(masked, j, dq):
        start = pl.multiple_of(j * key_rows, key_rows)
        keys = pl.ds(start, key_rows)
        s = nn(k_ref[0, keys, :], qt)
        if masked:
            place = start + lax.broadcasted_iota(jnp.int32, (key_rows, 1), 0)
            s = jnp.where(place < limit, s, masked_score)
        p = jnp.exp(s - lse)
        dp = nn(v_ref[0, keys, :], dout)
        ds = (p * (dp - delta)).astype(low)
        dk_acc[:, keys] += nt(qt, ds)
        dv_acc[:, keys] += nt(dout, p.astype(low))
        return dq + nn(kt_ref[0, :, keys], ds)

    free, need = key_steps(i, seq_len, query_rows, key_rows)
    dq = jnp.zeros((HEAD_DIM, GROUP * query_rows), full)
    dq = lax.fori_loop(0, free, lambda j, c: step(False, j, c), dq)
    dq = lax.fori_loop(free, need, lambda j, c: step(True, j, c), dq) * attn_mult
    for h in range(GROUP):
        dq_ref[0, h] = dq[:, h * query_rows : (h + 1) * query_rows].astype(low)

    @pl.when(i == pl.num_programs(1) - 1)
    def _():
        dk_ref[0] = dk_acc[...].astype(low)
        dv_ref[0] = dv_acc[...].astype(low)

def attention_backward(qt, k_rows, v_rows, kt, limit, out, lse, d_out):
    kv_here, _, _, seq_len = qt.shape
    shard_len = d_out.shape[2]
    query_rows = min(256, shard_len)
    key_rows = min(512, seq_len)
    per = shard_len // query_rows
    quarter = lambda g, i: (g, 0, 0, i)
    whole = lambda g, i: (g, 0, 0)
    return pl.pallas_call(
        functools.partial(backward_kernel, seq_len, query_rows, key_rows),
        grid=(kv_here, seq_len // query_rows),
        in_specs=[
            pl.BlockSpec((1, query_rows), lambda g, i: (0, i)),
            pl.BlockSpec((1, GROUP, HEAD_DIM, query_rows), quarter),
            pl.BlockSpec((1, seq_len, HEAD_DIM), whole),
            pl.BlockSpec((1, seq_len, HEAD_DIM), whole),
            pl.BlockSpec((1, HEAD_DIM, seq_len), whole),
            pl.BlockSpec((1, GROUP, HEAD_DIM, query_rows), quarter),
            pl.BlockSpec((1, GROUP, 1, query_rows), quarter),
            pl.BlockSpec((1, GROUP * HEAD_DIM, query_rows), lambda g, i: (i // per, g, i % per)),
        ],
        out_specs=[
            pl.BlockSpec((1, GROUP, HEAD_DIM, query_rows), quarter),
            pl.BlockSpec((1, HEAD_DIM, seq_len), whole),
            pl.BlockSpec((1, HEAD_DIM, seq_len), whole),
        ],
        out_shape=[
            jax.ShapeDtypeStruct((kv_here, GROUP, HEAD_DIM, seq_len), low),
            jax.ShapeDtypeStruct((kv_here, HEAD_DIM, seq_len), low),
            jax.ShapeDtypeStruct((kv_here, HEAD_DIM, seq_len), low),
        ],
        scratch_shapes=[pltpu.VMEM((HEAD_DIM, seq_len), full), pltpu.VMEM((HEAD_DIM, seq_len), full)],
        compiler_params=pltpu.CompilerParams(vmem_limit_bytes=40 * 2**20),
        name="attention_backward",
    )(limit, qt, k_rows, v_rows, kt, out, lse, d_out)


def shards(
    inputs,
    teacher,
    routes,
    valid_mask,
    block_lengths,
    gain_one,
    w_qkv,
    w_out,
    gain_two,
    w_router,
    w_gate,
    w_up,
    w_down,
):
    seq_devs = lax.axis_size("seq")
    me = lax.axis_index("seq")
    seqs_here, shard_len, width = inputs.shape
    assert seqs_here == 1
    seq_len = shard_len * seq_devs
    tokens_all = lax.axis_size("fsdp") * seq_len
    kv_here = KV_HEADS // seq_devs
    heads_w = kv_here * GROUP * HEAD_DIM
    group_w = kv_here * (GROUP + 2) * HEAD_DIM
    experts_here = w_gate.shape[0]
    expert_total = experts_here * seq_devs
    top_count = routes.shape[2]
    capacity = 3 * shard_len * top_count // (2 * expert_total)
    slots = -(-capacity // 16) * 16
    x_low = inputs.reshape(shard_len, width)

    own_qkv = lax.dynamic_slice_in_dim(w_qkv, me * group_w, group_w, 1)
    small = jnp.concatenate(
        [gain_one[:, None], gain_two[:, None], w_router], axis=1
    )
    small = lax.all_gather(small, "fsdp", axis=0, tiled=True)
    full_qkv = lax.all_gather(own_qkv, "fsdp", axis=0, tiled=True)
    full_out = lax.all_gather(w_out, "fsdp", axis=0, tiled=True)
    full_gate = lax.all_gather(w_gate, "fsdp", axis=1, tiled=True)
    full_up = lax.all_gather(w_up, "fsdp", axis=1, tiled=True)
    full_down = lax.all_gather(w_down, "fsdp", axis=1, tiled=True)
    full_g1 = small[:, 0].astype(full)
    full_g2 = small[:, 1].astype(full)
    full_router = small[:, 2:]
    valid_rows = valid_mask.reshape(shard_len).astype(full)
    valid_count = lax.psum(jnp.sum(valid_rows), ("fsdp", "seq"))

    routes_rel = jnp.stack(line_gather(routes.reshape(shard_len, top_count).T))
    routes_rel = jnp.swapaxes(routes_rel, 1, 2)
    expert_ids = jnp.arange(expert_total, dtype=jnp.int32)
    member = jnp.any(routes_rel[:, :, :, None] == expert_ids, axis=2)
    own_member = lax.dynamic_slice_in_dim(member, me * experts_here, experts_here, 2)
    own_member = jnp.transpose(own_member, (2, 0, 1)).astype(low)
    earlier = jnp.arange(shard_len)[:, None] < jnp.arange(shard_len)[None, :]
    slot_of = dot("ent,tu->enu", own_member, earlier.astype(low)).astype(jnp.int32)
    slot_of = jnp.where(own_member > 0, slot_of, -1)
    onehot = slot_of[:, :, None, :] == jnp.arange(slots, dtype=jnp.int32)[None, None, :, None]
    pick = onehot.astype(low)

    x_all = by_place(line_gather(x_low)).reshape(seq_len, width)
    x_all, valid_count = lax.optimization_barrier((x_all, valid_count))
    normed_one = rms_norm(x_all.astype(full), full_g1).astype(low)
    qkv_rows = dot("td,dc->ct", normed_one, full_qkv)
    qkv_rows = qkv_rows.reshape(kv_here, GROUP + 2, HEAD_DIM, seq_len)
    positions = jnp.arange(seq_len, dtype=jnp.int32)
    cosine, sine_vals = rope_tables(positions.astype(full), HEAD_DIM)
    turned = rotate(qkv_rows[:, : GROUP + 1], cosine, sine_vals).astype(low)
    query = turned[:, :GROUP] * jnp.asarray(attn_mult, low)
    key = turned[:, GROUP]
    value = qkv_rows[:, GROUP + 1].astype(low)
    key_rows = jnp.swapaxes(key, 1, 2)
    value_rows = jnp.swapaxes(value, 1, 2)
    limit = block_limits(block_lengths[0], positions)[None]
    attended, out_heads, lse = attention_forward(query, key_rows, value, limit, shard_len)
    attn_rows = lax.all_to_all(attended, "seq", split_axis=0, concat_axis=0, tiled=True)
    attn_rows = attn_rows.reshape(HEADS * HEAD_DIM, shard_len)
    projected = dot("kt,kd->td", attn_rows, full_out)
    hidden = x_low.astype(full) + resid_mult * projected
    normed_two, norm_two_pull = jax.vjp(rms_norm, hidden, full_g2)

    tokens = jnp.stack(line_gather(normed_two.astype(low)))
    logits = dot("ntd,de->nte", tokens, full_router)
    chosen = jnp.where(member, logits, masked_score)
    gate_exp = jnp.where(member, jnp.exp(chosen - jnp.max(chosen, axis=2, keepdims=True)), 0.0)
    gates = gate_exp / jnp.sum(gate_exp, axis=2, keepdims=True)
    own_gates = lax.dynamic_slice_in_dim(gates, me * experts_here, experts_here, 2)
    slot_gates = jnp.sum(
        onehot.astype(full) * jnp.transpose(own_gates, (2, 0, 1))[:, :, None, :], axis=3
    )
    expert_in = dot("enct,ntd->encd", pick, tokens).astype(low)
    expert_in = expert_in.reshape(experts_here, seq_devs * slots, width)
    gate_act = dot("erd,edf->erf", expert_in, full_gate)
    up_act = dot("erd,edf->erf", expert_in, full_up)
    act_out, act_pull = jax.vjp(swiglu, gate_act, up_act)
    act_low = act_out.astype(low)
    expert_out = dot("erf,efd->erd", act_low, full_down).astype(low)
    expert_out = expert_out.reshape(experts_here, seq_devs, slots, width)
    gated_pick = pick * slot_gates.astype(low)[..., None]
    mix_parts = dot("enct,encd->ntd", gated_pick, expert_out)
    mixture = line_scatter([mix_parts[k] for k in range(seq_devs)])
    output_f32 = hidden + resid_mult * mixture
    activations = output_f32.astype(low).reshape(1, shard_len, width)
    error_rows = output_f32 - teacher.astype(full).reshape(shard_len, width)
    weighted = valid_rows[:, None] * error_rows
    squares = jnp.sum(weighted * error_rows)
    d_out = weighted * (tokens_all / valid_count)

    d_mix = resid_mult * d_out
    mix_dot = jnp.stack(line_gather(jnp.sum(d_mix * mixture, axis=1)))
    d_tokens = jnp.stack(line_gather(d_mix.astype(low)))
    d_rows = dot("enct,ntd->encd", pick, d_tokens).astype(low)
    d_rows = d_rows.reshape(experts_here, seq_devs * slots, width)
    d_act_raw = dot("erd,efd->erf", d_rows, full_down)
    row_gates = slot_gates.reshape(experts_here, seq_devs * slots, 1)
    d_slot_gates = jnp.sum(d_act_raw * act_low.astype(full), axis=2)
    down_part = dot("erf,erd->efd", (act_low.astype(full) * row_gates).astype(low), d_rows)
    d_gate_act, d_up_act = act_pull(d_act_raw * row_gates)
    d_gate_low = d_gate_act.astype(low)
    d_up_low = d_up_act.astype(low)
    gate_part = dot("erd,erf->edf", expert_in, d_gate_low)
    up_part = dot("erd,erf->edf", expert_in, d_up_low)
    d_expert_in = dot("erf,edf->erd", d_gate_low, full_gate)
    d_expert_in = (d_expert_in + dot("erf,edf->erd", d_up_low, full_up)).astype(low)
    d_expert_in = d_expert_in.reshape(experts_here, seq_devs, slots, width)
    d_gates = jnp.sum(
        onehot.astype(full)
        * d_slot_gates.reshape(experts_here, seq_devs, slots)[..., None],
        axis=2,
    )
    d_gates = jnp.transpose(d_gates, (1, 2, 0))
    d_logits = (own_gates * (d_gates - mix_dot[:, :, None])).astype(low)
    own_router = lax.dynamic_slice_in_dim(full_router, me * experts_here, experts_here, 1)
    d_normed_parts = dot("enct,encd->ntd", pick, d_expert_in) + dot(
        "nte,de->ntd", d_logits, own_router
    )
    router_part = dot("ntd,nte->de", tokens, d_logits)
    d_normed_two = line_scatter([d_normed_parts[k] for k in range(seq_devs)])
    d_normed_two, gate_part, up_part, down_part = lax.optimization_barrier(
        (d_normed_two, gate_part.astype(low), up_part.astype(low), down_part.astype(low))
    )
    gate_part, up_part, down_part = (
        lax.psum_scatter(part, "fsdp", scatter_dimension=1, tiled=True)
        for part in (gate_part, up_part, down_part)
    )

    d_hidden_norm, gain_two_part = norm_two_pull(d_normed_two)
    d_hidden = d_out + d_hidden_norm
    d_proj = (resid_mult * d_hidden).astype(low)
    d_attended = dot("kd,td->kt", full_out, d_proj).astype(low)
    d_heads = lax.all_to_all(
        d_attended.reshape(seq_devs, heads_w, shard_len), "seq", split_axis=0, concat_axis=0, tiled=True
    )
    out_part = dot("kt,td->kd", attn_rows, d_proj).astype(low)
    query_grad, key_grad, value_grad = attention_backward(
        query, key_rows, value_rows, key, limit, out_heads, lse, d_heads
    )
    d_turned = jnp.concatenate([query_grad, key_grad[:, None]], axis=1).astype(full)
    d_turned = rotate(d_turned, cosine, -sine_vals).astype(low)
    d_qkv = jnp.concatenate([d_turned, value_grad[:, None]], axis=1).reshape(group_w, seq_len)
    qkv_part = dot("td,ct->dc", normed_one, d_qkv).astype(low)
    d_normed_parts = dot("ct,dc->td", d_qkv, full_qkv).reshape(seq_devs, shard_len, width)
    d_normed_parts = d_normed_parts[(me - jnp.arange(seq_devs)) % seq_devs]
    d_normed_one = line_scatter([d_normed_parts[k] for k in range(seq_devs)])
    x_rows = x_low.astype(full)
    _, norm_one_pull = jax.vjp(lambda v: rms_norm(v, full_g1), x_rows)
    input_grad = (d_hidden + norm_one_pull(d_normed_one)[0]).reshape(1, shard_len, width)

    def rows_sum(part):
        return lax.psum_scatter(part, "fsdp", scatter_dimension=0, tiled=True)

    gate_grad = gate_part.astype(full)
    up_grad = up_part.astype(full)
    down_grad = down_part.astype(full)
    own_columns = jnp.zeros((width, expert_total), full)
    own_columns = lax.dynamic_update_slice_in_dim(
        own_columns, router_part, me * experts_here, 1
    )
    dense_part = jnp.concatenate(
        [out_part, own_columns.astype(low), gain_two_part[:, None].astype(low)], axis=1
    )
    dense_part = lax.psum(rows_sum(dense_part), "seq").astype(full)
    out_grad = dense_part[:, :width]
    router_grad = dense_part[:, width : width + expert_total]
    gain_two_grad = dense_part[:, width + expert_total]
    qkv_grad = lax.all_gather(rows_sum(qkv_part), "seq", axis=1, tiled=True).astype(full)
    gain_one_grad = jnp.sum(qkv_grad * w_qkv.astype(full), axis=1) / gain_one.astype(full)
    squares, input_grad = lax.optimization_barrier((squares, input_grad))
    loss_value = lax.psum(squares, ("fsdp", "seq")) / (valid_count * width)
    return (
        activations,
        loss_value,
        input_grad,
        gain_one_grad,
        qkv_grad,
        out_grad,
        gain_two_grad,
        router_grad,
        gate_grad,
        up_grad,
        down_grad,
    )


def solution(mesh):
    return jax.shard_map(
        shards,
        mesh=mesh,
        in_specs=(
            P("fsdp", "seq", None),
            P("fsdp", "seq", None),
            P("fsdp", "seq", None),
            P("fsdp", "seq"),
            P("fsdp", None),
            P("fsdp"),
            P("fsdp", None),
            P("fsdp", None),
            P("fsdp"),
            P("fsdp", None),
            P("seq", "fsdp", None),
            P("seq", "fsdp", None),
            P("seq", "fsdp", None),
        ),
        out_specs=(
            P("fsdp", "seq", None),
            P(),
            P("fsdp", "seq", None),
            P("fsdp"),
            P("fsdp", None),
            P("fsdp", None),
            P("fsdp"),
            P("fsdp", None),
            P("seq", "fsdp", None),
            P("seq", "fsdp", None),
            P("seq", "fsdp", None),
        ),
        check_vma=False,
    )
```

```python
import functools

import jax
import jax.numpy as jnp
from jax import lax
from jax.experimental import pallas as pl
from jax.experimental.pallas import tpu as pltpu
from jax.sharding import PartitionSpec as P

HEADS = 24
KV_HEADS = 8
HEAD_DIM = 64
BLOCK = 256
GROUP = 3
QKV_W = 2560


epsilon = 1e-06
attn_mult = 0.015625
resid_mult = 0.22
rope_base = 10000.0
masked_score = -1e30

low = jnp.bfloat16
full = jnp.float32


def dot(spec, left, right):
    return jnp.einsum(spec, left, right, preferred_element_type=full)


def rms_norm(values, gain_vec):
    inv_rms = lax.rsqrt(jnp.mean(values * values, axis=-1, keepdims=True) + epsilon)
    return values * inv_rms * gain_vec


def rope_tables(positions, head_dim):
    half_dim = head_dim // 2
    frequency = rope_base ** (-(2.0 * jnp.arange(half_dim, dtype=full)) / head_dim)
    angles = frequency[:, None] * positions[None, :]
    return (jnp.cos(angles), jnp.sin(angles))


def rotate(values, cosine, sine_vals):
    half_dim = values.shape[-2] // 2
    front_half = values[..., :half_dim, :]
    back_half = values[..., half_dim:, :]
    return jnp.concatenate(
        [front_half * cosine - back_half * sine_vals, back_half * cosine + front_half * sine_vals],
        axis=-2,
    )


def block_limits(lengths_row, positions):
    block_ends = jnp.cumsum(lengths_row)
    open_ends = jnp.where(block_ends[None, :] > positions[:, None], block_ends[None, :], positions.shape[0])
    return jnp.min(open_ends, axis=1).astype(jnp.int32)


def line_gather(block):
    n = lax.axis_size("seq")
    me = lax.axis_index("seq")
    rights, lefts = [block], [block]
    for k in range(1, n):
        rights.append(lax.ppermute(rights[-1], "seq", [(i, i + 1) for i in range(k - 1, n - 1)]))
        lefts.append(lax.ppermute(lefts[-1], "seq", [(i, i - 1) for i in range(1, n - k + 1)]))
    return [block] + [jnp.where(me >= k, rights[k], lefts[n - k]) for k in range(1, n)]


def line_scatter(parts):
    n = lax.axis_size("seq")
    right = left = None
    for k in range(n - 1, 0, -1):
        to_right, to_left = parts[n - k], parts[k]
        if right is not None:
            to_right = to_right + right.astype(full)
            to_left = to_left + left.astype(full)
        right = lax.ppermute(to_right.astype(low), "seq", [(i, i + 1) for i in range(n - k)])
        left = lax.ppermute(to_left.astype(low), "seq", [(i, i - 1) for i in range(k, n)])
    return parts[0] + (right.astype(full) + left.astype(full))


def by_place(blocks):
    n = lax.axis_size("seq")
    me = lax.axis_index("seq")
    placed = jnp.zeros((n,) + blocks[0].shape, blocks[0].dtype)
    for k, block in enumerate(blocks):
        placed = lax.dynamic_update_index_in_dim(placed, block, (me - k) % n, 0)
    return placed


def from_place(placed):
    n = lax.axis_size("seq")
    me = lax.axis_index("seq")
    return [lax.dynamic_index_in_dim(placed, (me - k) % n, 0, keepdims=False) for k in range(n)]


def swap(value, axis, bit):
    return lax.ppermute(value, axis, [(i, i ^ bit) for i in range(lax.axis_size(axis))])


def total(value, *axes):
    for axis in axes:
        for step in range(lax.axis_size(axis).bit_length() - 1):
            value = value + swap(value, axis, 1 << step)
    return value


def halving_bits():
    bits = [1 << step for step in range(lax.axis_size("fsdp").bit_length() - 1)]
    return tuple(bits), tuple(bits[:1] + bits[:0:-1])


def halving_sum(keep, send, bits):
    for bit in bits:
        here = swap(send, "fsdp", bit)
        half = keep.shape[0] // 2
        if half == 0:
            return keep[0].astype(full) + here[0].astype(full)
        send = (keep[half:].astype(full) + here[half:].astype(full)).astype(low)
        keep = (keep[:half].astype(full) + here[:half].astype(full)).astype(low)


def rows_sum(part, bits):
    devs = lax.axis_size("fsdp")
    order = lax.axis_index("fsdp") ^ jnp.array(halving_masks(bits), jnp.int32)
    blocks = part.reshape(devs, part.shape[0] // devs, part.shape[1])[order]
    return halving_sum(blocks[: devs // 2], blocks[devs // 2 :], bits)


def nt(a, b):
    return lax.dot_general(a, b, (((1,), (1,)), ((), ())), preferred_element_type=full)

def nn(a, b):
    return lax.dot_general(a, b, (((1,), (0,)), ((), ())), preferred_element_type=full)

def tn(a, b):
    return lax.dot_general(a, b, (((0,), (0,)), ((), ())), preferred_element_type=full)


def beside(ref):
    return jnp.concatenate([ref[0, h] for h in range(GROUP)], axis=1)

def key_steps(i, seq_len, query_rows, key_rows):
    free = (i * query_rows) // key_rows
    need = ((i + 1) * query_rows + BLOCK - 1 + key_rows - 1) // key_rows
    return free, jnp.minimum(need, seq_len // key_rows)

def forward_kernel(seq_len, query_rows, key_rows, limit_ref, q_ref, k_ref, vt_ref, low_ref, out_ref, lse_ref):
    i = pl.program_id(1)
    qt = beside(q_ref)
    width = GROUP * query_rows
    limit = jnp.concatenate([limit_ref[...]] * GROUP, axis=1)

    def step(masked, j, carry):
        peak, total, acc = carry
        start = pl.multiple_of(j * key_rows, key_rows)
        s = nn(k_ref[0, pl.ds(start, key_rows), :], qt)
        if masked:
            place = start + lax.broadcasted_iota(jnp.int32, (key_rows, 1), 0)
            s = jnp.where(place < limit, s, masked_score)
        new_peak = jnp.maximum(peak, jnp.max(s, axis=0, keepdims=True))
        shrink = jnp.exp(peak - new_peak)
        p = jnp.exp(s - new_peak)
        total = shrink * total + jnp.sum(p, axis=0, keepdims=True)
        acc = shrink * acc + nn(vt_ref[0, :, pl.ds(start, key_rows)], p.astype(low))
        return new_peak, total, acc

    free, need = key_steps(i, seq_len, query_rows, key_rows)
    carry = (
        jnp.full((1, width), masked_score, full),
        jnp.zeros((1, width), full),
        jnp.zeros((HEAD_DIM, width), full),
    )
    carry = lax.fori_loop(0, free, lambda j, c: step(False, j, c), carry)
    peak, total, acc = lax.fori_loop(free, need, lambda j, c: step(True, j, c), carry)
    out = acc / total
    lse = peak + jnp.log(total)
    for h in range(GROUP):
        cols = slice(h * query_rows, (h + 1) * query_rows)
        out_ref[0, h] = out[:, cols]
        low_ref[0, pl.ds(h * HEAD_DIM, HEAD_DIM), :] = out[:, cols].astype(low)
        lse_ref[0, h] = lse[:, cols]

def attention_forward(qt, k_rows, vt, limit, shard_len):
    kv_here, _, _, seq_len = qt.shape
    query_rows = min(256, shard_len)
    key_rows = min(512, seq_len)
    per = shard_len // query_rows
    return pl.pallas_call(
        functools.partial(forward_kernel, seq_len, query_rows, key_rows),
        grid=(kv_here, seq_len // query_rows),
        in_specs=[
            pl.BlockSpec((1, query_rows), lambda g, i: (0, i)),
            pl.BlockSpec((1, GROUP, HEAD_DIM, query_rows), lambda g, i: (g, 0, 0, i)),
            pl.BlockSpec((1, seq_len, HEAD_DIM), lambda g, i: (g, 0, 0)),
            pl.BlockSpec((1, HEAD_DIM, seq_len), lambda g, i: (g, 0, 0)),
        ],
        out_specs=[
            pl.BlockSpec((1, GROUP * HEAD_DIM, query_rows), lambda g, i: (i // per, g, i % per)),
            pl.BlockSpec((1, GROUP, HEAD_DIM, query_rows), lambda g, i: (g, 0, 0, i)),
            pl.BlockSpec((1, GROUP, 1, query_rows), lambda g, i: (g, 0, 0, i)),
        ],
        out_shape=[
            jax.ShapeDtypeStruct((seq_len // shard_len, kv_here * GROUP * HEAD_DIM, shard_len), low),
            jax.ShapeDtypeStruct((kv_here, GROUP, HEAD_DIM, seq_len), full),
            jax.ShapeDtypeStruct((kv_here, GROUP, 1, seq_len), full),
        ],
        compiler_params=vmem(40),
        name="attention_forward",
    )(limit, qt, k_rows, vt)

def backward_kernel(seq_len, query_rows, key_rows, limit_ref, q_ref, k_ref, v_ref, kt_ref, out_ref, lse_ref, dout_ref, dq_ref, dk_ref, dv_ref, dk_acc, dv_acc):
    i = pl.program_id(1)

    @pl.when(i == 0)
    def _():
        dk_acc[...] = jnp.zeros_like(dk_acc)
        dv_acc[...] = jnp.zeros_like(dv_acc)

    qt = beside(q_ref)
    limit = jnp.concatenate([limit_ref[...]] * GROUP, axis=1)
    dout = jnp.concatenate([dout_ref[0, pl.ds(h * HEAD_DIM, HEAD_DIM), :] for h in range(GROUP)], axis=1)
    delta = jnp.sum(dout.astype(full) * beside(out_ref), axis=0, keepdims=True)
    lse = beside(lse_ref)

    def step(masked, j, dq):
        start = pl.multiple_of(j * key_rows, key_rows)
        keys = pl.ds(start, key_rows)
        s = nn(k_ref[0, keys, :], qt)
        if masked:
            place = start + lax.broadcasted_iota(jnp.int32, (key_rows, 1), 0)
            s = jnp.where(place < limit, s, masked_score)
        p = jnp.exp(s - lse)
        dp = nn(v_ref[0, keys, :], dout)
        ds = (p * (dp - delta)).astype(low)
        dk_acc[:, keys] += nt(qt, ds)
        dv_acc[:, keys] += nt(dout, p.astype(low))
        return dq + nn(kt_ref[0, :, keys], ds)

    free, need = key_steps(i, seq_len, query_rows, key_rows)
    dq = jnp.zeros((HEAD_DIM, GROUP * query_rows), full)
    dq = lax.fori_loop(0, free, lambda j, c: step(False, j, c), dq)
    dq = lax.fori_loop(free, need, lambda j, c: step(True, j, c), dq) * attn_mult
    for h in range(GROUP):
        dq_ref[0, h] = dq[:, h * query_rows : (h + 1) * query_rows].astype(low)

    @pl.when(i == pl.num_programs(1) - 1)
    def _():
        dk_ref[0] = dk_acc[...].astype(low)
        dv_ref[0] = dv_acc[...].astype(low)

def attention_backward(qt, k_rows, v_rows, kt, limit, out, lse, d_out):
    kv_here, _, _, seq_len = qt.shape
    shard_len = d_out.shape[2]
    query_rows = min(256, shard_len)
    key_rows = min(512, seq_len)
    per = shard_len // query_rows
    quarter = lambda g, i: (g, 0, 0, i)
    whole = lambda g, i: (g, 0, 0)
    return pl.pallas_call(
        functools.partial(backward_kernel, seq_len, query_rows, key_rows),
        grid=(kv_here, seq_len // query_rows),
        in_specs=[
            pl.BlockSpec((1, query_rows), lambda g, i: (0, i)),
            pl.BlockSpec((1, GROUP, HEAD_DIM, query_rows), quarter),
            pl.BlockSpec((1, seq_len, HEAD_DIM), whole),
            pl.BlockSpec((1, seq_len, HEAD_DIM), whole),
            pl.BlockSpec((1, HEAD_DIM, seq_len), whole),
            pl.BlockSpec((1, GROUP, HEAD_DIM, query_rows), quarter),
            pl.BlockSpec((1, GROUP, 1, query_rows), quarter),
            pl.BlockSpec((1, GROUP * HEAD_DIM, query_rows), lambda g, i: (i // per, g, i % per)),
        ],
        out_specs=[
            pl.BlockSpec((1, GROUP, HEAD_DIM, query_rows), quarter),
            pl.BlockSpec((1, HEAD_DIM, seq_len), whole),
            pl.BlockSpec((1, HEAD_DIM, seq_len), whole),
        ],
        out_shape=[
            jax.ShapeDtypeStruct((kv_here, GROUP, HEAD_DIM, seq_len), low),
            jax.ShapeDtypeStruct((kv_here, HEAD_DIM, seq_len), low),
            jax.ShapeDtypeStruct((kv_here, HEAD_DIM, seq_len), low),
        ],
        scratch_shapes=[pltpu.VMEM((HEAD_DIM, seq_len), full), pltpu.VMEM((HEAD_DIM, seq_len), full)],
        compiler_params=vmem(40),
        name="attention_backward",
    )(limit, qt, k_rows, v_rows, kt, out, lse, d_out)


def vmem(mib):
    return pltpu.CompilerParams(vmem_limit_bytes=mib * 2**20)


def pick_kernel(slots, slot_ref, tok_ref, out_ref, pick_ref):
    experts, width = out_ref.shape[0], out_ref.shape[3]
    place = lax.broadcasted_iota(jnp.int32, (slots, 1), 0)
    for e in range(experts):
        pick_ref[e * slots : (e + 1) * slots, :] = (place == slot_ref[0, e : e + 1, :]).astype(low)
    for col in range(0, width, 256):
        rows = nn(pick_ref[...], tok_ref[0, :, col : col + 256]).astype(low)
        out_ref[:, 0, :, col : col + 256] = rows.reshape(experts, slots, 256)


def pick_rows(slot_of, tokens, slots):
    n, experts, shard_len = slot_of.shape
    width = tokens.shape[2]
    return pl.pallas_call(
        functools.partial(pick_kernel, slots),
        grid=(n,),
        in_specs=[
            pl.BlockSpec((1, experts, shard_len), lambda k: (k, 0, 0)),
            pl.BlockSpec((1, shard_len, width), lambda k: (k, 0, 0)),
        ],
        out_specs=pl.BlockSpec((experts, 1, slots, width), lambda k: (0, k, 0, 0)),
        out_shape=jax.ShapeDtypeStruct((experts, n, slots, width), low),
        scratch_shapes=[pltpu.VMEM((experts * slots, shard_len), low)],
        compiler_params=vmem(48),
        name="pick_rows",
    )(slot_of, tokens)


def put_kernel(slots, slot_ref, gate_ref, rows_ref, out_ref, pick_ref):
    experts, width = rows_ref.shape[0], rows_ref.shape[3]
    place = lax.broadcasted_iota(jnp.int32, (slots, 1), 0)
    for e in range(experts):
        put = jnp.where(place == slot_ref[0, e : e + 1, :], gate_ref[0, e : e + 1, :], 0.0)
        pick_ref[e * slots : (e + 1) * slots, :] = put.astype(low)
    for col in range(0, width, 256):
        rows = rows_ref[:, 0, :, col : col + 256].reshape(experts * slots, 256)
        out_ref[0, :, col : col + 256] = tn(pick_ref[...], rows).astype(low)


def put_rows(slot_of, gates, rows):
    n, experts, shard_len = slot_of.shape
    _, _, slots, width = rows.shape
    return pl.pallas_call(
        functools.partial(put_kernel, slots),
        grid=(n,),
        in_specs=[
            pl.BlockSpec((1, experts, shard_len), lambda k: (k, 0, 0)),
            pl.BlockSpec((1, experts, shard_len), lambda k: (k, 0, 0)),
            pl.BlockSpec((experts, 1, slots, width), lambda k: (0, k, 0, 0)),
        ],
        out_specs=pl.BlockSpec((1, shard_len, width), lambda k: (k, 0, 0)),
        out_shape=jax.ShapeDtypeStruct((n, shard_len, width), low),
        scratch_shapes=[pltpu.VMEM((experts * slots, shard_len), low)],
        compiler_params=vmem(48),
        name="put_rows",
    )(slot_of, gates, rows)


def experts_kernel(x_ref, wg_ref, wu_ref, wd_ref, g_ref, u_ref, y_ref):
    g = nn(x_ref[0], wg_ref[0])
    u = nn(x_ref[0], wu_ref[0])
    g_ref[0] = g.astype(low)
    u_ref[0] = u.astype(low)
    act = (g * jax.nn.sigmoid(g) * u).astype(low)
    y_ref[0] = nn(act, wd_ref[0]).astype(low)


def one(*shape):
    return pl.BlockSpec((1,) + shape, lambda e, *_: (e, 0, 0))


def experts_forward(rows, w_gate, w_up, w_down):
    experts, count, width = rows.shape
    hidden = w_gate.shape[2]
    return pl.pallas_call(
        experts_kernel,
        grid=(experts,),
        in_specs=[one(count, width), one(width, hidden), one(width, hidden), one(hidden, width)],
        out_specs=[one(count, hidden), one(count, hidden), one(count, width)],
        out_shape=[
            jax.ShapeDtypeStruct((experts, count, hidden), low),
            jax.ShapeDtypeStruct((experts, count, hidden), low),
            jax.ShapeDtypeStruct((experts, count, width), low),
        ],
        compiler_params=vmem(48),
        name="experts_forward",
    )(rows, w_gate, w_up, w_down)


def experts_back_kernel(
    d_ref, gate_ref, g_ref, u_ref, wg_ref, wu_ref, wd_ref, dx_ref, dgu_ref, act_ref, dot_ref
):
    hidden = g_ref.shape[2]
    d_act = nt(d_ref[0], wd_ref[0])
    g, u = g_ref[0].astype(full), u_ref[0].astype(full)
    gate = gate_ref[0]
    sig = jax.nn.sigmoid(g)
    silu = g * sig
    act = silu * u
    dot_ref[0] = jnp.sum(d_act * act, axis=1, keepdims=True)
    act_ref[0] = (act * gate).astype(low)
    d_act = d_act * gate
    d_g = (d_act * u * (sig + silu * (1.0 - sig))).astype(low)
    d_u = (d_act * silu).astype(low)
    dgu_ref[0, :, :hidden] = d_g
    dgu_ref[0, :, hidden:] = d_u
    dx_ref[0] = (nt(d_g, wg_ref[0]) + nt(d_u, wu_ref[0])).astype(low)


def experts_backward(d_rows, row_gates, g, u, w_gate, w_up, w_down):
    experts, count, width = d_rows.shape
    hidden = w_gate.shape[2]
    return pl.pallas_call(
        experts_back_kernel,
        grid=(experts,),
        in_specs=[
            one(count, width),
            one(count, 1),
            one(count, hidden),
            one(count, hidden),
            one(width, hidden),
            one(width, hidden),
            one(hidden, width),
        ],
        out_specs=[one(count, width), one(count, 2 * hidden), one(count, hidden), one(count, 1)],
        out_shape=[
            jax.ShapeDtypeStruct((experts, count, width), low),
            jax.ShapeDtypeStruct((experts, count, 2 * hidden), low),
            jax.ShapeDtypeStruct((experts, count, hidden), low),
            jax.ShapeDtypeStruct((experts, count, 1), full),
        ],
        compiler_params=vmem(56),
        name="experts_backward",
    )(d_rows, row_gates, g, u, w_gate, w_up, w_down)


def halving_masks(bits):
    masks = [0]
    for bit in reversed(bits):
        masks = masks + [mask ^ bit for mask in masks]
    return masks


def weight_grads_kernel(
    bits_a, bits_b, me_ref, x_ref, d_ref, dgu_ref, act_ref, *refs
):
    outs, (gu_acc, d_acc) = refs[:8], refs[8:]
    hidden, width = act_ref.shape[2], x_ref.shape[2]
    me = me_ref[0]
    gu_acc[...] = tn(x_ref[0], dgu_ref[0])
    d_acc[...] = tn(act_ref[0], d_ref[0])
    parts = (
        (gu_acc, slice(0, hidden), bits_a),
        (gu_acc, slice(hidden, 2 * hidden), bits_b),
        (d_acc, slice(0, width // 2), bits_a),
        (d_acc, slice(width // 2, width), bits_b),
    )
    for part, (acc, cols, bits) in enumerate(parts):
        keep, send = outs[2 * part], outs[2 * part + 1]
        rows = keep.shape[2]
        for place, mask in enumerate(halving_masks(bits)):
            start = pl.multiple_of((me ^ mask) * rows, rows)
            out = keep if place < keep.shape[0] else send
            out[place % keep.shape[0], 0] = acc[pl.ds(start, rows), cols].astype(low)


def weight_grads(me, rows, d_rows, d_gu, act, bits_a, bits_b):
    experts, count, width = rows.shape
    hidden = act.shape[2]
    devs = 2 ** len(bits_a)
    shapes = [(width // devs, hidden)] * 2 + [(hidden // devs, width // 2)] * 2
    out_specs, out_shape = [], []
    for shape in shapes:
        for _ in range(2):
            out_specs.append(pl.BlockSpec((devs // 2, 1) + shape, lambda e, *_: (0, e, 0, 0)))
            out_shape.append(jax.ShapeDtypeStruct((devs // 2, experts) + shape, low))
    outs = pl.pallas_call(
        functools.partial(weight_grads_kernel, bits_a, bits_b),
        grid_spec=pltpu.PrefetchScalarGridSpec(
            num_scalar_prefetch=1,
            grid=(experts,),
            in_specs=[one(count, width), one(count, width), one(count, 2 * hidden), one(count, hidden)],
            out_specs=out_specs,
            scratch_shapes=[pltpu.VMEM((width, 2 * hidden), full), pltpu.VMEM((hidden, width), full)],
        ),
        out_shape=out_shape,
        compiler_params=vmem(56),
        name="weight_grads",
    )(me, rows, d_rows, d_gu, act)
    return [(outs[i], outs[i + 1]) for i in range(0, 8, 2)]


def shards(
    inputs,
    teacher,
    routes,
    valid_mask,
    block_lengths,
    gain_one,
    w_qkv,
    w_out,
    gain_two,
    w_router,
    w_gate,
    w_up,
    w_down,
):
    seq_devs = lax.axis_size("seq")
    me = lax.axis_index("seq")
    seqs_here, shard_len, width = inputs.shape
    assert seqs_here == 1
    seq_len = shard_len * seq_devs
    tokens_all = lax.axis_size("fsdp") * seq_len
    kv_here = KV_HEADS // seq_devs
    heads_w = kv_here * GROUP * HEAD_DIM
    group_w = kv_here * (GROUP + 2) * HEAD_DIM
    experts_here = w_gate.shape[0]
    expert_total = experts_here * seq_devs
    top_count = routes.shape[2]
    capacity = 3 * shard_len * top_count // (2 * expert_total)
    slots = -(-capacity // 16) * 16
    x_low = inputs.reshape(shard_len, width)

    own_qkv = lax.dynamic_slice_in_dim(w_qkv, me * group_w, group_w, 1)
    small = jnp.concatenate(
        [gain_one[:, None], gain_two[:, None], w_router], axis=1
    )
    small = lax.all_gather(small, "fsdp", axis=0, tiled=True)
    full_qkv = lax.all_gather(own_qkv, "fsdp", axis=0, tiled=True)
    full_out = lax.all_gather(w_out, "fsdp", axis=0, tiled=True)
    full_gate = lax.all_gather(w_gate, "fsdp", axis=1, tiled=True)
    full_up = lax.all_gather(w_up, "fsdp", axis=1, tiled=True)
    full_down = lax.all_gather(w_down, "fsdp", axis=1, tiled=True)
    full_g1 = small[:, 0].astype(full)
    full_g2 = small[:, 1].astype(full)
    full_router = small[:, 2:]
    valid_rows = valid_mask.reshape(shard_len).astype(full)

    routes_low = jnp.concatenate([routes.reshape(shard_len, top_count).T, valid_mask], axis=0)
    routes_rel = jnp.stack(line_gather(routes_low))
    valid_count = total(jnp.sum(routes_rel[:, top_count]).astype(full).reshape(1, 1), "fsdp")[0, 0]
    expert_ids = jnp.arange(expert_total, dtype=jnp.int32)
    member = jnp.any(routes_rel[:, :top_count, None, :] == expert_ids[:, None], axis=1)
    own_member = lax.dynamic_slice_in_dim(member, me * experts_here, experts_here, 1)
    earlier = jnp.arange(shard_len)[:, None] < jnp.arange(shard_len)[None, :]
    slot_of = dot("net,tu->neu", own_member.astype(low), earlier.astype(low)).astype(jnp.int32)
    slot_of = jnp.where(own_member, slot_of, -1)
    onehot = slot_of[:, :, None, :] == jnp.arange(slots, dtype=jnp.int32)[:, None]

    x_all = by_place(line_gather(x_low)).reshape(seq_len, width)
    normed_one = rms_norm(x_all.astype(full), full_g1).astype(low)
    qkv_rows = dot("td,dc->ct", normed_one, full_qkv)
    qkv_rows = qkv_rows.reshape(kv_here, GROUP + 2, HEAD_DIM, seq_len)
    positions = jnp.arange(seq_len, dtype=jnp.int32)
    cosine, sine_vals = rope_tables(positions.astype(full), HEAD_DIM)
    turned = rotate(qkv_rows[:, : GROUP + 1], cosine, sine_vals).astype(low)
    query = turned[:, :GROUP] * jnp.asarray(attn_mult, low)
    key = turned[:, GROUP]
    value = qkv_rows[:, GROUP + 1].astype(low)
    key_rows = jnp.swapaxes(key, 1, 2)
    value_rows = jnp.swapaxes(value, 1, 2)
    limit = block_limits(block_lengths[0], positions)[None]
    attended, out_heads, lse = attention_forward(query, key_rows, value, limit, shard_len)
    attn_rows = lax.all_to_all(attended, "seq", split_axis=0, concat_axis=0, tiled=True)
    attn_rows = attn_rows.reshape(HEADS * HEAD_DIM, shard_len)
    projected = dot("kt,kd->td", attn_rows, full_out)
    hidden = x_low.astype(full) + resid_mult * projected
    normed_two, norm_two_pull = jax.vjp(rms_norm, hidden, full_g2)

    tokens = jnp.stack(line_gather(normed_two.astype(low)))
    logits = dot("ntd,de->net", tokens, full_router)
    chosen = jnp.where(member, logits, masked_score)
    gate_exp = jnp.where(member, jnp.exp(chosen - jnp.max(chosen, axis=1, keepdims=True)), 0.0)
    gates = gate_exp / jnp.sum(gate_exp, axis=1, keepdims=True)
    own_gates = lax.dynamic_slice_in_dim(gates, me * experts_here, experts_here, 1)
    row_gates = jnp.sum(jnp.where(onehot, own_gates[:, :, None, :], 0.0), axis=3)
    row_gates = jnp.swapaxes(row_gates, 0, 1).reshape(experts_here, seq_devs * slots, 1)
    expert_in = pick_rows(slot_of, tokens, slots).reshape(experts_here, seq_devs * slots, width)
    gate_act, up_act, expert_out = experts_forward(expert_in, full_gate, full_up, full_down)
    expert_out = expert_out.reshape(experts_here, seq_devs, slots, width)
    mix_parts = put_rows(slot_of, own_gates, expert_out)
    mixture = line_scatter([mix_parts[k].astype(full) for k in range(seq_devs)])
    output_f32 = hidden + resid_mult * mixture
    activations = output_f32.astype(low).reshape(1, shard_len, width)
    error_rows = output_f32 - teacher.astype(full).reshape(shard_len, width)
    weighted = valid_rows[:, None] * error_rows
    squares = jnp.sum(weighted * error_rows)
    d_out = weighted * (tokens_all / valid_count)

    d_mix = resid_mult * d_out
    mix_dot = jnp.stack(line_gather(jnp.sum(d_mix * mixture, axis=1)))
    d_tokens = jnp.stack(line_gather(d_mix.astype(low)))
    d_rows = pick_rows(slot_of, d_tokens, slots).reshape(experts_here, seq_devs * slots, width)
    d_expert_in, d_gate_up, act_low, d_row_gates = experts_backward(
        d_rows, row_gates, gate_act, up_act, full_gate, full_up, full_down
    )
    d_expert_in = d_expert_in.reshape(experts_here, seq_devs, slots, width)
    d_row_gates = jnp.swapaxes(d_row_gates.reshape(experts_here, seq_devs, slots), 0, 1)
    d_gates = jnp.sum(jnp.where(onehot, d_row_gates[..., None], 0.0), axis=2)
    d_logits = (own_gates * (d_gates - mix_dot[:, None, :])).astype(low)
    own_router = lax.dynamic_slice_in_dim(full_router, me * experts_here, experts_here, 1)
    d_normed_parts = put_rows(slot_of, own_member.astype(full), d_expert_in)
    d_routed = dot("net,de->ntd", d_logits, own_router)
    router_part = dot("ntd,net->de", tokens, d_logits)
    d_normed_two = line_scatter(
        [d_normed_parts[k].astype(full) + d_routed[k] for k in range(seq_devs)]
    )
    order_a, order_b = halving_bits()
    expert_parts = weight_grads(
        lax.axis_index("fsdp").reshape(1), expert_in, d_rows, d_gate_up, act_low, order_a, order_b
    )
    d_normed_two, expert_parts = lax.optimization_barrier((d_normed_two, expert_parts))
    gate_grad, up_grad, down_left, down_right = (
        halving_sum(keep, send, order)
        for (keep, send), order in zip(expert_parts, (order_a, order_b, order_a, order_b))
    )
    down_grad = jnp.concatenate([down_left, down_right], axis=2)

    d_hidden_norm, gain_two_part = norm_two_pull(d_normed_two)
    d_hidden = d_out + d_hidden_norm
    d_proj = (resid_mult * d_hidden).astype(low)
    d_attended = dot("kd,td->kt", full_out, d_proj).astype(low)
    d_heads = lax.all_to_all(
        d_attended.reshape(seq_devs, heads_w, shard_len), "seq", split_axis=0, concat_axis=0, tiled=True
    )
    out_part = dot("kt,td->kd", attn_rows, d_proj).astype(low)
    query_grad, key_grad, value_grad = attention_backward(
        query, key_rows, value_rows, key, limit, out_heads, lse, d_heads
    )
    d_turned = jnp.concatenate([query_grad, key_grad[:, None]], axis=1).astype(full)
    d_turned = rotate(d_turned, cosine, -sine_vals).astype(low)
    d_qkv = jnp.concatenate([d_turned, value_grad[:, None]], axis=1).reshape(group_w, seq_len)
    qkv_part = dot("td,ct->dc", normed_one, d_qkv).astype(low)
    d_normed_parts = dot("ct,dc->td", d_qkv, full_qkv).astype(low)
    d_normed_parts = from_place(d_normed_parts.reshape(seq_devs, shard_len, width))
    d_normed_one = line_scatter([part.astype(full) for part in d_normed_parts])
    x_rows = x_low.astype(full)
    _, norm_one_pull = jax.vjp(lambda v: rms_norm(v, full_g1), x_rows)
    input_grad = (d_hidden + norm_one_pull(d_normed_one)[0]).reshape(1, shard_len, width)

    own_columns = jnp.zeros((width, expert_total), full)
    own_columns = lax.dynamic_update_slice_in_dim(
        own_columns, router_part, me * experts_here, 1
    )
    rest = jnp.concatenate([own_columns.astype(low), gain_two_part[:, None].astype(low)], axis=1)
    middle = width // 2
    dense = jnp.concatenate(
        [
            rows_sum(out_part[:, :middle], order_a),
            rows_sum(jnp.concatenate([out_part[:, middle:], rest], axis=1), order_b),
        ],
        axis=1,
    )
    dense = lax.psum(dense.astype(low), "seq").astype(full)
    out_grad = dense[:, :width]
    router_grad = dense[:, width : width + expert_total]
    gain_two_grad = dense[:, width + expert_total]
    middle = group_w // 2
    own_grad = jnp.concatenate(
        [rows_sum(qkv_part[:, :middle], order_a), rows_sum(qkv_part[:, middle:], order_b)], axis=1
    )
    qkv_grad = by_place(line_gather(own_grad.astype(low)))
    qkv_grad = jnp.swapaxes(qkv_grad, 0, 1).reshape(-1, QKV_W).astype(full)
    gain_one_grad = jnp.sum(qkv_grad * w_qkv.astype(full), axis=1) / gain_one.astype(full)
    squares = total(squares.reshape(1, 1), "seq", "fsdp")[0, 0]
    loss_value = squares / (valid_count * width)
    return (
        activations,
        loss_value,
        input_grad,
        gain_one_grad,
        qkv_grad,
        out_grad,
        gain_two_grad,
        router_grad,
        gate_grad,
        up_grad,
        down_grad,
    )


def solution(mesh):
    return jax.shard_map(
        shards,
        mesh=mesh,
        in_specs=(
            P("fsdp", "seq", None),
            P("fsdp", "seq", None),
            P("fsdp", "seq", None),
            P("fsdp", "seq"),
            P("fsdp", None),
            P("fsdp"),
            P("fsdp", None),
            P("fsdp", None),
            P("fsdp"),
            P("fsdp", None),
            P("seq", "fsdp", None),
            P("seq", "fsdp", None),
            P("seq", "fsdp", None),
        ),
        out_specs=(
            P("fsdp", "seq", None),
            P(),
            P("fsdp", "seq", None),
            P("fsdp"),
            P("fsdp", None),
            P("fsdp", None),
            P("fsdp"),
            P("fsdp", None),
            P("seq", "fsdp", None),
            P("seq", "fsdp", None),
            P("seq", "fsdp", None),
        ),
        check_vma=False,
    )
```

```python
import functools

import jax
import jax.numpy as jnp
from jax import lax
from jax.experimental import pallas as pl
from jax.experimental.pallas import tpu as pltpu
from jax.sharding import PartitionSpec as P

HEADS = 24
KV_HEADS = 8
HEAD_DIM = 64
BLOCK = 256
GROUP = 3
QKV_W = 2560


epsilon = 1e-06
attn_mult = 0.015625
resid_mult = 0.22
rope_base = 10000.0
masked_score = -1e30

low = jnp.bfloat16
full = jnp.float32


def dot(spec, left, right):
    return jnp.einsum(spec, left, right, preferred_element_type=full)


def rms_norm(values, gain_vec):
    inv_rms = lax.rsqrt(jnp.mean(values * values, axis=-1, keepdims=True) + epsilon)
    return values * inv_rms * gain_vec


def rope_tables(positions, head_dim):
    half_dim = head_dim // 2
    frequency = rope_base ** (-(2.0 * jnp.arange(half_dim, dtype=full)) / head_dim)
    angles = frequency[:, None] * positions[None, :]
    return (jnp.cos(angles), jnp.sin(angles))


def rotate(values, cosine, sine_vals):
    half_dim = values.shape[-2] // 2
    front_half = values[..., :half_dim, :]
    back_half = values[..., half_dim:, :]
    return jnp.concatenate(
        [front_half * cosine - back_half * sine_vals, back_half * cosine + front_half * sine_vals],
        axis=-2,
    )


def block_limits(lengths_row, positions):
    block_ends = jnp.cumsum(lengths_row)
    open_ends = jnp.where(block_ends[None, :] > positions[:, None], block_ends[None, :], positions.shape[0])
    return jnp.min(open_ends, axis=1).astype(jnp.int32)


def tie(*groups):
    return lax.optimization_barrier(groups)


def line_move(right, left, k):
    n = lax.axis_size("seq")
    return (
        lax.ppermute(right, "seq", [(i, i + 1) for i in range(k - 1, n - 1)]),
        lax.ppermute(left, "seq", [(i, i - 1) for i in range(1, n - k + 1)]),
    )


def line_gather(block):
    n = lax.axis_size("seq")
    rights, lefts = [block], [block]
    for k in range(1, n):
        right, left = line_move(rights[-1], lefts[-1], k)
        rights.append(right)
        lefts.append(left)
    return nearest(rights, lefts)


def nearest(rights, lefts):
    n = lax.axis_size("seq")
    me = lax.axis_index("seq")
    return [rights[0]] + [jnp.where(me >= k, rights[k], lefts[n - k]) for k in range(1, n)]


def arrival_order(n):
    order = []
    for me in range(n):
        both = min(me, n - 1 - me)
        places = [me]
        for k in range(1, n):
            places += [me - k] if me >= k and (k <= both or me > n - 1 - me) else []
            places += [me + k] if me + k < n and (k <= both or me < n - 1 - me) else []
        order.append(places)
    return order


def arrived(rights, lefts, turn):
    n = lax.axis_size("seq")
    me = lax.axis_index("seq")
    sources = {}
    for dev, places in enumerate(arrival_order(n)):
        gap = dev - places[turn]
        sources.setdefault(gap, []).append(dev)
    block = None
    for gap, devs in sources.items():
        moved = rights[gap] if gap >= 0 else lefts[-gap]
        if block is None:
            block = moved
        else:
            mine = jnp.array([dev in devs for dev in range(n)])[me]
            block = jnp.where(mine, moved, block)
    return block


def at_place(placed, place):
    return lax.dynamic_index_in_dim(placed, place % lax.axis_size("seq"), 0, keepdims=False)


def line_send(parts, k, right, left):
    me = lax.axis_index("seq")
    to_right, to_left = at_place(parts, me + k), at_place(parts, me - k)
    if right is not None:
        to_right = (to_right.astype(full) + right.astype(full)).astype(low)
        to_left = (to_left.astype(full) + left.astype(full)).astype(low)
    return to_right, to_left


def line_pass(to_right, to_left, k):
    n = lax.axis_size("seq")
    return (
        lax.ppermute(to_right, "seq", [(i, i + 1) for i in range(n - k)]),
        lax.ppermute(to_left, "seq", [(i, i - 1) for i in range(k, n)]),
    )


def line_end(parts, right, left):
    own = at_place(parts, lax.axis_index("seq")).astype(full)
    return own + (right.astype(full) + left.astype(full))


def by_place(blocks):
    n = lax.axis_size("seq")
    me = lax.axis_index("seq")
    placed = jnp.zeros((n,) + blocks[0].shape, blocks[0].dtype)
    for k, block in enumerate(blocks):
        placed = lax.dynamic_update_index_in_dim(placed, block, (me - k) % n, 0)
    return placed


def exchange(blocks):
    n = lax.axis_size("seq")
    me = lax.axis_index("seq")
    rights, lefts = [at_place(blocks, me)], [at_place(blocks, me)]
    for k in range(1, n):
        to_right, to_left = at_place(blocks, me + k), at_place(blocks, me - k)
        rights.append(lax.ppermute(to_right, "seq", [(i, i + k) for i in range(n - k)]))
        lefts.append(lax.ppermute(to_left, "seq", [(i, i - k) for i in range(k, n)]))
    return rights, lefts


def swap(value, axis, bit):
    return lax.ppermute(value, axis, [(i, i ^ bit) for i in range(lax.axis_size(axis))])


def total(value, *axes):
    for axis in axes:
        for step in range(lax.axis_size(axis).bit_length() - 1):
            value = value + swap(value, axis, 1 << step)
    return value


def fsdp_bits():
    bits = [1 << step for step in range(lax.axis_size("fsdp").bit_length() - 1)]
    return tuple(bits), tuple(bits[:1] + bits[:0:-1])


def doubling_gather(block, bits):
    blocks = block[None]
    for bit in bits:
        blocks = jnp.concatenate([blocks, swap(blocks, "fsdp", bit)])
    return blocks


def halve(keep, here):
    half = keep.shape[0] // 2
    if half == 0:
        return keep[0].astype(full) + here[0].astype(full)
    added = [
        (keep[cut].astype(full) + here[cut].astype(full)).astype(low)
        for cut in (slice(half, None), slice(0, half))
    ]
    return tuple(added)


def nt(a, b):
    return lax.dot_general(a, b, (((1,), (1,)), ((), ())), preferred_element_type=full)

def nn(a, b):
    return lax.dot_general(a, b, (((1,), (0,)), ((), ())), preferred_element_type=full)

def tn(a, b):
    return lax.dot_general(a, b, (((0,), (0,)), ((), ())), preferred_element_type=full)


def beside(ref):
    return jnp.concatenate([ref[0, h] for h in range(GROUP)], axis=1)

def key_steps(i, seq_len, query_rows, key_rows):
    free = (i * query_rows) // key_rows
    need = ((i + 1) * query_rows + BLOCK - 1 + key_rows - 1) // key_rows
    return free, jnp.minimum(need, seq_len // key_rows)

def forward_kernel(seq_len, query_rows, key_rows, limit_ref, q_ref, k_ref, vt_ref, low_ref, out_ref, lse_ref):
    i = pl.program_id(1)
    qt = beside(q_ref)
    width = GROUP * query_rows
    limit = jnp.concatenate([limit_ref[...]] * GROUP, axis=1)

    def step(masked, j, carry):
        peak, total, acc = carry
        start = pl.multiple_of(j * key_rows, key_rows)
        s = nn(k_ref[0, pl.ds(start, key_rows), :], qt)
        if masked:
            place = start + lax.broadcasted_iota(jnp.int32, (key_rows, 1), 0)
            s = jnp.where(place < limit, s, masked_score)
        new_peak = jnp.maximum(peak, jnp.max(s, axis=0, keepdims=True))
        shrink = jnp.exp(peak - new_peak)
        p = jnp.exp(s - new_peak)
        total = shrink * total + jnp.sum(p, axis=0, keepdims=True)
        acc = shrink * acc + nn(vt_ref[0, :, pl.ds(start, key_rows)], p.astype(low))
        return new_peak, total, acc

    free, need = key_steps(i, seq_len, query_rows, key_rows)
    carry = (
        jnp.full((1, width), masked_score, full),
        jnp.zeros((1, width), full),
        jnp.zeros((HEAD_DIM, width), full),
    )
    carry = lax.fori_loop(0, free, lambda j, c: step(False, j, c), carry)
    peak, total, acc = lax.fori_loop(free, need, lambda j, c: step(True, j, c), carry)
    out = acc / total
    lse = peak + jnp.log(total)
    for h in range(GROUP):
        cols = slice(h * query_rows, (h + 1) * query_rows)
        out_ref[0, h] = out[:, cols]
        low_ref[0, pl.ds(h * HEAD_DIM, HEAD_DIM), :] = out[:, cols].astype(low)
        lse_ref[0, h] = lse[:, cols]

def attention_forward(qt, k_rows, vt, limit, shard_len):
    kv_here, _, _, seq_len = qt.shape
    query_rows = min(256, shard_len)
    key_rows = min(512, seq_len)
    per = shard_len // query_rows
    return pl.pallas_call(
        functools.partial(forward_kernel, seq_len, query_rows, key_rows),
        grid=(kv_here, seq_len // query_rows),
        in_specs=[
            pl.BlockSpec((1, query_rows), lambda g, i: (0, i)),
            pl.BlockSpec((1, GROUP, HEAD_DIM, query_rows), lambda g, i: (g, 0, 0, i)),
            pl.BlockSpec((1, seq_len, HEAD_DIM), lambda g, i: (g, 0, 0)),
            pl.BlockSpec((1, HEAD_DIM, seq_len), lambda g, i: (g, 0, 0)),
        ],
        out_specs=[
            pl.BlockSpec((1, GROUP * HEAD_DIM, query_rows), lambda g, i: (i // per, g, i % per)),
            pl.BlockSpec((1, GROUP, HEAD_DIM, query_rows), lambda g, i: (g, 0, 0, i)),
            pl.BlockSpec((1, GROUP, 1, query_rows), lambda g, i: (g, 0, 0, i)),
        ],
        out_shape=[
            jax.ShapeDtypeStruct((seq_len // shard_len, kv_here * GROUP * HEAD_DIM, shard_len), low),
            jax.ShapeDtypeStruct((kv_here, GROUP, HEAD_DIM, seq_len), full),
            jax.ShapeDtypeStruct((kv_here, GROUP, 1, seq_len), full),
        ],
        compiler_params=vmem(40),
        name="attention_forward",
    )(limit, qt, k_rows, vt)

def backward_kernel(seq_len, query_rows, key_rows, limit_ref, q_ref, k_ref, v_ref, kt_ref, out_ref, lse_ref, dout_ref, dq_ref, dk_ref, dv_ref, dk_acc, dv_acc):
    i = pl.program_id(1)

    @pl.when(i == 0)
    def _():
        dk_acc[...] = jnp.zeros_like(dk_acc)
        dv_acc[...] = jnp.zeros_like(dv_acc)

    qt = beside(q_ref)
    limit = jnp.concatenate([limit_ref[...]] * GROUP, axis=1)
    dout = jnp.concatenate([dout_ref[0, pl.ds(h * HEAD_DIM, HEAD_DIM), :] for h in range(GROUP)], axis=1)
    delta = jnp.sum(dout.astype(full) * beside(out_ref), axis=0, keepdims=True)
    lse = beside(lse_ref)

    def step(masked, j, dq):
        start = pl.multiple_of(j * key_rows, key_rows)
        keys = pl.ds(start, key_rows)
        s = nn(k_ref[0, keys, :], qt)
        if masked:
            place = start + lax.broadcasted_iota(jnp.int32, (key_rows, 1), 0)
            s = jnp.where(place < limit, s, masked_score)
        p = jnp.exp(s - lse)
        dp = nn(v_ref[0, keys, :], dout)
        ds = (p * (dp - delta)).astype(low)
        dk_acc[:, keys] += nt(qt, ds)
        dv_acc[:, keys] += nt(dout, p.astype(low))
        return dq + nn(kt_ref[0, :, keys], ds)

    free, need = key_steps(i, seq_len, query_rows, key_rows)
    dq = jnp.zeros((HEAD_DIM, GROUP * query_rows), full)
    dq = lax.fori_loop(0, free, lambda j, c: step(False, j, c), dq)
    dq = lax.fori_loop(free, need, lambda j, c: step(True, j, c), dq) * attn_mult
    for h in range(GROUP):
        dq_ref[0, h] = dq[:, h * query_rows : (h + 1) * query_rows].astype(low)

    @pl.when(i == pl.num_programs(1) - 1)
    def _():
        dk_ref[0] = dk_acc[...].astype(low)
        dv_ref[0] = dv_acc[...].astype(low)

def attention_backward(qt, k_rows, v_rows, kt, limit, out, lse, d_out):
    kv_here, _, _, seq_len = qt.shape
    shard_len = d_out.shape[2]
    query_rows = min(256, shard_len)
    key_rows = min(512, seq_len)
    per = shard_len // query_rows
    quarter = lambda g, i: (g, 0, 0, i)
    whole = lambda g, i: (g, 0, 0)
    return pl.pallas_call(
        functools.partial(backward_kernel, seq_len, query_rows, key_rows),
        grid=(kv_here, seq_len // query_rows),
        in_specs=[
            pl.BlockSpec((1, query_rows), lambda g, i: (0, i)),
            pl.BlockSpec((1, GROUP, HEAD_DIM, query_rows), quarter),
            pl.BlockSpec((1, seq_len, HEAD_DIM), whole),
            pl.BlockSpec((1, seq_len, HEAD_DIM), whole),
            pl.BlockSpec((1, HEAD_DIM, seq_len), whole),
            pl.BlockSpec((1, GROUP, HEAD_DIM, query_rows), quarter),
            pl.BlockSpec((1, GROUP, 1, query_rows), quarter),
            pl.BlockSpec((1, GROUP * HEAD_DIM, query_rows), lambda g, i: (i // per, g, i % per)),
        ],
        out_specs=[
            pl.BlockSpec((1, GROUP, HEAD_DIM, query_rows), quarter),
            pl.BlockSpec((1, HEAD_DIM, seq_len), whole),
            pl.BlockSpec((1, HEAD_DIM, seq_len), whole),
        ],
        out_shape=[
            jax.ShapeDtypeStruct((kv_here, GROUP, HEAD_DIM, seq_len), low),
            jax.ShapeDtypeStruct((kv_here, HEAD_DIM, seq_len), low),
            jax.ShapeDtypeStruct((kv_here, HEAD_DIM, seq_len), low),
        ],
        scratch_shapes=[pltpu.VMEM((HEAD_DIM, seq_len), full), pltpu.VMEM((HEAD_DIM, seq_len), full)],
        compiler_params=vmem(40),
        name="attention_backward",
    )(limit, qt, k_rows, v_rows, kt, out, lse, d_out)


def vmem(mib):
    return pltpu.CompilerParams(vmem_limit_bytes=mib * 2**20)


def own_row(ref, row):
    return ref[pl.ds(row, 1), :]


def experts_kernel(
    at_ref, tok_ref, slot_ref, member_ref, router_ref, wg_ref, wu_ref, wd_ref, *refs
):
    part_ref, x_ref, g_ref, u_ref, gates_ref, acc, gates_all = refs[-7:]
    e, experts = pl.program_id(0), pl.num_programs(0)
    slots = x_ref.shape[2]

    @pl.when(e == 0)
    def _():
        member = member_ref[...] > 0
        chosen = jnp.where(member, nt(router_ref[...], tok_ref[...]), masked_score)
        chosen = jnp.exp(chosen - jnp.max(chosen, axis=0, keepdims=True))
        chosen = jnp.where(member, chosen, 0.0)
        gates_all[...] = chosen / jnp.sum(chosen, axis=0, keepdims=True)
        acc[...] = jnp.zeros_like(acc)

    gate_row = own_row(gates_all, at_ref[1] * experts + e)
    gates_ref[pl.ds(e, 1), :] = gate_row
    place = lax.broadcasted_iota(jnp.int32, (slots, 1), 0)
    here = place == own_row(slot_ref, e)
    x = nn(jnp.where(here, 1.0, 0.0).astype(low), tok_ref[...]).astype(low)
    x_ref[0, 0] = x
    g = nn(x, wg_ref[0])
    u = nn(x, wu_ref[0])
    g_ref[0, 0] = g.astype(low)
    u_ref[0, 0] = u.astype(low)
    act = (g * jax.nn.sigmoid(g) * u).astype(low)
    y = nn(act, wd_ref[0]).astype(low)
    acc[...] += tn(jnp.where(here, gate_row, 0.0).astype(low), y)

    @pl.when(e == experts - 1)
    def _():
        part_ref[0] = acc[...].astype(low)


def back_kernel(
    at_ref, tok_ref, slot_ref, gates_ref, mix_ref, router_ref, g_ref, u_ref, wg_ref, wu_ref, wd_ref, *refs
):
    part_ref, d_ref, dgu_ref, act_ref, dlog_ref, acc, dlog_all = refs[-7:]
    e, experts = pl.program_id(0), pl.num_programs(0)
    slots, hidden = g_ref.shape[2:]

    @pl.when(e == 0)
    def _():
        dlog_all[...] = jnp.zeros_like(dlog_all)
        acc[...] = jnp.zeros_like(acc)

    place = lax.broadcasted_iota(jnp.int32, (slots, 1), 0)
    here = place == own_row(slot_ref, e)
    pick = jnp.where(here, 1.0, 0.0).astype(low)
    gate_row = own_row(gates_ref, e)
    gate = jnp.sum(jnp.where(here, gate_row, 0.0), axis=1, keepdims=True)
    d = nn(pick, tok_ref[...]).astype(low)
    d_ref[0, 0] = d
    d_act = nt(d, wd_ref[0])
    g, u = g_ref[0, 0].astype(full), u_ref[0, 0].astype(full)
    sig = jax.nn.sigmoid(g)
    silu = g * sig
    act = silu * u
    d_gate = jnp.sum(d_act * act, axis=1, keepdims=True)
    d_gate = jnp.sum(jnp.where(here, d_gate, 0.0), axis=0, keepdims=True)
    dlog_all[pl.ds(e, 1), :] = gate_row * (d_gate - mix_ref[...])
    act_ref[0, 0] = (act * gate).astype(low)
    d_act = d_act * gate
    d_g = (d_act * u * (sig + silu * (1.0 - sig))).astype(low)
    d_u = (d_act * silu).astype(low)
    dgu_ref[0, 0, :, :hidden] = d_g
    dgu_ref[0, 0, :, hidden:] = d_u
    dx = (nt(d_g, wg_ref[0]) + nt(d_u, wu_ref[0])).astype(low)
    acc[...] += tn(pick, dx)

    @pl.when(e == experts - 1)
    def _():
        dlog = dlog_all[...].astype(low)
        dlog_ref[...] = dlog
        part_ref[0] = (acc[...] + tn(dlog, router_ref[...])).astype(low)


def by_expert(*shape):
    return pl.BlockSpec((1,) + shape, lambda e, at: (e, 0, 0))


def in_turn(turn, *shape):
    return pl.BlockSpec((1, 1) + shape, lambda e, at: (e, turn, 0, 0))


def same(*shape):
    return pl.BlockSpec(shape, lambda e, at: (0, 0))


def in_place(*shape):
    return pl.BlockSpec((1,) + shape, lambda e, at: (at[0], 0, 0))


def shard_call(kernel, name, at, inputs, in_specs, out_specs, out_shape, buffers, scratch, experts):
    first = len(inputs) + 1
    aliases = {first + i: i for i in range(len(buffers))}
    return pl.pallas_call(
        kernel,
        grid_spec=pltpu.PrefetchScalarGridSpec(
            num_scalar_prefetch=1,
            grid=(experts,),
            in_specs=in_specs + [pl.BlockSpec(memory_space=pl.ANY)] * len(buffers),
            out_specs=out_specs,
            scratch_shapes=scratch,
        ),
        out_shape=out_shape,
        input_output_aliases=aliases,
        compiler_params=vmem(48),
        name=name,
    )(at, *inputs, *buffers)


def experts_forward(turn, devs, at, tokens, slot_of, member, router, w_gate, w_up, w_down, slots, buffers):
    experts, width, hidden = w_gate.shape
    count = tokens.shape[0]
    total_experts = member.shape[0]
    return shard_call(
        experts_kernel,
        "experts_forward",
        at,
        [tokens, slot_of, member, router, w_gate, w_up, w_down],
        [
            same(count, width),
            same(experts, count),
            same(total_experts, count),
            same(total_experts, width),
            by_expert(width, hidden),
            by_expert(width, hidden),
            by_expert(hidden, width),
        ],
        [
            in_place(count, width),
            in_turn(turn, slots, width),
            in_turn(turn, slots, hidden),
            in_turn(turn, slots, hidden),
            same(experts, count),
        ],
        [
            jax.ShapeDtypeStruct((devs, count, width), low),
            jax.ShapeDtypeStruct((experts, devs, slots, width), low),
            jax.ShapeDtypeStruct((experts, devs, slots, hidden), low),
            jax.ShapeDtypeStruct((experts, devs, slots, hidden), low),
            jax.ShapeDtypeStruct((experts, count), full),
        ],
        buffers,
        [pltpu.VMEM((count, width), full), pltpu.VMEM((total_experts, count), full)],
        experts,
    )


def experts_backward(
    turn, devs, at, d_tokens, slot_of, gates, mix_dot, router, g, u, w_gate, w_up, w_down, buffers
):
    experts, width, hidden = w_gate.shape
    count = d_tokens.shape[0]
    slots = g.shape[2]
    lines = router.shape[0]
    return shard_call(
        back_kernel,
        "experts_backward",
        at,
        [d_tokens, slot_of, gates, mix_dot, router, g, u, w_gate, w_up, w_down],
        [
            same(count, width),
            same(experts, count),
            same(experts, count),
            same(1, count),
            same(lines, width),
            in_turn(turn, slots, hidden),
            in_turn(turn, slots, hidden),
            by_expert(width, hidden),
            by_expert(width, hidden),
            by_expert(hidden, width),
        ],
        [
            in_place(count, width),
            in_turn(turn, slots, width),
            in_turn(turn, slots, 2 * hidden),
            in_turn(turn, slots, hidden),
            same(lines, count),
        ],
        [
            jax.ShapeDtypeStruct((devs, count, width), low),
            jax.ShapeDtypeStruct((experts, devs, slots, width), low),
            jax.ShapeDtypeStruct((experts, devs, slots, 2 * hidden), low),
            jax.ShapeDtypeStruct((experts, devs, slots, hidden), low),
            jax.ShapeDtypeStruct((lines, count), low),
        ],
        buffers,
        [pltpu.VMEM((count, width), full), pltpu.VMEM((lines, count), full)],
        experts,
    )


def halving_masks(bits):
    masks = [0]
    for bit in reversed(bits):
        masks = masks + [mask ^ bit for mask in masks]
    return masks


def gate_up_kernel(bits_a, bits_b, me_ref, x_ref, dgu_ref, *refs):
    outs, acc = refs[:4], refs[4]
    hidden = outs[0].shape[3]
    acc[...] = tn(x_ref[0], dgu_ref[0])
    for part, bits in enumerate((bits_a, bits_b)):
        keep, send = outs[2 * part], outs[2 * part + 1]
        rows = keep.shape[2]
        for place, mask in enumerate(halving_masks(bits)):
            start = pl.multiple_of((me_ref[0] ^ mask) * rows, rows)
            out = keep if place < keep.shape[0] else send
            block = acc[pl.ds(start, rows), part * hidden : (part + 1) * hidden]
            out[place % keep.shape[0], 0] = block.astype(low)


def gate_up_grads(me, rows, d_gu, bits_a, bits_b):
    experts, count, width = rows.shape
    hidden = d_gu.shape[2] // 2
    devs = 2 ** len(bits_a)
    shape = (width // devs, hidden)
    outs = pl.pallas_call(
        functools.partial(gate_up_kernel, bits_a, bits_b),
        grid_spec=pltpu.PrefetchScalarGridSpec(
            num_scalar_prefetch=1,
            grid=(experts,),
            in_specs=[by_expert(count, width), by_expert(count, 2 * hidden)],
            out_specs=[pl.BlockSpec((devs // 2, 1) + shape, lambda e, me: (0, e, 0, 0))] * 4,
            scratch_shapes=[pltpu.VMEM((width, 2 * hidden), full)],
        ),
        out_shape=[jax.ShapeDtypeStruct((devs // 2, experts) + shape, low)] * 4,
        compiler_params=vmem(48),
        name="gate_up_grads",
    )(me, rows, d_gu)
    return (outs[0], outs[1]), (outs[2], outs[3])


def down_kernel(act_ref, d_ref, out_ref):
    out_ref[0] = tn(act_ref[0], d_ref[0]).astype(low)


def down_grads(act, d_rows):
    experts, count, hidden = act.shape
    width = d_rows.shape[2]
    one = lambda *shape: pl.BlockSpec((1,) + shape, lambda e: (e, 0, 0))
    return pl.pallas_call(
        down_kernel,
        grid=(experts,),
        in_specs=[one(count, hidden), one(count, width)],
        out_specs=one(hidden, width),
        out_shape=jax.ShapeDtypeStruct((experts, hidden, width), low),
        compiler_params=vmem(48),
        name="down_grads",
    )(act, d_rows)


def join_kernel(me_ref, left_ref, right_ref, out_ref):
    half = left_ref.shape[3]
    out_ref[:, :, :half] = left_ref[0]
    out_ref[:, :, half:] = right_ref[0]


def join_rows(me, left, right, bits_left, bits_right):
    devs, experts, rows, half = left.shape

    def place(bits):
        def index(block, me_ref):
            mask = me_ref[0] ^ block
            spot = sum(((mask // bit) % 2) * 2**i for i, bit in enumerate(bits))
            return (spot, 0, 0, 0)

        return pl.BlockSpec((1, experts, rows, half), index)

    return pl.pallas_call(
        join_kernel,
        grid_spec=pltpu.PrefetchScalarGridSpec(
            num_scalar_prefetch=1,
            grid=(devs,),
            in_specs=[place(bits_left), place(bits_right)],
            out_specs=pl.BlockSpec((experts, rows, 2 * half), lambda block, me_ref: (0, block, 0)),
        ),
        out_shape=jax.ShapeDtypeStruct((experts, devs * rows, 2 * half), low),
        compiler_params=vmem(40),
        name="join_rows",
    )(me, left, right)


def shards(
    inputs,
    teacher,
    routes,
    valid_mask,
    block_lengths,
    gain_one,
    w_qkv,
    w_out,
    gain_two,
    w_router,
    w_gate,
    w_up,
    w_down,
):
    n = lax.axis_size("seq")
    me = lax.axis_index("seq")
    mine = lax.axis_index("fsdp")
    seqs_here, shard_len, width = inputs.shape
    assert seqs_here == 1
    seq_len = shard_len * n
    tokens_all = lax.axis_size("fsdp") * seq_len
    kv_here = KV_HEADS // n
    heads_w = kv_here * GROUP * HEAD_DIM
    group_w = kv_here * (GROUP + 2) * HEAD_DIM
    experts_here = w_gate.shape[0]
    expert_total = experts_here * n
    top_count = routes.shape[2]
    capacity = 3 * shard_len * top_count // (2 * expert_total)
    slots = -(-capacity // 16) * 16
    slot_rows = n * slots
    order_a, order_b = fsdp_bits()
    order = jnp.array(arrival_order(n), jnp.int32)[me]
    x_low = inputs.reshape(shard_len, width)

    own_qkv = lax.dynamic_slice_in_dim(w_qkv, me * group_w, group_w, 1)
    small = jnp.concatenate([gain_one[:, None], gain_two[:, None], w_router], axis=1)
    small = doubling_gather(small, order_a)
    small = small[mine ^ jnp.arange(small.shape[0])].reshape(width, 2 + expert_total)
    full_qkv = lax.all_gather(own_qkv, "fsdp", axis=0, tiled=True)
    full_out = lax.all_gather(w_out, "fsdp", axis=0, tiled=True)
    full_gate = lax.all_gather(w_gate, "fsdp", axis=1, tiled=True)
    full_up = lax.all_gather(w_up, "fsdp", axis=1, tiled=True)
    down_a, down_b = order_a[1:] + order_a[:1], order_b[1:] + order_b[:1]
    full_down = join_rows(
        mine.reshape(1),
        doubling_gather(w_down[:, :, : width // 2], down_a),
        doubling_gather(w_down[:, :, width // 2 :], down_b),
        down_a,
        down_b,
    )
    full_g1 = small[:, 0].astype(full)
    full_g2 = small[:, 1].astype(full)
    router = small[:, 2:].T
    own_router = lax.dynamic_slice_in_dim(router, me * experts_here, experts_here, 0)
    own_router = jnp.pad(own_router, ((0, -experts_here % 16), (0, 0)))
    valid_rows = valid_mask.reshape(shard_len).astype(full)

    routes_low = jnp.concatenate([routes.reshape(shard_len, top_count).T, valid_mask], axis=0)
    routes_all = by_place(line_gather(routes_low))[order]
    valid_count = total(jnp.sum(routes_all[:, top_count]).astype(full).reshape(1, 1), "fsdp")[0, 0]
    expert_ids = jnp.arange(expert_total, dtype=jnp.int32)
    member = jnp.any(routes_all[:, :top_count, None, :] == expert_ids[:, None], axis=1)
    own_member = lax.dynamic_slice_in_dim(member, me * experts_here, experts_here, 1)
    earlier = jnp.arange(shard_len)[:, None] < jnp.arange(shard_len)[None, :]
    slot_of = dot("net,tu->neu", own_member.astype(low), earlier.astype(low)).astype(jnp.int32)
    slot_of = jnp.where(own_member, slot_of, -1)
    member = member.astype(full)

    x_all = by_place(line_gather(x_low)).reshape(seq_len, width)
    normed_one = rms_norm(x_all.astype(full), full_g1).astype(low)
    qkv_rows = dot("td,dc->ct", normed_one, full_qkv)
    qkv_rows = qkv_rows.reshape(kv_here, GROUP + 2, HEAD_DIM, seq_len)
    positions = jnp.arange(seq_len, dtype=jnp.int32)
    cosine, sine_vals = rope_tables(positions.astype(full), HEAD_DIM)
    turned = rotate(qkv_rows[:, : GROUP + 1], cosine, sine_vals).astype(low)
    query = turned[:, :GROUP] * jnp.asarray(attn_mult, low)
    key = turned[:, GROUP]
    value = qkv_rows[:, GROUP + 1].astype(low)
    key_rows = jnp.swapaxes(key, 1, 2)
    value_rows = jnp.swapaxes(value, 1, 2)
    limit = block_limits(block_lengths[0], positions)[None]
    attended, out_heads, lse = attention_forward(query, key_rows, value, limit, shard_len)
    moved = exchange(attended)
    moved, slot_of, member, own_router = tie(moved, slot_of, member, own_router)
    attn_rows = by_place(nearest(*moved)).reshape(HEADS * HEAD_DIM, shard_len)
    projected = dot("kt,kd->td", attn_rows, full_out)
    hidden = x_low.astype(full) + resid_mult * projected
    normed_two, norm_two_pull = jax.vjp(rms_norm, hidden, full_g2)

    tokens = [normed_two.astype(low)]
    rights, lefts = [tokens[0]], [tokens[0]]
    buffers, gates = [], []
    for turn in range(n):
        if turn < n - 1:
            right, left, tokens[turn] = tie(rights[turn], lefts[turn], tokens[turn])
            right, left = line_move(right, left, turn + 1)
        *buffers, shard_gates = experts_forward(
            turn, n, jnp.stack([order[turn], me]), tokens[turn], slot_of[turn], member[turn],
            router, full_gate, full_up, full_down, slots, buffers,
        )
        if turn < n - 1:
            right, left, shard_gates = tie(right, left, shard_gates)
            rights.append(right)
            lefts.append(left)
            tokens.append(arrived(rights, lefts, turn + 1))
        gates.append(shard_gates)
    mix_parts, expert_in, gate_act, up_act = buffers
    right = left = None
    for k in range(n - 1, 0, -1):
        right, left = line_pass(*line_send(mix_parts, k, right, left), k)
    mixture = line_end(mix_parts, right, left)
    output_f32 = hidden + resid_mult * mixture
    activations = output_f32.astype(low).reshape(1, shard_len, width)
    error_rows = output_f32 - teacher.astype(full).reshape(shard_len, width)
    weighted = valid_rows[:, None] * error_rows
    squares = jnp.sum(weighted * error_rows)
    d_out = weighted * (tokens_all / valid_count)

    d_mix = resid_mult * d_out
    d_tokens = d_mix.astype(low)
    mix_dot = jnp.sum(d_mix * mixture, axis=1)[None]
    rights, lefts = [d_tokens], [d_tokens]
    dot_rights, dot_lefts = [mix_dot], [mix_dot]
    buffers, d_logits = [], []
    for turn in range(n):
        if turn < n - 1:
            (right, left), (dot_right, dot_left), d_tokens = tie(
                (rights[turn], lefts[turn]), (dot_rights[turn], dot_lefts[turn]), d_tokens
            )
            dot_right, dot_left = line_move(dot_right, dot_left, turn + 1)
            right, left = line_move(right, left, turn + 1)
        *buffers, shard_logits = experts_backward(
            turn, n, jnp.stack([order[turn], me]), d_tokens, slot_of[turn], gates[turn], mix_dot,
            own_router, gate_act, up_act, full_gate, full_up, full_down, buffers,
        )
        if turn < n - 1:
            right, left, dot_right, dot_left, shard_logits = tie(
                right, left, dot_right, dot_left, shard_logits
            )
            rights.append(right)
            lefts.append(left)
            dot_rights.append(dot_right)
            dot_lefts.append(dot_left)
            d_tokens = arrived(rights, lefts, turn + 1)
            mix_dot = arrived(dot_rights, dot_lefts, turn + 1)
        d_logits.append(shard_logits)
    d_parts, d_rows, d_gate_up, act_low = buffers
    expert_in = expert_in.reshape(experts_here, slot_rows, width)
    d_rows = d_rows.reshape(experts_here, slot_rows, width)
    d_gate_up = d_gate_up.reshape(experts_here, slot_rows, -1)
    act_low = act_low.reshape(experts_here, slot_rows, -1)

    right = left = None
    for k in range(n - 1, 0, -1):
        moving = line_send(d_parts, k, right, left)
        if k == n - 1:
            moving, expert_in, d_gate_up = tie(moving, expert_in, d_gate_up)
            right, left = line_pass(*moving, k)
            gate_pair, up_pair = gate_up_grads(
                mine.reshape(1), expert_in, d_gate_up, order_a, order_b
            )
            right, left, gate_pair, up_pair = tie(right, left, gate_pair, up_pair)
        elif k == n - 2:
            moving, gate_pair, up_pair, act_low, d_rows = tie(
                moving, gate_pair, up_pair, act_low, d_rows
            )
            right, left = line_pass(*moving, k)
            gate_here = swap(gate_pair[1], "fsdp", order_a[0])
            up_here = swap(up_pair[1], "fsdp", order_b[0])
            down_part = down_grads(act_low, d_rows)
            right, left, gate_here, up_here, down_part = tie(
                right, left, gate_here, up_here, down_part
            )
        elif k == n - 3:
            moving, gate_here, up_here = tie(moving, gate_here, up_here)
            right, left = line_pass(*moving, k)
            gate_send, gate_keep = halve(gate_pair[0], gate_here)
            up_send, up_keep = halve(up_pair[0], up_here)
            right, left, gate_send, up_send = tie(right, left, gate_send, up_send)
        else:
            right, left = line_pass(*moving, k)
    d_normed_two = line_end(d_parts, right, left)
    down_sum = lax.psum_scatter(down_part, "fsdp", scatter_dimension=1, tiled=True)

    d_hidden_norm, gain_two_part = norm_two_pull(d_normed_two)
    d_hidden = d_out + d_hidden_norm
    d_proj = (resid_mult * d_hidden).astype(low)
    d_attended = dot("kd,td->kt", full_out, d_proj).astype(low)
    d_attended, gate_send, up_send = tie(d_attended, gate_send, up_send)
    moved = exchange(d_attended.reshape(n, heads_w, shard_len))
    gate_here = swap(gate_send, "fsdp", order_a[1])
    up_here = swap(up_send, "fsdp", order_b[1])
    out_part = dot("kt,td->kd", attn_rows, d_proj).astype(low)
    router_part = sum(
        dot("td,et->de", shard, shard_logits[:experts_here])
        for shard, shard_logits in zip(tokens, d_logits)
    )
    moved, out_part, router_part = tie(moved, out_part, router_part)
    d_heads = by_place(nearest(*moved))
    query_grad, key_grad, value_grad = attention_backward(
        query, key_rows, value_rows, key, limit, out_heads, lse, d_heads
    )
    (query_grad, key_grad, value_grad), gate_here, up_here = tie(
        (query_grad, key_grad, value_grad), gate_here, up_here
    )
    d_turned = jnp.concatenate([query_grad, key_grad[:, None]], axis=1).astype(full)
    d_turned = rotate(d_turned, cosine, -sine_vals).astype(low)
    d_qkv = jnp.concatenate([d_turned, value_grad[:, None]], axis=1).reshape(group_w, seq_len)
    d_parts = dot("ct,dc->td", d_qkv, full_qkv).astype(low).reshape(n, shard_len, width)
    moving = line_send(d_parts, n - 1, None, None)
    moving, d_qkv, gate_here, up_here = tie(moving, d_qkv, gate_here, up_here)
    right, left = line_pass(*moving, n - 1)
    qkv_part = dot("td,ct->dc", normed_one, d_qkv).astype(low)
    qkv_sum = lax.psum_scatter(qkv_part, "fsdp", scatter_dimension=0, tiled=True)
    gate_send, gate_keep = halve(gate_keep, gate_here)
    up_send, up_keep = halve(up_keep, up_here)
    right, left, qkv_part, gate_send, up_send = tie(right, left, qkv_part, gate_send, up_send)
    gate_here = swap(gate_send, "fsdp", order_a[2])
    up_here = swap(up_send, "fsdp", order_b[2])
    for k in range(n - 2, 0, -1):
        right, left = line_pass(*line_send(d_parts, k, right, left), k)
    d_normed_one = line_end(d_parts, right, left)
    _, norm_one_pull = jax.vjp(lambda v: rms_norm(v, full_g1), x_low.astype(full))
    input_grad = (d_hidden + norm_one_pull(d_normed_one)[0]).reshape(1, shard_len, width)

    input_grad, gate_here, up_here, down_sum, qkv_sum = tie(
        input_grad, gate_here, up_here, down_sum, qkv_sum
    )
    for bit_a, bit_b in zip(order_a[3:], order_b[3:]):
        gate_send, gate_keep = halve(gate_keep, gate_here)
        up_send, up_keep = halve(up_keep, up_here)
        gate_here = swap(gate_send, "fsdp", bit_a)
        up_here = swap(up_send, "fsdp", bit_b)
    gate_grad = halve(gate_keep, gate_here)
    up_grad = halve(up_keep, up_here)
    down_grad = down_sum.astype(full)
    own_columns = jnp.zeros((width, expert_total), full)
    own_columns = lax.dynamic_update_slice_in_dim(own_columns, router_part, me * experts_here, 1)
    rest = jnp.concatenate([own_columns.astype(low), gain_two_part[:, None].astype(low)], axis=1)
    dense = [
        lax.psum_scatter(part, "fsdp", scatter_dimension=0, tiled=True) for part in (out_part, rest)
    ]
    out_sum, rest = lax.psum(dense, "seq")
    out_grad = out_sum.astype(full)
    router_grad = rest[:, :expert_total].astype(full)
    gain_two_grad = rest[:, expert_total].astype(full)
    qkv_grad = by_place(line_gather(qkv_sum))
    qkv_grad = jnp.swapaxes(qkv_grad, 0, 1).reshape(-1, QKV_W).astype(full)
    gain_one_grad = jnp.sum(qkv_grad * w_qkv.astype(full), axis=1) / gain_one.astype(full)
    squares = total(squares.reshape(1, 1), "seq", "fsdp")[0, 0]
    loss_value = squares / (valid_count * width)
    return (
        activations,
        loss_value,
        input_grad,
        gain_one_grad,
        qkv_grad,
        out_grad,
        gain_two_grad,
        router_grad,
        gate_grad,
        up_grad,
        down_grad,
    )


def solution(mesh):
    return jax.shard_map(
        shards,
        mesh=mesh,
        in_specs=(
            P("fsdp", "seq", None),
            P("fsdp", "seq", None),
            P("fsdp", "seq", None),
            P("fsdp", "seq"),
            P("fsdp", None),
            P("fsdp"),
            P("fsdp", None),
            P("fsdp", None),
            P("fsdp"),
            P("fsdp", None),
            P("seq", "fsdp", None),
            P("seq", "fsdp", None),
            P("seq", "fsdp", None),
        ),
        out_specs=(
            P("fsdp", "seq", None),
            P(),
            P("fsdp", "seq", None),
            P("fsdp"),
            P("fsdp", None),
            P("fsdp", None),
            P("fsdp"),
            P("fsdp", None),
            P("seq", "fsdp", None),
            P("seq", "fsdp", None),
            P("seq", "fsdp", None),
        ),
        check_vma=False,
    )
```

```python
import functools

import jax
import jax.numpy as jnp
from jax import lax
from jax.experimental import pallas as pl
from jax.experimental.pallas import tpu as pltpu
from jax.sharding import PartitionSpec as P

HEADS = 24
KV_HEADS = 8
HEAD_DIM = 64
BLOCK = 256
GROUP = 3
QKV_W = 2560


epsilon = 1e-06
attn_mult = 0.015625
resid_mult = 0.22
rope_base = 10000.0
masked_score = -1e30

low = jnp.bfloat16
full = jnp.float32


def dot(spec, left, right):
    return jnp.einsum(spec, left, right, preferred_element_type=full)


def rms_norm(values, gain_vec):
    inv_rms = lax.rsqrt(jnp.mean(values * values, axis=-1, keepdims=True) + epsilon)
    return values * inv_rms * gain_vec


def rope_tables(positions, head_dim):
    half_dim = head_dim // 2
    frequency = rope_base ** (-(2.0 * jnp.arange(half_dim, dtype=full)) / head_dim)
    angles = frequency[:, None] * positions[None, :]
    return (jnp.cos(angles), jnp.sin(angles))


def rotate(values, cosine, sine_vals):
    half_dim = values.shape[-2] // 2
    front_half = values[..., :half_dim, :]
    back_half = values[..., half_dim:, :]
    return jnp.concatenate(
        [front_half * cosine - back_half * sine_vals, back_half * cosine + front_half * sine_vals],
        axis=-2,
    )


def block_limits(lengths_row, positions):
    block_ends = jnp.cumsum(lengths_row)
    open_ends = jnp.where(block_ends[None, :] > positions[:, None], block_ends[None, :], positions.shape[0])
    return jnp.min(open_ends, axis=1).astype(jnp.int32)


def tie(*groups):
    return lax.optimization_barrier(groups)


def line_move(right, left, k):
    n = lax.axis_size("seq")
    return (
        lax.ppermute(right, "seq", [(i, i + 1) for i in range(k - 1, n - 1)]),
        lax.ppermute(left, "seq", [(i, i - 1) for i in range(1, n - k + 1)]),
    )


def line_gather(block):
    n = lax.axis_size("seq")
    rights, lefts = [block], [block]
    for k in range(1, n):
        right, left = tie(*line_move(rights[-1], lefts[-1], k))
        rights.append(right)
        lefts.append(left)
    return nearest(rights, lefts)


def nearest(rights, lefts):
    n = lax.axis_size("seq")
    me = lax.axis_index("seq")
    return [rights[0]] + [jnp.where(me >= k, rights[k], lefts[n - k]) for k in range(1, n)]


def arrival_order(n):
    order = []
    for me in range(n):
        both = min(me, n - 1 - me)
        places = [me]
        for k in range(1, n):
            places += [me - k] if me >= k and (k <= both or me > n - 1 - me) else []
            places += [me + k] if me + k < n and (k <= both or me < n - 1 - me) else []
        order.append(places)
    return order


def arrived(rights, lefts, turn):
    n = lax.axis_size("seq")
    me = lax.axis_index("seq")
    sources = {}
    for dev, places in enumerate(arrival_order(n)):
        gap = dev - places[turn]
        sources.setdefault(gap, []).append(dev)
    block = None
    for gap, devs in sources.items():
        moved = rights[gap] if gap >= 0 else lefts[-gap]
        if block is None:
            block = moved
        else:
            mine = jnp.array([dev in devs for dev in range(n)])[me]
            block = jnp.where(mine, moved, block)
    return block


def at_place(placed, place):
    return lax.dynamic_index_in_dim(placed, place % lax.axis_size("seq"), 0, keepdims=False)


def line_send(parts, k, right, left):
    me = lax.axis_index("seq")
    to_right, to_left = at_place(parts, me + k), at_place(parts, me - k)
    if right is not None:
        to_right = (to_right.astype(full) + right.astype(full)).astype(low)
        to_left = (to_left.astype(full) + left.astype(full)).astype(low)
    return to_right, to_left


def line_pass(to_right, to_left, k):
    n = lax.axis_size("seq")
    return (
        lax.ppermute(to_right, "seq", [(i, i + 1) for i in range(n - k)]),
        lax.ppermute(to_left, "seq", [(i, i - 1) for i in range(k, n)]),
    )


def line_end(parts, right, left):
    own = at_place(parts, lax.axis_index("seq")).astype(full)
    return own + (right.astype(full) + left.astype(full))


def by_place(blocks):
    n = lax.axis_size("seq")
    me = lax.axis_index("seq")
    placed = jnp.zeros((n,) + blocks[0].shape, blocks[0].dtype)
    for k, block in enumerate(blocks):
        placed = lax.dynamic_update_index_in_dim(placed, block, (me - k) % n, 0)
    return placed


def exchange(blocks):
    n = lax.axis_size("seq")
    me = lax.axis_index("seq")
    rights, lefts = [at_place(blocks, me)], [at_place(blocks, me)]
    for k in range(1, n):
        to_right, to_left = at_place(blocks, me + k), at_place(blocks, me - k)
        rights.append(lax.ppermute(to_right, "seq", [(i, i + k) for i in range(n - k)]))
        lefts.append(lax.ppermute(to_left, "seq", [(i, i - k) for i in range(k, n)]))
    return rights, lefts


def swap(value, axis, bit):
    return lax.ppermute(value, axis, [(i, i ^ bit) for i in range(lax.axis_size(axis))])


def total(value, *axes):
    for axis in axes:
        for step in range(lax.axis_size(axis).bit_length() - 1):
            value = value + swap(value, axis, 1 << step)
    return value


def fsdp_bits():
    bits = [1 << step for step in range(lax.axis_size("fsdp").bit_length() - 1)]
    return tuple(bits), tuple(bits[:1] + bits[:0:-1])


def total_steps(value, *axes):
    for axis in axes:
        for step in range(lax.axis_size(axis).bit_length() - 1):
            here = swap(value, axis, 1 << step)
            here = yield here
            value = value + here
    while True:
        yield value


def doubling_gather(block, bits):
    blocks = block[None]
    for bit in bits:
        blocks = jnp.concatenate([blocks, swap(blocks, "fsdp", bit)])
    return blocks


def halve(keep, here):
    half = keep.shape[0] // 2
    if half == 0:
        return keep[0].astype(full) + here[0].astype(full)
    added = [
        (keep[cut].astype(full) + here[cut].astype(full)).astype(low)
        for cut in (slice(half, None), slice(0, half))
    ]
    return tuple(added)


def nt(a, b):
    return lax.dot_general(a, b, (((1,), (1,)), ((), ())), preferred_element_type=full)

def nn(a, b):
    return lax.dot_general(a, b, (((1,), (0,)), ((), ())), preferred_element_type=full)

def tn(a, b):
    return lax.dot_general(a, b, (((0,), (0,)), ((), ())), preferred_element_type=full)


def beside(ref):
    return jnp.concatenate([ref[0, h] for h in range(GROUP)], axis=1)

def key_steps(i, seq_len, query_rows, key_rows):
    free = (i * query_rows) // key_rows
    need = ((i + 1) * query_rows + BLOCK - 1 + key_rows - 1) // key_rows
    return free, jnp.minimum(need, seq_len // key_rows)

def forward_kernel(seq_len, query_rows, key_rows, limit_ref, q_ref, k_ref, vt_ref, low_ref, out_ref, lse_ref):
    i = pl.program_id(1)
    qt = beside(q_ref)
    width = GROUP * query_rows
    limit = jnp.concatenate([limit_ref[...]] * GROUP, axis=1)

    def step(masked, j, carry):
        peak, total, acc = carry
        start = pl.multiple_of(j * key_rows, key_rows)
        s = nn(k_ref[0, pl.ds(start, key_rows), :], qt)
        if masked:
            place = start + lax.broadcasted_iota(jnp.int32, (key_rows, 1), 0)
            s = jnp.where(place < limit, s, masked_score)
        new_peak = jnp.maximum(peak, jnp.max(s, axis=0, keepdims=True))
        shrink = jnp.exp(peak - new_peak)
        p = jnp.exp(s - new_peak)
        total = shrink * total + jnp.sum(p, axis=0, keepdims=True)
        acc = shrink * acc + nn(vt_ref[0, :, pl.ds(start, key_rows)], p.astype(low))
        return new_peak, total, acc

    free, need = key_steps(i, seq_len, query_rows, key_rows)
    carry = (
        jnp.full((1, width), masked_score, full),
        jnp.zeros((1, width), full),
        jnp.zeros((HEAD_DIM, width), full),
    )
    carry = lax.fori_loop(0, free, lambda j, c: step(False, j, c), carry)
    peak, total, acc = lax.fori_loop(free, need, lambda j, c: step(True, j, c), carry)
    out = acc / total
    lse = peak + jnp.log(total)
    for h in range(GROUP):
        cols = slice(h * query_rows, (h + 1) * query_rows)
        out_ref[0, h] = out[:, cols]
        low_ref[0, pl.ds(h * HEAD_DIM, HEAD_DIM), :] = out[:, cols].astype(low)
        lse_ref[0, h] = lse[:, cols]

def attention_forward(qt, k_rows, vt, limit, shard_len):
    kv_here, _, _, seq_len = qt.shape
    query_rows = min(256, shard_len)
    key_rows = min(512, seq_len)
    per = shard_len // query_rows
    return pl.pallas_call(
        functools.partial(forward_kernel, seq_len, query_rows, key_rows),
        grid=(kv_here, seq_len // query_rows),
        in_specs=[
            pl.BlockSpec((1, query_rows), lambda g, i: (0, i)),
            pl.BlockSpec((1, GROUP, HEAD_DIM, query_rows), lambda g, i: (g, 0, 0, i)),
            pl.BlockSpec((1, seq_len, HEAD_DIM), lambda g, i: (g, 0, 0)),
            pl.BlockSpec((1, HEAD_DIM, seq_len), lambda g, i: (g, 0, 0)),
        ],
        out_specs=[
            pl.BlockSpec((1, GROUP * HEAD_DIM, query_rows), lambda g, i: (i // per, g, i % per)),
            pl.BlockSpec((1, GROUP, HEAD_DIM, query_rows), lambda g, i: (g, 0, 0, i)),
            pl.BlockSpec((1, GROUP, 1, query_rows), lambda g, i: (g, 0, 0, i)),
        ],
        out_shape=[
            jax.ShapeDtypeStruct((seq_len // shard_len, kv_here * GROUP * HEAD_DIM, shard_len), low),
            jax.ShapeDtypeStruct((kv_here, GROUP, HEAD_DIM, seq_len), full),
            jax.ShapeDtypeStruct((kv_here, GROUP, 1, seq_len), full),
        ],
        compiler_params=vmem(40),
        name="attention_forward",
    )(limit, qt, k_rows, vt)

def backward_kernel(seq_len, query_rows, key_rows, limit_ref, q_ref, k_ref, v_ref, kt_ref, out_ref, lse_ref, dout_ref, dq_ref, dk_ref, dv_ref, dk_acc, dv_acc):
    i = pl.program_id(1)

    @pl.when(i == 0)
    def _():
        dk_acc[...] = jnp.zeros_like(dk_acc)
        dv_acc[...] = jnp.zeros_like(dv_acc)

    qt = beside(q_ref)
    limit = jnp.concatenate([limit_ref[...]] * GROUP, axis=1)
    dout = jnp.concatenate([dout_ref[0, pl.ds(h * HEAD_DIM, HEAD_DIM), :] for h in range(GROUP)], axis=1)
    delta = jnp.sum(dout.astype(full) * beside(out_ref), axis=0, keepdims=True)
    lse = beside(lse_ref)

    def step(masked, j, dq):
        start = pl.multiple_of(j * key_rows, key_rows)
        keys = pl.ds(start, key_rows)
        s = nn(k_ref[0, keys, :], qt)
        if masked:
            place = start + lax.broadcasted_iota(jnp.int32, (key_rows, 1), 0)
            s = jnp.where(place < limit, s, masked_score)
        p = jnp.exp(s - lse)
        dp = nn(v_ref[0, keys, :], dout)
        ds = (p * (dp - delta)).astype(low)
        dk_acc[:, keys] += nt(qt, ds)
        dv_acc[:, keys] += nt(dout, p.astype(low))
        return dq + nn(kt_ref[0, :, keys], ds)

    free, need = key_steps(i, seq_len, query_rows, key_rows)
    dq = jnp.zeros((HEAD_DIM, GROUP * query_rows), full)
    dq = lax.fori_loop(0, free, lambda j, c: step(False, j, c), dq)
    dq = lax.fori_loop(free, need, lambda j, c: step(True, j, c), dq) * attn_mult
    for h in range(GROUP):
        dq_ref[0, h] = dq[:, h * query_rows : (h + 1) * query_rows].astype(low)

    @pl.when(i == pl.num_programs(1) - 1)
    def _():
        dk_ref[0] = dk_acc[...].astype(low)
        dv_ref[0] = dv_acc[...].astype(low)

def attention_backward(qt, k_rows, v_rows, kt, limit, out, lse, d_out):
    kv_here, _, _, seq_len = qt.shape
    shard_len = d_out.shape[2]
    query_rows = min(256, shard_len)
    key_rows = min(512, seq_len)
    per = shard_len // query_rows
    quarter = lambda g, i: (g, 0, 0, i)
    whole = lambda g, i: (g, 0, 0)
    return pl.pallas_call(
        functools.partial(backward_kernel, seq_len, query_rows, key_rows),
        grid=(kv_here, seq_len // query_rows),
        in_specs=[
            pl.BlockSpec((1, query_rows), lambda g, i: (0, i)),
            pl.BlockSpec((1, GROUP, HEAD_DIM, query_rows), quarter),
            pl.BlockSpec((1, seq_len, HEAD_DIM), whole),
            pl.BlockSpec((1, seq_len, HEAD_DIM), whole),
            pl.BlockSpec((1, HEAD_DIM, seq_len), whole),
            pl.BlockSpec((1, GROUP, HEAD_DIM, query_rows), quarter),
            pl.BlockSpec((1, GROUP, 1, query_rows), quarter),
            pl.BlockSpec((1, GROUP * HEAD_DIM, query_rows), lambda g, i: (i // per, g, i % per)),
        ],
        out_specs=[
            pl.BlockSpec((1, GROUP, HEAD_DIM, query_rows), quarter),
            pl.BlockSpec((1, HEAD_DIM, seq_len), whole),
            pl.BlockSpec((1, HEAD_DIM, seq_len), whole),
        ],
        out_shape=[
            jax.ShapeDtypeStruct((kv_here, GROUP, HEAD_DIM, seq_len), low),
            jax.ShapeDtypeStruct((kv_here, HEAD_DIM, seq_len), low),
            jax.ShapeDtypeStruct((kv_here, HEAD_DIM, seq_len), low),
        ],
        scratch_shapes=[pltpu.VMEM((HEAD_DIM, seq_len), full), pltpu.VMEM((HEAD_DIM, seq_len), full)],
        compiler_params=vmem(40),
        name="attention_backward",
    )(limit, qt, k_rows, v_rows, kt, out, lse, d_out)


def vmem(mib):
    return pltpu.CompilerParams(vmem_limit_bytes=mib * 2**20)


def own_row(ref, row):
    return ref[pl.ds(row, 1), :]


def experts_kernel(
    base, every, at_ref, tok_ref, slot_ref, member_ref, router_ref, wg_ref, wu_ref, wd_ref, *refs
):
    part_ref, x_ref, g_ref, u_ref, gates_ref, acc, gates_all = refs[-7:]
    e, experts = pl.program_id(0), pl.num_programs(0)
    slots = x_ref.shape[2]

    @pl.when(e == 0)
    def _():
        member = member_ref[...] > 0
        chosen = jnp.where(member, nt(router_ref[...], tok_ref[...]), masked_score)
        chosen = jnp.exp(chosen - jnp.max(chosen, axis=0, keepdims=True))
        chosen = jnp.where(member, chosen, 0.0)
        gates_all[...] = chosen / jnp.sum(chosen, axis=0, keepdims=True)
        acc[...] = refs[0][...].astype(full) if base else jnp.zeros_like(acc)

    gate_row = own_row(gates_all, at_ref[1] * every + base + e)
    gates_ref[pl.ds(e, 1), :] = gate_row
    place = lax.broadcasted_iota(jnp.int32, (slots, 1), 0)
    here = place == own_row(slot_ref, base + e)
    x = nn(jnp.where(here, 1.0, 0.0).astype(low), tok_ref[...]).astype(low)
    x_ref[0, 0] = x
    g = nn(x, wg_ref[0])
    u = nn(x, wu_ref[0])
    g_ref[0, 0] = g.astype(low)
    u_ref[0, 0] = u.astype(low)
    act = (g * jax.nn.sigmoid(g) * u).astype(low)
    y = nn(act, wd_ref[0]).astype(low)
    acc[...] += tn(jnp.where(here, gate_row, 0.0).astype(low), y)

    @pl.when(e == experts - 1)
    def _():
        part_ref[...] = acc[...].astype(low).reshape(part_ref.shape)


def back_kernel(
    base, at_ref, tok_ref, slot_ref, gates_ref, mix_ref, router_ref, g_ref, u_ref, wg_ref, wu_ref, wd_ref, *refs
):
    part_ref, d_ref, dgu_ref, act_ref, dlog_ref, acc, dlog_all = refs[-7:]
    e, experts = pl.program_id(0), pl.num_programs(0)
    slots, hidden = g_ref.shape[2:]

    @pl.when(e == 0)
    def _():
        dlog_all[...] = jnp.zeros_like(dlog_all)
        acc[...] = refs[0][...].astype(full) if base else jnp.zeros_like(acc)

    place = lax.broadcasted_iota(jnp.int32, (slots, 1), 0)
    here = place == own_row(slot_ref, base + e)
    pick = jnp.where(here, 1.0, 0.0).astype(low)
    gate_row = own_row(gates_ref, e)
    gate = jnp.sum(jnp.where(here, gate_row, 0.0), axis=1, keepdims=True)
    d = nn(pick, tok_ref[...]).astype(low)
    d_ref[0, 0] = d
    d_act = nt(d, wd_ref[0])
    g, u = g_ref[0, 0].astype(full), u_ref[0, 0].astype(full)
    sig = jax.nn.sigmoid(g)
    silu = g * sig
    act = silu * u
    d_gate = jnp.sum(d_act * act, axis=1, keepdims=True)
    d_gate = jnp.sum(jnp.where(here, d_gate, 0.0), axis=0, keepdims=True)
    dlog_all[pl.ds(e, 1), :] = gate_row * (d_gate - mix_ref[...])
    act_ref[0, 0] = (act * gate).astype(low)
    d_act = d_act * gate
    d_g = (d_act * u * (sig + silu * (1.0 - sig))).astype(low)
    d_u = (d_act * silu).astype(low)
    dgu_ref[0, 0, :, :hidden] = d_g
    dgu_ref[0, 0, :, hidden:] = d_u
    dx = (nt(d_g, wg_ref[0]) + nt(d_u, wu_ref[0])).astype(low)
    acc[...] += tn(pick, dx)

    @pl.when(e == experts - 1)
    def _():
        dlog = dlog_all[...].astype(low)
        dlog_ref[...] = dlog
        part = acc[...] + tn(dlog, router_ref[...])
        part_ref[...] = part.astype(low).reshape(part_ref.shape)


def by_expert(*shape):
    return pl.BlockSpec((1,) + shape, lambda e, at: (e, 0, 0))


def in_turn(base, turn, *shape):
    return pl.BlockSpec((1, 1) + shape, lambda e, at: (base + e, turn, 0, 0))


def same(*shape):
    return pl.BlockSpec(shape, lambda e, at: (0, 0))


def in_place(*shape):
    return pl.BlockSpec((1,) + shape, lambda e, at: (at[0], 0, 0))


def shard_call(kernel, name, at, inputs, in_specs, outs, buffers, scratch, experts, partial):
    last = partial is not None
    buffers = list(buffers)
    part_out, rest_out = outs[0], outs[1:]
    if not last:
        shape = part_out[1].shape[1:]
        part_out = (same(*shape), jax.ShapeDtypeStruct(shape, low))
    else:
        inputs, in_specs = inputs + [partial], in_specs + [same(*partial.shape)]
    kept = buffers[0] if buffers else None
    passed = [] if not buffers else (buffers if last and kept is not None else buffers[1:])
    start = len(inputs) + 1
    skip = 0 if last and kept is not None else 1
    aliases = {start + i: i + skip for i in range(len(passed))}
    results = pl.pallas_call(
        kernel,
        grid_spec=pltpu.PrefetchScalarGridSpec(
            num_scalar_prefetch=1,
            grid=(experts,),
            in_specs=in_specs + [pl.BlockSpec(memory_space=pl.ANY)] * len(passed),
            out_specs=[part_out[0]] + [spec for spec, _ in rest_out],
            scratch_shapes=scratch,
        ),
        out_shape=[part_out[1]] + [shape for _, shape in rest_out],
        input_output_aliases=aliases,
        compiler_params=vmem(48),
        name=name,
    )(at, *inputs, *passed)
    if last:
        return None, list(results[:-1]), results[-1]
    return results[0], [kept] + list(results[1:-1]), results[-1]


def experts_forward(
    base, every, turn, devs, at, tokens, slot_of, member, router, weights, slots, buffers, partial
):
    experts, width, hidden = weights[0].shape
    count = tokens.shape[0]
    total_experts = member.shape[0]
    return shard_call(
        functools.partial(experts_kernel, base, every),
        "experts_forward",
        at,
        [tokens, slot_of, member, router, *weights],
        [
            same(count, width),
            same(every, count),
            same(total_experts, count),
            same(total_experts, width),
            by_expert(width, hidden),
            by_expert(width, hidden),
            by_expert(hidden, width),
        ],
        [
            (in_place(count, width), jax.ShapeDtypeStruct((devs, count, width), low)),
            (
                in_turn(base, turn, slots, width),
                jax.ShapeDtypeStruct((every, devs, slots, width), low),
            ),
            (
                in_turn(base, turn, slots, hidden),
                jax.ShapeDtypeStruct((every, devs, slots, hidden), low),
            ),
            (
                in_turn(base, turn, slots, hidden),
                jax.ShapeDtypeStruct((every, devs, slots, hidden), low),
            ),
            (same(experts, count), jax.ShapeDtypeStruct((experts, count), full)),
        ],
        buffers,
        [pltpu.VMEM((count, width), full), pltpu.VMEM((total_experts, count), full)],
        experts,
        partial,
    )


def experts_backward(
    base, turn, devs, at, d_tokens, slot_of, gates, mix_dot, router, g, u, weights, buffers, partial
):
    experts, width, hidden = weights[0].shape
    count = d_tokens.shape[0]
    every, _, slots, _ = g.shape
    lines = router.shape[0]
    return shard_call(
        functools.partial(back_kernel, base),
        "experts_backward",
        at,
        [d_tokens, slot_of, gates, mix_dot, router, g, u, *weights],
        [
            same(count, width),
            same(every, count),
            same(experts, count),
            same(1, count),
            same(lines, width),
            in_turn(base, turn, slots, hidden),
            in_turn(base, turn, slots, hidden),
            by_expert(width, hidden),
            by_expert(width, hidden),
            by_expert(hidden, width),
        ],
        [
            (in_place(count, width), jax.ShapeDtypeStruct((devs, count, width), low)),
            (
                in_turn(base, turn, slots, width),
                jax.ShapeDtypeStruct((every, devs, slots, width), low),
            ),
            (
                in_turn(base, turn, slots, 2 * hidden),
                jax.ShapeDtypeStruct((every, devs, slots, 2 * hidden), low),
            ),
            (
                in_turn(base, turn, slots, hidden),
                jax.ShapeDtypeStruct((every, devs, slots, hidden), low),
            ),
            (same(lines, count), jax.ShapeDtypeStruct((lines, count), low)),
        ],
        buffers,
        [pltpu.VMEM((count, width), full), pltpu.VMEM((lines, count), full)],
        experts,
        partial,
    )


def halving_masks(bits):
    masks = [0]
    for bit in reversed(bits):
        masks = masks + [mask ^ bit for mask in masks]
    return masks


def gate_up_kernel(bits_a, bits_b, me_ref, x_ref, dgu_ref, *refs):
    outs, acc = refs[:4], refs[4]
    hidden = outs[0].shape[3]
    acc[...] = tn(x_ref[0], dgu_ref[0])
    for part, bits in enumerate((bits_a, bits_b)):
        keep, send = outs[2 * part], outs[2 * part + 1]
        rows = keep.shape[2]
        for place, mask in enumerate(halving_masks(bits)):
            start = pl.multiple_of((me_ref[0] ^ mask) * rows, rows)
            out = keep if place < keep.shape[0] else send
            block = acc[pl.ds(start, rows), part * hidden : (part + 1) * hidden]
            out[place % keep.shape[0], 0] = block.astype(low)


def gate_up_grads(me, rows, d_gu, bits_a, bits_b):
    experts, count, width = rows.shape
    hidden = d_gu.shape[2] // 2
    devs = 2 ** len(bits_a)
    shape = (width // devs, hidden)
    outs = pl.pallas_call(
        functools.partial(gate_up_kernel, bits_a, bits_b),
        grid_spec=pltpu.PrefetchScalarGridSpec(
            num_scalar_prefetch=1,
            grid=(experts,),
            in_specs=[by_expert(count, width), by_expert(count, 2 * hidden)],
            out_specs=[pl.BlockSpec((devs // 2, 1) + shape, lambda e, me: (0, e, 0, 0))] * 4,
            scratch_shapes=[pltpu.VMEM((width, 2 * hidden), full)],
        ),
        out_shape=[jax.ShapeDtypeStruct((devs // 2, experts) + shape, low)] * 4,
        compiler_params=vmem(48),
        name="gate_up_grads",
    )(me, rows, d_gu)
    return (outs[0], outs[1]), (outs[2], outs[3])


def down_kernel(act_ref, d_ref, out_ref):
    out_ref[0] = tn(act_ref[0], d_ref[0]).astype(low)


def down_grads(act, d_rows):
    experts, count, hidden = act.shape
    width = d_rows.shape[2]
    one = lambda *shape: pl.BlockSpec((1,) + shape, lambda e: (e, 0, 0))
    return pl.pallas_call(
        down_kernel,
        grid=(experts,),
        in_specs=[one(count, hidden), one(count, width)],
        out_specs=one(hidden, width),
        out_shape=jax.ShapeDtypeStruct((experts, hidden, width), low),
        compiler_params=vmem(48),
        name="down_grads",
    )(act, d_rows)


def shards(
    inputs,
    teacher,
    routes,
    valid_mask,
    block_lengths,
    gain_one,
    w_qkv,
    w_out,
    gain_two,
    w_router,
    w_gate,
    w_up,
    w_down,
):
    n = lax.axis_size("seq")
    me = lax.axis_index("seq")
    mine = lax.axis_index("fsdp")
    seqs_here, shard_len, width = inputs.shape
    assert seqs_here == 1
    seq_len = shard_len * n
    tokens_all = lax.axis_size("fsdp") * seq_len
    kv_here = KV_HEADS // n
    heads_w = kv_here * GROUP * HEAD_DIM
    group_w = kv_here * (GROUP + 2) * HEAD_DIM
    experts_here = w_gate.shape[0]
    expert_total = experts_here * n
    top_count = routes.shape[2]
    capacity = 3 * shard_len * top_count // (2 * expert_total)
    slots = -(-capacity // 16) * 16
    slot_rows = n * slots
    order_a, order_b = fsdp_bits()
    order = jnp.array(arrival_order(n), jnp.int32)[me]
    x_low = inputs.reshape(shard_len, width)

    own_qkv = lax.dynamic_slice_in_dim(w_qkv, me * group_w, group_w, 1)
    small = jnp.concatenate([gain_one[:, None], gain_two[:, None], w_router], axis=1)
    small = doubling_gather(small, order_a)
    small = small[mine ^ jnp.arange(small.shape[0])].reshape(width, 2 + expert_total)
    full_qkv = lax.all_gather(own_qkv, "fsdp", axis=0, tiled=True)
    full_out = lax.all_gather(w_out, "fsdp", axis=0, tiled=True)
    cut = -(-7 * experts_here // 10)
    weights = [
        [lax.all_gather(w[group], "fsdp", axis=1, tiled=True) for w in (w_gate, w_up, w_down)]
        for group in (slice(0, cut), slice(cut, None))
    ]
    bases = (0, cut)
    full_g1 = small[:, 0].astype(full)
    full_g2 = small[:, 1].astype(full)
    router = small[:, 2:].T
    own_router = lax.dynamic_slice_in_dim(router, me * experts_here, experts_here, 0)
    own_routers = [
        jnp.pad(rows, ((0, -rows.shape[0] % 16), (0, 0)))
        for rows in (own_router[:cut], own_router[cut:])
    ]
    valid_rows = valid_mask.reshape(shard_len).astype(full)

    routes_low = jnp.concatenate([routes.reshape(shard_len, top_count).T, valid_mask], axis=0)
    routes_all = by_place(line_gather(routes_low))[order]
    valid_count = total(jnp.sum(routes_all[:, top_count]).astype(full).reshape(1, 1), "fsdp")[0, 0]
    expert_ids = jnp.arange(expert_total, dtype=jnp.int32)
    member = jnp.any(routes_all[:, :top_count, None, :] == expert_ids[:, None], axis=1)
    own_member = lax.dynamic_slice_in_dim(member, me * experts_here, experts_here, 1)
    earlier = jnp.arange(shard_len)[:, None] < jnp.arange(shard_len)[None, :]
    slot_of = dot("net,tu->neu", own_member.astype(low), earlier.astype(low)).astype(jnp.int32)
    slot_of = jnp.where(own_member, slot_of, -1)
    member = member.astype(full)

    x_all = by_place(line_gather(x_low)).reshape(seq_len, width)
    normed_one = rms_norm(x_all.astype(full), full_g1).astype(low)
    qkv_rows = dot("td,dc->ct", normed_one, full_qkv)
    qkv_rows = qkv_rows.reshape(kv_here, GROUP + 2, HEAD_DIM, seq_len)
    positions = jnp.arange(seq_len, dtype=jnp.int32)
    cosine, sine_vals = rope_tables(positions.astype(full), HEAD_DIM)
    turned = rotate(qkv_rows[:, : GROUP + 1], cosine, sine_vals).astype(low)
    query = turned[:, :GROUP] * jnp.asarray(attn_mult, low)
    key = turned[:, GROUP]
    value = qkv_rows[:, GROUP + 1].astype(low)
    key_rows = jnp.swapaxes(key, 1, 2)
    value_rows = jnp.swapaxes(value, 1, 2)
    limit = block_limits(block_lengths[0], positions)[None]
    attended, out_heads, lse = attention_forward(query, key_rows, value, limit, shard_len)
    moved = exchange(attended)
    moved, slot_of, member, own_routers = tie(moved, slot_of, member, own_routers)
    attn_rows = by_place(nearest(*moved)).reshape(HEADS * HEAD_DIM, shard_len)
    projected = dot("kt,kd->td", attn_rows, full_out)
    hidden = x_low.astype(full) + resid_mult * projected
    normed_two, norm_two_pull = jax.vjp(rms_norm, hidden, full_g2)

    tokens = [normed_two.astype(low)]
    rights, lefts = [tokens[0]], [tokens[0]]
    buffers, gates = [None], []
    partials = []
    for turn in range(n):
        if turn < n - 1:
            right, left, tokens[turn] = tie(rights[turn], lefts[turn], tokens[turn])
            right, left = line_move(right, left, turn + 1)
        partial, buffers, shard_gates = experts_forward(
            0, experts_here, turn, n, jnp.stack([order[turn], me]), tokens[turn], slot_of[turn],
            member[turn], router, weights[0], slots, buffers, None,
        )
        partials.append(partial)
        if turn < n - 1:
            right, left, shard_gates = tie(right, left, shard_gates)
            rights.append(right)
            lefts.append(left)
            tokens.append(arrived(rights, lefts, turn + 1))
        gates.append([shard_gates])
    for turn in range(n):
        _, buffers, shard_gates = experts_forward(
            cut, experts_here, turn, n, jnp.stack([order[turn], me]), tokens[turn], slot_of[turn],
            member[turn], router, weights[1], slots, buffers, partials[turn],
        )
        gates[turn].append(shard_gates)
    mix_parts, expert_in, gate_act, up_act = buffers
    right = left = None
    for k in range(n - 1, 0, -1):
        moving = tie(*line_send(mix_parts, k, right, left))
        right, left = tie(*line_pass(*moving, k))
    mixture = line_end(mix_parts, right, left)
    output_f32 = hidden + resid_mult * mixture
    activations = output_f32.astype(low).reshape(1, shard_len, width)
    error_rows = output_f32 - teacher.astype(full).reshape(shard_len, width)
    weighted = valid_rows[:, None] * error_rows
    loss_steps = total_steps(jnp.sum(weighted * error_rows).reshape(1, 1), "seq", "fsdp")
    squares = next(loss_steps)
    d_out = weighted * (tokens_all / valid_count)

    d_mix = resid_mult * d_out
    d_tokens = d_mix.astype(low)
    mix_dot = jnp.sum(d_mix * mixture, axis=1)[None]
    rights, lefts = [d_tokens], [d_tokens]
    dot_rights, dot_lefts = [mix_dot], [mix_dot]
    buffers, d_logits = [None], []
    for turn in range(n):
        if turn < n - 1:
            (right, left), (dot_right, dot_left), d_tokens = tie(
                (rights[turn], lefts[turn]), (dot_rights[turn], dot_lefts[turn]), d_tokens
            )
            dot_right, dot_left = line_move(dot_right, dot_left, turn + 1)
            right, left = line_move(right, left, turn + 1)
        partial, shard_logits = None, []
        for group in (0, 1):
            partial, buffers, group_logits = experts_backward(
                bases[group], turn, n, jnp.stack([order[turn], me]), d_tokens, slot_of[turn],
                gates[turn][group], mix_dot, own_routers[group], gate_act, up_act, weights[group],
                buffers, partial,
            )
            shard_logits.append(group_logits)
        if turn < n - 1:
            right, left, dot_right, dot_left, shard_logits, squares = tie(
                right, left, dot_right, dot_left, shard_logits, squares
            )
            squares = loss_steps.send(squares)
            rights.append(right)
            lefts.append(left)
            dot_rights.append(dot_right)
            dot_lefts.append(dot_left)
            d_tokens = arrived(rights, lefts, turn + 1)
            mix_dot = arrived(dot_rights, dot_lefts, turn + 1)
        d_logits.append(shard_logits)
    d_parts, d_rows, d_gate_up, act_low = buffers
    expert_in = expert_in.reshape(experts_here, slot_rows, width)
    d_rows = d_rows.reshape(experts_here, slot_rows, width)
    d_gate_up = d_gate_up.reshape(experts_here, slot_rows, -1)
    act_low = act_low.reshape(experts_here, slot_rows, -1)

    right = left = None
    for k in range(n - 1, 0, -1):
        moving = line_send(d_parts, k, right, left)
        if k == n - 1:
            moving, expert_in, d_gate_up = tie(moving, expert_in, d_gate_up)
            right, left = line_pass(*moving, k)
            gate_pair, up_pair = gate_up_grads(
                mine.reshape(1), expert_in, d_gate_up, order_a, order_b
            )
            right, left, gate_pair, up_pair, squares = tie(right, left, gate_pair, up_pair, squares)
        elif k == n - 2:
            moving, gate_pair, up_pair, act_low, d_rows = tie(
                moving, gate_pair, up_pair, act_low, d_rows
            )
            right, left = line_pass(*moving, k)
            gate_here = swap(gate_pair[1], "fsdp", order_a[0])
            up_here = swap(up_pair[1], "fsdp", order_b[0])
            down_part = down_grads(act_low, d_rows)
            right, left, gate_here, up_here, down_part, squares = tie(
                right, left, gate_here, up_here, down_part, squares
            )
        elif k == n - 3:
            moving, gate_here, up_here = tie(moving, gate_here, up_here)
            right, left = line_pass(*moving, k)
            gate_send, gate_keep = halve(gate_pair[0], gate_here)
            up_send, up_keep = halve(up_pair[0], up_here)
            right, left, gate_send, up_send, squares = tie(right, left, gate_send, up_send, squares)
        else:
            right, left, squares = tie(*line_pass(*tie(*moving), k), squares)
        squares = loss_steps.send(squares)
    d_normed_two = line_end(d_parts, right, left)
    down_sum = lax.psum_scatter(down_part, "fsdp", scatter_dimension=1, tiled=True)

    d_hidden_norm, gain_two_part = norm_two_pull(d_normed_two)
    d_hidden = d_out + d_hidden_norm
    d_proj = (resid_mult * d_hidden).astype(low)
    d_attended = dot("kd,td->kt", full_out, d_proj).astype(low)
    moved = exchange(d_attended.reshape(n, heads_w, shard_len))
    gate_here = swap(gate_send, "fsdp", order_a[1])
    up_here = swap(up_send, "fsdp", order_b[1])
    out_part = dot("kt,td->kd", attn_rows, d_proj).astype(low)
    d_logits = [
        jnp.concatenate([first[:cut], second[: experts_here - cut]]) for first, second in d_logits
    ]
    router_part = sum(
        dot("td,et->de", shard, shard_logits) for shard, shard_logits in zip(tokens, d_logits)
    )
    moved, out_part, router_part = tie(moved, out_part, router_part)
    out_sum = lax.psum_scatter(out_part, "fsdp", scatter_dimension=0, tiled=True)
    d_heads = by_place(nearest(*moved))
    query_grad, key_grad, value_grad = attention_backward(
        query, key_rows, value_rows, key, limit, out_heads, lse, d_heads
    )
    (query_grad, key_grad, value_grad), gate_here, up_here, down_sum, out_sum = tie(
        (query_grad, key_grad, value_grad), gate_here, up_here, down_sum, out_sum
    )
    out_sum = lax.psum(out_sum, "seq")
    d_turned = jnp.concatenate([query_grad, key_grad[:, None]], axis=1).astype(full)
    d_turned = rotate(d_turned, cosine, -sine_vals).astype(low)
    d_qkv = jnp.concatenate([d_turned, value_grad[:, None]], axis=1).reshape(group_w, seq_len)
    d_parts = dot("ct,dc->td", d_qkv, full_qkv).astype(low).reshape(n, shard_len, width)
    moving = line_send(d_parts, n - 1, None, None)
    moving, d_qkv, gate_here, up_here = tie(moving, d_qkv, gate_here, up_here)
    right, left = line_pass(*moving, n - 1)
    own_columns = jnp.zeros((width, expert_total), full)
    own_columns = lax.dynamic_update_slice_in_dim(own_columns, router_part, me * experts_here, 1)
    qkv_part = jnp.concatenate(
        [dot("td,ct->dc", normed_one, d_qkv), own_columns, gain_two_part[:, None]], axis=1
    ).astype(low)
    qkv_sum = lax.psum_scatter(qkv_part, "fsdp", scatter_dimension=0, tiled=True)
    gate_send, gate_keep = halve(gate_keep, gate_here)
    up_send, up_keep = halve(up_keep, up_here)
    right, left, qkv_part, gate_send, up_send = tie(right, left, qkv_part, gate_send, up_send)
    gate_here = swap(gate_send, "fsdp", order_a[2])
    up_here = swap(up_send, "fsdp", order_b[2])
    for k in range(n - 2, 0, -1):
        moving = tie(*line_send(d_parts, k, right, left))
        right, left = line_pass(*moving, k)
        if k == 1:
            right, left, qkv_sum = tie(right, left, qkv_sum)
        else:
            right, left = tie(right, left)
    d_normed_one = line_end(d_parts, right, left)
    _, norm_one_pull = jax.vjp(lambda v: rms_norm(v, full_g1), x_low.astype(full))
    input_grad = (d_hidden + norm_one_pull(d_normed_one)[0]).reshape(1, shard_len, width)

    input_grad, gate_here, up_here, qkv_sum, out_sum = tie(
        input_grad, gate_here, up_here, qkv_sum, out_sum
    )
    for bit_a, bit_b in zip(order_a[3:], order_b[3:]):
        gate_send, gate_keep = halve(gate_keep, gate_here)
        up_send, up_keep = halve(up_keep, up_here)
        gate_here = swap(gate_send, "fsdp", bit_a)
        up_here = swap(up_send, "fsdp", bit_b)
    gate_grad = halve(gate_keep, gate_here)
    up_grad = halve(up_keep, up_here)
    down_grad = down_sum.astype(full)
    out_grad = out_sum.astype(full)
    sums = by_place(line_gather(qkv_sum)).astype(full)
    qkv_grad = jnp.swapaxes(sums[:, :, :group_w], 0, 1).reshape(-1, QKV_W)
    rest = jnp.sum(sums[:, :, group_w:], axis=0)
    router_grad, gain_two_grad = rest[:, :expert_total], rest[:, expert_total]
    gain_one_grad = jnp.sum(qkv_grad * w_qkv.astype(full), axis=1) / gain_one.astype(full)
    for _ in range(2):
        squares = loss_steps.send(squares)
    loss_value = squares[0, 0] / (valid_count * width)
    return (
        activations,
        loss_value,
        input_grad,
        gain_one_grad,
        qkv_grad,
        out_grad,
        gain_two_grad,
        router_grad,
        gate_grad,
        up_grad,
        down_grad,
    )


def solution(mesh):
    return jax.shard_map(
        shards,
        mesh=mesh,
        in_specs=(
            P("fsdp", "seq", None),
            P("fsdp", "seq", None),
            P("fsdp", "seq", None),
            P("fsdp", "seq"),
            P("fsdp", None),
            P("fsdp"),
            P("fsdp", None),
            P("fsdp", None),
            P("fsdp"),
            P("fsdp", None),
            P("seq", "fsdp", None),
            P("seq", "fsdp", None),
            P("seq", "fsdp", None),
        ),
        out_specs=(
            P("fsdp", "seq", None),
            P(),
            P("fsdp", "seq", None),
            P("fsdp"),
            P("fsdp", None),
            P("fsdp", None),
            P("fsdp"),
            P("fsdp", None),
            P("seq", "fsdp", None),
            P("seq", "fsdp", None),
            P("seq", "fsdp", None),
        ),
        check_vma=False,
    )
```

```python
import functools

import jax
import jax.numpy as jnp
from jax import lax
from jax.experimental import pallas as pl
from jax.experimental.pallas import tpu as pltpu
from jax.sharding import PartitionSpec as P

HEADS = 24
KV_HEADS = 8
HEAD_DIM = 64
BLOCK = 256
GROUP = 3
QKV_W = 2560


epsilon = 1e-06
attn_mult = 0.015625
resid_mult = 0.22
rope_base = 10000.0
masked_score = -1e30

low = jnp.bfloat16
full = jnp.float32


def dot(spec, left, right):
    return jnp.einsum(spec, left, right, preferred_element_type=full)


def rms_norm(values, gain_vec):
    inv_rms = lax.rsqrt(jnp.mean(values * values, axis=-1, keepdims=True) + epsilon)
    return values * inv_rms * gain_vec


def rope_tables(positions, head_dim):
    half_dim = head_dim // 2
    frequency = rope_base ** (-(2.0 * jnp.arange(half_dim, dtype=full)) / head_dim)
    angles = frequency[:, None] * positions[None, :]
    return (jnp.cos(angles), jnp.sin(angles))


def rotate(values, cosine, sine_vals):
    half_dim = values.shape[-2] // 2
    front_half = values[..., :half_dim, :]
    back_half = values[..., half_dim:, :]
    return jnp.concatenate(
        [front_half * cosine - back_half * sine_vals, back_half * cosine + front_half * sine_vals],
        axis=-2,
    )


def block_limits(lengths_row, positions):
    block_ends = jnp.cumsum(lengths_row)
    open_ends = jnp.where(block_ends[None, :] > positions[:, None], block_ends[None, :], positions.shape[0])
    return jnp.min(open_ends, axis=1).astype(jnp.int32)


def tie(*groups):
    return lax.optimization_barrier(groups)


def line_move(right, left, k):
    n = lax.axis_size("seq")
    return (
        lax.ppermute(right, "seq", [(i, i + 1) for i in range(k - 1, n - 1)]),
        lax.ppermute(left, "seq", [(i, i - 1) for i in range(1, n - k + 1)]),
    )


def line_gather(block):
    n = lax.axis_size("seq")
    rights, lefts = [block], [block]
    for k in range(1, n):
        right, left = tie(*line_move(rights[-1], lefts[-1], k))
        rights.append(right)
        lefts.append(left)
    return nearest(rights, lefts)


def nearest(rights, lefts):
    n = lax.axis_size("seq")
    me = lax.axis_index("seq")
    return [rights[0]] + [jnp.where(me >= k, rights[k], lefts[n - k]) for k in range(1, n)]


def arrival_order(n):
    order = []
    for me in range(n):
        both = min(me, n - 1 - me)
        places = [me]
        for k in range(1, n):
            places += [me - k] if me >= k and (k <= both or me > n - 1 - me) else []
            places += [me + k] if me + k < n and (k <= both or me < n - 1 - me) else []
        order.append(places)
    return order


def arrived(rights, lefts, turn):
    n = lax.axis_size("seq")
    me = lax.axis_index("seq")
    sources = {}
    for dev, places in enumerate(arrival_order(n)):
        gap = dev - places[turn]
        sources.setdefault(gap, []).append(dev)
    block = None
    for gap, devs in sources.items():
        moved = rights[gap] if gap >= 0 else lefts[-gap]
        if block is None:
            block = moved
        else:
            mine = jnp.array([dev in devs for dev in range(n)])[me]
            block = jnp.where(mine, moved, block)
    return block


def at_place(placed, place):
    return lax.dynamic_index_in_dim(placed, place % lax.axis_size("seq"), 0, keepdims=False)


def line_send(parts, k, right, left):
    me = lax.axis_index("seq")
    to_right, to_left = at_place(parts, me + k), at_place(parts, me - k)
    if right is not None:
        to_right = (to_right.astype(full) + right.astype(full)).astype(low)
        to_left = (to_left.astype(full) + left.astype(full)).astype(low)
    return to_right, to_left


def line_pass(to_right, to_left, k):
    n = lax.axis_size("seq")
    return (
        lax.ppermute(to_right, "seq", [(i, i + 1) for i in range(n - k)]),
        lax.ppermute(to_left, "seq", [(i, i - 1) for i in range(k, n)]),
    )


def line_end(parts, right, left):
    own = at_place(parts, lax.axis_index("seq")).astype(full)
    return own + (right.astype(full) + left.astype(full))


def by_place(blocks):
    n = lax.axis_size("seq")
    me = lax.axis_index("seq")
    placed = jnp.zeros((n,) + blocks[0].shape, blocks[0].dtype)
    for k, block in enumerate(blocks):
        placed = lax.dynamic_update_index_in_dim(placed, block, (me - k) % n, 0)
    return placed


def exchange(blocks):
    n = lax.axis_size("seq")
    me = lax.axis_index("seq")
    rights, lefts = [at_place(blocks, me)], [at_place(blocks, me)]
    for k in range(1, n):
        to_right, to_left = at_place(blocks, me + k), at_place(blocks, me - k)
        rights.append(lax.ppermute(to_right, "seq", [(i, i + k) for i in range(n - k)]))
        lefts.append(lax.ppermute(to_left, "seq", [(i, i - k) for i in range(k, n)]))
    return rights, lefts


def swap(value, axis, bit):
    return lax.ppermute(value, axis, [(i, i ^ bit) for i in range(lax.axis_size(axis))])


def total(value, *axes):
    for axis in axes:
        for step in range(lax.axis_size(axis).bit_length() - 1):
            value = value + swap(value, axis, 1 << step)
    return value


def fsdp_bits():
    bits = [1 << step for step in range(lax.axis_size("fsdp").bit_length() - 1)]
    return tuple(bits), tuple(bits[:1] + bits[:0:-1])


def total_steps(value, *axes):
    for axis in axes:
        for step in range(lax.axis_size(axis).bit_length() - 1):
            here = swap(value, axis, 1 << step)
            here = yield here
            value = value + here
    while True:
        yield value


class Halving:
    def __init__(self, keep, send, bits):
        self.terms, self.send, self.bits = [keep], send, list(bits)

    def go(self):
        self.terms = self.terms + [swap(self.send, "fsdp", self.bits.pop(0))]

    def add(self):
        half = self.terms[0].shape[0] // 2
        if half:
            self.send = sum(term[half:].astype(full) for term in self.terms).astype(low)
            self.terms = [term[:half] for term in self.terms]

    def finish(self):
        while self.bits:
            self.go()
            self.add()
        return sum(term[0].astype(full) for term in self.terms)


def land(sums, *others):
    tied = tie([each.terms[-1] for each in sums], *others)
    for each, here in zip(sums, tied[0]):
        each.terms = each.terms[:-1] + [here]
    return tied[1:]


def leave(sums, *others):
    tied = tie([each.send for each in sums], *others)
    for each, send in zip(sums, tied[0]):
        each.send = send
    return tied[1:]


def nt(a, b):
    return lax.dot_general(a, b, (((1,), (1,)), ((), ())), preferred_element_type=full)

def nn(a, b):
    return lax.dot_general(a, b, (((1,), (0,)), ((), ())), preferred_element_type=full)

def tn(a, b):
    return lax.dot_general(a, b, (((0,), (0,)), ((), ())), preferred_element_type=full)


def beside(ref):
    return jnp.concatenate([ref[0, h] for h in range(GROUP)], axis=1)

def key_steps(i, seq_len, query_rows, key_rows):
    free = (i * query_rows) // key_rows
    need = ((i + 1) * query_rows + BLOCK - 1 + key_rows - 1) // key_rows
    return free, jnp.minimum(need, seq_len // key_rows)

def forward_kernel(seq_len, query_rows, key_rows, limit_ref, q_ref, k_ref, vt_ref, low_ref, out_ref, lse_ref):
    i = pl.program_id(1)
    qt = beside(q_ref)
    width = GROUP * query_rows
    limit = jnp.concatenate([limit_ref[...]] * GROUP, axis=1)

    def step(masked, j, carry):
        peak, total, acc = carry
        start = pl.multiple_of(j * key_rows, key_rows)
        s = nn(k_ref[0, pl.ds(start, key_rows), :], qt)
        if masked:
            place = start + lax.broadcasted_iota(jnp.int32, (key_rows, 1), 0)
            s = jnp.where(place < limit, s, masked_score)
        new_peak = jnp.maximum(peak, jnp.max(s, axis=0, keepdims=True))
        shrink = jnp.exp(peak - new_peak)
        p = jnp.exp(s - new_peak)
        total = shrink * total + jnp.sum(p, axis=0, keepdims=True)
        acc = shrink * acc + nn(vt_ref[0, :, pl.ds(start, key_rows)], p.astype(low))
        return new_peak, total, acc

    free, need = key_steps(i, seq_len, query_rows, key_rows)
    carry = (
        jnp.full((1, width), masked_score, full),
        jnp.zeros((1, width), full),
        jnp.zeros((HEAD_DIM, width), full),
    )
    carry = lax.fori_loop(0, free, lambda j, c: step(False, j, c), carry)
    peak, total, acc = lax.fori_loop(free, need, lambda j, c: step(True, j, c), carry)
    out = acc / total
    lse = peak + jnp.log(total)
    for h in range(GROUP):
        cols = slice(h * query_rows, (h + 1) * query_rows)
        out_ref[0, h] = out[:, cols]
        low_ref[0, pl.ds(h * HEAD_DIM, HEAD_DIM), :] = out[:, cols].astype(low)
        lse_ref[0, h] = lse[:, cols]

def attention_forward(qt, k_rows, vt, limit, shard_len):
    kv_here, _, _, seq_len = qt.shape
    query_rows = min(256, shard_len)
    key_rows = min(512, seq_len)
    per = shard_len // query_rows
    return pl.pallas_call(
        functools.partial(forward_kernel, seq_len, query_rows, key_rows),
        grid=(kv_here, seq_len // query_rows),
        in_specs=[
            pl.BlockSpec((1, query_rows), lambda g, i: (0, i)),
            pl.BlockSpec((1, GROUP, HEAD_DIM, query_rows), lambda g, i: (g, 0, 0, i)),
            pl.BlockSpec((1, seq_len, HEAD_DIM), lambda g, i: (g, 0, 0)),
            pl.BlockSpec((1, HEAD_DIM, seq_len), lambda g, i: (g, 0, 0)),
        ],
        out_specs=[
            pl.BlockSpec((1, GROUP * HEAD_DIM, query_rows), lambda g, i: (i // per, g, i % per)),
            pl.BlockSpec((1, GROUP, HEAD_DIM, query_rows), lambda g, i: (g, 0, 0, i)),
            pl.BlockSpec((1, GROUP, 1, query_rows), lambda g, i: (g, 0, 0, i)),
        ],
        out_shape=[
            jax.ShapeDtypeStruct((seq_len // shard_len, kv_here * GROUP * HEAD_DIM, shard_len), low),
            jax.ShapeDtypeStruct((kv_here, GROUP, HEAD_DIM, seq_len), full),
            jax.ShapeDtypeStruct((kv_here, GROUP, 1, seq_len), full),
        ],
        compiler_params=vmem(40),
        name="attention_forward",
    )(limit, qt, k_rows, vt)

def backward_kernel(seq_len, query_rows, key_rows, limit_ref, q_ref, k_ref, v_ref, kt_ref, out_ref, lse_ref, dout_ref, dq_ref, dk_ref, dv_ref, dk_acc, dv_acc):
    i = pl.program_id(1)

    @pl.when(i == 0)
    def _():
        dk_acc[...] = jnp.zeros_like(dk_acc)
        dv_acc[...] = jnp.zeros_like(dv_acc)

    qt = beside(q_ref)
    limit = jnp.concatenate([limit_ref[...]] * GROUP, axis=1)
    dout = jnp.concatenate([dout_ref[0, pl.ds(h * HEAD_DIM, HEAD_DIM), :] for h in range(GROUP)], axis=1)
    delta = jnp.sum(dout.astype(full) * beside(out_ref), axis=0, keepdims=True)
    lse = beside(lse_ref)

    def step(masked, j, dq):
        start = pl.multiple_of(j * key_rows, key_rows)
        keys = pl.ds(start, key_rows)
        s = nn(k_ref[0, keys, :], qt)
        if masked:
            place = start + lax.broadcasted_iota(jnp.int32, (key_rows, 1), 0)
            s = jnp.where(place < limit, s, masked_score)
        p = jnp.exp(s - lse)
        dp = nn(v_ref[0, keys, :], dout)
        ds = (p * (dp - delta)).astype(low)
        dk_acc[:, keys] += nt(qt, ds)
        dv_acc[:, keys] += nt(dout, p.astype(low))
        return dq + nn(kt_ref[0, :, keys], ds)

    free, need = key_steps(i, seq_len, query_rows, key_rows)
    dq = jnp.zeros((HEAD_DIM, GROUP * query_rows), full)
    dq = lax.fori_loop(0, free, lambda j, c: step(False, j, c), dq)
    dq = lax.fori_loop(free, need, lambda j, c: step(True, j, c), dq) * attn_mult
    for h in range(GROUP):
        dq_ref[0, h] = dq[:, h * query_rows : (h + 1) * query_rows].astype(low)

    @pl.when(i == pl.num_programs(1) - 1)
    def _():
        dk_ref[0] = dk_acc[...].astype(low)
        dv_ref[0] = dv_acc[...].astype(low)

def attention_backward(qt, k_rows, v_rows, kt, limit, out, lse, d_out):
    kv_here, _, _, seq_len = qt.shape
    shard_len = d_out.shape[2]
    query_rows = min(256, shard_len)
    key_rows = min(512, seq_len)
    per = shard_len // query_rows
    quarter = lambda g, i: (g, 0, 0, i)
    whole = lambda g, i: (g, 0, 0)
    return pl.pallas_call(
        functools.partial(backward_kernel, seq_len, query_rows, key_rows),
        grid=(kv_here, seq_len // query_rows),
        in_specs=[
            pl.BlockSpec((1, query_rows), lambda g, i: (0, i)),
            pl.BlockSpec((1, GROUP, HEAD_DIM, query_rows), quarter),
            pl.BlockSpec((1, seq_len, HEAD_DIM), whole),
            pl.BlockSpec((1, seq_len, HEAD_DIM), whole),
            pl.BlockSpec((1, HEAD_DIM, seq_len), whole),
            pl.BlockSpec((1, GROUP, HEAD_DIM, query_rows), quarter),
            pl.BlockSpec((1, GROUP, 1, query_rows), quarter),
            pl.BlockSpec((1, GROUP * HEAD_DIM, query_rows), lambda g, i: (i // per, g, i % per)),
        ],
        out_specs=[
            pl.BlockSpec((1, GROUP, HEAD_DIM, query_rows), quarter),
            pl.BlockSpec((1, HEAD_DIM, seq_len), whole),
            pl.BlockSpec((1, HEAD_DIM, seq_len), whole),
        ],
        out_shape=[
            jax.ShapeDtypeStruct((kv_here, GROUP, HEAD_DIM, seq_len), low),
            jax.ShapeDtypeStruct((kv_here, HEAD_DIM, seq_len), low),
            jax.ShapeDtypeStruct((kv_here, HEAD_DIM, seq_len), low),
        ],
        scratch_shapes=[pltpu.VMEM((HEAD_DIM, seq_len), full), pltpu.VMEM((HEAD_DIM, seq_len), full)],
        compiler_params=vmem(40),
        name="attention_backward",
    )(limit, qt, k_rows, v_rows, kt, out, lse, d_out)


def vmem(mib):
    return pltpu.CompilerParams(vmem_limit_bytes=mib * 2**20)


def own_row(ref, row):
    return ref[pl.ds(row, 1), :]


def join_down(rows, block_ref, down_ref):
    hidden, width = down_ref.shape
    chunks = width // hidden
    for dev in range(hidden // rows):
        for chunk in range(chunks):
            start = (dev * chunks + chunk) * rows
            down_ref[dev * rows : (dev + 1) * rows, chunk * hidden : (chunk + 1) * hidden] = (
                block_ref[0, start : start + rows, :]
            )


def experts_kernel(
    few, at_ref, tok_ref, slot_ref, member_ref, router_ref, wgu_ref, wd_ref, *refs
):
    part_ref, x_ref, gu_ref, gates_ref, acc, gates_all, down = refs[-7:]
    e, experts = pl.program_id(0), pl.num_programs(0)
    slots = x_ref.shape[2]

    @pl.when(e == 0)
    def _():
        member = member_ref[...] > 0
        chosen = jnp.where(member, nt(router_ref[...], tok_ref[...]), masked_score)
        chosen = jnp.exp(chosen - jnp.max(chosen, axis=0, keepdims=True))
        chosen = jnp.where(member, chosen, 0.0)
        gates_all[...] = chosen / jnp.sum(chosen, axis=0, keepdims=True)
        acc[...] = jnp.zeros_like(acc)

    gate_row = own_row(gates_all, at_ref[1] * experts + e)
    gates_ref[pl.ds(e, 1), :] = gate_row
    place = lax.broadcasted_iota(jnp.int32, (slots, 1), 0)
    here = place == own_row(slot_ref, e)
    x = nn(jnp.where(here, 1.0, 0.0).astype(low), tok_ref[...]).astype(low)
    x_ref[0, 0] = x
    gu = nn(x, wgu_ref[0])
    gu_ref[0, 0] = gu.astype(low)
    hidden = gu.shape[1] // 2
    g, u = gu[:, :hidden], gu[:, hidden:]
    act = (g * jax.nn.sigmoid(g) * u).astype(low)
    join_down(few, wd_ref, down)
    y = nn(act, down[...]).astype(low)
    acc[...] += tn(jnp.where(here, gate_row, 0.0).astype(low), y)

    @pl.when(e == experts - 1)
    def _():
        part_ref[0] = acc[...].astype(low)


def back_kernel(
    few, at_ref, tok_ref, slot_ref, gates_ref, mix_ref, router_ref, gu_ref, wgu_ref, wd_ref, *refs
):
    part_ref, d_ref, dgu_ref, act_ref, dlog_ref, acc, dlog_all, down = refs[-8:]
    e, experts = pl.program_id(0), pl.num_programs(0)
    slots, hidden = gu_ref.shape[2], gu_ref.shape[3] // 2

    @pl.when(e == 0)
    def _():
        dlog_all[...] = jnp.zeros_like(dlog_all)
        acc[...] = jnp.zeros_like(acc)

    place = lax.broadcasted_iota(jnp.int32, (slots, 1), 0)
    here = place == own_row(slot_ref, e)
    pick = jnp.where(here, 1.0, 0.0).astype(low)
    gate_row = own_row(gates_ref, e)
    gate = jnp.sum(jnp.where(here, gate_row, 0.0), axis=1, keepdims=True)
    d = nn(pick, tok_ref[...]).astype(low)
    d_ref[0, 0] = d
    join_down(few, wd_ref, down)
    d_act = nt(d, down[...])
    g, u = gu_ref[0, 0, :, :hidden].astype(full), gu_ref[0, 0, :, hidden:].astype(full)
    sig = jax.nn.sigmoid(g)
    silu = g * sig
    act = silu * u
    d_gate = jnp.sum(d_act * act, axis=1, keepdims=True)
    d_gate = jnp.sum(jnp.where(here, d_gate, 0.0), axis=0, keepdims=True)
    dlog_all[pl.ds(e, 1), :] = gate_row * (d_gate - mix_ref[...])
    act_ref[0, 0] = (act * gate).astype(low)
    d_act = d_act * gate
    d_g = (d_act * u * (sig + silu * (1.0 - sig))).astype(low)
    d_u = (d_act * silu).astype(low)
    dgu_ref[0, 0, :, :hidden] = d_g
    dgu_ref[0, 0, :, hidden:] = d_u
    dx = nt(dgu_ref[0, 0], wgu_ref[0]).astype(low)
    acc[...] += tn(pick, dx)

    @pl.when(e == experts - 1)
    def _():
        dlog = dlog_all[...].astype(low)
        dlog_ref[...] = dlog
        part_ref[0] = (acc[...] + tn(dlog, router_ref[...])).astype(low)


def by_expert(*shape):
    return pl.BlockSpec((1,) + shape, lambda e, at: (e, 0, 0))


def in_turn(turn, *shape):
    return pl.BlockSpec((1, 1) + shape, lambda e, at: (e, turn, 0, 0))


def same(*shape):
    return pl.BlockSpec(shape, lambda e, at: (0, 0))


def in_place(*shape):
    return pl.BlockSpec((1,) + shape, lambda e, at: (at[0], 0, 0))


def shard_call(kernel, name, at, inputs, in_specs, out_specs, out_shape, buffers, scratch, experts):
    first = len(inputs) + 1
    aliases = {first + i: i for i in range(len(buffers))}
    return pl.pallas_call(
        kernel,
        grid_spec=pltpu.PrefetchScalarGridSpec(
            num_scalar_prefetch=1,
            grid=(experts,),
            in_specs=in_specs + [pl.BlockSpec(memory_space=pl.ANY)] * len(buffers),
            out_specs=out_specs,
            scratch_shapes=scratch,
        ),
        out_shape=out_shape,
        input_output_aliases=aliases,
        compiler_params=vmem(48),
        name=name,
    )(at, *inputs, *buffers)


def weight_specs(width, hidden):
    return [
        pl.BlockSpec((1, width, 2 * hidden), lambda e, at: (e, 0, 0)),
        pl.BlockSpec((1, width, hidden), lambda e, at: (e, 0, 2)),
    ]


def experts_forward(turn, devs, at, tokens, slot_of, member, router, weights, few, slots, buffers):
    experts, width, columns = weights.shape
    hidden = columns // 3
    count = tokens.shape[0]
    total_experts = member.shape[0]
    return shard_call(
        functools.partial(experts_kernel, few),
        "experts_forward",
        at,
        [tokens, slot_of, member, router, weights, weights],
        [
            same(count, width),
            same(experts, count),
            same(total_experts, count),
            same(total_experts, width),
            *weight_specs(width, hidden),
        ],
        [
            in_place(count, width),
            in_turn(turn, slots, width),
            in_turn(turn, slots, 2 * hidden),
            same(experts, count),
        ],
        [
            jax.ShapeDtypeStruct((devs, count, width), low),
            jax.ShapeDtypeStruct((experts, devs, slots, width), low),
            jax.ShapeDtypeStruct((experts, devs, slots, 2 * hidden), low),
            jax.ShapeDtypeStruct((experts, count), full),
        ],
        buffers,
        [
            pltpu.VMEM((count, width), full),
            pltpu.VMEM((total_experts, count), full),
            pltpu.VMEM((hidden, width), low),
        ],
        experts,
    )


def experts_backward(
    turn, devs, at, d_tokens, slot_of, gates, mix_dot, router, gu, weights, few, buffers
):
    experts, width, columns = weights.shape
    hidden = columns // 3
    count = d_tokens.shape[0]
    slots = gu.shape[2]
    lines = router.shape[0]
    return shard_call(
        functools.partial(back_kernel, few),
        "experts_backward",
        at,
        [d_tokens, slot_of, gates, mix_dot, router, gu, weights, weights],
        [
            same(count, width),
            same(experts, count),
            same(experts, count),
            same(1, count),
            same(lines, width),
            in_turn(turn, slots, 2 * hidden),
            *weight_specs(width, hidden),
        ],
        [
            in_place(count, width),
            in_turn(turn, slots, width),
            in_turn(turn, slots, 2 * hidden),
            in_turn(turn, slots, hidden),
            same(lines, count),
        ],
        [
            jax.ShapeDtypeStruct((devs, count, width), low),
            jax.ShapeDtypeStruct((experts, devs, slots, width), low),
            jax.ShapeDtypeStruct((experts, devs, slots, 2 * hidden), low),
            jax.ShapeDtypeStruct((experts, devs, slots, hidden), low),
            jax.ShapeDtypeStruct((lines, count), low),
        ],
        buffers,
        [
            pltpu.VMEM((count, width), full),
            pltpu.VMEM((lines, count), full),
            pltpu.VMEM((hidden, width), low),
        ],
        experts,
    )


def halving_masks(bits):
    masks = [0]
    for bit in reversed(bits):
        masks = masks + [mask ^ bit for mask in masks]
    return masks


def grads_kernel(bits_a, bits_b, me_ref, x_ref, dgu_ref, act_ref, d_ref, *refs):
    outs, gu_acc, down_acc = refs[-6:-2], refs[-2], refs[-1]
    hidden, width = act_ref.shape[2], d_ref.shape[2]
    gu_acc[...] = tn(x_ref[0], dgu_ref[0])
    down_acc[...] = tn(act_ref[0], d_ref[0])
    chunks = width // hidden
    for part, bits in enumerate((bits_a, bits_b)):
        keep, send = outs[2 * part], outs[2 * part + 1]
        rows = keep.shape[2]
        few = rows // chunks
        for place, mask in enumerate(halving_masks(bits)):
            out = keep if place < keep.shape[0] else send
            spot = place % keep.shape[0]
            start = pl.multiple_of((me_ref[0] ^ mask) * rows, rows)
            block = gu_acc[pl.ds(start, rows), part * hidden : (part + 1) * hidden]
            out[spot, 0, :, :hidden] = block.astype(low)
            start = pl.multiple_of((me_ref[0] ^ mask) * few, few)
            for chunk in range(chunks):
                first = part * (width // 2) + chunk * (hidden // 2)
                block = down_acc[pl.ds(start, few), first : first + hidden // 2]
                out[spot, 0, chunk * few : (chunk + 1) * few, hidden:] = block.astype(low)


def weight_grads(me, rows, d_gu, act, d_rows, bits_a, bits_b, first, stop, buffers):
    experts, count, width = rows.shape
    hidden = act.shape[2]
    devs = 2 ** len(bits_a)
    shape = (width // devs, hidden + hidden // 2)

    def part(*block):
        return pl.BlockSpec((1,) + block, lambda e, me: (first + e, 0, 0))

    return pl.pallas_call(
        functools.partial(grads_kernel, bits_a, bits_b),
        grid_spec=pltpu.PrefetchScalarGridSpec(
            num_scalar_prefetch=1,
            grid=(stop - first,),
            in_specs=[part(count, width), part(count, 2 * hidden), part(count, hidden), part(count, width)]
            + [pl.BlockSpec(memory_space=pl.ANY)] * len(buffers),
            out_specs=[pl.BlockSpec((devs // 2, 1) + shape, lambda e, me: (0, first + e, 0, 0))] * 4,
            scratch_shapes=[pltpu.VMEM((width, 2 * hidden), full), pltpu.VMEM((hidden, width), full)],
        ),
        out_shape=[jax.ShapeDtypeStruct((devs // 2, experts) + shape, low)] * 4,
        input_output_aliases={5 + i: i for i in range(len(buffers))},
        compiler_params=vmem(56),
        name="weight_grads",
    )(me, rows, d_gu, act, d_rows, *buffers)


def shards(
    inputs,
    teacher,
    routes,
    valid_mask,
    block_lengths,
    gain_one,
    w_qkv,
    w_out,
    gain_two,
    w_router,
    w_gate,
    w_up,
    w_down,
):
    n = lax.axis_size("seq")
    me = lax.axis_index("seq")
    mine = lax.axis_index("fsdp")
    seqs_here, shard_len, width = inputs.shape
    assert seqs_here == 1
    seq_len = shard_len * n
    tokens_all = lax.axis_size("fsdp") * seq_len
    kv_here = KV_HEADS // n
    heads_w = kv_here * GROUP * HEAD_DIM
    group_w = kv_here * (GROUP + 2) * HEAD_DIM
    experts_here = w_gate.shape[0]
    expert_total = experts_here * n
    top_count = routes.shape[2]
    capacity = 3 * shard_len * top_count // (2 * expert_total)
    slots = -(-capacity // 16) * 16
    slot_rows = n * slots
    order_a, order_b = fsdp_bits()
    order = jnp.array(arrival_order(n), jnp.int32)[me]
    x_low = inputs.reshape(shard_len, width)

    own_qkv = lax.dynamic_slice_in_dim(w_qkv, me * group_w, group_w, 1)
    small = jnp.concatenate([gain_one[:, None], gain_two[:, None], w_router], axis=1)
    small = jnp.pad(small, ((0, 0), (0, -small.shape[1] % 128)))
    first = lax.all_gather(
        jnp.concatenate([own_qkv, small, w_out], axis=1), "fsdp", axis=0, tiled=True
    )
    full_qkv = first[:, :group_w]
    small = first[:, group_w : group_w + 2 + expert_total]
    full_out = first[:, -width:]
    hidden_w = w_gate.shape[2]
    down_chunks = [
        w_down[:, :, start : start + hidden_w] for start in range(0, width, hidden_w)
    ]
    weights = lax.all_gather(
        jnp.concatenate([w_gate, w_up, jnp.concatenate(down_chunks, axis=1)], axis=2),
        "fsdp",
        axis=1,
        tiled=True,
    )

    routes_low = jnp.concatenate([routes.reshape(shard_len, top_count).T, valid_mask], axis=0)
    routes_low = jnp.pad(
        routes_low.astype(low), ((0, -routes_low.shape[0] % 16), (0, width - shard_len))
    )
    x_blocks = line_gather(jnp.concatenate([x_low, routes_low], axis=0))
    routes_blocks = [
        block[shard_len : shard_len + top_count + 1, :shard_len].astype(jnp.int32)
        for block in x_blocks
    ]
    x_blocks = [block[:shard_len] for block in x_blocks]
    full_g1 = small[:, 0].astype(full)
    full_g2 = small[:, 1].astype(full)
    router = small[:, 2:].T
    own_router = lax.dynamic_slice_in_dim(router, me * experts_here, experts_here, 0)
    own_router = jnp.pad(own_router, ((0, -experts_here % 16), (0, 0)))
    valid_rows = valid_mask.reshape(shard_len).astype(full)

    routes_all = by_place(routes_blocks)[order]
    valid_count = total(jnp.sum(routes_all[:, top_count]).astype(full).reshape(1, 1), "fsdp")[0, 0]
    expert_ids = jnp.arange(expert_total, dtype=jnp.int32)
    member = jnp.any(routes_all[:, :top_count, None, :] == expert_ids[:, None], axis=1)
    own_member = lax.dynamic_slice_in_dim(member, me * experts_here, experts_here, 1)
    earlier = jnp.arange(shard_len)[:, None] < jnp.arange(shard_len)[None, :]
    slot_of = dot("net,tu->neu", own_member.astype(low), earlier.astype(low)).astype(jnp.int32)
    slot_of = jnp.where(own_member, slot_of, -1)
    member = member.astype(full)

    x_all = by_place(x_blocks).reshape(seq_len, width)
    normed_one = rms_norm(x_all.astype(full), full_g1).astype(low)
    qkv_rows = dot("td,dc->ct", normed_one, full_qkv)
    qkv_rows = qkv_rows.reshape(kv_here, GROUP + 2, HEAD_DIM, seq_len)
    positions = jnp.arange(seq_len, dtype=jnp.int32)
    cosine, sine_vals = rope_tables(positions.astype(full), HEAD_DIM)
    turned = rotate(qkv_rows[:, : GROUP + 1], cosine, sine_vals).astype(low)
    query = turned[:, :GROUP] * jnp.asarray(attn_mult, low)
    key = turned[:, GROUP]
    value = qkv_rows[:, GROUP + 1].astype(low)
    key_rows = jnp.swapaxes(key, 1, 2)
    value_rows = jnp.swapaxes(value, 1, 2)
    limit = block_limits(block_lengths[0], positions)[None]
    attended, out_heads, lse = attention_forward(query, key_rows, value, limit, shard_len)
    moved = exchange(attended)
    moved, slot_of, member, own_router = tie(moved, slot_of, member, own_router)
    attn_rows = by_place(nearest(*moved)).reshape(HEADS * HEAD_DIM, shard_len)
    projected = dot("kt,kd->td", attn_rows, full_out)
    hidden = x_low.astype(full) + resid_mult * projected
    normed_two, norm_two_pull = jax.vjp(rms_norm, hidden, full_g2)

    tokens = [normed_two.astype(low)]
    rights, lefts = [tokens[0]], [tokens[0]]
    buffers, gates = [], []
    for turn in range(n):
        if turn < n - 1:
            right, left, tokens[turn] = tie(rights[turn], lefts[turn], tokens[turn])
            right, left = line_move(right, left, turn + 1)
        *buffers, shard_gates = experts_forward(
            turn, n, jnp.stack([order[turn], me]), tokens[turn], slot_of[turn], member[turn],
            router, weights, w_down.shape[1], slots, buffers,
        )
        if turn < n - 1:
            right, left, shard_gates = tie(right, left, shard_gates)
            rights.append(right)
            lefts.append(left)
            tokens.append(arrived(rights, lefts, turn + 1))
        gates.append(shard_gates)
    mix_parts, expert_in, gate_up = buffers
    right = left = None
    for k in range(n - 1, 0, -1):
        moving = tie(*line_send(mix_parts, k, right, left))
        right, left = tie(*line_pass(*moving, k))
    mixture = line_end(mix_parts, right, left)
    output_f32 = hidden + resid_mult * mixture
    activations = output_f32.astype(low).reshape(1, shard_len, width)
    error_rows = output_f32 - teacher.astype(full).reshape(shard_len, width)
    weighted = valid_rows[:, None] * error_rows
    loss_steps = total_steps(jnp.sum(weighted * error_rows).reshape(1, 1), "seq", "fsdp")
    squares = next(loss_steps)
    d_out = weighted * (tokens_all / valid_count)

    d_mix = resid_mult * d_out
    d_tokens = d_mix.astype(low)
    mix_dot = jnp.sum(d_mix * mixture, axis=1)[None]
    rights, lefts = [d_tokens], [d_tokens]
    dot_rights, dot_lefts = [mix_dot], [mix_dot]
    buffers, d_logits = [], []
    for turn in range(n):
        if turn < n - 1:
            (right, left), (dot_right, dot_left), d_tokens = tie(
                (rights[turn], lefts[turn]), (dot_rights[turn], dot_lefts[turn]), d_tokens
            )
            dot_right, dot_left = line_move(dot_right, dot_left, turn + 1)
            right, left = line_move(right, left, turn + 1)
        *buffers, shard_logits = experts_backward(
            turn, n, jnp.stack([order[turn], me]), d_tokens, slot_of[turn], gates[turn], mix_dot,
            own_router, gate_up, weights, w_down.shape[1], buffers,
        )
        if turn < n - 1:
            right, left, dot_right, dot_left, shard_logits, squares = tie(
                right, left, dot_right, dot_left, shard_logits, squares
            )
            squares = loss_steps.send(squares)
            rights.append(right)
            lefts.append(left)
            dot_rights.append(dot_right)
            dot_lefts.append(dot_left)
            d_tokens = arrived(rights, lefts, turn + 1)
            mix_dot = arrived(dot_rights, dot_lefts, turn + 1)
        d_logits.append(shard_logits)
    d_parts, d_rows, d_gate_up, act_low = buffers
    expert_in = expert_in.reshape(experts_here, slot_rows, width)
    d_rows = d_rows.reshape(experts_here, slot_rows, width)
    d_gate_up = d_gate_up.reshape(experts_here, slot_rows, -1)
    act_low = act_low.reshape(experts_here, slot_rows, -1)

    right = left = None
    grads = []
    cut = (experts_here + 1) // 2
    for k in range(n - 1, 0, -1):
        moving = line_send(d_parts, k, right, left)
        if k >= n - 2:
            moving, d_rows, grads = tie(moving, d_rows, grads)
            right, left = line_pass(*moving, k)
            part = (0, cut) if k == n - 1 else (cut, experts_here)
            grads = weight_grads(
                mine.reshape(1), expert_in, d_gate_up, act_low, d_rows, order_a, order_b, *part, grads
            )
            right, left, grads, squares = tie(right, left, grads, squares)
        else:
            right, left, squares = tie(*line_pass(*tie(*moving), k), squares)
        squares = loss_steps.send(squares)
    expert_sums = [Halving(*grads[:2], order_a), Halving(*grads[2:], order_b)]
    for each in expert_sums:
        each.go()
    d_normed_two = line_end(d_parts, right, left)

    d_hidden_norm, gain_two_part = norm_two_pull(d_normed_two)
    d_hidden = d_out + d_hidden_norm
    d_proj = (resid_mult * d_hidden).astype(low)
    d_attended = dot("kd,td->kt", full_out, d_proj).astype(low)
    moved = exchange(d_attended.reshape(n, heads_w, shard_len))
    for each in expert_sums:
        each.add()
    out_part = dot("kt,td->kd", attn_rows, d_proj).astype(low)
    router_part = sum(
        dot("td,et->de", shard, shard_logits[:experts_here])
        for shard, shard_logits in zip(tokens, d_logits)
    )
    moved, out_part, router_part = leave(expert_sums, moved, out_part, router_part)
    for each in expert_sums:
        each.go()
    out_sum = lax.psum_scatter(out_part, "fsdp", scatter_dimension=0, tiled=True)
    d_heads = by_place(nearest(*moved))
    query_grad, key_grad, value_grad = attention_backward(
        query, key_rows, value_rows, key, limit, out_heads, lse, d_heads
    )
    (query_grad, key_grad, value_grad), out_sum = tie((query_grad, key_grad, value_grad), out_sum)
    out_sum = lax.psum(out_sum, "seq")
    d_turned = jnp.concatenate([query_grad, key_grad[:, None]], axis=1).astype(full)
    d_turned = rotate(d_turned, cosine, -sine_vals).astype(low)
    d_qkv = jnp.concatenate([d_turned, value_grad[:, None]], axis=1).reshape(group_w, seq_len)
    d_parts = dot("ct,dc->td", d_qkv, full_qkv).astype(low).reshape(n, shard_len, width)

    right = left = None
    for k in range(n - 1, 0, -1):
        moving = line_send(d_parts, k, right, left)
        if k == n - 1:
            moving, d_qkv = tie(moving, d_qkv)
            right, left = line_pass(*moving, k)
            own_columns = jnp.zeros((width, expert_total), full)
            own_columns = lax.dynamic_update_slice_in_dim(
                own_columns, router_part, me * experts_here, 1
            )
            qkv_part = jnp.concatenate(
                [dot("td,ct->dc", normed_one, d_qkv), own_columns, gain_two_part[:, None]], axis=1
            ).astype(low)
            qkv_sum = lax.psum_scatter(qkv_part, "fsdp", scatter_dimension=0, tiled=True)
            right, left, qkv_part = land(expert_sums, right, left, qkv_part)
            for each in expert_sums:
                each.add()
        else:
            right, left = line_pass(*moving, k)
            if k == n - 2:
                for each in expert_sums:
                    each.go()
            if k == 1:
                right, left, qkv_sum = tie(right, left, qkv_sum)
            else:
                right, left = tie(right, left)
    d_normed_one = line_end(d_parts, right, left)
    sums = line_gather(qkv_sum)
    _, norm_one_pull = jax.vjp(lambda v: rms_norm(v, full_g1), x_low.astype(full))
    input_grad = (d_hidden + norm_one_pull(d_normed_one)[0]).reshape(1, shard_len, width)
    input_grad, out_sum = land(expert_sums, input_grad, out_sum)
    for each in expert_sums:
        each.add()
    left_sum, right_sum = (each.finish() for each in expert_sums)
    gate_grad, up_grad = left_sum[:, :, :hidden_w], right_sum[:, :, :hidden_w]
    few = w_down.shape[1]
    down_grad = jnp.concatenate(
        [
            part[:, start : start + few, hidden_w:]
            for part in (left_sum, right_sum)
            for start in range(0, part.shape[1], few)
        ],
        axis=2,
    )
    out_grad = out_sum.astype(full)
    sums = by_place(sums).astype(full)
    qkv_grad = jnp.swapaxes(sums[:, :, :group_w], 0, 1).reshape(-1, QKV_W)
    rest = jnp.sum(sums[:, :, group_w:], axis=0)
    router_grad, gain_two_grad = rest[:, :expert_total], rest[:, expert_total]
    gain_one_grad = jnp.sum(qkv_grad * w_qkv.astype(full), axis=1) / gain_one.astype(full)
    for _ in range(2):
        squares = loss_steps.send(squares)
    loss_value = squares[0, 0] / (valid_count * width)
    return (
        activations,
        loss_value,
        input_grad,
        gain_one_grad,
        qkv_grad,
        out_grad,
        gain_two_grad,
        router_grad,
        gate_grad,
        up_grad,
        down_grad,
    )


def solution(mesh):
    return jax.shard_map(
        shards,
        mesh=mesh,
        in_specs=(
            P("fsdp", "seq", None),
            P("fsdp", "seq", None),
            P("fsdp", "seq", None),
            P("fsdp", "seq"),
            P("fsdp", None),
            P("fsdp"),
            P("fsdp", None),
            P("fsdp", None),
            P("fsdp"),
            P("fsdp", None),
            P("seq", "fsdp", None),
            P("seq", "fsdp", None),
            P("seq", "fsdp", None),
        ),
        out_specs=(
            P("fsdp", "seq", None),
            P(),
            P("fsdp", "seq", None),
            P("fsdp"),
            P("fsdp", None),
            P("fsdp", None),
            P("fsdp"),
            P("fsdp", None),
            P("seq", "fsdp", None),
            P("seq", "fsdp", None),
            P("seq", "fsdp", None),
        ),
        check_vma=False,
    )
```

```python
import functools

import jax
import jax.numpy as jnp
from jax import lax
from jax.experimental import pallas as pl
from jax.experimental.pallas import tpu as pltpu
from jax.sharding import PartitionSpec as P

HEADS = 24
KV_HEADS = 8
HEAD_DIM = 64
BLOCK = 256
GROUP = 3
QKV_W = 2560


epsilon = 1e-06
attn_mult = 0.015625
resid_mult = 0.22
rope_base = 10000.0
masked_score = -1e30

low = jnp.bfloat16
full = jnp.float32


def dot(spec, left, right):
    return jnp.einsum(spec, left, right, preferred_element_type=full)


def rms_norm(values, gain_vec):
    inv_rms = lax.rsqrt(jnp.mean(values * values, axis=-1, keepdims=True) + epsilon)
    return values * inv_rms * gain_vec


def rope_tables(positions, head_dim):
    half_dim = head_dim // 2
    frequency = rope_base ** (-(2.0 * jnp.arange(half_dim, dtype=full)) / head_dim)
    angles = frequency[:, None] * positions[None, :]
    return (jnp.cos(angles), jnp.sin(angles))


def rotate(values, cosine, sine_vals):
    half_dim = values.shape[-2] // 2
    front_half = values[..., :half_dim, :]
    back_half = values[..., half_dim:, :]
    return jnp.concatenate(
        [front_half * cosine - back_half * sine_vals, back_half * cosine + front_half * sine_vals],
        axis=-2,
    )


def block_limits(lengths_row, positions):
    block_ends = jnp.cumsum(lengths_row)
    open_ends = jnp.where(block_ends[None, :] > positions[:, None], block_ends[None, :], positions.shape[0])
    return jnp.min(open_ends, axis=1).astype(jnp.int32)


def tie(*groups):
    return lax.optimization_barrier(groups)


def line_move(right, left, k):
    n = lax.axis_size("seq")
    return (
        lax.ppermute(right, "seq", [(i, i + 1) for i in range(k - 1, n - 1)]),
        lax.ppermute(left, "seq", [(i, i - 1) for i in range(1, n - k + 1)]),
    )


def line_gather(block):
    n = lax.axis_size("seq")
    rights, lefts = [block], [block]
    for k in range(1, n):
        right, left = tie(*line_move(rights[-1], lefts[-1], k))
        rights.append(right)
        lefts.append(left)
    return nearest(rights, lefts)


def nearest(rights, lefts):
    n = lax.axis_size("seq")
    me = lax.axis_index("seq")
    return [rights[0]] + [jnp.where(me >= k, rights[k], lefts[n - k]) for k in range(1, n)]


def arrival_order(n):
    order = []
    for me in range(n):
        both = min(me, n - 1 - me)
        places = [me]
        for k in range(1, n):
            places += [me - k] if me >= k and (k <= both or me > n - 1 - me) else []
            places += [me + k] if me + k < n and (k <= both or me < n - 1 - me) else []
        order.append(places)
    return order


def arrived(rights, lefts, turn):
    n = lax.axis_size("seq")
    me = lax.axis_index("seq")
    sources = {}
    for dev, places in enumerate(arrival_order(n)):
        gap = dev - places[turn]
        sources.setdefault(gap, []).append(dev)
    block = None
    for gap, devs in sources.items():
        moved = rights[gap] if gap >= 0 else lefts[-gap]
        if block is None:
            block = moved
        else:
            mine = jnp.array([dev in devs for dev in range(n)])[me]
            block = jnp.where(mine, moved, block)
    return block


def at_place(placed, place):
    return lax.dynamic_index_in_dim(placed, place % lax.axis_size("seq"), 0, keepdims=False)


def line_send(parts, k, right, left):
    me = lax.axis_index("seq")
    to_right, to_left = at_place(parts, me + k), at_place(parts, me - k)
    if right is not None:
        to_right = (to_right.astype(full) + right.astype(full)).astype(low)
        to_left = (to_left.astype(full) + left.astype(full)).astype(low)
    return to_right, to_left


def line_pass(to_right, to_left, k):
    n = lax.axis_size("seq")
    return (
        lax.ppermute(to_right, "seq", [(i, i + 1) for i in range(n - k)]),
        lax.ppermute(to_left, "seq", [(i, i - 1) for i in range(k, n)]),
    )


def line_end(parts, right, left):
    own = at_place(parts, lax.axis_index("seq")).astype(full)
    return own + (right.astype(full) + left.astype(full))


def by_place(blocks):
    n = lax.axis_size("seq")
    me = lax.axis_index("seq")
    placed = jnp.zeros((n,) + blocks[0].shape, blocks[0].dtype)
    for k, block in enumerate(blocks):
        placed = lax.dynamic_update_index_in_dim(placed, block, (me - k) % n, 0)
    return placed


def exchange(blocks):
    n = lax.axis_size("seq")
    me = lax.axis_index("seq")
    rights, lefts = [at_place(blocks, me)], [at_place(blocks, me)]
    for k in range(1, n):
        to_right, to_left = at_place(blocks, me + k), at_place(blocks, me - k)
        rights.append(lax.ppermute(to_right, "seq", [(i, i + k) for i in range(n - k)]))
        lefts.append(lax.ppermute(to_left, "seq", [(i, i - k) for i in range(k, n)]))
    return rights, lefts


def swap(value, axis, bit):
    return lax.ppermute(value, axis, [(i, i ^ bit) for i in range(lax.axis_size(axis))])


def total(value, *axes):
    for axis in axes:
        for step in range(lax.axis_size(axis).bit_length() - 1):
            value = value + swap(value, axis, 1 << step)
    return value


def fsdp_bits():
    bits = [1 << step for step in range(lax.axis_size("fsdp").bit_length() - 1)]
    return tuple(bits), tuple(bits[:1] + bits[:0:-1])


def total_steps(value, *axes):
    for axis in axes:
        for step in range(lax.axis_size(axis).bit_length() - 1):
            here = swap(value, axis, 1 << step)
            here = yield here
            value = value + here
    while True:
        yield value


class Halving:
    def __init__(self, keep, send, bits):
        self.terms, self.send, self.bits = [keep], send, list(bits)

    def go(self):
        self.terms = self.terms + [swap(self.send, "fsdp", self.bits.pop(0))]

    def add(self):
        half = self.terms[0].shape[0] // 2
        if half:
            self.send = sum(term[half:].astype(full) for term in self.terms).astype(low)
            self.terms = [term[:half] for term in self.terms]

    def finish(self):
        while self.bits:
            self.go()
            self.add()
        return sum(term[0].astype(full) for term in self.terms)


def rows_halving(part, bits):
    devs = lax.axis_size("fsdp")
    order = lax.axis_index("fsdp") ^ jnp.array(halving_masks(bits), jnp.int32)
    blocks = part.reshape(devs, part.shape[0] // devs, part.shape[1])[order]
    return Halving(blocks[: devs // 2], blocks[devs // 2 :], bits)


def land(sums, *others):
    tied = tie([each.terms[-1] for each in sums], *others)
    for each, here in zip(sums, tied[0]):
        each.terms = each.terms[:-1] + [here]
    return tied[1:]


def leave(sums, *others):
    tied = tie([each.send for each in sums], *others)
    for each, send in zip(sums, tied[0]):
        each.send = send
    return tied[1:]


def nt(a, b):
    return lax.dot_general(a, b, (((1,), (1,)), ((), ())), preferred_element_type=full)

def nn(a, b):
    return lax.dot_general(a, b, (((1,), (0,)), ((), ())), preferred_element_type=full)

def tn(a, b):
    return lax.dot_general(a, b, (((0,), (0,)), ((), ())), preferred_element_type=full)


def beside(rows):
    return jnp.concatenate([rows[h] for h in range(GROUP)], axis=1)

def key_steps(i, seq_len, query_rows, key_rows):
    free = (i * query_rows) // key_rows
    need = ((i + 1) * query_rows + BLOCK - 1 + key_rows - 1) // key_rows
    return free, jnp.minimum(need, seq_len // key_rows)

def forward_kernel(seq_len, query_rows, key_rows, limit_ref, q_ref, k_ref, vt_ref, low_ref, out_ref, lse_ref):
    i = pl.program_id(1)
    qt = beside(q_ref[0, 0])
    width = GROUP * query_rows
    limit = jnp.concatenate([limit_ref[...]] * GROUP, axis=1)

    def step(masked, j, carry):
        peak, total, acc = carry
        start = pl.multiple_of(j * key_rows, key_rows)
        s = nn(k_ref[0, pl.ds(start, key_rows), :], qt)
        if masked:
            place = start + lax.broadcasted_iota(jnp.int32, (key_rows, 1), 0)
            s = jnp.where(place < limit, s, masked_score)
        new_peak = jnp.maximum(peak, jnp.max(s, axis=0, keepdims=True))
        shrink = jnp.exp(peak - new_peak)
        p = jnp.exp(s - new_peak)
        total = shrink * total + jnp.sum(p, axis=0, keepdims=True)
        acc = shrink * acc + nn(vt_ref[0, :, pl.ds(start, key_rows)], p.astype(low))
        return new_peak, total, acc

    free, need = key_steps(i, seq_len, query_rows, key_rows)
    carry = (
        jnp.full((1, width), masked_score, full),
        jnp.zeros((1, width), full),
        jnp.zeros((HEAD_DIM, width), full),
    )
    carry = lax.fori_loop(0, free, lambda j, c: step(False, j, c), carry)
    peak, total, acc = lax.fori_loop(free, need, lambda j, c: step(True, j, c), carry)
    out = acc / total
    lse = peak + jnp.log(total)
    for h in range(GROUP):
        cols = slice(h * query_rows, (h + 1) * query_rows)
        out_ref[0, h] = out[:, cols]
        low_ref[0, pl.ds(h * HEAD_DIM, HEAD_DIM), :] = out[:, cols].astype(low)
        lse_ref[0, h] = lse[:, cols]

def query_spec(query_rows, per):
    return pl.BlockSpec(
        (1, 1, GROUP, HEAD_DIM, query_rows), lambda g, i: (i // per, g, 0, 0, i % per)
    )


def attention_forward(heads, k_rows, vt, limit):
    kv_here, shard_len = heads.shape[1], heads.shape[4]
    seq_len = k_rows.shape[1]
    query_rows = min(256, shard_len)
    key_rows = min(512, seq_len)
    per = shard_len // query_rows
    return pl.pallas_call(
        functools.partial(forward_kernel, seq_len, query_rows, key_rows),
        grid=(kv_here, seq_len // query_rows),
        in_specs=[
            pl.BlockSpec((1, query_rows), lambda g, i: (0, i)),
            query_spec(query_rows, per),
            pl.BlockSpec((1, seq_len, HEAD_DIM), lambda g, i: (g, 0, 0)),
            pl.BlockSpec((1, HEAD_DIM, seq_len), lambda g, i: (g, 0, 0)),
        ],
        out_specs=[
            pl.BlockSpec((1, GROUP * HEAD_DIM, query_rows), lambda g, i: (i // per, g, i % per)),
            pl.BlockSpec((1, GROUP, HEAD_DIM, query_rows), lambda g, i: (g, 0, 0, i)),
            pl.BlockSpec((1, GROUP, 1, query_rows), lambda g, i: (g, 0, 0, i)),
        ],
        out_shape=[
            jax.ShapeDtypeStruct((seq_len // shard_len, kv_here * GROUP * HEAD_DIM, shard_len), low),
            jax.ShapeDtypeStruct((kv_here, GROUP, HEAD_DIM, seq_len), full),
            jax.ShapeDtypeStruct((kv_here, GROUP, 1, seq_len), full),
        ],
        compiler_params=vmem(40),
        name="attention_forward",
    )(limit, heads, k_rows, vt)

def backward_kernel(seq_len, query_rows, key_rows, limit_ref, q_ref, k_ref, v_ref, kt_ref, out_ref, lse_ref, dout_ref, dq_ref, dk_ref, dv_ref, dk_acc, dv_acc):
    i = pl.program_id(1)

    @pl.when(i == 0)
    def _():
        dk_acc[...] = jnp.zeros_like(dk_acc)
        dv_acc[...] = jnp.zeros_like(dv_acc)

    qt = beside(q_ref[0, 0])
    limit = jnp.concatenate([limit_ref[...]] * GROUP, axis=1)
    dout = jnp.concatenate([dout_ref[0, pl.ds(h * HEAD_DIM, HEAD_DIM), :] for h in range(GROUP)], axis=1)
    delta = jnp.sum(dout.astype(full) * beside(out_ref[0]), axis=0, keepdims=True)
    lse = beside(lse_ref[0])

    def step(masked, j, dq):
        start = pl.multiple_of(j * key_rows, key_rows)
        keys = pl.ds(start, key_rows)
        s = nn(k_ref[0, keys, :], qt)
        if masked:
            place = start + lax.broadcasted_iota(jnp.int32, (key_rows, 1), 0)
            s = jnp.where(place < limit, s, masked_score)
        p = jnp.exp(s - lse)
        dp = nn(v_ref[0, keys, :], dout)
        ds = (p * (dp - delta)).astype(low)
        dk_acc[:, keys] += nt(qt, ds)
        dv_acc[:, keys] += nt(dout, p.astype(low))
        return dq + nn(kt_ref[0, :, keys], ds)

    free, need = key_steps(i, seq_len, query_rows, key_rows)
    dq = jnp.zeros((HEAD_DIM, GROUP * query_rows), full)
    dq = lax.fori_loop(0, free, lambda j, c: step(False, j, c), dq)
    dq = lax.fori_loop(free, need, lambda j, c: step(True, j, c), dq) * attn_mult
    for h in range(GROUP):
        dq_ref[0, h] = dq[:, h * query_rows : (h + 1) * query_rows].astype(low)

    @pl.when(i == pl.num_programs(1) - 1)
    def _():
        dk_ref[0] = dk_acc[...].astype(low)
        dv_ref[0] = dv_acc[...].astype(low)

def attention_backward(heads, k_rows, v_rows, kt, limit, out, lse, d_out):
    kv_here, shard_len = heads.shape[1], heads.shape[4]
    seq_len = k_rows.shape[1]
    query_rows = min(256, shard_len)
    key_rows = min(512, seq_len)
    per = shard_len // query_rows
    quarter = lambda g, i: (g, 0, 0, i)
    whole = lambda g, i: (g, 0, 0)
    return pl.pallas_call(
        functools.partial(backward_kernel, seq_len, query_rows, key_rows),
        grid=(kv_here, seq_len // query_rows),
        in_specs=[
            pl.BlockSpec((1, query_rows), lambda g, i: (0, i)),
            query_spec(query_rows, per),
            pl.BlockSpec((1, seq_len, HEAD_DIM), whole),
            pl.BlockSpec((1, seq_len, HEAD_DIM), whole),
            pl.BlockSpec((1, HEAD_DIM, seq_len), whole),
            pl.BlockSpec((1, GROUP, HEAD_DIM, query_rows), quarter),
            pl.BlockSpec((1, GROUP, 1, query_rows), quarter),
            pl.BlockSpec((1, GROUP * HEAD_DIM, query_rows), lambda g, i: (i // per, g, i % per)),
        ],
        out_specs=[
            pl.BlockSpec((1, GROUP, HEAD_DIM, query_rows), quarter),
            pl.BlockSpec((1, HEAD_DIM, seq_len), whole),
            pl.BlockSpec((1, HEAD_DIM, seq_len), whole),
        ],
        out_shape=[
            jax.ShapeDtypeStruct((kv_here, GROUP, HEAD_DIM, seq_len), low),
            jax.ShapeDtypeStruct((kv_here, HEAD_DIM, seq_len), low),
            jax.ShapeDtypeStruct((kv_here, HEAD_DIM, seq_len), low),
        ],
        scratch_shapes=[pltpu.VMEM((HEAD_DIM, seq_len), full), pltpu.VMEM((HEAD_DIM, seq_len), full)],
        compiler_params=vmem(40),
        name="attention_backward",
    )(limit, heads, k_rows, v_rows, kt, out, lse, d_out)


def vmem(mib):
    return pltpu.CompilerParams(vmem_limit_bytes=mib * 2**20)


def own_row(ref, row):
    return ref[pl.ds(row, 1), :]


def join_down(rows, block_ref, down_ref):
    hidden, width = down_ref.shape
    chunks = width // hidden
    for dev in range(hidden // rows):
        for chunk in range(chunks):
            start = (dev * chunks + chunk) * rows
            down_ref[dev * rows : (dev + 1) * rows, chunk * hidden : (chunk + 1) * hidden] = (
                block_ref[0, start : start + rows, :]
            )


def experts_kernel(
    few, at_ref, tok_ref, slot_ref, member_ref, router_ref, wgu_ref, wd_ref, *refs
):
    part_ref, x_ref, gu_ref, gates_ref, acc, gates_all, down = refs[-7:]
    e, experts = pl.program_id(0), pl.num_programs(0)
    slots = x_ref.shape[2]

    @pl.when(e == 0)
    def _():
        member = member_ref[...] > 0
        chosen = jnp.where(member, nt(router_ref[...], tok_ref[...]), masked_score)
        chosen = jnp.exp(chosen - jnp.max(chosen, axis=0, keepdims=True))
        chosen = jnp.where(member, chosen, 0.0)
        gates_all[...] = chosen / jnp.sum(chosen, axis=0, keepdims=True)
        acc[...] = jnp.zeros_like(acc)

    gate_row = own_row(gates_all, at_ref[1] * experts + e)
    gates_ref[pl.ds(e, 1), :] = gate_row
    place = lax.broadcasted_iota(jnp.int32, (slots, 1), 0)
    here = place == own_row(slot_ref, e)
    x = nn(jnp.where(here, 1.0, 0.0).astype(low), tok_ref[...]).astype(low)
    x_ref[0, 0] = x
    gu = nn(x, wgu_ref[0])
    gu_ref[0, 0] = gu.astype(low)
    hidden = gu.shape[1] // 2
    g, u = gu[:, :hidden], gu[:, hidden:]
    act = (g * jax.nn.sigmoid(g) * u).astype(low)
    join_down(few, wd_ref, down)
    y = nn(act, down[...]).astype(low)
    acc[...] += tn(jnp.where(here, gate_row, 0.0).astype(low), y)

    @pl.when(e == experts - 1)
    def _():
        part_ref[0] = acc[...].astype(low)


def back_kernel(
    few, at_ref, tok_ref, slot_ref, gates_ref, mix_ref, router_ref, gu_ref, wgu_ref, wd_ref, *refs
):
    part_ref, d_ref, dgu_ref, act_ref, dlog_ref, acc, dlog_all, down = refs[-8:]
    e, experts = pl.program_id(0), pl.num_programs(0)
    slots, hidden = gu_ref.shape[2], gu_ref.shape[3] // 2

    @pl.when(e == 0)
    def _():
        dlog_all[...] = jnp.zeros_like(dlog_all)
        acc[...] = jnp.zeros_like(acc)

    place = lax.broadcasted_iota(jnp.int32, (slots, 1), 0)
    here = place == own_row(slot_ref, e)
    pick = jnp.where(here, 1.0, 0.0).astype(low)
    gate_row = own_row(gates_ref, e)
    gate = jnp.sum(jnp.where(here, gate_row, 0.0), axis=1, keepdims=True)
    d = nn(pick, tok_ref[...]).astype(low)
    d_ref[0, 0] = d
    join_down(few, wd_ref, down)
    d_act = nt(d, down[...])
    g, u = gu_ref[0, 0, :, :hidden].astype(full), gu_ref[0, 0, :, hidden:].astype(full)
    sig = jax.nn.sigmoid(g)
    silu = g * sig
    act = silu * u
    d_gate = jnp.sum(d_act * act, axis=1, keepdims=True)
    d_gate = jnp.sum(jnp.where(here, d_gate, 0.0), axis=0, keepdims=True)
    dlog_all[pl.ds(e, 1), :] = gate_row * (d_gate - mix_ref[...])
    act_ref[0, 0] = (act * gate).astype(low)
    d_act = d_act * gate
    d_g = (d_act * u * (sig + silu * (1.0 - sig))).astype(low)
    d_u = (d_act * silu).astype(low)
    dgu_ref[0, 0, :, :hidden] = d_g
    dgu_ref[0, 0, :, hidden:] = d_u
    dx = nt(dgu_ref[0, 0], wgu_ref[0]).astype(low)
    acc[...] += tn(pick, dx)

    @pl.when(e == experts - 1)
    def _():
        dlog = dlog_all[...].astype(low)
        dlog_ref[...] = dlog
        part_ref[0] = (acc[...] + tn(dlog, router_ref[...])).astype(low)


def by_expert(*shape):
    return pl.BlockSpec((1,) + shape, lambda e, at: (e, 0, 0))


def in_turn(turn, *shape):
    return pl.BlockSpec((1, 1) + shape, lambda e, at: (e, turn, 0, 0))


def same(*shape):
    return pl.BlockSpec(shape, lambda e, at: (0, 0))


def in_place(*shape):
    return pl.BlockSpec((1,) + shape, lambda e, at: (at[0], 0, 0))


def shard_call(kernel, name, at, inputs, in_specs, out_specs, out_shape, buffers, scratch, experts):
    first = len(inputs) + 1
    aliases = {first + i: i for i in range(len(buffers))}
    return pl.pallas_call(
        kernel,
        grid_spec=pltpu.PrefetchScalarGridSpec(
            num_scalar_prefetch=1,
            grid=(experts,),
            in_specs=in_specs + [pl.BlockSpec(memory_space=pl.ANY)] * len(buffers),
            out_specs=out_specs,
            scratch_shapes=scratch,
        ),
        out_shape=out_shape,
        input_output_aliases=aliases,
        compiler_params=vmem(48),
        name=name,
    )(at, *inputs, *buffers)


def weight_specs(width, hidden):
    return [
        pl.BlockSpec((1, width, 2 * hidden), lambda e, at: (e, 0, 0)),
        pl.BlockSpec((1, width, hidden), lambda e, at: (e, 0, 2)),
    ]


def experts_forward(turn, devs, at, tokens, slot_of, member, router, weights, few, slots, buffers):
    experts, width, columns = weights.shape
    hidden = columns // 3
    count = tokens.shape[0]
    total_experts = member.shape[0]
    return shard_call(
        functools.partial(experts_kernel, few),
        "experts_forward",
        at,
        [tokens, slot_of, member, router, weights, weights],
        [
            same(count, width),
            same(experts, count),
            same(total_experts, count),
            same(total_experts, width),
            *weight_specs(width, hidden),
        ],
        [
            in_place(count, width),
            in_turn(turn, slots, width),
            in_turn(turn, slots, 2 * hidden),
            same(experts, count),
        ],
        [
            jax.ShapeDtypeStruct((devs, count, width), low),
            jax.ShapeDtypeStruct((experts, devs, slots, width), low),
            jax.ShapeDtypeStruct((experts, devs, slots, 2 * hidden), low),
            jax.ShapeDtypeStruct((experts, count), full),
        ],
        buffers,
        [
            pltpu.VMEM((count, width), full),
            pltpu.VMEM((total_experts, count), full),
            pltpu.VMEM((hidden, width), low),
        ],
        experts,
    )


def experts_backward(
    turn, devs, at, d_tokens, slot_of, gates, mix_dot, router, gu, weights, few, buffers
):
    experts, width, columns = weights.shape
    hidden = columns // 3
    count = d_tokens.shape[0]
    slots = gu.shape[2]
    lines = router.shape[0]
    return shard_call(
        functools.partial(back_kernel, few),
        "experts_backward",
        at,
        [d_tokens, slot_of, gates, mix_dot, router, gu, weights, weights],
        [
            same(count, width),
            same(experts, count),
            same(experts, count),
            same(1, count),
            same(lines, width),
            in_turn(turn, slots, 2 * hidden),
            *weight_specs(width, hidden),
        ],
        [
            in_place(count, width),
            in_turn(turn, slots, width),
            in_turn(turn, slots, 2 * hidden),
            in_turn(turn, slots, hidden),
            same(lines, count),
        ],
        [
            jax.ShapeDtypeStruct((devs, count, width), low),
            jax.ShapeDtypeStruct((experts, devs, slots, width), low),
            jax.ShapeDtypeStruct((experts, devs, slots, 2 * hidden), low),
            jax.ShapeDtypeStruct((experts, devs, slots, hidden), low),
            jax.ShapeDtypeStruct((lines, count), low),
        ],
        buffers,
        [
            pltpu.VMEM((count, width), full),
            pltpu.VMEM((lines, count), full),
            pltpu.VMEM((hidden, width), low),
        ],
        experts,
    )


def halving_masks(bits):
    masks = [0]
    for bit in reversed(bits):
        masks = masks + [mask ^ bit for mask in masks]
    return masks


def grads_kernel(bits_a, bits_b, me_ref, x_ref, dgu_ref, act_ref, d_ref, *refs):
    outs, gu_acc, down_acc = refs[-6:-2], refs[-2], refs[-1]
    hidden, width = act_ref.shape[2], d_ref.shape[2]
    gu_acc[...] = tn(x_ref[0], dgu_ref[0])
    down_acc[...] = tn(act_ref[0], d_ref[0])
    chunks = width // hidden
    for part, bits in enumerate((bits_a, bits_b)):
        keep, send = outs[2 * part], outs[2 * part + 1]
        rows = keep.shape[2]
        few = rows // chunks
        for place, mask in enumerate(halving_masks(bits)):
            out = keep if place < keep.shape[0] else send
            spot = place % keep.shape[0]
            start = pl.multiple_of((me_ref[0] ^ mask) * rows, rows)
            block = gu_acc[pl.ds(start, rows), part * hidden : (part + 1) * hidden]
            out[spot, 0, :, :hidden] = block.astype(low)
            start = pl.multiple_of((me_ref[0] ^ mask) * few, few)
            for chunk in range(chunks):
                first = part * (width // 2) + chunk * (hidden // 2)
                block = down_acc[pl.ds(start, few), first : first + hidden // 2]
                out[spot, 0, chunk * few : (chunk + 1) * few, hidden:] = block.astype(low)


def weight_grads(me, rows, d_gu, act, d_rows, bits_a, bits_b, first, stop):
    _, count, width = rows.shape
    hidden = act.shape[2]
    devs = 2 ** len(bits_a)
    shape = (width // devs, hidden + hidden // 2)

    def part(*block):
        return pl.BlockSpec((1,) + block, lambda e, me: (first + e, 0, 0))

    return pl.pallas_call(
        functools.partial(grads_kernel, bits_a, bits_b),
        grid_spec=pltpu.PrefetchScalarGridSpec(
            num_scalar_prefetch=1,
            grid=(stop - first,),
            in_specs=[part(count, width), part(count, 2 * hidden), part(count, hidden), part(count, width)],
            out_specs=[pl.BlockSpec((devs // 2, 1) + shape, lambda e, me: (0, e, 0, 0))] * 4,
            scratch_shapes=[pltpu.VMEM((width, 2 * hidden), full), pltpu.VMEM((hidden, width), full)],
        ),
        out_shape=[jax.ShapeDtypeStruct((devs // 2, stop - first) + shape, low)] * 4,
        compiler_params=vmem(56),
        name="weight_grads",
    )(me, rows, d_gu, act, d_rows)


def shards(
    inputs,
    teacher,
    routes,
    valid_mask,
    block_lengths,
    gain_one,
    w_qkv,
    w_out,
    gain_two,
    w_router,
    w_gate,
    w_up,
    w_down,
):
    n = lax.axis_size("seq")
    me = lax.axis_index("seq")
    mine = lax.axis_index("fsdp")
    seqs_here, shard_len, width = inputs.shape
    assert seqs_here == 1
    seq_len = shard_len * n
    tokens_all = lax.axis_size("fsdp") * seq_len
    kv_here = KV_HEADS // n
    heads_w = kv_here * GROUP * HEAD_DIM
    group_w = kv_here * (GROUP + 2) * HEAD_DIM
    experts_here = w_gate.shape[0]
    expert_total = experts_here * n
    top_count = routes.shape[2]
    capacity = 3 * shard_len * top_count // (2 * expert_total)
    slots = -(-capacity // 16) * 16
    slot_rows = n * slots
    order_a, order_b = fsdp_bits()
    order = jnp.array(arrival_order(n), jnp.int32)[me]
    x_low = inputs.reshape(shard_len, width)

    own_qkv = lax.dynamic_slice_in_dim(w_qkv, me * group_w, group_w, 1)
    small = jnp.concatenate([gain_one[:, None], gain_two[:, None], w_router], axis=1)
    small = jnp.pad(small, ((0, 0), (0, -small.shape[1] % 128)))
    first = lax.all_gather(
        jnp.concatenate([own_qkv, small, w_out], axis=1), "fsdp", axis=0, tiled=True
    )
    full_qkv = first[:, :group_w]
    small = first[:, group_w : group_w + 2 + expert_total]
    full_out = first[:, -width:]
    full_g1 = small[:, 0].astype(full)
    full_g2 = small[:, 1].astype(full)
    router = small[:, 2:].T
    own_router = lax.dynamic_slice_in_dim(router, me * experts_here, experts_here, 0)
    own_router = jnp.pad(own_router, ((0, -experts_here % 16), (0, 0)))
    valid_rows = valid_mask.reshape(shard_len).astype(full)

    routes_low = jnp.concatenate([routes.reshape(shard_len, top_count).T, valid_mask], axis=0)
    routes_low = jnp.pad(
        routes_low.astype(low), ((0, -routes_low.shape[0] % 16), (0, width - shard_len))
    )
    block = jnp.concatenate([x_low, routes_low], axis=0)
    positions = jnp.arange(seq_len, dtype=jnp.int32)
    cosine, sine_vals = rope_tables(positions.astype(full), HEAD_DIM)
    limit = block_limits(block_lengths[0], positions)[None]
    rights, lefts = [block], [block]
    normed_one = jnp.zeros((seq_len, width), low)
    heads = jnp.zeros((n, kv_here, GROUP + 2, HEAD_DIM, shard_len), low)
    routes_all = []
    expert_weights = (w_gate, w_up, w_down)
    for turn in range(n):
        if turn < n - 1:
            right, left, block = tie(rights[turn], lefts[turn], block)
            right, left = line_move(right, left, turn + 1)
        start = order[turn] * shard_len
        normed = rms_norm(block[:shard_len].astype(full), full_g1).astype(low)
        projected = dot("td,dc->ct", normed, full_qkv)
        projected = projected.reshape(kv_here, GROUP + 2, HEAD_DIM, shard_len)
        turned = rotate(
            projected[:, : GROUP + 1],
            lax.dynamic_slice_in_dim(cosine, start, shard_len, 1),
            lax.dynamic_slice_in_dim(sine_vals, start, shard_len, 1),
        ).astype(low)
        turned = jnp.concatenate(
            [
                turned[:, :GROUP] * jnp.asarray(attn_mult, low),
                turned[:, GROUP:],
                projected[:, GROUP + 1 :].astype(low),
            ],
            axis=1,
        )
        heads = lax.dynamic_update_index_in_dim(heads, turned, order[turn], 0)
        normed_one = lax.dynamic_update_slice_in_dim(normed_one, normed, start, 0)
        routes_all.append(block[shard_len : shard_len + top_count + 1, :shard_len])
        if turn < n - 1:
            if turn == 0:
                right, left, expert_weights = tie(right, left, expert_weights)
            else:
                right, left, heads, normed_one = tie(right, left, heads, normed_one)
            rights.append(right)
            lefts.append(left)
            block = arrived(rights, lefts, turn + 1)

    w_gate, w_up, w_down = expert_weights
    hidden_w = w_gate.shape[2]
    down_chunks = [
        w_down[:, :, start : start + hidden_w] for start in range(0, width, hidden_w)
    ]
    weights = lax.all_gather(
        jnp.concatenate([w_gate, w_up, jnp.concatenate(down_chunks, axis=1)], axis=2),
        "fsdp",
        axis=1,
        tiled=True,
    )

    routes_all = jnp.stack(routes_all).astype(jnp.int32)
    valid_count = total(jnp.sum(routes_all[:, top_count]).astype(full).reshape(1, 1), "fsdp")[0, 0]
    expert_ids = jnp.arange(expert_total, dtype=jnp.int32)
    member = jnp.any(routes_all[:, :top_count, None, :] == expert_ids[:, None], axis=1)
    own_member = lax.dynamic_slice_in_dim(member, me * experts_here, experts_here, 1)
    earlier = jnp.arange(shard_len)[:, None] < jnp.arange(shard_len)[None, :]
    slot_of = dot("net,tu->neu", own_member.astype(low), earlier.astype(low)).astype(jnp.int32)
    slot_of = jnp.where(own_member, slot_of, -1)
    member = member.astype(full)

    key = jnp.moveaxis(heads[:, :, GROUP], 0, 2).reshape(kv_here, HEAD_DIM, seq_len)
    value = jnp.moveaxis(heads[:, :, GROUP + 1], 0, 2).reshape(kv_here, HEAD_DIM, seq_len)
    key_rows = jnp.swapaxes(key, 1, 2)
    value_rows = jnp.swapaxes(value, 1, 2)
    attended, out_heads, lse = attention_forward(heads, key_rows, value, limit)
    moved = exchange(attended)
    moved, slot_of, member, own_router = tie(moved, slot_of, member, own_router)
    attn_rows = by_place(nearest(*moved)).reshape(HEADS * HEAD_DIM, shard_len)
    projected = dot("kt,kd->td", attn_rows, full_out)
    hidden = x_low.astype(full) + resid_mult * projected
    normed_two, norm_two_pull = jax.vjp(rms_norm, hidden, full_g2)

    tokens = [normed_two.astype(low)]
    rights, lefts = [tokens[0]], [tokens[0]]
    buffers, gates = [], []
    for turn in range(n):
        if turn < n - 1:
            right, left, tokens[turn] = tie(rights[turn], lefts[turn], tokens[turn])
            right, left = line_move(right, left, turn + 1)
        *buffers, shard_gates = experts_forward(
            turn, n, jnp.stack([order[turn], me]), tokens[turn], slot_of[turn], member[turn],
            router, weights, w_down.shape[1], slots, buffers,
        )
        if turn < n - 1:
            right, left, shard_gates = tie(right, left, shard_gates)
            rights.append(right)
            lefts.append(left)
            tokens.append(arrived(rights, lefts, turn + 1))
        gates.append(shard_gates)
    mix_parts, expert_in, gate_up = buffers
    right = left = None
    for k in range(n - 1, 0, -1):
        moving = tie(*line_send(mix_parts, k, right, left))
        right, left = tie(*line_pass(*moving, k))
    mixture = line_end(mix_parts, right, left)
    output_f32 = hidden + resid_mult * mixture
    activations = output_f32.astype(low).reshape(1, shard_len, width)
    error_rows = output_f32 - teacher.astype(full).reshape(shard_len, width)
    weighted = valid_rows[:, None] * error_rows
    loss_steps = total_steps(jnp.sum(weighted * error_rows).reshape(1, 1), "seq", "fsdp")
    squares = next(loss_steps)
    d_out = weighted * (tokens_all / valid_count)

    d_mix = resid_mult * d_out
    d_tokens = d_mix.astype(low)
    mix_dot = jnp.sum(d_mix * mixture, axis=1)[None]
    rights, lefts = [d_tokens], [d_tokens]
    dot_rights, dot_lefts = [mix_dot], [mix_dot]
    buffers, d_logits = [], []
    for turn in range(n):
        if turn < n - 1:
            (right, left), (dot_right, dot_left), d_tokens = tie(
                (rights[turn], lefts[turn]), (dot_rights[turn], dot_lefts[turn]), d_tokens
            )
            dot_right, dot_left = line_move(dot_right, dot_left, turn + 1)
            right, left = line_move(right, left, turn + 1)
        *buffers, shard_logits = experts_backward(
            turn, n, jnp.stack([order[turn], me]), d_tokens, slot_of[turn], gates[turn], mix_dot,
            own_router, gate_up, weights, w_down.shape[1], buffers,
        )
        if turn < n - 1:
            right, left, dot_right, dot_left, shard_logits, squares = tie(
                right, left, dot_right, dot_left, shard_logits, squares
            )
            squares = loss_steps.send(squares)
            rights.append(right)
            lefts.append(left)
            dot_rights.append(dot_right)
            dot_lefts.append(dot_left)
            d_tokens = arrived(rights, lefts, turn + 1)
            mix_dot = arrived(dot_rights, dot_lefts, turn + 1)
        d_logits.append(shard_logits)
    d_parts, d_rows, d_gate_up, act_low = buffers
    expert_in = expert_in.reshape(experts_here, slot_rows, width)
    d_rows = d_rows.reshape(experts_here, slot_rows, width)
    d_gate_up = d_gate_up.reshape(experts_here, slot_rows, -1)
    act_low = act_low.reshape(experts_here, slot_rows, -1)

    right = left = None
    cut = (experts_here + 1) // 2
    sums = [None, None]
    for k in range(n - 1, 0, -1):
        moving = line_send(d_parts, k, right, left)
        if k >= n - 2:
            half = n - 1 - k
            moving, d_rows = tie(moving, d_rows)
            right, left = line_pass(*moving, k)
            if half:
                for each in sums[0]:
                    each.go()
            grads = weight_grads(
                mine.reshape(1), expert_in, d_gate_up, act_low, d_rows, order_a, order_b,
                *((cut, experts_here) if half else (0, cut)),
            )
            right, left, grads, squares = tie(right, left, grads, squares)
            sums[half] = [Halving(*grads[:2], order_a), Halving(*grads[2:], order_b)]
        elif k == n - 3:
            (moving,) = leave(sums[1], moving)
            right, left = line_pass(*moving, k)
            for each in sums[1]:
                each.go()
            for each in sums[0]:
                each.add()
            right, left, squares = leave(sums[0], right, left, squares)
            for each in sums[0]:
                each.go()
        else:
            right, left, squares = tie(*line_pass(*tie(*moving), k), squares)
        squares = loss_steps.send(squares)
    d_normed_two = line_end(d_parts, right, left)

    d_hidden_norm, gain_two_part = norm_two_pull(d_normed_two)
    d_hidden = d_out + d_hidden_norm
    d_proj = (resid_mult * d_hidden).astype(low)
    d_attended = dot("kd,td->kt", full_out, d_proj).astype(low)
    moved = exchange(d_attended.reshape(n, heads_w, shard_len))
    for each in sums[1]:
        each.add()
    out_part = dot("kt,td->kd", attn_rows, d_proj).astype(low)
    out_sum = lax.psum_scatter(out_part, "fsdp", scatter_dimension=0, tiled=True)
    router_part = sum(
        dot("td,et->de", shard, shard_logits[:experts_here])
        for shard, shard_logits in zip(tokens, d_logits)
    )
    moved, out_part, router_part = leave(sums[1], moved, out_part, router_part)
    for each in sums[1]:
        each.go()
    (moved,) = land(sums[0], moved)
    d_heads = by_place(nearest(*moved))
    for each in sums[0]:
        each.add()
    (d_heads,) = leave(sums[0], d_heads)
    for each in sums[0]:
        each.go()
    query_grad, key_grad, value_grad = attention_backward(
        heads, key_rows, value_rows, key, limit, out_heads, lse, d_heads
    )
    d_turned = jnp.concatenate([query_grad, key_grad[:, None]], axis=1).astype(full)
    d_turned = rotate(d_turned, cosine, -sine_vals).astype(low)
    d_qkv = jnp.concatenate([d_turned, value_grad[:, None]], axis=1).reshape(group_w, seq_len)
    d_parts = dot("ct,dc->td", d_qkv, full_qkv).astype(low).reshape(n, shard_len, width)

    right = left = None
    for k in range(n - 1, 0, -1):
        moving = line_send(d_parts, k, right, left)
        if k == n - 1:
            moving, d_qkv = tie(moving, d_qkv)
            right, left = line_pass(*moving, k)
            own_columns = jnp.zeros((width, expert_total), full)
            own_columns = lax.dynamic_update_slice_in_dim(
                own_columns, router_part, me * experts_here, 1
            )
            qkv_part = jnp.concatenate(
                [dot("td,ct->dc", normed_one, d_qkv), own_columns, gain_two_part[:, None]], axis=1
            ).astype(low)
            qkv_sum = rows_halving(qkv_part, order_a)
            (right, left) = land(sums[1], right, left)
            for each in sums[1]:
                each.add()
            right, left = leave(sums[1] + [qkv_sum], right, left)
            qkv_sum.go()
            qkv_sum.add()
            qkv_sum.go()
            for each in sums[1]:
                each.go()
        else:
            right, left = line_pass(*tie(*moving), k)
            if k == n - 2:
                right, left, out_sum = land([qkv_sum] + sums[0], right, left, out_sum)
                qkv_sum.add()
                qkv_sum.go()
                for each in sums[0]:
                    each.add()
                out_sum = lax.psum(out_sum, "seq")
            elif k == 1:
                right, left = land([qkv_sum], right, left)
            else:
                right, left = tie(right, left)
    qkv_sum.add()
    blocks = line_gather(qkv_sum.finish().astype(low))
    d_normed_one = line_end(d_parts, right, left)
    _, norm_one_pull = jax.vjp(lambda v: rms_norm(v, full_g1), x_low.astype(full))
    input_grad = (d_hidden + norm_one_pull(d_normed_one)[0]).reshape(1, shard_len, width)
    input_grad, out_sum = land(sums[1], input_grad, out_sum)
    for each in sums[1]:
        each.add()
    left_sum, right_sum = (
        jnp.concatenate([sums[0][side].finish(), sums[1][side].finish()]) for side in (0, 1)
    )
    gate_grad, up_grad = left_sum[:, :, :hidden_w], right_sum[:, :, :hidden_w]
    few = w_down.shape[1]
    down_grad = jnp.concatenate(
        [
            part[:, start : start + few, hidden_w:]
            for part in (left_sum, right_sum)
            for start in range(0, part.shape[1], few)
        ],
        axis=2,
    )
    out_grad = out_sum.astype(full)
    qkv_grad = jnp.zeros((w_qkv.shape[0], QKV_W), full)
    rest = 0.0
    for k, block in enumerate(blocks):
        block = block.astype(full)
        qkv_grad = lax.dynamic_update_slice_in_dim(
            qkv_grad, block[:, :group_w], ((me - k) % n) * group_w, 1
        )
        rest = rest + block[:, group_w:]
    router_grad, gain_two_grad = rest[:, :expert_total], rest[:, expert_total]
    gain_one_grad = jnp.sum(qkv_grad * w_qkv.astype(full), axis=1) / gain_one.astype(full)
    for _ in range(2):
        squares = loss_steps.send(squares)
    loss_value = squares[0, 0] / (valid_count * width)
    return (
        activations,
        loss_value,
        input_grad,
        gain_one_grad,
        qkv_grad,
        out_grad,
        gain_two_grad,
        router_grad,
        gate_grad,
        up_grad,
        down_grad,
    )


def solution(mesh):
    return jax.shard_map(
        shards,
        mesh=mesh,
        in_specs=(
            P("fsdp", "seq", None),
            P("fsdp", "seq", None),
            P("fsdp", "seq", None),
            P("fsdp", "seq"),
            P("fsdp", None),
            P("fsdp"),
            P("fsdp", None),
            P("fsdp", None),
            P("fsdp"),
            P("fsdp", None),
            P("seq", "fsdp", None),
            P("seq", "fsdp", None),
            P("seq", "fsdp", None),
        ),
        out_specs=(
            P("fsdp", "seq", None),
            P(),
            P("fsdp", "seq", None),
            P("fsdp"),
            P("fsdp", None),
            P("fsdp", None),
            P("fsdp"),
            P("fsdp", None),
            P("seq", "fsdp", None),
            P("seq", "fsdp", None),
            P("seq", "fsdp", None),
        ),
        check_vma=False,
    )
```

```python
import functools

import jax
import jax.numpy as jnp
from jax import lax
from jax.experimental import pallas as pl
from jax.experimental.pallas import tpu as pltpu
from jax.sharding import PartitionSpec as P

HEADS = 24
KV_HEADS = 8
HEAD_DIM = 64
BLOCK = 256
GROUP = 3
QKV_W = 2560


epsilon = 1e-06
attn_mult = 0.015625
resid_mult = 0.22
rope_base = 10000.0
masked_score = -1e30

low = jnp.bfloat16
full = jnp.float32


def dot(spec, left, right):
    return jnp.einsum(spec, left, right, preferred_element_type=full)


def rms_norm(values, gain_vec):
    inv_rms = lax.rsqrt(jnp.mean(values * values, axis=-1, keepdims=True) + epsilon)
    return values * inv_rms * gain_vec


def rope_tables(positions, head_dim):
    half_dim = head_dim // 2
    frequency = rope_base ** (-(2.0 * jnp.arange(half_dim, dtype=full)) / head_dim)
    angles = frequency[:, None] * positions[None, :]
    return (jnp.cos(angles), jnp.sin(angles))


def rotate(values, cosine, sine_vals):
    half_dim = values.shape[-2] // 2
    front_half = values[..., :half_dim, :]
    back_half = values[..., half_dim:, :]
    return jnp.concatenate(
        [front_half * cosine - back_half * sine_vals, back_half * cosine + front_half * sine_vals],
        axis=-2,
    )


def block_limits(lengths_row, positions):
    block_ends = jnp.cumsum(lengths_row)
    open_ends = jnp.where(block_ends[None, :] > positions[:, None], block_ends[None, :], positions.shape[0])
    return jnp.min(open_ends, axis=1).astype(jnp.int32)


def tie(*groups):
    return lax.optimization_barrier(groups)


def line_move(right, left, k):
    n = lax.axis_size("seq")
    return (
        lax.ppermute(right, "seq", [(i, i + 1) for i in range(k - 1, n - 1)]),
        lax.ppermute(left, "seq", [(i, i - 1) for i in range(1, n - k + 1)]),
    )


def line_gather(block):
    n = lax.axis_size("seq")
    rights, lefts = [block], [block]
    for k in range(1, n):
        right, left = tie(*line_move(rights[-1], lefts[-1], k))
        rights.append(right)
        lefts.append(left)
    return nearest(rights, lefts)


def nearest(rights, lefts):
    n = lax.axis_size("seq")
    me = lax.axis_index("seq")
    return [rights[0]] + [jnp.where(me >= k, rights[k], lefts[n - k]) for k in range(1, n)]


def arrival_order(n):
    order = []
    for me in range(n):
        both = min(me, n - 1 - me)
        places = [me]
        for k in range(1, n):
            places += [me - k] if me >= k and (k <= both or me > n - 1 - me) else []
            places += [me + k] if me + k < n and (k <= both or me < n - 1 - me) else []
        order.append(places)
    return order


def arrived(rights, lefts, turn):
    n = lax.axis_size("seq")
    me = lax.axis_index("seq")
    sources = {}
    for dev, places in enumerate(arrival_order(n)):
        gap = dev - places[turn]
        sources.setdefault(gap, []).append(dev)
    block = None
    for gap, devs in sources.items():
        moved = rights[gap] if gap >= 0 else lefts[-gap]
        if block is None:
            block = moved
        else:
            mine = jnp.array([dev in devs for dev in range(n)])[me]
            block = jnp.where(mine, moved, block)
    return block


def at_place(placed, place):
    return lax.dynamic_index_in_dim(placed, place % lax.axis_size("seq"), 0, keepdims=False)


def line_send(parts, k, right, left):
    me = lax.axis_index("seq")
    to_right, to_left = at_place(parts, me + k), at_place(parts, me - k)
    if right is not None:
        to_right = (to_right.astype(full) + right.astype(full)).astype(low)
        to_left = (to_left.astype(full) + left.astype(full)).astype(low)
    return to_right, to_left


def line_pass(to_right, to_left, k):
    n = lax.axis_size("seq")
    return (
        lax.ppermute(to_right, "seq", [(i, i + 1) for i in range(n - k)]),
        lax.ppermute(to_left, "seq", [(i, i - 1) for i in range(k, n)]),
    )


def line_end(parts, right, left):
    own = at_place(parts, lax.axis_index("seq")).astype(full)
    return own + (right.astype(full) + left.astype(full))


def by_place(blocks):
    n = lax.axis_size("seq")
    me = lax.axis_index("seq")
    placed = jnp.zeros((n,) + blocks[0].shape, blocks[0].dtype)
    for k, block in enumerate(blocks):
        placed = lax.dynamic_update_index_in_dim(placed, block, (me - k) % n, 0)
    return placed


def exchange(blocks):
    n = lax.axis_size("seq")
    me = lax.axis_index("seq")
    own = at_place(blocks, me)
    rights, lefts = [own] * n, [own] * n
    for k in range(n - 1, 0, -1):
        to_right, to_left = at_place(blocks, me + k), at_place(blocks, me - k)
        rights[k] = lax.ppermute(to_right, "seq", [(i, i + k) for i in range(n - k)])
        lefts[k] = lax.ppermute(to_left, "seq", [(i, i - k) for i in range(k, n)])
    return rights, lefts


def swap(value, axis, bit):
    return lax.ppermute(value, axis, [(i, i ^ bit) for i in range(lax.axis_size(axis))])


def total(value, *axes):
    for axis in axes:
        for step in range(lax.axis_size(axis).bit_length() - 1):
            value = value + swap(value, axis, 1 << step)
    return value


def fsdp_bits():
    bits = [1 << step for step in range(lax.axis_size("fsdp").bit_length() - 1)]
    return tuple(bits), tuple(bits[:1] + bits[:0:-1])


def total_steps(value, *axes):
    for axis in axes:
        for step in range(lax.axis_size(axis).bit_length() - 1):
            here = swap(value, axis, 1 << step)
            here = yield here
            value = value + here
    while True:
        yield value


class Halving:
    def __init__(self, keep, send, bits):
        self.terms, self.send, self.bits = [keep], send, list(bits)

    def go(self):
        self.terms = self.terms + [swap(self.send, "fsdp", self.bits.pop(0))]

    def add(self):
        half = self.terms[0].shape[0] // 2
        if half:
            self.send = sum(term[half:].astype(full) for term in self.terms).astype(low)
            self.terms = [term[:half] for term in self.terms]

    def finish(self):
        while self.bits:
            self.go()
            self.add()
        return sum(term[0].astype(full) for term in self.terms)


def rows_halving(part, bits):
    devs = lax.axis_size("fsdp")
    order = lax.axis_index("fsdp") ^ jnp.array(halving_masks(bits), jnp.int32)
    blocks = part.reshape(devs, part.shape[0] // devs, part.shape[1])[order]
    return Halving(blocks[: devs // 2], blocks[devs // 2 :], bits)


def land(sums, *others):
    tied = tie([each.terms[-1] for each in sums], *others)
    for each, here in zip(sums, tied[0]):
        each.terms = each.terms[:-1] + [here]
    return tied[1:]


def leave(sums, *others):
    tied = tie([each.send for each in sums], *others)
    for each, send in zip(sums, tied[0]):
        each.send = send
    return tied[1:]


def nt(a, b):
    return lax.dot_general(a, b, (((1,), (1,)), ((), ())), preferred_element_type=full)

def nn(a, b):
    return lax.dot_general(a, b, (((1,), (0,)), ((), ())), preferred_element_type=full)

def tn(a, b):
    return lax.dot_general(a, b, (((0,), (0,)), ((), ())), preferred_element_type=full)


def beside(rows):
    return jnp.concatenate([rows[h] for h in range(GROUP)], axis=1)

def key_steps(i, seq_len, query_rows, key_rows):
    free = (i * query_rows) // key_rows
    need = ((i + 1) * query_rows + BLOCK - 1 + key_rows - 1) // key_rows
    return free, jnp.minimum(need, seq_len // key_rows)

def forward_kernel(seq_len, query_rows, key_rows, limit_ref, q_ref, k_ref, vt_ref, low_ref, out_ref, lse_ref):
    i = pl.program_id(1)
    qt = beside(q_ref[0, 0])
    width = GROUP * query_rows
    limit = jnp.concatenate([limit_ref[...]] * GROUP, axis=1)

    def step(masked, j, carry):
        peak, total, acc = carry
        start = pl.multiple_of(j * key_rows, key_rows)
        s = nn(k_ref[0, pl.ds(start, key_rows), :], qt)
        if masked:
            place = start + lax.broadcasted_iota(jnp.int32, (key_rows, 1), 0)
            s = jnp.where(place < limit, s, masked_score)
        new_peak = jnp.maximum(peak, jnp.max(s, axis=0, keepdims=True))
        shrink = jnp.exp(peak - new_peak)
        p = jnp.exp(s - new_peak)
        total = shrink * total + jnp.sum(p, axis=0, keepdims=True)
        acc = shrink * acc + nn(vt_ref[0, :, pl.ds(start, key_rows)], p.astype(low))
        return new_peak, total, acc

    free, need = key_steps(i, seq_len, query_rows, key_rows)
    carry = (
        jnp.full((1, width), masked_score, full),
        jnp.zeros((1, width), full),
        jnp.zeros((HEAD_DIM, width), full),
    )
    carry = lax.fori_loop(0, free, lambda j, c: step(False, j, c), carry)
    peak, total, acc = lax.fori_loop(free, need, lambda j, c: step(True, j, c), carry)
    out = acc / total
    lse = peak + jnp.log(total)
    for h in range(GROUP):
        cols = slice(h * query_rows, (h + 1) * query_rows)
        out_ref[0, h] = out[:, cols]
        low_ref[0, pl.ds(h * HEAD_DIM, HEAD_DIM), :] = out[:, cols].astype(low)
        lse_ref[0, h] = lse[:, cols]

def query_spec(query_rows, per):
    return pl.BlockSpec(
        (1, 1, GROUP, HEAD_DIM, query_rows), lambda g, i: (i // per, g, 0, 0, i % per)
    )


def attention_forward(heads, k_rows, vt, limit):
    kv_here, shard_len = heads.shape[1], heads.shape[4]
    seq_len = k_rows.shape[1]
    query_rows = min(256, shard_len)
    key_rows = min(512, seq_len)
    per = shard_len // query_rows
    return pl.pallas_call(
        functools.partial(forward_kernel, seq_len, query_rows, key_rows),
        grid=(kv_here, seq_len // query_rows),
        in_specs=[
            pl.BlockSpec((1, query_rows), lambda g, i: (0, i)),
            query_spec(query_rows, per),
            pl.BlockSpec((1, seq_len, HEAD_DIM), lambda g, i: (g, 0, 0)),
            pl.BlockSpec((1, HEAD_DIM, seq_len), lambda g, i: (g, 0, 0)),
        ],
        out_specs=[
            pl.BlockSpec((1, GROUP * HEAD_DIM, query_rows), lambda g, i: (i // per, g, i % per)),
            pl.BlockSpec((1, GROUP, HEAD_DIM, query_rows), lambda g, i: (g, 0, 0, i)),
            pl.BlockSpec((1, GROUP, 1, query_rows), lambda g, i: (g, 0, 0, i)),
        ],
        out_shape=[
            jax.ShapeDtypeStruct((seq_len // shard_len, kv_here * GROUP * HEAD_DIM, shard_len), low),
            jax.ShapeDtypeStruct((kv_here, GROUP, HEAD_DIM, seq_len), full),
            jax.ShapeDtypeStruct((kv_here, GROUP, 1, seq_len), full),
        ],
        compiler_params=vmem(40),
        name="attention_forward",
    )(limit, heads, k_rows, vt)

def backward_kernel(seq_len, query_rows, key_rows, limit_ref, q_ref, k_ref, v_ref, kt_ref, out_ref, lse_ref, dout_ref, dq_ref, dk_ref, dv_ref, dk_acc, dv_acc):
    i = pl.program_id(1)

    @pl.when(i == 0)
    def _():
        dk_acc[...] = jnp.zeros_like(dk_acc)
        dv_acc[...] = jnp.zeros_like(dv_acc)

    qt = beside(q_ref[0, 0])
    limit = jnp.concatenate([limit_ref[...]] * GROUP, axis=1)
    dout = jnp.concatenate([dout_ref[0, pl.ds(h * HEAD_DIM, HEAD_DIM), :] for h in range(GROUP)], axis=1)
    delta = jnp.sum(dout.astype(full) * beside(out_ref[0]), axis=0, keepdims=True)
    lse = beside(lse_ref[0])

    def step(masked, j, dq):
        start = pl.multiple_of(j * key_rows, key_rows)
        keys = pl.ds(start, key_rows)
        s = nn(k_ref[0, keys, :], qt)
        if masked:
            place = start + lax.broadcasted_iota(jnp.int32, (key_rows, 1), 0)
            s = jnp.where(place < limit, s, masked_score)
        p = jnp.exp(s - lse)
        dp = nn(v_ref[0, keys, :], dout)
        ds = (p * (dp - delta)).astype(low)
        dk_acc[:, keys] += nt(qt, ds)
        dv_acc[:, keys] += nt(dout, p.astype(low))
        return dq + nn(kt_ref[0, :, keys], ds)

    free, need = key_steps(i, seq_len, query_rows, key_rows)
    dq = jnp.zeros((HEAD_DIM, GROUP * query_rows), full)
    dq = lax.fori_loop(0, free, lambda j, c: step(False, j, c), dq)
    dq = lax.fori_loop(free, need, lambda j, c: step(True, j, c), dq) * attn_mult
    for h in range(GROUP):
        dq_ref[0, h] = dq[:, h * query_rows : (h + 1) * query_rows].astype(low)

    @pl.when(i == pl.num_programs(1) - 1)
    def _():
        dk_ref[0] = dk_acc[...].astype(low)
        dv_ref[0] = dv_acc[...].astype(low)

def attention_backward(heads, k_rows, v_rows, kt, limit, out, lse, d_out):
    kv_here, shard_len = heads.shape[1], heads.shape[4]
    seq_len = k_rows.shape[1]
    query_rows = min(256, shard_len)
    key_rows = min(512, seq_len)
    per = shard_len // query_rows
    quarter = lambda g, i: (g, 0, 0, i)
    whole = lambda g, i: (g, 0, 0)
    return pl.pallas_call(
        functools.partial(backward_kernel, seq_len, query_rows, key_rows),
        grid=(kv_here, seq_len // query_rows),
        in_specs=[
            pl.BlockSpec((1, query_rows), lambda g, i: (0, i)),
            query_spec(query_rows, per),
            pl.BlockSpec((1, seq_len, HEAD_DIM), whole),
            pl.BlockSpec((1, seq_len, HEAD_DIM), whole),
            pl.BlockSpec((1, HEAD_DIM, seq_len), whole),
            pl.BlockSpec((1, GROUP, HEAD_DIM, query_rows), quarter),
            pl.BlockSpec((1, GROUP, 1, query_rows), quarter),
            pl.BlockSpec((1, GROUP * HEAD_DIM, query_rows), lambda g, i: (i // per, g, i % per)),
        ],
        out_specs=[
            pl.BlockSpec((1, GROUP, HEAD_DIM, query_rows), quarter),
            pl.BlockSpec((1, HEAD_DIM, seq_len), whole),
            pl.BlockSpec((1, HEAD_DIM, seq_len), whole),
        ],
        out_shape=[
            jax.ShapeDtypeStruct((kv_here, GROUP, HEAD_DIM, seq_len), low),
            jax.ShapeDtypeStruct((kv_here, HEAD_DIM, seq_len), low),
            jax.ShapeDtypeStruct((kv_here, HEAD_DIM, seq_len), low),
        ],
        scratch_shapes=[pltpu.VMEM((HEAD_DIM, seq_len), full), pltpu.VMEM((HEAD_DIM, seq_len), full)],
        compiler_params=vmem(40),
        name="attention_backward",
    )(limit, heads, k_rows, v_rows, kt, out, lse, d_out)


def vmem(mib):
    return pltpu.CompilerParams(vmem_limit_bytes=mib * 2**20)


def own_row(ref, row):
    return ref[pl.ds(row, 1), :]


def join_down(rows, block_ref, down_ref):
    hidden, width = down_ref.shape
    chunks = width // hidden
    for dev in range(hidden // rows):
        for chunk in range(chunks):
            start = (dev * chunks + chunk) * rows
            down_ref[dev * rows : (dev + 1) * rows, chunk * hidden : (chunk + 1) * hidden] = (
                block_ref[0, start : start + rows, :]
            )


def experts_kernel(
    few, at_ref, tok_ref, slot_ref, member_ref, router_ref, wgu_ref, wd_ref, *refs
):
    part_ref, x_ref, gu_ref, gates_ref, acc, gates_all, down = refs[-7:]
    e, experts = pl.program_id(0), pl.num_programs(0)
    slots = x_ref.shape[2]

    @pl.when(e == 0)
    def _():
        member = member_ref[...] > 0
        chosen = jnp.where(member, nt(router_ref[...], tok_ref[...]), masked_score)
        chosen = jnp.exp(chosen - jnp.max(chosen, axis=0, keepdims=True))
        chosen = jnp.where(member, chosen, 0.0)
        gates_all[...] = chosen / jnp.sum(chosen, axis=0, keepdims=True)
        acc[...] = jnp.zeros_like(acc)

    gate_row = own_row(gates_all, at_ref[1] * experts + e)
    gates_ref[pl.ds(e, 1), :] = gate_row
    place = lax.broadcasted_iota(jnp.int32, (slots, 1), 0)
    here = place == own_row(slot_ref, e)
    x = nn(jnp.where(here, 1.0, 0.0).astype(low), tok_ref[...]).astype(low)
    x_ref[0, 0] = x
    gu = nn(x, wgu_ref[0])
    gu_ref[0, 0] = gu.astype(low)
    hidden = gu.shape[1] // 2
    g, u = gu[:, :hidden], gu[:, hidden:]
    act = (g * jax.nn.sigmoid(g) * u).astype(low)
    join_down(few, wd_ref, down)
    y = nn(act, down[...]).astype(low)
    acc[...] += tn(jnp.where(here, gate_row, 0.0).astype(low), y)

    @pl.when(e == experts - 1)
    def _():
        part_ref[0] = acc[...].astype(low)


def back_kernel(
    few, at_ref, tok_ref, slot_ref, gates_ref, mix_ref, router_ref, gu_ref, wgu_ref, wd_ref, *refs
):
    part_ref, d_ref, dgu_ref, act_ref, dlog_ref, acc, dlog_all, down = refs[-8:]
    e, experts = pl.program_id(0), pl.num_programs(0)
    slots, hidden = gu_ref.shape[2], gu_ref.shape[3] // 2

    @pl.when(e == 0)
    def _():
        dlog_all[...] = jnp.zeros_like(dlog_all)
        acc[...] = jnp.zeros_like(acc)

    place = lax.broadcasted_iota(jnp.int32, (slots, 1), 0)
    here = place == own_row(slot_ref, e)
    pick = jnp.where(here, 1.0, 0.0).astype(low)
    gate_row = own_row(gates_ref, e)
    gate = jnp.sum(jnp.where(here, gate_row, 0.0), axis=1, keepdims=True)
    d = nn(pick, tok_ref[...]).astype(low)
    d_ref[0, 0] = d
    join_down(few, wd_ref, down)
    d_act = nt(d, down[...])
    g, u = gu_ref[0, 0, :, :hidden].astype(full), gu_ref[0, 0, :, hidden:].astype(full)
    sig = jax.nn.sigmoid(g)
    silu = g * sig
    act = silu * u
    d_gate = jnp.sum(d_act * act, axis=1, keepdims=True)
    d_gate = jnp.sum(jnp.where(here, d_gate, 0.0), axis=0, keepdims=True)
    dlog_all[pl.ds(e, 1), :] = gate_row * (d_gate - mix_ref[...])
    act_ref[0, 0] = (act * gate).astype(low)
    d_act = d_act * gate
    d_g = (d_act * u * (sig + silu * (1.0 - sig))).astype(low)
    d_u = (d_act * silu).astype(low)
    dgu_ref[0, 0, :, :hidden] = d_g
    dgu_ref[0, 0, :, hidden:] = d_u
    dx = nt(dgu_ref[0, 0], wgu_ref[0]).astype(low)
    acc[...] += tn(pick, dx)

    @pl.when(e == experts - 1)
    def _():
        dlog = dlog_all[...].astype(low)
        dlog_ref[...] = dlog
        part_ref[0] = (acc[...] + tn(dlog, router_ref[...])).astype(low)


def by_expert(*shape):
    return pl.BlockSpec((1,) + shape, lambda e, at: (e, 0, 0))


def in_turn(turn, *shape):
    return pl.BlockSpec((1, 1) + shape, lambda e, at: (e, turn, 0, 0))


def same(*shape):
    return pl.BlockSpec(shape, lambda e, at: (0, 0))


def in_place(*shape):
    return pl.BlockSpec((1,) + shape, lambda e, at: (at[0], 0, 0))


def shard_call(kernel, name, at, inputs, in_specs, out_specs, out_shape, buffers, scratch, experts):
    first = len(inputs) + 1
    aliases = {first + i: i for i in range(len(buffers))}
    return pl.pallas_call(
        kernel,
        grid_spec=pltpu.PrefetchScalarGridSpec(
            num_scalar_prefetch=1,
            grid=(experts,),
            in_specs=in_specs + [pl.BlockSpec(memory_space=pl.ANY)] * len(buffers),
            out_specs=out_specs,
            scratch_shapes=scratch,
        ),
        out_shape=out_shape,
        input_output_aliases=aliases,
        compiler_params=vmem(48),
        name=name,
    )(at, *inputs, *buffers)


def weight_specs(width, hidden):
    return [
        pl.BlockSpec((1, width, 2 * hidden), lambda e, at: (e, 0, 0)),
        pl.BlockSpec((1, width, hidden), lambda e, at: (e, 0, 2)),
    ]


def experts_forward(turn, devs, at, tokens, slot_of, member, router, weights, few, slots, buffers):
    experts, width, columns = weights.shape
    hidden = columns // 3
    count = tokens.shape[0]
    total_experts = member.shape[0]
    return shard_call(
        functools.partial(experts_kernel, few),
        "experts_forward",
        at,
        [tokens, slot_of, member, router, weights, weights],
        [
            same(count, width),
            same(experts, count),
            same(total_experts, count),
            same(total_experts, width),
            *weight_specs(width, hidden),
        ],
        [
            in_place(count, width),
            in_turn(turn, slots, width),
            in_turn(turn, slots, 2 * hidden),
            same(experts, count),
        ],
        [
            jax.ShapeDtypeStruct((devs, count, width), low),
            jax.ShapeDtypeStruct((experts, devs, slots, width), low),
            jax.ShapeDtypeStruct((experts, devs, slots, 2 * hidden), low),
            jax.ShapeDtypeStruct((experts, count), full),
        ],
        buffers,
        [
            pltpu.VMEM((count, width), full),
            pltpu.VMEM((total_experts, count), full),
            pltpu.VMEM((hidden, width), low),
        ],
        experts,
    )


def experts_backward(
    turn, devs, at, d_tokens, slot_of, gates, mix_dot, router, gu, weights, few, buffers
):
    experts, width, columns = weights.shape
    hidden = columns // 3
    count = d_tokens.shape[0]
    slots = gu.shape[2]
    lines = router.shape[0]
    return shard_call(
        functools.partial(back_kernel, few),
        "experts_backward",
        at,
        [d_tokens, slot_of, gates, mix_dot, router, gu, weights, weights],
        [
            same(count, width),
            same(experts, count),
            same(experts, count),
            same(1, count),
            same(lines, width),
            in_turn(turn, slots, 2 * hidden),
            *weight_specs(width, hidden),
        ],
        [
            in_place(count, width),
            in_turn(turn, slots, width),
            in_turn(turn, slots, 2 * hidden),
            in_turn(turn, slots, hidden),
            same(lines, count),
        ],
        [
            jax.ShapeDtypeStruct((devs, count, width), low),
            jax.ShapeDtypeStruct((experts, devs, slots, width), low),
            jax.ShapeDtypeStruct((experts, devs, slots, 2 * hidden), low),
            jax.ShapeDtypeStruct((experts, devs, slots, hidden), low),
            jax.ShapeDtypeStruct((lines, count), low),
        ],
        buffers,
        [
            pltpu.VMEM((count, width), full),
            pltpu.VMEM((lines, count), full),
            pltpu.VMEM((hidden, width), low),
        ],
        experts,
    )


def halving_masks(bits):
    masks = [0]
    for bit in reversed(bits):
        masks = masks + [mask ^ bit for mask in masks]
    return masks


def grads_kernel(few, x_ref, dgu_ref, act_ref, d_ref, *refs):
    out_ref, down = refs[-2], refs[-1]
    hidden, width = down.shape
    out_ref[0, :, : 2 * hidden] = tn(x_ref[0], dgu_ref[0]).astype(low)
    down[...] = tn(act_ref[0], d_ref[0]).astype(low)
    chunks = width // hidden
    for dev in range(hidden // few):
        for chunk in range(chunks):
            start = (dev * chunks + chunk) * few
            out_ref[0, start : start + few, 2 * hidden :] = down[
                dev * few : (dev + 1) * few, chunk * hidden : (chunk + 1) * hidden
            ]


def weight_grads(rows, d_gu, act, d_rows, few, first, stop, buffers):
    experts, count, width = rows.shape
    hidden = act.shape[2]

    def part(*block):
        return pl.BlockSpec((1,) + block, lambda e: (first + e, 0, 0))

    return pl.pallas_call(
        functools.partial(grads_kernel, few),
        grid=(stop - first,),
        in_specs=[part(count, width), part(count, 2 * hidden), part(count, hidden), part(count, width)]
        + [pl.BlockSpec(memory_space=pl.ANY)] * len(buffers),
        out_specs=part(width, 3 * hidden),
        out_shape=jax.ShapeDtypeStruct((experts, width, 3 * hidden), low),
        scratch_shapes=[pltpu.VMEM((hidden, width), low)],
        input_output_aliases={4 + i: i for i in range(len(buffers))},
        compiler_params=vmem(56),
        name="weight_grads",
    )(rows, d_gu, act, d_rows, *buffers)


def shards(
    inputs,
    teacher,
    routes,
    valid_mask,
    block_lengths,
    gain_one,
    w_qkv,
    w_out,
    gain_two,
    w_router,
    w_gate,
    w_up,
    w_down,
):
    n = lax.axis_size("seq")
    me = lax.axis_index("seq")
    mine = lax.axis_index("fsdp")
    seqs_here, shard_len, width = inputs.shape
    assert seqs_here == 1
    seq_len = shard_len * n
    tokens_all = lax.axis_size("fsdp") * seq_len
    kv_here = KV_HEADS // n
    heads_w = kv_here * GROUP * HEAD_DIM
    group_w = kv_here * (GROUP + 2) * HEAD_DIM
    experts_here = w_gate.shape[0]
    expert_total = experts_here * n
    top_count = routes.shape[2]
    capacity = 3 * shard_len * top_count // (2 * expert_total)
    slots = -(-capacity // 16) * 16
    slot_rows = n * slots
    order_a, order_b = fsdp_bits()
    order = jnp.array(arrival_order(n), jnp.int32)[me]
    x_low = inputs.reshape(shard_len, width)

    own_qkv = lax.dynamic_slice_in_dim(w_qkv, me * group_w, group_w, 1)
    small = jnp.concatenate([gain_one[:, None], gain_two[:, None], w_router], axis=1)
    small = jnp.pad(small, ((0, 0), (0, -small.shape[1] % 128)))
    first = lax.all_gather(
        jnp.concatenate([own_qkv, small, w_out], axis=1), "fsdp", axis=0, tiled=True
    )
    full_qkv = first[:, :group_w]
    small = first[:, group_w : group_w + 2 + expert_total]
    full_out = first[:, -width:]
    full_g1 = small[:, 0].astype(full)
    full_g2 = small[:, 1].astype(full)
    router = small[:, 2:].T
    own_router = lax.dynamic_slice_in_dim(router, me * experts_here, experts_here, 0)
    own_router = jnp.pad(own_router, ((0, -experts_here % 16), (0, 0)))
    valid_rows = valid_mask.reshape(shard_len).astype(full)

    routes_low = jnp.concatenate([routes.reshape(shard_len, top_count).T, valid_mask], axis=0)
    routes_low = jnp.pad(
        routes_low.astype(low), ((0, -routes_low.shape[0] % 16), (0, width - shard_len))
    )
    block = jnp.concatenate([x_low, routes_low], axis=0)
    positions = jnp.arange(seq_len, dtype=jnp.int32)
    cosine, sine_vals = rope_tables(positions.astype(full), HEAD_DIM)
    limit = block_limits(block_lengths[0], positions)[None]
    rights, lefts = [block], [block]
    normed_one = jnp.zeros((seq_len, width), low)
    heads = jnp.zeros((n, kv_here, GROUP + 2, HEAD_DIM, shard_len), low)
    routes_all = []
    expert_weights = (w_gate, w_up, w_down)
    for turn in range(n):
        if turn < n - 1:
            right, left = line_move(rights[turn], lefts[turn], turn + 1)
        start = order[turn] * shard_len
        normed = rms_norm(block[:shard_len].astype(full), full_g1).astype(low)
        projected = dot("td,dc->ct", normed, full_qkv)
        projected = projected.reshape(kv_here, GROUP + 2, HEAD_DIM, shard_len)
        turned = rotate(
            projected[:, : GROUP + 1],
            lax.dynamic_slice_in_dim(cosine, start, shard_len, 1),
            lax.dynamic_slice_in_dim(sine_vals, start, shard_len, 1),
        ).astype(low)
        turned = jnp.concatenate(
            [
                turned[:, :GROUP] * jnp.asarray(attn_mult, low),
                turned[:, GROUP:],
                projected[:, GROUP + 1 :].astype(low),
            ],
            axis=1,
        )
        heads = lax.dynamic_update_index_in_dim(heads, turned, order[turn], 0)
        normed_one = lax.dynamic_update_slice_in_dim(normed_one, normed, start, 0)
        routes_all.append(block[shard_len : shard_len + top_count + 1, :shard_len])
        if turn < n - 1:
            if turn == 0:
                right, left, expert_weights = tie(right, left, expert_weights)
            else:
                right, left, heads, normed_one = tie(right, left, heads, normed_one)
            rights.append(right)
            lefts.append(left)
            block = arrived(rights, lefts, turn + 1)

    w_gate, w_up, w_down = expert_weights
    hidden_w = w_gate.shape[2]
    down_chunks = [
        w_down[:, :, start : start + hidden_w] for start in range(0, width, hidden_w)
    ]
    weights = lax.all_gather(
        jnp.concatenate([w_gate, w_up, jnp.concatenate(down_chunks, axis=1)], axis=2),
        "fsdp",
        axis=1,
        tiled=True,
    )

    routes_all = jnp.stack(routes_all).astype(jnp.int32)
    valid_count = total(jnp.sum(routes_all[:, top_count]).astype(full).reshape(1, 1), "fsdp")[0, 0]
    expert_ids = jnp.arange(expert_total, dtype=jnp.int32)
    member = jnp.any(routes_all[:, :top_count, None, :] == expert_ids[:, None], axis=1)
    own_member = lax.dynamic_slice_in_dim(member, me * experts_here, experts_here, 1)
    earlier = jnp.arange(shard_len)[:, None] < jnp.arange(shard_len)[None, :]
    slot_of = dot("net,tu->neu", own_member.astype(low), earlier.astype(low)).astype(jnp.int32)
    slot_of = jnp.where(own_member, slot_of, -1)
    member = member.astype(full)

    key = jnp.moveaxis(heads[:, :, GROUP], 0, 2).reshape(kv_here, HEAD_DIM, seq_len)
    value = jnp.moveaxis(heads[:, :, GROUP + 1], 0, 2).reshape(kv_here, HEAD_DIM, seq_len)
    key_rows = jnp.swapaxes(key, 1, 2)
    value_rows = jnp.swapaxes(value, 1, 2)
    attended, out_heads, lse = attention_forward(heads, key_rows, value, limit)
    moved = exchange(attended)
    moved, slot_of, member, own_router = tie(moved, slot_of, member, own_router)
    attn_rows = by_place(nearest(*moved)).reshape(HEADS * HEAD_DIM, shard_len)
    projected = dot("kt,kd->td", attn_rows, full_out)
    hidden = x_low.astype(full) + resid_mult * projected
    normed_two, norm_two_pull = jax.vjp(rms_norm, hidden, full_g2)

    tokens = [normed_two.astype(low)]
    rights, lefts = [tokens[0]], [tokens[0]]
    buffers, gates = [], []
    for turn in range(n):
        if turn < n - 1:
            right, left = line_move(rights[turn], lefts[turn], turn + 1)
        *buffers, shard_gates = experts_forward(
            turn, n, jnp.stack([order[turn], me]), tokens[turn], slot_of[turn], member[turn],
            router, weights, w_down.shape[1], slots, buffers,
        )
        if turn < n - 1:
            right, left, shard_gates = tie(right, left, shard_gates)
            rights.append(right)
            lefts.append(left)
            tokens.append(arrived(rights, lefts, turn + 1))
        gates.append(shard_gates)
    mix_parts, expert_in, gate_up = buffers
    right = left = None
    for k in range(n - 1, 0, -1):
        moving = tie(*line_send(mix_parts, k, right, left))
        right, left = tie(*line_pass(*moving, k))
    mixture = line_end(mix_parts, right, left)
    output_f32 = hidden + resid_mult * mixture
    activations = output_f32.astype(low).reshape(1, shard_len, width)
    error_rows = output_f32 - teacher.astype(full).reshape(shard_len, width)
    weighted = valid_rows[:, None] * error_rows
    loss_steps = total_steps(jnp.sum(weighted * error_rows).reshape(1, 1), "seq", "fsdp")
    squares = next(loss_steps)
    d_out = weighted * (tokens_all / valid_count)

    d_mix = resid_mult * d_out
    d_tokens = d_mix.astype(low)
    mix_dot = jnp.sum(d_mix * mixture, axis=1)[None]
    rights, lefts = [d_tokens], [d_tokens]
    dot_rights, dot_lefts = [mix_dot], [mix_dot]
    buffers, d_logits = [], []
    for turn in range(n):
        if turn < n - 1:
            dot_right, dot_left = line_move(dot_rights[turn], dot_lefts[turn], turn + 1)
            right, left = line_move(rights[turn], lefts[turn], turn + 1)
        *buffers, shard_logits = experts_backward(
            turn, n, jnp.stack([order[turn], me]), d_tokens, slot_of[turn], gates[turn], mix_dot,
            own_router, gate_up, weights, w_down.shape[1], buffers,
        )
        if turn < n - 1:
            right, left, dot_right, dot_left, shard_logits, squares = tie(
                right, left, dot_right, dot_left, shard_logits, squares
            )
            squares = loss_steps.send(squares)
            rights.append(right)
            lefts.append(left)
            dot_rights.append(dot_right)
            dot_lefts.append(dot_left)
            d_tokens = arrived(rights, lefts, turn + 1)
            mix_dot = arrived(dot_rights, dot_lefts, turn + 1)
        d_logits.append(shard_logits)
    d_parts, d_rows, d_gate_up, act_low = buffers
    expert_in = expert_in.reshape(experts_here, slot_rows, width)
    d_rows = d_rows.reshape(experts_here, slot_rows, width)
    d_gate_up = d_gate_up.reshape(experts_here, slot_rows, -1)
    act_low = act_low.reshape(experts_here, slot_rows, -1)

    right = left = None
    cut = (experts_here + 1) // 2
    grads = []
    for k in range(n - 1, 0, -1):
        moving = line_send(d_parts, k, right, left)
        if k >= n - 2:
            moving, d_rows = tie(moving, d_rows)
            right, left = line_pass(*moving, k)
            part = (0, cut) if k == n - 1 else (cut, experts_here)
            grads = [
                weight_grads(expert_in, d_gate_up, act_low, d_rows, w_down.shape[1], *part, grads)
            ]
            right, left, grads, squares = tie(right, left, grads, squares)
        else:
            right, left, squares = tie(*line_pass(*tie(*moving), k), squares)
        squares = loss_steps.send(squares)
    expert_sum = lax.psum_scatter(grads[0], "fsdp", scatter_dimension=1, tiled=True)
    d_normed_two = line_end(d_parts, right, left)

    d_hidden_norm, gain_two_part = norm_two_pull(d_normed_two)
    d_hidden = d_out + d_hidden_norm
    d_proj = (resid_mult * d_hidden).astype(low)
    out_part = dot("kt,td->kd", attn_rows, d_proj).astype(low)
    middle = width // 2
    out_sums = [
        rows_halving(out_part[:, :middle], order_a),
        rows_halving(out_part[:, middle:], order_b),
    ]
    d_attended = dot("kd,td->kt", full_out, d_proj).astype(low)
    d_attended, _ = tie(d_attended, [each.send for each in out_sums])
    moved = exchange(d_attended.reshape(n, heads_w, shard_len))
    for each in out_sums:
        each.go()
        each.add()
    router_part = sum(
        dot("td,et->de", shard, shard_logits[:experts_here])
        for shard, shard_logits in zip(tokens, d_logits)
    )
    moved, router_part = leave(out_sums, moved, router_part)
    for each in out_sums:
        each.go()
    d_heads = by_place(nearest(*moved))
    query_grad, key_grad, value_grad = attention_backward(
        heads, key_rows, value_rows, key, limit, out_heads, lse, d_heads
    )
    ((query_grad, key_grad, value_grad),) = land(out_sums, (query_grad, key_grad, value_grad))
    for each in out_sums:
        each.add()
        each.go()
    d_turned = jnp.concatenate([query_grad, key_grad[:, None]], axis=1).astype(full)
    d_turned = rotate(d_turned, cosine, -sine_vals).astype(low)
    d_qkv = jnp.concatenate([d_turned, value_grad[:, None]], axis=1).reshape(group_w, seq_len)
    d_parts = dot("ct,dc->td", d_qkv, full_qkv).astype(low).reshape(n, shard_len, width)
    own_columns = jnp.zeros((width, expert_total), full)
    own_columns = lax.dynamic_update_slice_in_dim(own_columns, router_part, me * experts_here, 1)
    (d_parts,) = land(out_sums, d_parts)
    for each in out_sums:
        each.add()

    out_sum = jnp.concatenate([each.finish() for each in out_sums], axis=1).astype(low)
    out_rows = out_sum.shape[0] // n
    out_parts = jnp.swapaxes(out_sum.reshape(out_sum.shape[0], n, width // n), 0, 1)
    d_parts = jnp.concatenate([d_parts, out_parts.reshape(n, out_rows, width)], axis=1)
    right = left = None
    for k in range(n - 1, 0, -1):
        moving = tie(*line_send(d_parts, k, right, left))
        if k == n - 1:
            moving, d_qkv = tie(moving, d_qkv)
        right, left = line_pass(*moving, k)
        if k == n - 1:
            qkv_part = jnp.concatenate(
                [dot("td,ct->dc", normed_one, d_qkv), own_columns, gain_two_part[:, None]], axis=1
            ).astype(low)
            qkv_sum = rows_halving(qkv_part, order_a)
            right, left = leave([qkv_sum], right, left)
            qkv_sum.go()
        elif k in (n - 2, n - 3):
            right, left = land([qkv_sum], right, left)
            qkv_sum.add()
            qkv_sum.go()
        else:
            right, left = tie(right, left)
    ended = line_end(d_parts, right, left)
    d_normed_one = ended[:shard_len]
    (ended,) = land([qkv_sum], ended)
    qkv_sum.add()
    out_own = ended[shard_len:].reshape(out_sum.shape[0], width // n)
    blocks = line_gather(jnp.concatenate([qkv_sum.finish(), out_own], axis=1).astype(low))
    _, norm_one_pull = jax.vjp(lambda v: rms_norm(v, full_g1), x_low.astype(full))
    input_grad = (d_hidden + norm_one_pull(d_normed_one)[0]).reshape(1, shard_len, width)
    input_grad, expert_sum = tie(input_grad, expert_sum)
    expert_sum = expert_sum.astype(full)
    gate_grad = expert_sum[:, :, :hidden_w]
    up_grad = expert_sum[:, :, hidden_w : 2 * hidden_w]
    few = w_down.shape[1]
    down_grad = jnp.concatenate(
        [
            expert_sum[:, start : start + few, 2 * hidden_w :]
            for start in range(0, expert_sum.shape[1], few)
        ],
        axis=2,
    )
    qkv_grad = jnp.zeros((w_qkv.shape[0], QKV_W), full)
    out_grad = jnp.zeros((w_out.shape[0], width), full)
    rest = 0.0
    for k, block in enumerate(blocks):
        block = block.astype(full)
        place = (me - k) % n
        qkv_grad = lax.dynamic_update_slice_in_dim(
            qkv_grad, block[:, :group_w], place * group_w, 1
        )
        out_grad = lax.dynamic_update_slice_in_dim(
            out_grad, block[:, -(width // n) :], place * (width // n), 1
        )
        rest = rest + block[:, group_w : -(width // n)]
    router_grad, gain_two_grad = rest[:, :expert_total], rest[:, expert_total]
    gain_one_grad = jnp.sum(qkv_grad * w_qkv.astype(full), axis=1) / gain_one.astype(full)
    for _ in range(2):
        squares = loss_steps.send(squares)
    loss_value = squares[0, 0] / (valid_count * width)
    return (
        activations,
        loss_value,
        input_grad,
        gain_one_grad,
        qkv_grad,
        out_grad,
        gain_two_grad,
        router_grad,
        gate_grad,
        up_grad,
        down_grad,
    )


def solution(mesh):
    return jax.shard_map(
        shards,
        mesh=mesh,
        in_specs=(
            P("fsdp", "seq", None),
            P("fsdp", "seq", None),
            P("fsdp", "seq", None),
            P("fsdp", "seq"),
            P("fsdp", None),
            P("fsdp"),
            P("fsdp", None),
            P("fsdp", None),
            P("fsdp"),
            P("fsdp", None),
            P("seq", "fsdp", None),
            P("seq", "fsdp", None),
            P("seq", "fsdp", None),
        ),
        out_specs=(
            P("fsdp", "seq", None),
            P(),
            P("fsdp", "seq", None),
            P("fsdp"),
            P("fsdp", None),
            P("fsdp", None),
            P("fsdp"),
            P("fsdp", None),
            P("seq", "fsdp", None),
            P("seq", "fsdp", None),
            P("seq", "fsdp", None),
        ),
        check_vma=False,
    )
```

```python
import functools

import jax
import jax.numpy as jnp
from jax import lax
from jax.experimental import pallas as pl
from jax.experimental.pallas import tpu as pltpu
from jax.sharding import PartitionSpec as P

HEADS = 24
KV_HEADS = 8
HEAD_DIM = 64
BLOCK = 256
GROUP = 3
QKV_W = 2560


epsilon = 1e-06
attn_mult = 0.015625
resid_mult = 0.22
rope_base = 10000.0
masked_score = -1e30

low = jnp.bfloat16
full = jnp.float32


def dot(spec, left, right):
    return jnp.einsum(spec, left, right, preferred_element_type=full)


def rms_norm(values, gain_vec):
    inv_rms = lax.rsqrt(jnp.mean(values * values, axis=-1, keepdims=True) + epsilon)
    return values * inv_rms * gain_vec


def rope_tables(positions, head_dim):
    half_dim = head_dim // 2
    frequency = rope_base ** (-(2.0 * jnp.arange(half_dim, dtype=full)) / head_dim)
    angles = frequency[:, None] * positions[None, :]
    return (jnp.cos(angles), jnp.sin(angles))


def rotate(values, cosine, sine_vals):
    half_dim = values.shape[-2] // 2
    front_half = values[..., :half_dim, :]
    back_half = values[..., half_dim:, :]
    return jnp.concatenate(
        [front_half * cosine - back_half * sine_vals, back_half * cosine + front_half * sine_vals],
        axis=-2,
    )


def block_limits(lengths_row, positions):
    block_ends = jnp.cumsum(lengths_row)
    open_ends = jnp.where(block_ends[None, :] > positions[:, None], block_ends[None, :], positions.shape[0])
    return jnp.min(open_ends, axis=1).astype(jnp.int32)


def tie(*groups):
    return lax.optimization_barrier(groups)


def line_move(right, left, k):
    n = lax.axis_size("seq")
    return (
        lax.ppermute(right, "seq", [(i, i + 1) for i in range(k - 1, n - 1)]),
        lax.ppermute(left, "seq", [(i, i - 1) for i in range(1, n - k + 1)]),
    )


def line_gather(block):
    n = lax.axis_size("seq")
    rights, lefts = [block], [block]
    for k in range(1, n):
        right, left = tie(*line_move(rights[-1], lefts[-1], k))
        rights.append(right)
        lefts.append(left)
    return nearest(rights, lefts)


def nearest(rights, lefts):
    n = lax.axis_size("seq")
    me = lax.axis_index("seq")
    return [rights[0]] + [jnp.where(me >= k, rights[k], lefts[n - k]) for k in range(1, n)]


def arrival_order(n):
    order = []
    for me in range(n):
        both = min(me, n - 1 - me)
        places = [me]
        for k in range(1, n):
            places += [me - k] if me >= k and (k <= both or me > n - 1 - me) else []
            places += [me + k] if me + k < n and (k <= both or me < n - 1 - me) else []
        order.append(places)
    return order


def arrived(rights, lefts, turn):
    n = lax.axis_size("seq")
    me = lax.axis_index("seq")
    sources = {}
    for dev, places in enumerate(arrival_order(n)):
        gap = dev - places[turn]
        sources.setdefault(gap, []).append(dev)
    block = None
    for gap, devs in sources.items():
        moved = rights[gap] if gap >= 0 else lefts[-gap]
        if block is None:
            block = moved
        else:
            mine = jnp.array([dev in devs for dev in range(n)])[me]
            block = jnp.where(mine, moved, block)
    return block


def at_place(placed, place):
    return lax.dynamic_index_in_dim(placed, place % lax.axis_size("seq"), 0, keepdims=False)


def line_send(parts, k, right, left):
    me = lax.axis_index("seq")
    to_right, to_left = at_place(parts, me + k), at_place(parts, me - k)
    if right is not None:
        to_right = (to_right.astype(full) + right.astype(full)).astype(low)
        to_left = (to_left.astype(full) + left.astype(full)).astype(low)
    return to_right, to_left


def line_pass(to_right, to_left, k):
    n = lax.axis_size("seq")
    return (
        lax.ppermute(to_right, "seq", [(i, i + 1) for i in range(n - k)]),
        lax.ppermute(to_left, "seq", [(i, i - 1) for i in range(k, n)]),
    )


class LineGather:
    def __init__(self, halves):
        self.rights, self.lefts = [[half] for half in halves], [[half] for half in halves]

    def go(self, h):
        step = len(self.rights[h])
        right, left = line_move(self.rights[h][-1], self.lefts[h][-1], step)
        self.rights[h].append(right)
        self.lefts[h].append(left)

    def land(self, h, other):
        spot = len(self.rights[h]) - 1
        moved = [(self.rights[part][spot], self.lefts[part][spot]) for part in range(h + 1)]
        moved, other = tie(moved, other)
        for part, (right, left) in enumerate(moved):
            self.rights[part][spot], self.lefts[part][spot] = right, left
        return other

    def block(self, turn):
        return [arrived(self.rights[h], self.lefts[h], turn) for h in (0, 1)]


def line_scatter(parts, work):
    n = lax.axis_size("seq")
    me = lax.axis_index("seq")
    middle = parts.shape[1] // 32 * 16
    halves = [parts[:, :middle], parts[:, middle:]]
    flying = [(None, None), (None, None)]
    before, given = (), []
    for k in range(n - 1, 0, -1):
        for h in (0, 1):
            if k < n - 1 and h:
                flying[h], before = tie(flying[h], before)
            elif k < n - 1:
                flying[h], given = tie(flying[h], given)
            before = line_send(halves[h], k, *flying[h])
            flying[h] = line_pass(*before, k)
        if n - 1 - k < len(work):
            given = work[n - 1 - k](before, given)
    sums = []
    flying[0], given = tie(flying[0], given)
    for h in (0, 1):
        own = at_place(halves[h], me).astype(full)
        sums.append(own + (flying[h][0].astype(full) + flying[h][1].astype(full)))
    return jnp.concatenate(sums), given


def by_place(blocks):
    n = lax.axis_size("seq")
    me = lax.axis_index("seq")
    placed = jnp.zeros((n,) + blocks[0].shape, blocks[0].dtype)
    for k, block in enumerate(blocks):
        placed = lax.dynamic_update_index_in_dim(placed, block, (me - k) % n, 0)
    return placed


def exchange(blocks):
    n = lax.axis_size("seq")
    me = lax.axis_index("seq")
    own = at_place(blocks, me)
    rights, lefts = [own] * n, [own] * n
    for k in range(n - 1, 0, -1):
        to_right, to_left = at_place(blocks, me + k), at_place(blocks, me - k)
        rights[k] = lax.ppermute(to_right, "seq", [(i, i + k) for i in range(n - k)])
        lefts[k] = lax.ppermute(to_left, "seq", [(i, i - k) for i in range(k, n)])
    return rights, lefts


def swap(value, axis, bit):
    return lax.ppermute(value, axis, [(i, i ^ bit) for i in range(lax.axis_size(axis))])


def total(value, *axes):
    for axis in axes:
        for step in range(lax.axis_size(axis).bit_length() - 1):
            value = value + swap(value, axis, 1 << step)
    return value


def fsdp_bits():
    bits = [1 << step for step in range(lax.axis_size("fsdp").bit_length() - 1)]
    return tuple(bits), tuple(bits[:1] + bits[:0:-1])


def total_steps(value, *axes):
    for axis in axes:
        for step in range(lax.axis_size(axis).bit_length() - 1):
            here = swap(value, axis, 1 << step)
            here = yield here
            value = value + here
    while True:
        yield value


class Halving:
    def __init__(self, keep, send, bits):
        self.terms, self.send, self.bits = [keep], send, list(bits)

    def go(self):
        self.terms = self.terms + [swap(self.send, "fsdp", self.bits.pop(0))]

    def add(self):
        half = self.terms[0].shape[0] // 2
        if half:
            self.send = sum(term[half:].astype(full) for term in self.terms).astype(low)
            self.terms = [term[:half] for term in self.terms]

    def finish(self):
        while self.bits:
            self.go()
            self.add()
        return sum(term[0].astype(full) for term in self.terms)


def rows_halving(part, bits):
    devs = lax.axis_size("fsdp")
    order = lax.axis_index("fsdp") ^ jnp.array(halving_masks(bits), jnp.int32)
    blocks = part.reshape(devs, part.shape[0] // devs, part.shape[1])[order]
    return Halving(blocks[: devs // 2], blocks[devs // 2 :], bits)


def land(sums, *others):
    tied = tie([each.terms[-1] for each in sums], *others)
    for each, here in zip(sums, tied[0]):
        each.terms = each.terms[:-1] + [here]
    return tied[1:]


def leave(sums, *others):
    tied = tie([each.send for each in sums], *others)
    for each, send in zip(sums, tied[0]):
        each.send = send
    return tied[1:]


def nt(a, b):
    return lax.dot_general(a, b, (((1,), (1,)), ((), ())), preferred_element_type=full)

def nn(a, b):
    return lax.dot_general(a, b, (((1,), (0,)), ((), ())), preferred_element_type=full)

def tn(a, b):
    return lax.dot_general(a, b, (((0,), (0,)), ((), ())), preferred_element_type=full)


def beside(rows):
    return jnp.concatenate([rows[h] for h in range(GROUP)], axis=1)

def key_steps(i, seq_len, query_rows, key_rows):
    free = (i * query_rows) // key_rows
    need = ((i + 1) * query_rows + BLOCK - 1 + key_rows - 1) // key_rows
    return free, jnp.minimum(need, seq_len // key_rows)

def forward_kernel(seq_len, query_rows, key_rows, limit_ref, q_ref, k_ref, vt_ref, low_ref, out_ref, lse_ref):
    i = pl.program_id(1)
    qt = beside(q_ref[0, 0])
    width = GROUP * query_rows
    limit = jnp.concatenate([limit_ref[...]] * GROUP, axis=1)

    def step(masked, j, carry):
        peak, total, acc = carry
        start = pl.multiple_of(j * key_rows, key_rows)
        s = nn(k_ref[0, pl.ds(start, key_rows), :], qt)
        if masked:
            place = start + lax.broadcasted_iota(jnp.int32, (key_rows, 1), 0)
            s = jnp.where(place < limit, s, masked_score)
        new_peak = jnp.maximum(peak, jnp.max(s, axis=0, keepdims=True))
        shrink = jnp.exp(peak - new_peak)
        p = jnp.exp(s - new_peak)
        total = shrink * total + jnp.sum(p, axis=0, keepdims=True)
        acc = shrink * acc + nn(vt_ref[0, :, pl.ds(start, key_rows)], p.astype(low))
        return new_peak, total, acc

    free, need = key_steps(i, seq_len, query_rows, key_rows)
    carry = (
        jnp.full((1, width), masked_score, full),
        jnp.zeros((1, width), full),
        jnp.zeros((HEAD_DIM, width), full),
    )
    carry = lax.fori_loop(0, free, lambda j, c: step(False, j, c), carry)
    peak, total, acc = lax.fori_loop(free, need, lambda j, c: step(True, j, c), carry)
    out = acc / total
    lse = peak + jnp.log(total)
    for h in range(GROUP):
        cols = slice(h * query_rows, (h + 1) * query_rows)
        out_ref[0, h] = out[:, cols]
        low_ref[0, pl.ds(h * HEAD_DIM, HEAD_DIM), :] = out[:, cols].astype(low)
        lse_ref[0, h] = lse[:, cols]

def query_spec(query_rows, per):
    return pl.BlockSpec(
        (1, 1, GROUP, HEAD_DIM, query_rows), lambda g, i: (i // per, g, 0, 0, i % per)
    )


def attention_forward(heads, k_rows, vt, limit):
    kv_here, shard_len = heads.shape[1], heads.shape[4]
    seq_len = k_rows.shape[1]
    query_rows = min(256, shard_len)
    key_rows = min(512, seq_len)
    per = shard_len // query_rows
    return pl.pallas_call(
        functools.partial(forward_kernel, seq_len, query_rows, key_rows),
        grid=(kv_here, seq_len // query_rows),
        in_specs=[
            pl.BlockSpec((1, query_rows), lambda g, i: (0, i)),
            query_spec(query_rows, per),
            pl.BlockSpec((1, seq_len, HEAD_DIM), lambda g, i: (g, 0, 0)),
            pl.BlockSpec((1, HEAD_DIM, seq_len), lambda g, i: (g, 0, 0)),
        ],
        out_specs=[
            pl.BlockSpec((1, GROUP * HEAD_DIM, query_rows), lambda g, i: (i // per, g, i % per)),
            pl.BlockSpec((1, GROUP, HEAD_DIM, query_rows), lambda g, i: (g, 0, 0, i)),
            pl.BlockSpec((1, GROUP, 1, query_rows), lambda g, i: (g, 0, 0, i)),
        ],
        out_shape=[
            jax.ShapeDtypeStruct((seq_len // shard_len, kv_here * GROUP * HEAD_DIM, shard_len), low),
            jax.ShapeDtypeStruct((kv_here, GROUP, HEAD_DIM, seq_len), full),
            jax.ShapeDtypeStruct((kv_here, GROUP, 1, seq_len), full),
        ],
        compiler_params=vmem(40),
        name="attention_forward",
    )(limit, heads, k_rows, vt)

def backward_kernel(seq_len, query_rows, key_rows, limit_ref, q_ref, k_ref, v_ref, kt_ref, out_ref, lse_ref, dout_ref, dq_ref, dk_ref, dv_ref, dk_acc, dv_acc):
    i = pl.program_id(1)

    @pl.when(i == 0)
    def _():
        dk_acc[...] = jnp.zeros_like(dk_acc)
        dv_acc[...] = jnp.zeros_like(dv_acc)

    qt = beside(q_ref[0, 0])
    limit = jnp.concatenate([limit_ref[...]] * GROUP, axis=1)
    dout = jnp.concatenate([dout_ref[0, pl.ds(h * HEAD_DIM, HEAD_DIM), :] for h in range(GROUP)], axis=1)
    delta = jnp.sum(dout.astype(full) * beside(out_ref[0]), axis=0, keepdims=True)
    lse = beside(lse_ref[0])

    def step(masked, j, dq):
        start = pl.multiple_of(j * key_rows, key_rows)
        keys = pl.ds(start, key_rows)
        s = nn(k_ref[0, keys, :], qt)
        if masked:
            place = start + lax.broadcasted_iota(jnp.int32, (key_rows, 1), 0)
            s = jnp.where(place < limit, s, masked_score)
        p = jnp.exp(s - lse)
        dp = nn(v_ref[0, keys, :], dout)
        ds = (p * (dp - delta)).astype(low)
        dk_acc[:, keys] += nt(qt, ds)
        dv_acc[:, keys] += nt(dout, p.astype(low))
        return dq + nn(kt_ref[0, :, keys], ds)

    free, need = key_steps(i, seq_len, query_rows, key_rows)
    dq = jnp.zeros((HEAD_DIM, GROUP * query_rows), full)
    dq = lax.fori_loop(0, free, lambda j, c: step(False, j, c), dq)
    dq = lax.fori_loop(free, need, lambda j, c: step(True, j, c), dq) * attn_mult
    for h in range(GROUP):
        dq_ref[0, h] = dq[:, h * query_rows : (h + 1) * query_rows].astype(low)

    @pl.when(i == pl.num_programs(1) - 1)
    def _():
        dk_ref[0] = dk_acc[...].astype(low)
        dv_ref[0] = dv_acc[...].astype(low)

def attention_backward(heads, k_rows, v_rows, kt, limit, out, lse, d_out):
    kv_here, shard_len = heads.shape[1], heads.shape[4]
    seq_len = k_rows.shape[1]
    query_rows = min(256, shard_len)
    key_rows = min(512, seq_len)
    per = shard_len // query_rows
    quarter = lambda g, i: (g, 0, 0, i)
    whole = lambda g, i: (g, 0, 0)
    return pl.pallas_call(
        functools.partial(backward_kernel, seq_len, query_rows, key_rows),
        grid=(kv_here, seq_len // query_rows),
        in_specs=[
            pl.BlockSpec((1, query_rows), lambda g, i: (0, i)),
            query_spec(query_rows, per),
            pl.BlockSpec((1, seq_len, HEAD_DIM), whole),
            pl.BlockSpec((1, seq_len, HEAD_DIM), whole),
            pl.BlockSpec((1, HEAD_DIM, seq_len), whole),
            pl.BlockSpec((1, GROUP, HEAD_DIM, query_rows), quarter),
            pl.BlockSpec((1, GROUP, 1, query_rows), quarter),
            pl.BlockSpec((1, GROUP * HEAD_DIM, query_rows), lambda g, i: (i // per, g, i % per)),
        ],
        out_specs=[
            pl.BlockSpec((1, GROUP, HEAD_DIM, query_rows), quarter),
            pl.BlockSpec((1, HEAD_DIM, seq_len), whole),
            pl.BlockSpec((1, HEAD_DIM, seq_len), whole),
        ],
        out_shape=[
            jax.ShapeDtypeStruct((kv_here, GROUP, HEAD_DIM, seq_len), low),
            jax.ShapeDtypeStruct((kv_here, HEAD_DIM, seq_len), low),
            jax.ShapeDtypeStruct((kv_here, HEAD_DIM, seq_len), low),
        ],
        scratch_shapes=[pltpu.VMEM((HEAD_DIM, seq_len), full), pltpu.VMEM((HEAD_DIM, seq_len), full)],
        compiler_params=vmem(40),
        name="attention_backward",
    )(limit, heads, k_rows, v_rows, kt, out, lse, d_out)


def vmem(mib):
    return pltpu.CompilerParams(vmem_limit_bytes=mib * 2**20)


def own_row(ref, row):
    return ref[pl.ds(row, 1), :]


def join_down(rows, block_ref, down_ref):
    hidden, width = down_ref.shape
    chunks = width // hidden
    for dev in range(hidden // rows):
        for chunk in range(chunks):
            start = (dev * chunks + chunk) * rows
            down_ref[dev * rows : (dev + 1) * rows, chunk * hidden : (chunk + 1) * hidden] = (
                block_ref[0, start : start + rows, :]
            )


def pick_rows(pick, tok_ref, more_ref):
    middle = tok_ref.shape[0]
    return (nn(pick[:, :middle], tok_ref[...]) + nn(pick[:, middle:], more_ref[:middle, :])).astype(low)


def experts_kernel(
    few, at_ref, tok_ref, more_ref, slot_ref, member_ref, router_ref, wgu_ref, wd_ref, *refs
):
    part_ref, x_ref, gu_ref, gates_ref, acc, gates_all, down = refs[-7:]
    e, experts = pl.program_id(0), pl.num_programs(0)
    slots = x_ref.shape[2]

    @pl.when(e == 0)
    def _():
        member = member_ref[...] > 0
        logits = [nt(router_ref[...], ref[...]) for ref in (tok_ref, more_ref)]
        chosen = jnp.where(member, jnp.concatenate(logits, axis=1), masked_score)
        chosen = jnp.exp(chosen - jnp.max(chosen, axis=0, keepdims=True))
        chosen = jnp.where(member, chosen, 0.0)
        gates_all[...] = chosen / jnp.sum(chosen, axis=0, keepdims=True)
        acc[...] = jnp.zeros_like(acc)

    gate_row = own_row(gates_all, at_ref[1] * experts + e)
    gates_ref[pl.ds(e, 1), :] = gate_row
    place = lax.broadcasted_iota(jnp.int32, (slots, 1), 0)
    here = place == own_row(slot_ref, e)
    x = pick_rows(jnp.where(here, 1.0, 0.0).astype(low), tok_ref, more_ref)
    x_ref[0, 0] = x
    gu = nn(x, wgu_ref[0])
    gu_ref[0, 0] = gu.astype(low)
    hidden = gu.shape[1] // 2
    g, u = gu[:, :hidden], gu[:, hidden:]
    act = (g * jax.nn.sigmoid(g) * u).astype(low)
    join_down(few, wd_ref, down)
    y = nn(act, down[...]).astype(low)
    acc[...] += tn(jnp.where(here, gate_row, 0.0).astype(low), y)

    @pl.when(e == experts - 1)
    def _():
        part_ref[0] = acc[...].astype(low)


def back_kernel(
    few, at_ref, tok_ref, more_ref, slot_ref, gates_ref, mix_ref, router_ref, gu_ref, wgu_ref, wd_ref, *refs
):
    part_ref, d_ref, dgu_ref, act_ref, dlog_ref, acc, dlog_all, down = refs[-8:]
    e, experts = pl.program_id(0), pl.num_programs(0)
    slots, hidden = gu_ref.shape[2], gu_ref.shape[3] // 2

    @pl.when(e == 0)
    def _():
        dlog_all[...] = jnp.zeros_like(dlog_all)
        acc[...] = jnp.zeros_like(acc)

    place = lax.broadcasted_iota(jnp.int32, (slots, 1), 0)
    here = place == own_row(slot_ref, e)
    pick = jnp.where(here, 1.0, 0.0).astype(low)
    gate_row = own_row(gates_ref, e)
    gate = jnp.sum(jnp.where(here, gate_row, 0.0), axis=1, keepdims=True)
    d = pick_rows(pick, tok_ref, more_ref)
    d_ref[0, 0] = d
    join_down(few, wd_ref, down)
    d_act = nt(d, down[...])
    g, u = gu_ref[0, 0, :, :hidden].astype(full), gu_ref[0, 0, :, hidden:].astype(full)
    sig = jax.nn.sigmoid(g)
    silu = g * sig
    act = silu * u
    d_gate = jnp.sum(d_act * act, axis=1, keepdims=True)
    d_gate = jnp.sum(jnp.where(here, d_gate, 0.0), axis=0, keepdims=True)
    dlog_all[pl.ds(e, 1), :] = gate_row * (d_gate - mix_ref[...])
    act_ref[0, 0] = (act * gate).astype(low)
    d_act = d_act * gate
    d_g = (d_act * u * (sig + silu * (1.0 - sig))).astype(low)
    d_u = (d_act * silu).astype(low)
    dgu_ref[0, 0, :, :hidden] = d_g
    dgu_ref[0, 0, :, hidden:] = d_u
    dx = nt(dgu_ref[0, 0], wgu_ref[0]).astype(low)
    acc[...] += tn(pick, dx)

    @pl.when(e == experts - 1)
    def _():
        dlog = dlog_all[...].astype(low)
        dlog_ref[...] = dlog
        part_ref[0] = (acc[...] + tn(dlog, router_ref[...])).astype(low)


def by_expert(*shape):
    return pl.BlockSpec((1,) + shape, lambda e, at: (e, 0, 0))


def in_turn(turn, *shape):
    return pl.BlockSpec((1, 1) + shape, lambda e, at: (e, turn, 0, 0))


def same(*shape):
    return pl.BlockSpec(shape, lambda e, at: (0, 0))


def in_place(*shape):
    return pl.BlockSpec((1,) + shape, lambda e, at: (at[0], 0, 0))


def shard_call(kernel, name, at, inputs, in_specs, out_specs, out_shape, buffers, scratch, experts):
    first = len(inputs) + 1
    aliases = {first + i: i for i in range(len(buffers))}
    return pl.pallas_call(
        kernel,
        grid_spec=pltpu.PrefetchScalarGridSpec(
            num_scalar_prefetch=1,
            grid=(experts,),
            in_specs=in_specs + [pl.BlockSpec(memory_space=pl.ANY)] * len(buffers),
            out_specs=out_specs,
            scratch_shapes=scratch,
        ),
        out_shape=out_shape,
        input_output_aliases=aliases,
        compiler_params=vmem(48),
        name=name,
    )(at, *inputs, *buffers)


def weight_specs(width, hidden):
    return [
        pl.BlockSpec((1, width, 2 * hidden), lambda e, at: (e, 0, 0)),
        pl.BlockSpec((1, width, hidden), lambda e, at: (e, 0, 2)),
    ]


def experts_forward(turn, devs, at, tokens, slot_of, member, router, weights, few, slots, buffers):
    experts, width, columns = weights.shape
    hidden = columns // 3
    count = 2 * tokens[0].shape[0]
    total_experts = member.shape[0]
    return shard_call(
        functools.partial(experts_kernel, few),
        "experts_forward",
        at,
        [*tokens, slot_of, member, router, weights, weights],
        [
            *(same(*half.shape) for half in tokens),
            same(experts, count),
            same(total_experts, count),
            same(total_experts, width),
            *weight_specs(width, hidden),
        ],
        [
            in_place(count, width),
            in_turn(turn, slots, width),
            in_turn(turn, slots, 2 * hidden),
            same(experts, count),
        ],
        [
            jax.ShapeDtypeStruct((devs, count, width), low),
            jax.ShapeDtypeStruct((experts, devs, slots, width), low),
            jax.ShapeDtypeStruct((experts, devs, slots, 2 * hidden), low),
            jax.ShapeDtypeStruct((experts, count), full),
        ],
        buffers,
        [
            pltpu.VMEM((count, width), full),
            pltpu.VMEM((total_experts, count), full),
            pltpu.VMEM((hidden, width), low),
        ],
        experts,
    )


def experts_backward(
    turn, devs, at, d_tokens, slot_of, gates, mix_dot, router, gu, weights, few, buffers
):
    experts, width, columns = weights.shape
    hidden = columns // 3
    count = 2 * d_tokens[0].shape[0]
    slots = gu.shape[2]
    lines = router.shape[0]
    return shard_call(
        functools.partial(back_kernel, few),
        "experts_backward",
        at,
        [*d_tokens, slot_of, gates, mix_dot, router, gu, weights, weights],
        [
            *(same(*half.shape) for half in d_tokens),
            same(experts, count),
            same(experts, count),
            same(1, count),
            same(lines, width),
            in_turn(turn, slots, 2 * hidden),
            *weight_specs(width, hidden),
        ],
        [
            in_place(count, width),
            in_turn(turn, slots, width),
            in_turn(turn, slots, 2 * hidden),
            in_turn(turn, slots, hidden),
            same(lines, count),
        ],
        [
            jax.ShapeDtypeStruct((devs, count, width), low),
            jax.ShapeDtypeStruct((experts, devs, slots, width), low),
            jax.ShapeDtypeStruct((experts, devs, slots, 2 * hidden), low),
            jax.ShapeDtypeStruct((experts, devs, slots, hidden), low),
            jax.ShapeDtypeStruct((lines, count), low),
        ],
        buffers,
        [
            pltpu.VMEM((count, width), full),
            pltpu.VMEM((lines, count), full),
            pltpu.VMEM((hidden, width), low),
        ],
        experts,
    )


def halving_masks(bits):
    masks = [0]
    for bit in reversed(bits):
        masks = masks + [mask ^ bit for mask in masks]
    return masks


def out_kernel(bits_a, bits_b, me_ref, rows_ref, d_ref, *refs):
    outs, acc = refs[:4], refs[4]
    half = outs[0].shape[2]
    for part, bits in enumerate((bits_a, bits_b)):
        keep, send = outs[2 * part], outs[2 * part + 1]
        rows = keep.shape[1]
        acc[...] = nn(rows_ref[...], d_ref[:, part * half : (part + 1) * half])
        for place, mask in enumerate(halving_masks(bits)):
            out = keep if place < keep.shape[0] else send
            start = pl.multiple_of((me_ref[0] ^ mask) * rows, rows)
            out[place % keep.shape[0]] = acc[pl.ds(start, rows), :].astype(low)


def out_grads(me, rows, d_proj, bits_a, bits_b):
    (height, count), width = rows.shape, d_proj.shape[1]
    devs = 2 ** len(bits_a)
    shape = (devs // 2, height // devs, width // 2)
    outs = pl.pallas_call(
        functools.partial(out_kernel, bits_a, bits_b),
        grid_spec=pltpu.PrefetchScalarGridSpec(
            num_scalar_prefetch=1,
            grid=(1,),
            in_specs=[same(height, count), same(count, width)],
            out_specs=[pl.BlockSpec(shape, lambda e, me: (0, 0, 0))] * 4,
            scratch_shapes=[pltpu.VMEM((height, width // 2), full)],
        ),
        out_shape=[jax.ShapeDtypeStruct(shape, low)] * 4,
        compiler_params=vmem(48),
        name="out_grads",
    )(me, rows, d_proj)
    return (outs[0], outs[1]), (outs[2], outs[3])


def grads_kernel(few, x_ref, dgu_ref, act_ref, d_ref, *refs):
    out_ref, down = refs[-2], refs[-1]
    hidden, width = down.shape
    out_ref[0, :, : 2 * hidden] = tn(x_ref[0], dgu_ref[0]).astype(low)
    down[...] = tn(act_ref[0], d_ref[0]).astype(low)
    chunks = width // hidden
    for dev in range(hidden // few):
        for chunk in range(chunks):
            start = (dev * chunks + chunk) * few
            out_ref[0, start : start + few, 2 * hidden :] = down[
                dev * few : (dev + 1) * few, chunk * hidden : (chunk + 1) * hidden
            ]


def weight_grads(rows, d_gu, act, d_rows, few, first, stop, buffers):
    experts, count, width = rows.shape
    hidden = act.shape[2]

    def part(*block):
        return pl.BlockSpec((1,) + block, lambda e: (first + e, 0, 0))

    return pl.pallas_call(
        functools.partial(grads_kernel, few),
        grid=(stop - first,),
        in_specs=[part(count, width), part(count, 2 * hidden), part(count, hidden), part(count, width)]
        + [pl.BlockSpec(memory_space=pl.ANY)] * len(buffers),
        out_specs=part(width, 3 * hidden),
        out_shape=jax.ShapeDtypeStruct((experts, width, 3 * hidden), low),
        scratch_shapes=[pltpu.VMEM((hidden, width), low)],
        input_output_aliases={4 + i: i for i in range(len(buffers))},
        compiler_params=vmem(56),
        name="weight_grads",
    )(rows, d_gu, act, d_rows, *buffers)


def shards(
    inputs,
    teacher,
    routes,
    valid_mask,
    block_lengths,
    gain_one,
    w_qkv,
    w_out,
    gain_two,
    w_router,
    w_gate,
    w_up,
    w_down,
):
    n = lax.axis_size("seq")
    me = lax.axis_index("seq")
    mine = lax.axis_index("fsdp")
    seqs_here, shard_len, width = inputs.shape
    assert seqs_here == 1
    seq_len = shard_len * n
    tokens_all = lax.axis_size("fsdp") * seq_len
    kv_here = KV_HEADS // n
    heads_w = kv_here * GROUP * HEAD_DIM
    group_w = kv_here * (GROUP + 2) * HEAD_DIM
    experts_here = w_gate.shape[0]
    expert_total = experts_here * n
    top_count = routes.shape[2]
    capacity = 3 * shard_len * top_count // (2 * expert_total)
    slots = -(-capacity // 16) * 16
    slot_rows = n * slots
    order_a, order_b = fsdp_bits()
    order = jnp.array(arrival_order(n), jnp.int32)[me]
    x_low = inputs.reshape(shard_len, width)

    own_qkv = lax.dynamic_slice_in_dim(w_qkv, me * group_w, group_w, 1)
    small = jnp.concatenate([gain_one[:, None], gain_two[:, None], w_router], axis=1)
    small = jnp.pad(small, ((0, 0), (0, -small.shape[1] % 128)))
    first = lax.all_gather(
        jnp.concatenate([own_qkv, small, w_out], axis=1), "fsdp", axis=0, tiled=True
    )
    full_qkv = first[:, :group_w]
    small = first[:, group_w : group_w + 2 + expert_total]
    full_out = first[:, -width:]
    full_g1 = small[:, 0].astype(full)
    full_g2 = small[:, 1].astype(full)
    router = small[:, 2:].T
    own_router = lax.dynamic_slice_in_dim(router, me * experts_here, experts_here, 0)
    own_router = jnp.pad(own_router, ((0, -experts_here % 16), (0, 0)))
    valid_rows = valid_mask.reshape(shard_len).astype(full)

    routes_low = jnp.concatenate([routes.reshape(shard_len, top_count).T, valid_mask], axis=0)
    routes_low = jnp.pad(
        routes_low.astype(low), ((0, -routes_low.shape[0] % 16), (0, width - shard_len))
    )
    middle = shard_len // 2
    halves = (x_low[:middle], jnp.concatenate([x_low[middle:], routes_low], axis=0))
    positions = jnp.arange(seq_len, dtype=jnp.int32)
    cosine, sine_vals = rope_tables(positions.astype(full), HEAD_DIM)
    limit = block_limits(block_lengths[0], positions)[None]
    normed_one = jnp.zeros((seq_len, width), low)
    heads = jnp.zeros((n, kv_here, GROUP + 2, HEAD_DIM, shard_len), low)
    routes_all = []
    line = LineGather(halves)
    signal = swap(x_low[:1, :128], "fsdp", order_a[0])
    expert_weights, _ = tie((w_gate, w_up, w_down), signal)
    for turn in range(n):
        if turn:
            line.land(0, heads if turn > 1 else ())
            if turn < n - 1:
                line.go(0)
            line.land(1, ())
            if turn < n - 1:
                line.go(1)
        else:
            line.go(0)
            line.go(1)
        block = jnp.concatenate(line.block(turn))
        start = order[turn] * shard_len
        normed = rms_norm(block[:shard_len].astype(full), full_g1).astype(low)
        projected = dot("td,dc->ct", normed, full_qkv)
        projected = projected.reshape(kv_here, GROUP + 2, HEAD_DIM, shard_len)
        turned = rotate(
            projected[:, : GROUP + 1],
            lax.dynamic_slice_in_dim(cosine, start, shard_len, 1),
            lax.dynamic_slice_in_dim(sine_vals, start, shard_len, 1),
        ).astype(low)
        turned = jnp.concatenate(
            [
                turned[:, :GROUP] * jnp.asarray(attn_mult, low),
                turned[:, GROUP:],
                projected[:, GROUP + 1 :].astype(low),
            ],
            axis=1,
        )
        heads = lax.dynamic_update_index_in_dim(heads, turned, order[turn], 0)
        normed_one = lax.dynamic_update_slice_in_dim(normed_one, normed, start, 0)
        routes_all.append(block[shard_len : shard_len + top_count + 1, :shard_len])

    w_gate, w_up, w_down = expert_weights
    hidden_w = w_gate.shape[2]
    down_chunks = [
        w_down[:, :, start : start + hidden_w] for start in range(0, width, hidden_w)
    ]
    weights = lax.all_gather(
        jnp.concatenate([w_gate, w_up, jnp.concatenate(down_chunks, axis=1)], axis=2),
        "fsdp",
        axis=1,
        tiled=True,
    )

    routes_all = jnp.stack(routes_all).astype(jnp.int32)
    valid_count = total(jnp.sum(routes_all[:, top_count]).astype(full).reshape(1, 1), "fsdp")[0, 0]
    expert_ids = jnp.arange(expert_total, dtype=jnp.int32)
    member = jnp.any(routes_all[:, :top_count, None, :] == expert_ids[:, None], axis=1)
    own_member = lax.dynamic_slice_in_dim(member, me * experts_here, experts_here, 1)
    earlier = jnp.arange(shard_len)[:, None] < jnp.arange(shard_len)[None, :]
    slot_of = dot("net,tu->neu", own_member.astype(low), earlier.astype(low)).astype(jnp.int32)
    slot_of = jnp.where(own_member, slot_of, -1)
    member = member.astype(full)

    key = jnp.moveaxis(heads[:, :, GROUP], 0, 2).reshape(kv_here, HEAD_DIM, seq_len)
    value = jnp.moveaxis(heads[:, :, GROUP + 1], 0, 2).reshape(kv_here, HEAD_DIM, seq_len)
    key_rows = jnp.swapaxes(key, 1, 2)
    value_rows = jnp.swapaxes(value, 1, 2)
    attended, out_heads, lse = attention_forward(heads, key_rows, value, limit)
    moved = exchange(attended)
    moved, slot_of, member, own_router = tie(moved, slot_of, member, own_router)
    attn_rows = by_place(nearest(*moved)).reshape(HEADS * HEAD_DIM, shard_len)
    projected = dot("kt,kd->td", attn_rows, full_out)
    hidden = x_low.astype(full) + resid_mult * projected
    normed_two, norm_two_pull = jax.vjp(rms_norm, hidden, full_g2)

    normed_low = normed_two.astype(low)
    line = LineGather((normed_low[:middle], normed_low[middle:]))
    buffers, gates, tokens = [], [], []
    for turn in range(n):
        if turn:
            line.land(0, gates[-1])
            if turn < n - 1:
                line.go(0)
            line.land(1, ())
            if turn < n - 1:
                line.go(1)
        else:
            line.go(0)
            line.go(1)
        tokens.append(line.block(turn))
        *buffers, shard_gates = experts_forward(
            turn, n, jnp.stack([order[turn], me]), tokens[turn], slot_of[turn], member[turn],
            router, weights, w_down.shape[1], slots, buffers,
        )
        gates.append(shard_gates)
    mix_parts, expert_in, gate_up = buffers
    mixture, _ = line_scatter(mix_parts, ())
    output_f32 = hidden + resid_mult * mixture
    activations = output_f32.astype(low).reshape(1, shard_len, width)
    error_rows = output_f32 - teacher.astype(full).reshape(shard_len, width)
    weighted = valid_rows[:, None] * error_rows
    loss_steps = total_steps(jnp.sum(weighted * error_rows).reshape(1, 1), "seq", "fsdp")
    squares = next(loss_steps)
    d_out = weighted * (tokens_all / valid_count)

    d_mix = resid_mult * d_out
    d_tokens = d_mix.astype(low)
    mix_dot = jnp.sum(d_mix * mixture, axis=1)[None]
    mix_high = mix_dot.astype(low)
    mix_rows = jnp.concatenate([mix_high, (mix_dot - mix_high.astype(full)).astype(low)])
    mix_rows = jnp.pad(mix_rows, ((0, 14), (0, width - shard_len)))
    line = LineGather((d_tokens[:middle], jnp.concatenate([d_tokens[middle:], mix_rows])))
    buffers, d_logits = [], []
    for turn in range(n):
        if turn:
            line.land(0, d_logits[-1])
            if turn < n - 1:
                line.go(0)
            squares = line.land(1, squares)
            squares = loss_steps.send(squares)
            if turn < n - 1:
                line.go(1)
        else:
            line.go(0)
            line.go(1)
        d_block = line.block(turn)
        mix_dot = d_block[1][middle : middle + 2, :shard_len].astype(full)
        mix_dot = jnp.sum(mix_dot, axis=0, keepdims=True)
        *buffers, shard_logits = experts_backward(
            turn, n, jnp.stack([order[turn], me]), d_block, slot_of[turn], gates[turn], mix_dot,
            own_router, gate_up, weights, w_down.shape[1], buffers,
        )
        d_logits.append(shard_logits)
    d_parts, d_rows, d_gate_up, act_low = buffers
    expert_in = expert_in.reshape(experts_here, slot_rows, width)
    d_rows = d_rows.reshape(experts_here, slot_rows, width)
    d_gate_up = d_gate_up.reshape(experts_here, slot_rows, -1)
    act_low = act_low.reshape(experts_here, slot_rows, -1)

    cut = (experts_here + 1) // 2

    losses = [squares]

    def some_grads(first, stop):
        def make(before, grads):
            inputs, _, loss = tie((expert_in, d_gate_up, act_low, d_rows), before, losses[-1])
            losses.append(loss_steps.send(loss))
            return [weight_grads(*inputs, w_down.shape[1], first, stop, grads)]

        return make

    d_normed_two, grads = line_scatter(
        d_parts, (some_grads(0, cut), some_grads(cut, experts_here))
    )
    squares = losses[-1]
    expert_sum = lax.psum_scatter(grads[0], "fsdp", scatter_dimension=1, tiled=True)

    d_hidden_norm, gain_two_part = norm_two_pull(d_normed_two)
    d_hidden = d_out + d_hidden_norm
    d_proj = (resid_mult * d_hidden).astype(low)
    out_pairs = out_grads(mine.reshape(1), attn_rows, d_proj, order_a, order_b)
    out_sums = [Halving(*pair, bits) for pair, bits in zip(out_pairs, (order_a, order_b))]
    for each in out_sums:
        each.go()
    d_attended = dot("kd,td->kt", full_out, d_proj).astype(low)
    (d_attended,) = land(out_sums, d_attended)
    moved = exchange(d_attended.reshape(n, heads_w, shard_len))
    for each in out_sums:
        each.add()
    router_part = sum(
        dot("td,et->de", half, half_logits)
        for shard, shard_logits in zip(tokens, d_logits)
        for half, half_logits in (
            (shard[0], shard_logits[:experts_here, :middle]),
            (shard[1], shard_logits[:experts_here, middle:]),
        )
    )
    moved, router_part = leave(out_sums, moved, router_part)
    for each in out_sums:
        each.go()
    d_heads = by_place(nearest(*moved))
    query_grad, key_grad, value_grad = attention_backward(
        heads, key_rows, value_rows, key, limit, out_heads, lse, d_heads
    )
    ((query_grad, key_grad, value_grad),) = land(out_sums, (query_grad, key_grad, value_grad))
    for each in out_sums:
        each.add()
        each.go()
    d_turned = jnp.concatenate([query_grad, key_grad[:, None]], axis=1).astype(full)
    d_turned = rotate(d_turned, cosine, -sine_vals).astype(low)
    d_qkv = jnp.concatenate([d_turned, value_grad[:, None]], axis=1).reshape(group_w, seq_len)
    d_parts = dot("ct,dc->td", d_qkv, full_qkv).astype(low).reshape(n, shard_len, width)
    own_columns = jnp.zeros((width, expert_total), full)
    own_columns = lax.dynamic_update_slice_in_dim(own_columns, router_part, me * experts_here, 1)
    (d_parts,) = land(out_sums, d_parts)
    for each in out_sums:
        each.add()

    out_sum = jnp.concatenate([each.finish() for each in out_sums], axis=1).astype(low)
    out_rows = out_sum.shape[0] // n
    out_parts = jnp.swapaxes(out_sum.reshape(out_sum.shape[0], n, width // n), 0, 1)
    d_parts = jnp.concatenate([d_parts, out_parts.reshape(n, out_rows, width)], axis=1)
    sums = {}

    def first_work(before, _):
        rows, _ = tie(d_qkv, before)
        qkv_part = jnp.concatenate(
            [dot("td,ct->dc", normed_one, rows), own_columns, gain_two_part[:, None]], axis=1
        ).astype(low)
        sums["qkv"] = rows_halving(qkv_part, order_a)
        sums["qkv"].go()
        return sums["qkv"].send

    def next_work(before, _):
        land([sums["qkv"]], before)
        sums["qkv"].add()
        sums["qkv"].go()
        return sums["qkv"].send

    ended, _ = line_scatter(d_parts, (first_work, next_work, next_work))
    qkv_sum = sums["qkv"]
    d_normed_one = ended[:shard_len]
    (ended,) = land([qkv_sum], ended)
    qkv_sum.add()
    out_own = ended[shard_len:].reshape(out_sum.shape[0], width // n)
    block = jnp.concatenate([qkv_sum.finish(), out_own], axis=1).astype(low)
    rights, lefts = [block], [block]
    _, norm_one_pull = jax.vjp(lambda v: rms_norm(v, full_g1), x_low.astype(full))
    input_grad = (d_hidden + norm_one_pull(d_normed_one)[0]).reshape(1, shard_len, width)
    few = w_down.shape[1]
    last_work = [
        lambda: expert_sum[:, :, : 2 * hidden_w].astype(full),
        lambda: jnp.concatenate(
            [
                expert_sum[:, start : start + few, 2 * hidden_w :].astype(full)
                for start in range(0, expert_sum.shape[1], few)
            ],
            axis=2,
        ),
    ]
    done = [input_grad]
    for k in range(1, n):
        right, left = line_move(rights[-1], lefts[-1], k)
        if k < 3:
            done.append(last_work[k - 1]())
        right, left, done[-1] = tie(right, left, done[-1])
        rights.append(right)
        lefts.append(left)
    blocks = nearest(rights, lefts)
    input_grad, gate_up_grad, down_grad = done
    gate_grad, up_grad = gate_up_grad[:, :, :hidden_w], gate_up_grad[:, :, hidden_w:]
    qkv_grad = jnp.zeros((w_qkv.shape[0], QKV_W), full)
    out_grad = jnp.zeros((w_out.shape[0], width), full)
    rest = 0.0
    for k, block in enumerate(blocks):
        block = block.astype(full)
        place = (me - k) % n
        qkv_grad = lax.dynamic_update_slice_in_dim(
            qkv_grad, block[:, :group_w], place * group_w, 1
        )
        out_grad = lax.dynamic_update_slice_in_dim(
            out_grad, block[:, -(width // n) :], place * (width // n), 1
        )
        rest = rest + block[:, group_w : -(width // n)]
    router_grad, gain_two_grad = rest[:, :expert_total], rest[:, expert_total]
    gain_one_grad = jnp.sum(qkv_grad * w_qkv.astype(full), axis=1) / gain_one.astype(full)
    for _ in range(2):
        squares = loss_steps.send(squares)
    loss_value = squares[0, 0] / (valid_count * width)
    return (
        activations,
        loss_value,
        input_grad,
        gain_one_grad,
        qkv_grad,
        out_grad,
        gain_two_grad,
        router_grad,
        gate_grad,
        up_grad,
        down_grad,
    )


def solution(mesh):
    return jax.shard_map(
        shards,
        mesh=mesh,
        in_specs=(
            P("fsdp", "seq", None),
            P("fsdp", "seq", None),
            P("fsdp", "seq", None),
            P("fsdp", "seq"),
            P("fsdp", None),
            P("fsdp"),
            P("fsdp", None),
            P("fsdp", None),
            P("fsdp"),
            P("fsdp", None),
            P("seq", "fsdp", None),
            P("seq", "fsdp", None),
            P("seq", "fsdp", None),
        ),
        out_specs=(
            P("fsdp", "seq", None),
            P(),
            P("fsdp", "seq", None),
            P("fsdp"),
            P("fsdp", None),
            P("fsdp", None),
            P("fsdp"),
            P("fsdp", None),
            P("seq", "fsdp", None),
            P("seq", "fsdp", None),
            P("seq", "fsdp", None),
        ),
        check_vma=False,
    )
```

```python
import functools

import jax
import jax.numpy as jnp
from jax import lax
from jax.experimental import pallas as pl
from jax.experimental.pallas import tpu as pltpu
from jax.sharding import PartitionSpec as P

HEADS = 24
KV_HEADS = 8
HEAD_DIM = 64
BLOCK = 256
GROUP = 3
QKV_W = 2560


epsilon = 1e-06
attn_mult = 0.015625
resid_mult = 0.22
rope_base = 10000.0
masked_score = -1e30

low = jnp.bfloat16
full = jnp.float32


def dot(spec, left, right):
    return jnp.einsum(spec, left, right, preferred_element_type=full)


def rms_norm(values, gain_vec):
    inv_rms = lax.rsqrt(jnp.mean(values * values, axis=-1, keepdims=True) + epsilon)
    return values * inv_rms * gain_vec


def rope_tables(positions, head_dim):
    half_dim = head_dim // 2
    frequency = rope_base ** (-(2.0 * jnp.arange(half_dim, dtype=full)) / head_dim)
    angles = frequency[:, None] * positions[None, :]
    return (jnp.cos(angles), jnp.sin(angles))


def rotate(values, cosine, sine_vals):
    half_dim = values.shape[-2] // 2
    front_half = values[..., :half_dim, :]
    back_half = values[..., half_dim:, :]
    return jnp.concatenate(
        [front_half * cosine - back_half * sine_vals, back_half * cosine + front_half * sine_vals],
        axis=-2,
    )


def block_limits(lengths_row, positions):
    block_ends = jnp.cumsum(lengths_row)
    open_ends = jnp.where(block_ends[None, :] > positions[:, None], block_ends[None, :], positions.shape[0])
    return jnp.min(open_ends, axis=1).astype(jnp.int32)


def tie(*groups):
    return lax.optimization_barrier(groups)


def line_move(right, left, k):
    n = lax.axis_size("seq")
    return (
        lax.ppermute(right, "seq", [(i, i + 1) for i in range(k - 1, n - 1)]),
        lax.ppermute(left, "seq", [(i, i - 1) for i in range(1, n - k + 1)]),
    )


def line_gather(block):
    n = lax.axis_size("seq")
    rights, lefts = [block], [block]
    for k in range(1, n):
        right, left = tie(*line_move(rights[-1], lefts[-1], k))
        rights.append(right)
        lefts.append(left)
    return nearest(rights, lefts)


def nearest(rights, lefts):
    n = lax.axis_size("seq")
    me = lax.axis_index("seq")
    return [rights[0]] + [jnp.where(me >= k, rights[k], lefts[n - k]) for k in range(1, n)]


def arrival_order(n):
    order = []
    for me in range(n):
        both = min(me, n - 1 - me)
        places = [me]
        for k in range(1, n):
            places += [me - k] if me >= k and (k <= both or me > n - 1 - me) else []
            places += [me + k] if me + k < n and (k <= both or me < n - 1 - me) else []
        order.append(places)
    return order


def arrived(rights, lefts, turn):
    n = lax.axis_size("seq")
    me = lax.axis_index("seq")
    sources = {}
    for dev, places in enumerate(arrival_order(n)):
        gap = dev - places[turn]
        sources.setdefault(gap, []).append(dev)
    block = None
    for gap, devs in sources.items():
        moved = rights[gap] if gap >= 0 else lefts[-gap]
        if block is None:
            block = moved
        else:
            mine = jnp.array([dev in devs for dev in range(n)])[me]
            block = jnp.where(mine, moved, block)
    return block


def at_place(placed, place):
    return lax.dynamic_index_in_dim(placed, place % lax.axis_size("seq"), 0, keepdims=False)


def line_send(parts, k, right, left):
    me = lax.axis_index("seq")
    to_right, to_left = at_place(parts, me + k), at_place(parts, me - k)
    if right is not None:
        to_right = (to_right.astype(full) + right.astype(full)).astype(low)
        to_left = (to_left.astype(full) + left.astype(full)).astype(low)
    return to_right, to_left


def line_pass(to_right, to_left, k):
    n = lax.axis_size("seq")
    return (
        lax.ppermute(to_right, "seq", [(i, i + 1) for i in range(n - k)]),
        lax.ppermute(to_left, "seq", [(i, i - 1) for i in range(k, n)]),
    )


class Doubling:
    def __init__(self, block, bits):
        self.blocks, self.order, self.bits = block[None], bits, list(bits)
        self.away = self.late = False

    def go(self):
        self.here, self.away = swap(self.blocks, "fsdp", self.bits.pop(0)), True

    def land(self, other):
        other, here = tie(other, self.here)
        self.blocks, self.away = jnp.concatenate([self.blocks, here]), False
        return other

    def rows(self):
        while self.bits or self.away:
            if not self.away:
                self.go()
            self.land(())
        mask = lax.axis_index("fsdp") ^ jnp.arange(self.blocks.shape[0])
        spot = sum(((mask // bit) % 2) << i for i, bit in enumerate(self.order))
        return self.blocks[spot].reshape(-1, self.blocks.shape[2])


class LineGather:
    def __init__(self, halves):
        self.rights, self.lefts = [[half] for half in halves], [[half] for half in halves]
        self.landed = [0, 0]

    def go(self, h):
        step = len(self.rights[h])
        right, left = line_move(self.rights[h][-1], self.lefts[h][-1], step)
        self.rights[h].append(right)
        self.lefts[h].append(left)

    def land(self, h, other):
        spot = self.landed[h] = len(self.rights[h]) - 1
        if isinstance(other, Doubling):
            (self.rights[h][spot], self.lefts[h][spot]) = other.land(
                (self.rights[h][spot], self.lefts[h][spot])
            )
            other = ()
        moved = [(self.rights[part][spot], self.lefts[part][spot]) for part in range(h + 1)]
        moved, other = tie(moved, other)
        for part, (right, left) in enumerate(moved):
            self.rights[part][spot], self.lefts[part][spot] = right, left
        return other

    def hold(self, other):
        came = [(self.rights[h][-1 - self.ahead(h)], self.lefts[h][-1 - self.ahead(h)]) for h in (0, 1)]
        return tie(other, came)[0]

    def ahead(self, h):
        return len(self.rights[h]) - 1 - self.landed[h]

    def block(self, turn):
        return [arrived(self.rights[h], self.lefts[h], turn) for h in (0, 1)]


def line_scatter(halves, work):
    n = lax.axis_size("seq")
    me = lax.axis_index("seq")
    flying = [(None, None)] * len(halves)
    before, given = (), []
    for k in range(n - 1, 0, -1):
        for h, half in enumerate(halves):
            if k < n - 1 and h:
                flying[h], before = tie(flying[h], before)
            elif k < n - 1:
                flying[h], given = tie(flying[h], given)
            before = line_send(half, k, *flying[h])
            flying[h] = line_pass(*before, k)
        if n - 1 - k < len(work):
            given = work[n - 1 - k](before, given)
    sums = []
    flying[0], given = tie(flying[0], given)
    for half, (right, left) in zip(halves, flying):
        sums.append(at_place(half, me).astype(full) + (right.astype(full) + left.astype(full)))
    return jnp.concatenate(sums), given


def by_place(blocks):
    n = lax.axis_size("seq")
    me = lax.axis_index("seq")
    placed = jnp.zeros((n,) + blocks[0].shape, blocks[0].dtype)
    for k, block in enumerate(blocks):
        placed = lax.dynamic_update_index_in_dim(placed, block, (me - k) % n, 0)
    return placed


def exchange(blocks):
    n = lax.axis_size("seq")
    me = lax.axis_index("seq")
    own = at_place(blocks, me)
    rights, lefts = [own] * n, [own] * n
    for k in range(n - 1, 0, -1):
        to_right, to_left = at_place(blocks, me + k), at_place(blocks, me - k)
        rights[k] = lax.ppermute(to_right, "seq", [(i, i + k) for i in range(n - k)])
        lefts[k] = lax.ppermute(to_left, "seq", [(i, i - k) for i in range(k, n)])
    return rights, lefts


def swap(value, axis, bit):
    return lax.ppermute(value, axis, [(i, i ^ bit) for i in range(lax.axis_size(axis))])


def total(value, *axes):
    for axis in axes:
        for step in range(lax.axis_size(axis).bit_length() - 1):
            value = value + swap(value, axis, 1 << step)
    return value


def fsdp_bits():
    bits = [1 << step for step in range(lax.axis_size("fsdp").bit_length() - 1)]
    return tuple(bits), tuple(bits[:1] + bits[:0:-1])


def total_steps(value, *axes):
    for axis in axes:
        for step in range(lax.axis_size(axis).bit_length() - 1):
            here = swap(value, axis, 1 << step)
            here = yield here
            value = value + here
    while True:
        yield value


class Halving:
    def __init__(self, keep, send, bits):
        self.terms, self.send, self.bits = [keep], send, list(bits)

    def go(self):
        self.terms = self.terms + [swap(self.send, "fsdp", self.bits.pop(0))]

    def add(self):
        half = self.terms[0].shape[0] // 2
        if half:
            self.send = sum(term[half:].astype(full) for term in self.terms).astype(low)
            self.terms = [term[:half] for term in self.terms]

    def finish(self):
        while self.bits:
            self.go()
            self.add()
        return sum(term[0].astype(full) for term in self.terms)


def rows_halving(part, bits):
    devs = lax.axis_size("fsdp")
    order = lax.axis_index("fsdp") ^ jnp.array(halving_masks(bits), jnp.int32)
    blocks = part.reshape(devs, part.shape[0] // devs, part.shape[1])[order]
    return Halving(blocks[: devs // 2], blocks[devs // 2 :], bits)


def land(sums, *others):
    tied = tie([each.terms[-1] for each in sums], *others)
    for each, here in zip(sums, tied[0]):
        each.terms = each.terms[:-1] + [here]
    return tied[1:]


def leave(sums, *others):
    tied = tie([each.send for each in sums], *others)
    for each, send in zip(sums, tied[0]):
        each.send = send
    return tied[1:]


def nt(a, b):
    return lax.dot_general(a, b, (((1,), (1,)), ((), ())), preferred_element_type=full)

def nn(a, b):
    return lax.dot_general(a, b, (((1,), (0,)), ((), ())), preferred_element_type=full)

def tn(a, b):
    return lax.dot_general(a, b, (((0,), (0,)), ((), ())), preferred_element_type=full)


def beside(rows):
    return jnp.concatenate([rows[h] for h in range(GROUP)], axis=1)

def key_steps(i, seq_len, query_rows, key_rows):
    free = (i * query_rows) // key_rows
    need = ((i + 1) * query_rows + BLOCK - 1 + key_rows - 1) // key_rows
    return free, jnp.minimum(need, seq_len // key_rows)

def forward_kernel(seq_len, query_rows, key_rows, limit_ref, q_ref, k_ref, vt_ref, low_ref, out_ref, lse_ref):
    i = pl.program_id(1)
    qt = beside(q_ref[0, 0])
    width = GROUP * query_rows
    limit = jnp.concatenate([limit_ref[...]] * GROUP, axis=1)

    def step(masked, j, carry):
        peak, total, acc = carry
        start = pl.multiple_of(j * key_rows, key_rows)
        s = nn(k_ref[0, pl.ds(start, key_rows), :], qt)
        if masked:
            place = start + lax.broadcasted_iota(jnp.int32, (key_rows, 1), 0)
            s = jnp.where(place < limit, s, masked_score)
        new_peak = jnp.maximum(peak, jnp.max(s, axis=0, keepdims=True))
        shrink = jnp.exp(peak - new_peak)
        p = jnp.exp(s - new_peak)
        total = shrink * total + jnp.sum(p, axis=0, keepdims=True)
        acc = shrink * acc + nn(vt_ref[0, :, pl.ds(start, key_rows)], p.astype(low))
        return new_peak, total, acc

    free, need = key_steps(i, seq_len, query_rows, key_rows)
    carry = (
        jnp.full((1, width), masked_score, full),
        jnp.zeros((1, width), full),
        jnp.zeros((HEAD_DIM, width), full),
    )
    carry = lax.fori_loop(0, free, lambda j, c: step(False, j, c), carry)
    peak, total, acc = lax.fori_loop(free, need, lambda j, c: step(True, j, c), carry)
    out = acc / total
    lse = peak + jnp.log(total)
    for h in range(GROUP):
        cols = slice(h * query_rows, (h + 1) * query_rows)
        out_ref[0, h] = out[:, cols]
        low_ref[0, pl.ds(h * HEAD_DIM, HEAD_DIM), :] = out[:, cols].astype(low)
        lse_ref[0, h] = lse[:, cols]

def query_spec(query_rows, per):
    return pl.BlockSpec(
        (1, 1, GROUP, HEAD_DIM, query_rows), lambda g, i: (i // per, g, 0, 0, i % per)
    )


def attention_forward(heads, k_rows, vt, limit):
    kv_here, shard_len = heads.shape[1], heads.shape[4]
    seq_len = k_rows.shape[1]
    query_rows = min(256, shard_len)
    key_rows = min(512, seq_len)
    per = shard_len // query_rows
    return pl.pallas_call(
        functools.partial(forward_kernel, seq_len, query_rows, key_rows),
        grid=(kv_here, seq_len // query_rows),
        in_specs=[
            pl.BlockSpec((1, query_rows), lambda g, i: (0, i)),
            query_spec(query_rows, per),
            pl.BlockSpec((1, seq_len, HEAD_DIM), lambda g, i: (g, 0, 0)),
            pl.BlockSpec((1, HEAD_DIM, seq_len), lambda g, i: (g, 0, 0)),
        ],
        out_specs=[
            pl.BlockSpec((1, GROUP * HEAD_DIM, query_rows), lambda g, i: (i // per, g, i % per)),
            pl.BlockSpec((1, GROUP, HEAD_DIM, query_rows), lambda g, i: (g, 0, 0, i)),
            pl.BlockSpec((1, GROUP, 1, query_rows), lambda g, i: (g, 0, 0, i)),
        ],
        out_shape=[
            jax.ShapeDtypeStruct((seq_len // shard_len, kv_here * GROUP * HEAD_DIM, shard_len), low),
            jax.ShapeDtypeStruct((kv_here, GROUP, HEAD_DIM, seq_len), full),
            jax.ShapeDtypeStruct((kv_here, GROUP, 1, seq_len), full),
        ],
        compiler_params=vmem(40),
        name="attention_forward",
    )(limit, heads, k_rows, vt)

def backward_kernel(
    seq_len, query_rows, key_rows, per, me_ref, limit_ref, q_ref, k_ref, v_ref, kt_ref, out_ref, lse_ref, *refs
):
    blocks, (dq_ref, dk_ref, dv_ref, dk_acc, dv_acc, held) = refs[:-6], refs[-6:]
    i = pl.program_id(1)

    @pl.when(i == 0)
    def _():
        dk_acc[...] = jnp.zeros_like(dk_acc)
        dv_acc[...] = jnp.zeros_like(dv_acc)

    qt = beside(q_ref[0, 0])
    limit = jnp.concatenate([limit_ref[...]] * GROUP, axis=1)
    devs = (len(blocks) + 1) // 2
    gap = me_ref[0] - i // per
    for spot, block in enumerate(blocks):

        @pl.when(gap == (spot if spot < devs else devs - 1 - spot))
        def _():
            held[...] = block[...]

    dout = jnp.concatenate([held[pl.ds(h * HEAD_DIM, HEAD_DIM), :] for h in range(GROUP)], axis=1)
    delta = jnp.sum(dout.astype(full) * beside(out_ref[0]), axis=0, keepdims=True)
    lse = beside(lse_ref[0])

    def step(masked, j, dq):
        start = pl.multiple_of(j * key_rows, key_rows)
        keys = pl.ds(start, key_rows)
        s = nn(k_ref[0, keys, :], qt)
        if masked:
            place = start + lax.broadcasted_iota(jnp.int32, (key_rows, 1), 0)
            s = jnp.where(place < limit, s, masked_score)
        p = jnp.exp(s - lse)
        dp = nn(v_ref[0, keys, :], dout)
        ds = (p * (dp - delta)).astype(low)
        dk_acc[:, keys] += nt(qt, ds)
        dv_acc[:, keys] += nt(dout, p.astype(low))
        return dq + nn(kt_ref[0, :, keys], ds)

    free, need = key_steps(i, seq_len, query_rows, key_rows)
    dq = jnp.zeros((HEAD_DIM, GROUP * query_rows), full)
    dq = lax.fori_loop(0, free, lambda j, c: step(False, j, c), dq)
    dq = lax.fori_loop(free, need, lambda j, c: step(True, j, c), dq) * attn_mult
    for h in range(GROUP):
        dq_ref[0, h] = dq[:, h * query_rows : (h + 1) * query_rows].astype(low)

    @pl.when(i == pl.num_programs(1) - 1)
    def _():
        dk_ref[0] = dk_acc[...].astype(low)
        dv_ref[0] = dv_acc[...].astype(low)

def attention_backward(heads, k_rows, v_rows, kt, limit, out, lse, me, rights, lefts):
    blocks = [*rights, *lefts[1:]]
    kv_here, shard_len = heads.shape[1], heads.shape[4]
    seq_len = k_rows.shape[1]
    query_rows = min(256, shard_len)
    key_rows = min(512, seq_len)
    per = shard_len // query_rows
    quarter = lambda g, i, me: (g, 0, 0, i)
    whole = lambda g, i, me: (g, 0, 0)
    return pl.pallas_call(
        functools.partial(backward_kernel, seq_len, query_rows, key_rows, per),
        grid_spec=pltpu.PrefetchScalarGridSpec(
            num_scalar_prefetch=1,
            grid=(kv_here, seq_len // query_rows),
            in_specs=[
                pl.BlockSpec((1, query_rows), lambda g, i, me: (0, i)),
                pl.BlockSpec(
                    (1, 1, GROUP, HEAD_DIM, query_rows),
                    lambda g, i, me: (i // per, g, 0, 0, i % per),
                ),
                pl.BlockSpec((1, seq_len, HEAD_DIM), whole),
                pl.BlockSpec((1, seq_len, HEAD_DIM), whole),
                pl.BlockSpec((1, HEAD_DIM, seq_len), whole),
                pl.BlockSpec((1, GROUP, HEAD_DIM, query_rows), quarter),
                pl.BlockSpec((1, GROUP, 1, query_rows), quarter),
            ]
            + [pl.BlockSpec((GROUP * HEAD_DIM, query_rows), lambda g, i, me: (g, i % per))]
            * len(blocks),
            out_specs=[
                pl.BlockSpec((1, GROUP, HEAD_DIM, query_rows), quarter),
                pl.BlockSpec((1, HEAD_DIM, seq_len), whole),
                pl.BlockSpec((1, HEAD_DIM, seq_len), whole),
            ],
            scratch_shapes=[
                pltpu.VMEM((HEAD_DIM, seq_len), full),
                pltpu.VMEM((HEAD_DIM, seq_len), full),
                pltpu.VMEM((GROUP * HEAD_DIM, query_rows), low),
            ],
        ),
        out_shape=[
            jax.ShapeDtypeStruct((kv_here, GROUP, HEAD_DIM, seq_len), low),
            jax.ShapeDtypeStruct((kv_here, HEAD_DIM, seq_len), low),
            jax.ShapeDtypeStruct((kv_here, HEAD_DIM, seq_len), low),
        ],
        compiler_params=vmem(40),
        name="attention_backward",
    )(me, limit, heads, k_rows, v_rows, kt, out, lse, *blocks)


def vmem(mib):
    return pltpu.CompilerParams(vmem_limit_bytes=mib * 2**20)


def own_row(ref, row):
    return ref[pl.ds(row, 1), :]


def join_down(rows, block_ref, down_ref):
    hidden, width = down_ref.shape
    chunks = width // hidden
    for dev in range(hidden // rows):
        for chunk in range(chunks):
            start = (dev * chunks + chunk) * rows
            down_ref[dev * rows : (dev + 1) * rows, chunk * hidden : (chunk + 1) * hidden] = (
                block_ref[start : start + rows, :]
            )


def pick_rows(pick, tok_ref, more_ref):
    middle = tok_ref.shape[0]
    return (nn(pick[:, :middle], tok_ref[...]) + nn(pick[:, middle:], more_ref[:middle, :])).astype(low)


def experts_kernel(
    few, pair, at_ref, tok_ref, more_ref, slot_ref, member_ref, router_ref, wgu_ref, wd_ref, *refs
):
    part_ref, x_ref, gu_ref, gates_ref, acc, gates_all, down = refs[-7:]
    step, steps = pl.program_id(0), pl.num_programs(0)
    slots = x_ref.shape[2]

    @pl.when(step == 0)
    def _():
        member = member_ref[...] > 0
        logits = [nt(router_ref[...], ref[...]) for ref in (tok_ref, more_ref)]
        chosen = jnp.where(member, jnp.concatenate(logits, axis=1), masked_score)
        chosen = jnp.exp(chosen - jnp.max(chosen, axis=0, keepdims=True))
        chosen = jnp.where(member, chosen, 0.0)
        gates_all[...] = chosen / jnp.sum(chosen, axis=0, keepdims=True)
        acc[...] = jnp.zeros_like(acc)

    place = lax.broadcasted_iota(jnp.int32, (slots, 1), 0)
    puts, ys = [], []
    for i in range(pair):
        e = step * pair + i
        gate_row = own_row(gates_all, at_ref[1] * (steps * pair) + e)
        gates_ref[pl.ds(e, 1), :] = gate_row
        here = place == own_row(slot_ref, e)
        x = pick_rows(jnp.where(here, 1.0, 0.0).astype(low), tok_ref, more_ref)
        x_ref[i, 0] = x
        gu = nn(x, wgu_ref[i])
        gu_ref[i, 0] = gu.astype(low)
        hidden = gu.shape[1] // 2
        g, u = gu[:, :hidden], gu[:, hidden:]
        act = (g * jax.nn.sigmoid(g) * u).astype(low)
        join_down(few, wd_ref.at[i], down.at[i])
        ys.append(nn(act, down[i]).astype(low))
        puts.append(jnp.where(here, gate_row, 0.0).astype(low))
    acc[...] += tn(jnp.concatenate(puts), jnp.concatenate(ys))

    @pl.when(step == steps - 1)
    def _():
        part_ref[0] = acc[...].astype(low)


def back_kernel(
    few, pair, at_ref, tok_ref, more_ref, slot_ref, gates_ref, mix_ref, router_ref, gu_ref, wgu_ref, wd_ref, *refs
):
    part_ref, d_ref, dgu_ref, act_ref, dlog_ref, acc, dlog_all, down = refs[-8:]
    step, steps = pl.program_id(0), pl.num_programs(0)
    slots, hidden = gu_ref.shape[2], gu_ref.shape[3] // 2

    @pl.when(step == 0)
    def _():
        dlog_all[...] = jnp.zeros_like(dlog_all)
        acc[...] = jnp.zeros_like(acc)

    place = lax.broadcasted_iota(jnp.int32, (slots, 1), 0)
    puts, dxs = [], []
    for i in range(pair):
        e = step * pair + i
        here = place == own_row(slot_ref, e)
        pick = jnp.where(here, 1.0, 0.0).astype(low)
        gate_row = own_row(gates_ref, e)
        gate = jnp.sum(jnp.where(here, gate_row, 0.0), axis=1, keepdims=True)
        d = pick_rows(pick, tok_ref, more_ref)
        d_ref[i, 0] = d
        join_down(few, wd_ref.at[i], down.at[i])
        d_act = nt(d, down[i])
        g, u = gu_ref[i, 0, :, :hidden].astype(full), gu_ref[i, 0, :, hidden:].astype(full)
        sig = jax.nn.sigmoid(g)
        silu = g * sig
        act = silu * u
        d_gate = jnp.sum(d_act * act, axis=1, keepdims=True)
        d_gate = jnp.sum(jnp.where(here, d_gate, 0.0), axis=0, keepdims=True)
        dlog_all[pl.ds(e, 1), :] = gate_row * (d_gate - mix_ref[...])
        act_ref[i, 0] = (act * gate).astype(low)
        d_act = d_act * gate
        d_g = (d_act * u * (sig + silu * (1.0 - sig))).astype(low)
        d_u = (d_act * silu).astype(low)
        dgu_ref[i, 0, :, :hidden] = d_g
        dgu_ref[i, 0, :, hidden:] = d_u
        dxs.append(nt(dgu_ref[i, 0], wgu_ref[i]).astype(low))
        puts.append(pick)
    acc[...] += tn(jnp.concatenate(puts), jnp.concatenate(dxs))

    @pl.when(step == steps - 1)
    def _():
        dlog = dlog_all[...].astype(low)
        dlog_ref[...] = dlog
        part_ref[0] = (acc[...] + tn(dlog, router_ref[...])).astype(low)


def by_expert(*shape):
    return pl.BlockSpec((1,) + shape, lambda e, at: (e, 0, 0))


def in_turn(pair, turn, *shape):
    return pl.BlockSpec((pair, 1) + shape, lambda e, at: (e, turn, 0, 0))


def same(*shape):
    return pl.BlockSpec(shape, lambda e, at: (0, 0))


def in_place(*shape):
    return pl.BlockSpec((1,) + shape, lambda e, at: (at[0], 0, 0))


def shard_call(kernel, name, at, inputs, in_specs, out_specs, out_shape, buffers, scratch, experts):
    first = len(inputs) + 1
    aliases = {first + i: i for i in range(len(buffers))}
    return pl.pallas_call(
        kernel,
        grid_spec=pltpu.PrefetchScalarGridSpec(
            num_scalar_prefetch=1,
            grid=(experts,),
            in_specs=in_specs + [pl.BlockSpec(memory_space=pl.ANY)] * len(buffers),
            out_specs=out_specs,
            scratch_shapes=scratch,
        ),
        out_shape=out_shape,
        input_output_aliases=aliases,
        compiler_params=vmem(48),
        name=name,
    )(at, *inputs, *buffers)


def weight_specs(pair, width, hidden):
    return [
        pl.BlockSpec((pair, width, 2 * hidden), lambda e, at: (e, 0, 0)),
        pl.BlockSpec((pair, width, hidden), lambda e, at: (e, 0, 2)),
    ]


def experts_forward(turn, devs, at, tokens, slot_of, member, router, weights, few, slots, buffers):
    experts, width, columns = weights.shape
    hidden = columns // 3
    pair = 1 + (experts + 1) % 2
    count = 2 * tokens[0].shape[0]
    total_experts = member.shape[0]
    return shard_call(
        functools.partial(experts_kernel, few, pair),
        "experts_forward",
        at,
        [*tokens, slot_of, member, router, weights, weights],
        [
            *(same(*half.shape) for half in tokens),
            same(experts, count),
            same(total_experts, count),
            same(total_experts, width),
            *weight_specs(pair, width, hidden),
        ],
        [
            in_place(count, width),
            in_turn(pair, turn, slots, width),
            in_turn(pair, turn, slots, 2 * hidden),
            same(experts, count),
        ],
        [
            jax.ShapeDtypeStruct((devs, count, width), low),
            jax.ShapeDtypeStruct((experts, devs, slots, width), low),
            jax.ShapeDtypeStruct((experts, devs, slots, 2 * hidden), low),
            jax.ShapeDtypeStruct((experts, count), full),
        ],
        buffers,
        [
            pltpu.VMEM((count, width), full),
            pltpu.VMEM((total_experts, count), full),
            pltpu.VMEM((pair, hidden, width), low),
        ],
        experts // pair,
    )


def experts_backward(
    turn, devs, at, d_tokens, slot_of, gates, mix_dot, router, gu, weights, few, buffers
):
    experts, width, columns = weights.shape
    hidden = columns // 3
    pair = 1 + (experts + 1) % 2
    count = 2 * d_tokens[0].shape[0]
    slots = gu.shape[2]
    lines = router.shape[0]
    return shard_call(
        functools.partial(back_kernel, few, pair),
        "experts_backward",
        at,
        [*d_tokens, slot_of, gates, mix_dot, router, gu, weights, weights],
        [
            *(same(*half.shape) for half in d_tokens),
            same(experts, count),
            same(experts, count),
            same(1, count),
            same(lines, width),
            in_turn(pair, turn, slots, 2 * hidden),
            *weight_specs(pair, width, hidden),
        ],
        [
            in_place(count, width),
            in_turn(pair, turn, slots, width),
            in_turn(pair, turn, slots, 2 * hidden),
            in_turn(pair, turn, slots, hidden),
            same(lines, count),
        ],
        [
            jax.ShapeDtypeStruct((devs, count, width), low),
            jax.ShapeDtypeStruct((experts, devs, slots, width), low),
            jax.ShapeDtypeStruct((experts, devs, slots, 2 * hidden), low),
            jax.ShapeDtypeStruct((experts, devs, slots, hidden), low),
            jax.ShapeDtypeStruct((lines, count), low),
        ],
        buffers,
        [
            pltpu.VMEM((count, width), full),
            pltpu.VMEM((lines, count), full),
            pltpu.VMEM((pair, hidden, width), low),
        ],
        experts // pair,
    )


def halving_masks(bits):
    masks = [0]
    for bit in reversed(bits):
        masks = masks + [mask ^ bit for mask in masks]
    return masks


def out_kernel(bits_a, bits_b, me_ref, rows_ref, d_ref, *refs):
    outs, acc = refs[:4], refs[4]
    half = outs[0].shape[2]
    for part, bits in enumerate((bits_a, bits_b)):
        keep, send = outs[2 * part], outs[2 * part + 1]
        rows = keep.shape[1]
        acc[...] = nn(rows_ref[...], d_ref[:, part * half : (part + 1) * half])
        for place, mask in enumerate(halving_masks(bits)):
            out = keep if place < keep.shape[0] else send
            start = pl.multiple_of((me_ref[0] ^ mask) * rows, rows)
            out[place % keep.shape[0]] = acc[pl.ds(start, rows), :].astype(low)


def out_grads(me, rows, d_proj, bits_a, bits_b):
    (height, count), width = rows.shape, d_proj.shape[1]
    devs = 2 ** len(bits_a)
    shape = (devs // 2, height // devs, width // 2)
    outs = pl.pallas_call(
        functools.partial(out_kernel, bits_a, bits_b),
        grid_spec=pltpu.PrefetchScalarGridSpec(
            num_scalar_prefetch=1,
            grid=(1,),
            in_specs=[same(height, count), same(count, width)],
            out_specs=[pl.BlockSpec(shape, lambda e, me: (0, 0, 0))] * 4,
            scratch_shapes=[pltpu.VMEM((height, width // 2), full)],
        ),
        out_shape=[jax.ShapeDtypeStruct(shape, low)] * 4,
        compiler_params=vmem(48),
        name="out_grads",
    )(me, rows, d_proj)
    return (outs[0], outs[1]), (outs[2], outs[3])


def grads_kernel(few, x_ref, dgu_ref, act_ref, d_ref, *refs):
    out_ref, down = refs[-2], refs[-1]
    hidden, width = down.shape
    out_ref[0, :, : 2 * hidden] = tn(x_ref[0], dgu_ref[0]).astype(low)
    down[...] = tn(act_ref[0], d_ref[0]).astype(low)
    chunks = width // hidden
    for dev in range(hidden // few):
        for chunk in range(chunks):
            start = (dev * chunks + chunk) * few
            out_ref[0, start : start + few, 2 * hidden :] = down[
                dev * few : (dev + 1) * few, chunk * hidden : (chunk + 1) * hidden
            ]


def weight_grads(rows, d_gu, act, d_rows, few, first, stop, buffers):
    experts, count, width = rows.shape
    hidden = act.shape[2]

    def part(*block):
        return pl.BlockSpec((1,) + block, lambda e: (first + e, 0, 0))

    return pl.pallas_call(
        functools.partial(grads_kernel, few),
        grid=(stop - first,),
        in_specs=[part(count, width), part(count, 2 * hidden), part(count, hidden), part(count, width)]
        + [pl.BlockSpec(memory_space=pl.ANY)] * len(buffers),
        out_specs=part(width, 3 * hidden),
        out_shape=jax.ShapeDtypeStruct((experts, width, 3 * hidden), low),
        scratch_shapes=[pltpu.VMEM((hidden, width), low)],
        input_output_aliases={4 + i: i for i in range(len(buffers))},
        compiler_params=vmem(56),
        name="weight_grads",
    )(rows, d_gu, act, d_rows, *buffers)


def shards(
    inputs,
    teacher,
    routes,
    valid_mask,
    block_lengths,
    gain_one,
    w_qkv,
    w_out,
    gain_two,
    w_router,
    w_gate,
    w_up,
    w_down,
):
    n = lax.axis_size("seq")
    me = lax.axis_index("seq")
    mine = lax.axis_index("fsdp")
    seqs_here, shard_len, width = inputs.shape
    assert seqs_here == 1
    seq_len = shard_len * n
    tokens_all = lax.axis_size("fsdp") * seq_len
    kv_here = KV_HEADS // n
    heads_w = kv_here * GROUP * HEAD_DIM
    group_w = kv_here * (GROUP + 2) * HEAD_DIM
    experts_here = w_gate.shape[0]
    expert_total = experts_here * n
    top_count = routes.shape[2]
    capacity = 3 * shard_len * top_count // (2 * expert_total)
    slots = -(-capacity // 16) * 16
    slot_rows = n * slots
    order_a, order_b = fsdp_bits()
    order = jnp.array(arrival_order(n), jnp.int32)[me]
    x_low = inputs.reshape(shard_len, width)

    hidden_w = w_gate.shape[2]
    down_chunks = [
        w_down[:, :, start : start + hidden_w] for start in range(0, width, hidden_w)
    ]
    weights = lax.all_gather(
        jnp.concatenate([w_gate, w_up, jnp.concatenate(down_chunks, axis=1)], axis=2),
        "fsdp",
        axis=1,
        tiled=True,
    )

    own_qkv = lax.dynamic_slice_in_dim(w_qkv, me * group_w, group_w, 1)
    small = jnp.concatenate([gain_one[:, None], gain_two[:, None], w_router], axis=1)
    small = jnp.pad(small, ((0, 0), (0, -small.shape[1] % 128)))
    plane_first = order_a[1:] + order_a[:1]
    first = Doubling(jnp.concatenate([own_qkv, small], axis=1), plane_first)
    out = Doubling(w_out, plane_first)
    valid_rows = valid_mask.reshape(shard_len).astype(full)

    routes_low = jnp.concatenate([routes.reshape(shard_len, top_count).T, valid_mask], axis=0)
    routes_low = jnp.pad(
        routes_low.astype(low), ((0, -routes_low.shape[0] % 16), (0, width - shard_len))
    )
    middle = shard_len // 2
    halves = (x_low[:middle], jnp.concatenate([x_low[middle:], routes_low], axis=0))
    positions = jnp.arange(seq_len, dtype=jnp.int32)
    cosine, sine_vals = rope_tables(positions.astype(full), HEAD_DIM)
    limit = block_limits(block_lengths[0], positions)[None]
    normed_one = jnp.zeros((seq_len, width), low)
    heads = jnp.zeros((n, kv_here, GROUP + 2, HEAD_DIM, shard_len), low)
    routes_all = []
    line = LineGather(halves)
    line.go(0)
    line.go(1)
    first.go()
    x_blocks = [line.block(0)]
    for turn in range(1, n):
        for h in (0, 1):
            if first.away:
                line.land(h, first)
                (first if first.bits else out).go()
            elif out.away and not out.late:
                line.land(h, out)
                out.go()
                out.late = True
            else:
                line.land(h, ())
            if turn < n - 1:
                line.go(h)
        x_blocks.append(line.block(turn))
    first = first.rows()
    full_qkv = first[:, :group_w]
    small = first[:, group_w : group_w + 2 + expert_total]
    full_g1 = small[:, 0].astype(full)
    full_g2 = small[:, 1].astype(full)
    router = small[:, 2:].T
    own_router = lax.dynamic_slice_in_dim(router, me * experts_here, experts_here, 0)
    own_router = jnp.pad(own_router, ((0, -experts_here % 16), (0, 0)))
    for turn in range(n):
        if turn == n - 1:
            x_blocks[turn], heads, normed_one = tie(x_blocks[turn], heads, normed_one)
        block = jnp.concatenate(x_blocks[turn])
        start = order[turn] * shard_len
        normed = rms_norm(block[:shard_len].astype(full), full_g1).astype(low)
        projected = dot("td,dc->ct", normed, full_qkv)
        projected = projected.reshape(kv_here, GROUP + 2, HEAD_DIM, shard_len)
        turned = rotate(
            projected[:, : GROUP + 1],
            lax.dynamic_slice_in_dim(cosine, start, shard_len, 1),
            lax.dynamic_slice_in_dim(sine_vals, start, shard_len, 1),
        ).astype(low)
        turned = jnp.concatenate(
            [
                turned[:, :GROUP] * jnp.asarray(attn_mult, low),
                turned[:, GROUP:],
                projected[:, GROUP + 1 :].astype(low),
            ],
            axis=1,
        )
        heads = lax.dynamic_update_index_in_dim(heads, turned, order[turn], 0)
        normed_one = lax.dynamic_update_slice_in_dim(normed_one, normed, start, 0)
        routes_all.append(block[shard_len : shard_len + top_count + 1, :shard_len])

    routes_all = jnp.stack(routes_all).astype(jnp.int32)
    valid_count = total(jnp.sum(routes_all[:, top_count]).astype(full).reshape(1, 1), "fsdp")[0, 0]
    expert_ids = jnp.arange(expert_total, dtype=jnp.int32)
    member = jnp.any(routes_all[:, :top_count, None, :] == expert_ids[:, None], axis=1)
    own_member = lax.dynamic_slice_in_dim(member, me * experts_here, experts_here, 1)
    earlier = jnp.arange(shard_len)[:, None] < jnp.arange(shard_len)[None, :]
    slot_of = dot("net,tu->neu", own_member.astype(low), earlier.astype(low)).astype(jnp.int32)
    slot_of = jnp.where(own_member, slot_of, -1)
    member = member.astype(full)

    key = jnp.moveaxis(heads[:, :, GROUP], 0, 2).reshape(kv_here, HEAD_DIM, seq_len)
    value = jnp.moveaxis(heads[:, :, GROUP + 1], 0, 2).reshape(kv_here, HEAD_DIM, seq_len)
    key_rows = jnp.swapaxes(key, 1, 2)
    value_rows = jnp.swapaxes(value, 1, 2)
    attended, out_heads, lse = attention_forward(heads, key_rows, value, limit)
    if out.away:
        attended = out.land(attended)
    moved = exchange(attended)
    full_out = out.rows()
    moved, slot_of, member, own_router, valid_count, full_out = tie(
        moved, slot_of, member, own_router, valid_count, full_out
    )
    attn_rows = by_place(nearest(*moved)).reshape(HEADS * HEAD_DIM, shard_len)
    projected = dot("kt,kd->td", attn_rows, full_out)
    hidden = x_low.astype(full) + resid_mult * projected
    normed_two, norm_two_pull = jax.vjp(rms_norm, hidden, full_g2)

    normed_low = normed_two.astype(low)
    line = LineGather((normed_low[:middle], normed_low[middle:]))
    buffers, gates, tokens = [], [], []
    line.go(0)
    line.go(1)
    other = ()
    for turn in range(n):
        if turn < n - 1:
            for h in (0, 1):
                other = line.land(h, other)
                if turn < n - 2:
                    line.go(h)
            line_slots = line.hold(slot_of[turn])
        else:
            line_slots = slot_of[turn]
        tokens.append(line.block(turn))
        *buffers, shard_gates = experts_forward(
            turn, n, jnp.stack([order[turn], me]), tokens[turn], line_slots, member[turn],
            router, weights, w_down.shape[1], slots, buffers,
        )
        gates.append(shard_gates)
        other = shard_gates
    mix_parts, expert_in, gate_up = buffers
    mixture, _ = line_scatter([mix_parts[:, :middle], mix_parts[:, middle:]], ())
    output_f32 = hidden + resid_mult * mixture
    activations = output_f32.astype(low).reshape(1, shard_len, width)
    error_rows = output_f32 - teacher.astype(full).reshape(shard_len, width)
    weighted = valid_rows[:, None] * error_rows
    loss_steps = total_steps(jnp.sum(weighted * error_rows).reshape(1, 1), "seq", "fsdp")
    squares = next(loss_steps)
    d_out = weighted * (tokens_all / valid_count)

    d_mix = resid_mult * d_out
    d_tokens = d_mix.astype(low)
    mix_dot = jnp.sum(d_mix * mixture, axis=1)[None]
    mix_high = mix_dot.astype(low)
    mix_rows = jnp.concatenate([mix_high, (mix_dot - mix_high.astype(full)).astype(low)])
    mix_rows = jnp.pad(mix_rows, ((0, 14), (0, width - shard_len)))
    line = LineGather((d_tokens[:middle], jnp.concatenate([d_tokens[middle:], mix_rows])))
    buffers, d_logits = [], []
    for turn in range(n):
        if turn:
            line.land(0, d_logits[-1])
            if turn < n - 1:
                line.go(0)
            line.land(1, ())
            if turn < n - 1:
                line.go(1)
        else:
            line.go(0)
            line.go(1)
        d_block = line.block(turn)
        mix_dot = d_block[1][middle : middle + 2, :shard_len].astype(full)
        mix_dot = jnp.sum(mix_dot, axis=0, keepdims=True)
        *buffers, shard_logits = experts_backward(
            turn, n, jnp.stack([order[turn], me]), d_block, slot_of[turn], gates[turn], mix_dot,
            own_router, gate_up, weights, w_down.shape[1], buffers,
        )
        d_logits.append(shard_logits)
    d_parts, d_rows, d_gate_up, act_low = buffers
    expert_in = expert_in.reshape(experts_here, slot_rows, width)
    d_rows = d_rows.reshape(experts_here, slot_rows, width)
    d_gate_up = d_gate_up.reshape(experts_here, slot_rows, -1)
    act_low = act_low.reshape(experts_here, slot_rows, -1)

    cut = (experts_here + 1) // 2

    def some_grads(first, stop):
        def make(before, grads):
            inputs, _ = tie((expert_in, d_gate_up, act_low, d_rows), before)
            return [weight_grads(*inputs, w_down.shape[1], first, stop, grads)]

        return make

    d_normed_two, grads = line_scatter(
        [d_parts], (some_grads(0, cut), some_grads(cut, experts_here))
    )
    expert_sum = lax.psum_scatter(grads[0], "fsdp", scatter_dimension=1, tiled=True)

    d_hidden_norm, gain_two_part = norm_two_pull(d_normed_two)
    d_hidden = d_out + d_hidden_norm
    d_proj = (resid_mult * d_hidden).astype(low)
    out_pairs = out_grads(mine.reshape(1), attn_rows, d_proj, order_a, order_b)
    out_sums = [Halving(*pair, bits) for pair, bits in zip(out_pairs, (order_a, order_b))]
    for each in out_sums:
        each.go()
    d_attended = dot("kd,td->kt", full_out, d_proj).astype(low)
    (d_attended,) = land(out_sums, d_attended)
    moved = exchange(d_attended.reshape(n, heads_w, shard_len))
    for each in out_sums:
        each.add()
    router_part = sum(
        dot("td,et->de", half, half_logits)
        for shard, shard_logits in zip(tokens, d_logits)
        for half, half_logits in (
            (shard[0], shard_logits[:experts_here, :middle]),
            (shard[1], shard_logits[:experts_here, middle:]),
        )
    )
    moved, router_part, squares = leave(out_sums, moved, router_part, squares)
    squares = loss_steps.send(squares)
    for each in out_sums:
        each.go()
    query_grad, key_grad, value_grad = attention_backward(
        heads, key_rows, value_rows, key, limit, out_heads, lse, me.reshape(1), *moved
    )
    (query_grad, key_grad, value_grad), squares = land(
        out_sums, (query_grad, key_grad, value_grad), squares
    )
    squares = loss_steps.send(squares)
    for each in out_sums:
        each.add()
        each.go()
    d_turned = jnp.concatenate([query_grad, key_grad[:, None]], axis=1).astype(full)
    d_turned = rotate(d_turned, cosine, -sine_vals).astype(low)
    d_qkv = jnp.concatenate([d_turned, value_grad[:, None]], axis=1).reshape(group_w, seq_len)
    d_parts = dot("ct,dc->td", d_qkv, full_qkv).astype(low).reshape(n, shard_len, width)
    own_columns = jnp.zeros((width, expert_total), full)
    own_columns = lax.dynamic_update_slice_in_dim(own_columns, router_part, me * experts_here, 1)
    (d_parts,) = land(out_sums, d_parts)
    for each in out_sums:
        each.add()

    out_sum = jnp.concatenate([each.finish() for each in out_sums], axis=1).astype(low)
    out_rows = out_sum.shape[0] // n
    out_parts = jnp.swapaxes(out_sum.reshape(out_sum.shape[0], n, width // n), 0, 1)
    d_parts = [
        d_parts[:, :middle],
        jnp.concatenate([d_parts[:, middle:], out_parts.reshape(n, out_rows, width)], axis=1),
    ]
    sums = {}

    def first_work(before, _):
        rows, _ = tie(d_qkv, before)
        qkv_part = jnp.concatenate(
            [dot("td,ct->dc", normed_one, rows), own_columns, gain_two_part[:, None]], axis=1
        ).astype(low)
        sums["qkv"] = rows_halving(qkv_part, order_a)
        sums["qkv"].go()
        return sums["qkv"].send

    def next_work(before, _):
        land([sums["qkv"]], before)
        sums["qkv"].add()
        sums["qkv"].go()
        return sums["qkv"].send

    ended, _ = line_scatter(d_parts, (first_work, next_work, next_work))
    qkv_sum = sums["qkv"]
    d_normed_one = ended[:shard_len]
    (ended,) = land([qkv_sum], ended)
    qkv_sum.add()
    out_own = ended[shard_len:].reshape(out_sum.shape[0], width // n)
    block = jnp.concatenate([qkv_sum.finish(), out_own], axis=1).astype(low)
    rights, lefts = [block], [block]
    _, norm_one_pull = jax.vjp(lambda v: rms_norm(v, full_g1), x_low.astype(full))
    input_grad = (d_hidden + norm_one_pull(d_normed_one)[0]).reshape(1, shard_len, width)
    few = w_down.shape[1]
    last_work = [
        lambda: expert_sum[:, :, : 2 * hidden_w].astype(full),
        lambda: jnp.concatenate(
            [
                expert_sum[:, start : start + few, 2 * hidden_w :].astype(full)
                for start in range(0, expert_sum.shape[1], few)
            ],
            axis=2,
        ),
    ]
    done = [input_grad]
    for k in range(1, n):
        right, left = line_move(rights[-1], lefts[-1], k)
        if k < 3:
            done.append(last_work[k - 1]())
        right, left, done[-1], squares = tie(right, left, done[-1], squares)
        squares = loss_steps.send(squares)
        rights.append(right)
        lefts.append(left)
    blocks = nearest(rights, lefts)
    input_grad, gate_up_grad, down_grad = done
    gate_grad, up_grad = gate_up_grad[:, :, :hidden_w], gate_up_grad[:, :, hidden_w:]
    qkv_grad = jnp.zeros((w_qkv.shape[0], QKV_W), full)
    out_grad = jnp.zeros((w_out.shape[0], width), full)
    rest = 0.0
    for k, block in enumerate(blocks):
        block = block.astype(full)
        place = (me - k) % n
        qkv_grad = lax.dynamic_update_slice_in_dim(
            qkv_grad, block[:, :group_w], place * group_w, 1
        )
        out_grad = lax.dynamic_update_slice_in_dim(
            out_grad, block[:, -(width // n) :], place * (width // n), 1
        )
        rest = rest + block[:, group_w : -(width // n)]
    router_grad, gain_two_grad = rest[:, :expert_total], rest[:, expert_total]
    gain_one_grad = jnp.sum(qkv_grad * w_qkv.astype(full), axis=1) / gain_one.astype(full)
    for _ in range(4):
        squares = loss_steps.send(squares)
    loss_value = squares[0, 0] / (valid_count * width)
    return (
        activations,
        loss_value,
        input_grad,
        gain_one_grad,
        qkv_grad,
        out_grad,
        gain_two_grad,
        router_grad,
        gate_grad,
        up_grad,
        down_grad,
    )


def solution(mesh):
    return jax.shard_map(
        shards,
        mesh=mesh,
        in_specs=(
            P("fsdp", "seq", None),
            P("fsdp", "seq", None),
            P("fsdp", "seq", None),
            P("fsdp", "seq"),
            P("fsdp", None),
            P("fsdp"),
            P("fsdp", None),
            P("fsdp", None),
            P("fsdp"),
            P("fsdp", None),
            P("seq", "fsdp", None),
            P("seq", "fsdp", None),
            P("seq", "fsdp", None),
        ),
        out_specs=(
            P("fsdp", "seq", None),
            P(),
            P("fsdp", "seq", None),
            P("fsdp"),
            P("fsdp", None),
            P("fsdp", None),
            P("fsdp"),
            P("fsdp", None),
            P("seq", "fsdp", None),
            P("seq", "fsdp", None),
            P("seq", "fsdp", None),
        ),
        check_vma=False,
    )
```

```python
import functools

import jax
import jax.numpy as jnp
from jax import lax
from jax.experimental import pallas as pl
from jax.experimental.pallas import tpu as pltpu
from jax.sharding import PartitionSpec as P

HEADS = 24
KV_HEADS = 8
HEAD_DIM = 64
BLOCK = 256
GROUP = 3
QKV_W = 2560


epsilon = 1e-06
attn_mult = 0.015625
resid_mult = 0.22
rope_base = 10000.0
masked_score = -1e30

low = jnp.bfloat16
full = jnp.float32


def dot(spec, left, right):
    return jnp.einsum(spec, left, right, preferred_element_type=full)


def rms_norm(values, gain_vec):
    inv_rms = lax.rsqrt(jnp.mean(values * values, axis=-1, keepdims=True) + epsilon)
    return values * inv_rms * gain_vec


def rope_tables(positions, head_dim):
    half_dim = head_dim // 2
    frequency = rope_base ** (-(2.0 * jnp.arange(half_dim, dtype=full)) / head_dim)
    angles = frequency[:, None] * positions[None, :]
    return (jnp.cos(angles), jnp.sin(angles))


def rotate(values, cosine, sine_vals):
    half_dim = values.shape[-2] // 2
    front_half = values[..., :half_dim, :]
    back_half = values[..., half_dim:, :]
    return jnp.concatenate(
        [front_half * cosine - back_half * sine_vals, back_half * cosine + front_half * sine_vals],
        axis=-2,
    )


def block_limits(lengths_row, positions):
    block_ends = jnp.cumsum(lengths_row)
    open_ends = jnp.where(block_ends[None, :] > positions[:, None], block_ends[None, :], positions.shape[0])
    return jnp.min(open_ends, axis=1).astype(jnp.int32)


def tie(*groups):
    return lax.optimization_barrier(groups)


def line_move(right, left, k):
    n = lax.axis_size("seq")
    return (
        lax.ppermute(right, "seq", [(i, i + 1) for i in range(k - 1, n - 1)]),
        lax.ppermute(left, "seq", [(i, i - 1) for i in range(1, n - k + 1)]),
    )


def line_gather(block):
    n = lax.axis_size("seq")
    rights, lefts = [block], [block]
    for k in range(1, n):
        right, left = tie(*line_move(rights[-1], lefts[-1], k))
        rights.append(right)
        lefts.append(left)
    return nearest(rights, lefts)


def nearest(rights, lefts):
    n = lax.axis_size("seq")
    me = lax.axis_index("seq")
    return [rights[0]] + [jnp.where(me >= k, rights[k], lefts[n - k]) for k in range(1, n)]


def arrival_order(n):
    order = []
    for me in range(n):
        both = min(me, n - 1 - me)
        places = [me]
        for k in range(1, n):
            places += [me - k] if me >= k and (k <= both or me > n - 1 - me) else []
            places += [me + k] if me + k < n and (k <= both or me < n - 1 - me) else []
        order.append(places)
    return order


def arrived(rights, lefts, turn):
    n = lax.axis_size("seq")
    me = lax.axis_index("seq")
    sources = {}
    for dev, places in enumerate(arrival_order(n)):
        gap = dev - places[turn]
        sources.setdefault(gap, []).append(dev)
    block = None
    for gap, devs in sources.items():
        moved = rights[gap] if gap >= 0 else lefts[-gap]
        if block is None:
            block = moved
        else:
            mine = jnp.array([dev in devs for dev in range(n)])[me]
            block = jnp.where(mine, moved, block)
    return block


def at_place(placed, place):
    return lax.dynamic_index_in_dim(placed, place % lax.axis_size("seq"), 0, keepdims=False)


def line_send(parts, k, right, left):
    me = lax.axis_index("seq")
    to_right, to_left = at_place(parts, me + k), at_place(parts, me - k)
    if right is not None:
        to_right = (to_right.astype(full) + right.astype(full)).astype(low)
        to_left = (to_left.astype(full) + left.astype(full)).astype(low)
    return to_right, to_left


def line_pass(to_right, to_left, k):
    n = lax.axis_size("seq")
    return (
        lax.ppermute(to_right, "seq", [(i, i + 1) for i in range(n - k)]),
        lax.ppermute(to_left, "seq", [(i, i - 1) for i in range(k, n)]),
    )


class LineGather:
    def __init__(self, halves):
        self.rights, self.lefts = [[half] for half in halves], [[half] for half in halves]
        self.landed = [0, 0]

    def go(self, h):
        step = len(self.rights[h])
        right, left = line_move(self.rights[h][-1], self.lefts[h][-1], step)
        self.rights[h].append(right)
        self.lefts[h].append(left)

    def land(self, h, other):
        spot = self.landed[h] = len(self.rights[h]) - 1
        moved = [(self.rights[part][spot], self.lefts[part][spot]) for part in range(h + 1)]
        moved, other = tie(moved, other)
        for part, (right, left) in enumerate(moved):
            self.rights[part][spot], self.lefts[part][spot] = right, left
        return other

    def hold(self, other):
        came = [(self.rights[h][-1 - self.ahead(h)], self.lefts[h][-1 - self.ahead(h)]) for h in (0, 1)]
        return tie(other, came)[0]

    def ahead(self, h):
        return len(self.rights[h]) - 1 - self.landed[h]

    def block(self, turn):
        return [arrived(self.rights[h], self.lefts[h], turn) for h in (0, 1)]


def line_scatter(halves, work):
    n = lax.axis_size("seq")
    me = lax.axis_index("seq")
    flying = [(None, None)] * len(halves)
    before, given = (), []
    for k in range(n - 1, 0, -1):
        for h, half in enumerate(halves):
            if k < n - 1 and h:
                flying[h], before = tie(flying[h], before)
            elif k < n - 1:
                flying[h], given = tie(flying[h], given)
            before = line_send(half, k, *flying[h])
            flying[h] = line_pass(*before, k)
        if n - 1 - k < len(work):
            given = work[n - 1 - k](before, given)
    sums = []
    flying[0], given = tie(flying[0], given)
    for half, (right, left) in zip(halves, flying):
        sums.append(at_place(half, me).astype(full) + (right.astype(full) + left.astype(full)))
    return jnp.concatenate(sums), given


def by_place(blocks):
    n = lax.axis_size("seq")
    me = lax.axis_index("seq")
    placed = jnp.zeros((n,) + blocks[0].shape, blocks[0].dtype)
    for k, block in enumerate(blocks):
        placed = lax.dynamic_update_index_in_dim(placed, block, (me - k) % n, 0)
    return placed


def exchange(blocks):
    n = lax.axis_size("seq")
    me = lax.axis_index("seq")
    own = at_place(blocks, me)
    rights, lefts = [own] * n, [own] * n
    for k in range(n - 1, 0, -1):
        to_right, to_left = at_place(blocks, me + k), at_place(blocks, me - k)
        rights[k] = lax.ppermute(to_right, "seq", [(i, i + k) for i in range(n - k)])
        lefts[k] = lax.ppermute(to_left, "seq", [(i, i - k) for i in range(k, n)])
    return rights, lefts


def swap(value, axis, bit):
    return lax.ppermute(value, axis, [(i, i ^ bit) for i in range(lax.axis_size(axis))])


def total(value, *axes):
    for axis in axes:
        for step in range(lax.axis_size(axis).bit_length() - 1):
            value = value + swap(value, axis, 1 << step)
    return value


def fsdp_bits():
    bits = [1 << step for step in range(lax.axis_size("fsdp").bit_length() - 1)]
    return tuple(bits), tuple(bits[:1] + bits[:0:-1])


def total_steps(value, *axes):
    for axis in axes:
        for step in range(lax.axis_size(axis).bit_length() - 1):
            here = swap(value, axis, 1 << step)
            here = yield here
            value = value + here
    while True:
        yield value


class Halving:
    def __init__(self, keep, send, bits):
        self.terms, self.send, self.bits = [keep], send, list(bits)

    def go(self):
        self.terms = self.terms + [swap(self.send, "fsdp", self.bits.pop(0))]

    def add(self):
        half = self.terms[0].shape[0] // 2
        if half:
            self.send = sum(term[half:].astype(full) for term in self.terms).astype(low)
            self.terms = [term[:half] for term in self.terms]

    def finish(self):
        while self.bits:
            self.go()
            self.add()
        return sum(term[0].astype(full) for term in self.terms)


def rows_halving(part, bits):
    devs = lax.axis_size("fsdp")
    order = lax.axis_index("fsdp") ^ jnp.array(halving_masks(bits), jnp.int32)
    blocks = part.reshape(devs, part.shape[0] // devs, part.shape[1])[order]
    return Halving(blocks[: devs // 2], blocks[devs // 2 :], bits)


def land(sums, *others):
    tied = tie([each.terms[-1] for each in sums], *others)
    for each, here in zip(sums, tied[0]):
        each.terms = each.terms[:-1] + [here]
    return tied[1:]


def leave(sums, *others):
    tied = tie([each.send for each in sums], *others)
    for each, send in zip(sums, tied[0]):
        each.send = send
    return tied[1:]


def nt(a, b):
    return lax.dot_general(a, b, (((1,), (1,)), ((), ())), preferred_element_type=full)

def nn(a, b):
    return lax.dot_general(a, b, (((1,), (0,)), ((), ())), preferred_element_type=full)

def tn(a, b):
    return lax.dot_general(a, b, (((0,), (0,)), ((), ())), preferred_element_type=full)


def beside(rows):
    return jnp.concatenate([rows[h] for h in range(GROUP)], axis=1)

def key_steps(i, seq_len, query_rows, key_rows):
    free = (i * query_rows) // key_rows
    need = ((i + 1) * query_rows + BLOCK - 1 + key_rows - 1) // key_rows
    return free, jnp.minimum(need, seq_len // key_rows)

def forward_kernel(seq_len, query_rows, key_rows, limit_ref, q_ref, k_ref, vt_ref, low_ref, out_ref, lse_ref):
    i = pl.program_id(1)
    qt = beside(q_ref[0, 0])
    width = GROUP * query_rows
    limit = jnp.concatenate([limit_ref[...]] * GROUP, axis=1)

    def step(masked, j, carry):
        peak, total, acc = carry
        start = pl.multiple_of(j * key_rows, key_rows)
        s = nn(k_ref[0, pl.ds(start, key_rows), :], qt)
        if masked:
            place = start + lax.broadcasted_iota(jnp.int32, (key_rows, 1), 0)
            s = jnp.where(place < limit, s, masked_score)
        new_peak = jnp.maximum(peak, jnp.max(s, axis=0, keepdims=True))
        shrink = jnp.exp(peak - new_peak)
        p = jnp.exp(s - new_peak)
        total = shrink * total + jnp.sum(p, axis=0, keepdims=True)
        acc = shrink * acc + nn(vt_ref[0, :, pl.ds(start, key_rows)], p.astype(low))
        return new_peak, total, acc

    free, need = key_steps(i, seq_len, query_rows, key_rows)
    carry = (
        jnp.full((1, width), masked_score, full),
        jnp.zeros((1, width), full),
        jnp.zeros((HEAD_DIM, width), full),
    )
    carry = lax.fori_loop(0, free, lambda j, c: step(False, j, c), carry)
    peak, total, acc = lax.fori_loop(free, need, lambda j, c: step(True, j, c), carry)
    out = acc / total
    lse = peak + jnp.log(total)
    for h in range(GROUP):
        cols = slice(h * query_rows, (h + 1) * query_rows)
        out_ref[0, h] = out[:, cols]
        low_ref[0, pl.ds(h * HEAD_DIM, HEAD_DIM), :] = out[:, cols].astype(low)
        lse_ref[0, h] = lse[:, cols]

def query_spec(query_rows, per):
    return pl.BlockSpec(
        (1, 1, GROUP, HEAD_DIM, query_rows), lambda g, i: (i // per, g, 0, 0, i % per)
    )


def attention_forward(heads, k_rows, vt, limit):
    kv_here, shard_len = heads.shape[1], heads.shape[4]
    seq_len = k_rows.shape[1]
    query_rows = min(256, shard_len)
    key_rows = min(512, seq_len)
    per = shard_len // query_rows
    return pl.pallas_call(
        functools.partial(forward_kernel, seq_len, query_rows, key_rows),
        grid=(kv_here, seq_len // query_rows),
        in_specs=[
            pl.BlockSpec((1, query_rows), lambda g, i: (0, i)),
            query_spec(query_rows, per),
            pl.BlockSpec((1, seq_len, HEAD_DIM), lambda g, i: (g, 0, 0)),
            pl.BlockSpec((1, HEAD_DIM, seq_len), lambda g, i: (g, 0, 0)),
        ],
        out_specs=[
            pl.BlockSpec((1, GROUP * HEAD_DIM, query_rows), lambda g, i: (i // per, g, i % per)),
            pl.BlockSpec((1, GROUP, HEAD_DIM, query_rows), lambda g, i: (g, 0, 0, i)),
            pl.BlockSpec((1, GROUP, 1, query_rows), lambda g, i: (g, 0, 0, i)),
        ],
        out_shape=[
            jax.ShapeDtypeStruct((seq_len // shard_len, kv_here * GROUP * HEAD_DIM, shard_len), low),
            jax.ShapeDtypeStruct((kv_here, GROUP, HEAD_DIM, seq_len), full),
            jax.ShapeDtypeStruct((kv_here, GROUP, 1, seq_len), full),
        ],
        compiler_params=vmem(60),
        name="attention_forward",
    )(limit, heads, k_rows, vt)

def backward_kernel(
    seq_len, query_rows, key_rows, per, me_ref, limit_ref, q_ref, k_ref, v_ref, kt_ref, out_ref, lse_ref, *refs
):
    blocks, (dq_ref, dk_ref, dv_ref, dk_acc, dv_acc, held) = refs[:-6], refs[-6:]
    i = pl.program_id(1)

    @pl.when(i == 0)
    def _():
        dk_acc[...] = jnp.zeros_like(dk_acc)
        dv_acc[...] = jnp.zeros_like(dv_acc)

    qt = beside(q_ref[0, 0])
    limit = jnp.concatenate([limit_ref[...]] * GROUP, axis=1)
    devs = (len(blocks) + 1) // 2
    gap = me_ref[0] - i // per
    for spot, block in enumerate(blocks):

        @pl.when(gap == (spot if spot < devs else devs - 1 - spot))
        def _():
            held[...] = block[...]

    dout = jnp.concatenate([held[pl.ds(h * HEAD_DIM, HEAD_DIM), :] for h in range(GROUP)], axis=1)
    delta = jnp.sum(dout.astype(full) * beside(out_ref[0]), axis=0, keepdims=True)
    lse = beside(lse_ref[0])

    def step(masked, j, dq):
        start = pl.multiple_of(j * key_rows, key_rows)
        keys = pl.ds(start, key_rows)
        s = nn(k_ref[0, keys, :], qt)
        if masked:
            place = start + lax.broadcasted_iota(jnp.int32, (key_rows, 1), 0)
            s = jnp.where(place < limit, s, masked_score)
        p = jnp.exp(s - lse)
        dp = nn(v_ref[0, keys, :], dout)
        ds = (p * (dp - delta)).astype(low)
        dk_acc[:, keys] += nt(qt, ds)
        dv_acc[:, keys] += nt(dout, p.astype(low))
        return dq + nn(kt_ref[0, :, keys], ds)

    free, need = key_steps(i, seq_len, query_rows, key_rows)
    dq = jnp.zeros((HEAD_DIM, GROUP * query_rows), full)
    dq = lax.fori_loop(0, free, lambda j, c: step(False, j, c), dq)
    dq = lax.fori_loop(free, need, lambda j, c: step(True, j, c), dq) * attn_mult
    for h in range(GROUP):
        dq_ref[0, h] = dq[:, h * query_rows : (h + 1) * query_rows].astype(low)

    @pl.when(i == pl.num_programs(1) - 1)
    def _():
        dk_ref[0] = dk_acc[...].astype(low)
        dv_ref[0] = dv_acc[...].astype(low)

def attention_backward(heads, k_rows, v_rows, kt, limit, out, lse, me, rights, lefts):
    blocks = [*rights, *lefts[1:]]
    kv_here, shard_len = heads.shape[1], heads.shape[4]
    seq_len = k_rows.shape[1]
    query_rows = min(256, shard_len)
    key_rows = min(512, seq_len)
    per = shard_len // query_rows
    quarter = lambda g, i, me: (g, 0, 0, i)
    whole = lambda g, i, me: (g, 0, 0)
    return pl.pallas_call(
        functools.partial(backward_kernel, seq_len, query_rows, key_rows, per),
        grid_spec=pltpu.PrefetchScalarGridSpec(
            num_scalar_prefetch=1,
            grid=(kv_here, seq_len // query_rows),
            in_specs=[
                pl.BlockSpec((1, query_rows), lambda g, i, me: (0, i)),
                pl.BlockSpec(
                    (1, 1, GROUP, HEAD_DIM, query_rows),
                    lambda g, i, me: (i // per, g, 0, 0, i % per),
                ),
                pl.BlockSpec((1, seq_len, HEAD_DIM), whole),
                pl.BlockSpec((1, seq_len, HEAD_DIM), whole),
                pl.BlockSpec((1, HEAD_DIM, seq_len), whole),
                pl.BlockSpec((1, GROUP, HEAD_DIM, query_rows), quarter),
                pl.BlockSpec((1, GROUP, 1, query_rows), quarter),
            ]
            + [pl.BlockSpec((GROUP * HEAD_DIM, query_rows), lambda g, i, me: (g, i % per))]
            * len(blocks),
            out_specs=[
                pl.BlockSpec((1, GROUP, HEAD_DIM, query_rows), quarter),
                pl.BlockSpec((1, HEAD_DIM, seq_len), whole),
                pl.BlockSpec((1, HEAD_DIM, seq_len), whole),
            ],
            scratch_shapes=[
                pltpu.VMEM((HEAD_DIM, seq_len), full),
                pltpu.VMEM((HEAD_DIM, seq_len), full),
                pltpu.VMEM((GROUP * HEAD_DIM, query_rows), low),
            ],
        ),
        out_shape=[
            jax.ShapeDtypeStruct((kv_here, GROUP, HEAD_DIM, seq_len), low),
            jax.ShapeDtypeStruct((kv_here, HEAD_DIM, seq_len), low),
            jax.ShapeDtypeStruct((kv_here, HEAD_DIM, seq_len), low),
        ],
        compiler_params=vmem(60),
        name="attention_backward",
    )(me, limit, heads, k_rows, v_rows, kt, out, lse, *blocks)


def vmem(mib):
    return pltpu.CompilerParams(vmem_limit_bytes=mib * 2**20)


def own_row(ref, row):
    return ref[pl.ds(row, 1), :]


def join_down(rows, block_ref, down_ref):
    hidden, width = down_ref.shape
    chunks = width // hidden
    for dev in range(hidden // rows):
        for chunk in range(chunks):
            start = (dev * chunks + chunk) * rows
            down_ref[dev * rows : (dev + 1) * rows, chunk * hidden : (chunk + 1) * hidden] = (
                block_ref[start : start + rows, :]
            )


def pick_rows(pick, tok_ref, more_ref):
    middle = tok_ref.shape[0]
    return (nn(pick[:, :middle], tok_ref[...]) + nn(pick[:, middle:], more_ref[:middle, :])).astype(low)


def experts_kernel(
    few, pair, at_ref, tok_ref, more_ref, slot_ref, member_ref, router_ref, wgu_ref, wd_ref, *refs
):
    part_ref, x_ref, gu_ref, gates_ref, acc, gates_all, down = refs[-7:]
    step, steps = pl.program_id(0), pl.num_programs(0)
    slots = x_ref.shape[2]

    @pl.when(step == 0)
    def _():
        member = member_ref[...] > 0
        logits = [nt(router_ref[...], ref[...]) for ref in (tok_ref, more_ref)]
        chosen = jnp.where(member, jnp.concatenate(logits, axis=1), masked_score)
        chosen = jnp.exp(chosen - jnp.max(chosen, axis=0, keepdims=True))
        chosen = jnp.where(member, chosen, 0.0)
        gates_all[...] = chosen / jnp.sum(chosen, axis=0, keepdims=True)
        acc[...] = jnp.zeros_like(acc)

    place = lax.broadcasted_iota(jnp.int32, (slots, 1), 0)
    puts, ys = [], []
    for i in range(pair):
        e = step * pair + i
        gate_row = own_row(gates_all, at_ref[1] * (steps * pair) + e)
        gates_ref[pl.ds(e, 1), :] = gate_row
        here = place == own_row(slot_ref, e)
        x = pick_rows(jnp.where(here, 1.0, 0.0).astype(low), tok_ref, more_ref)
        x_ref[i, 0] = x
        gu = nn(x, wgu_ref[i])
        gu_ref[i, 0] = gu.astype(low)
        hidden = gu.shape[1] // 2
        g, u = gu[:, :hidden], gu[:, hidden:]
        act = (g * jax.nn.sigmoid(g) * u).astype(low)
        join_down(few, wd_ref.at[i], down.at[i])
        ys.append(nn(act, down[i]).astype(low))
        puts.append(jnp.where(here, gate_row, 0.0).astype(low))
    acc[...] += tn(jnp.concatenate(puts), jnp.concatenate(ys))

    @pl.when(step == steps - 1)
    def _():
        part_ref[0] = acc[...].astype(low)


def back_kernel(
    few, pair, at_ref, tok_ref, more_ref, slot_ref, gates_ref, mix_ref, router_ref, gu_ref, wgu_ref, wd_ref, *refs
):
    part_ref, d_ref, dgu_ref, act_ref, dlog_ref, acc, dlog_all, down = refs[-8:]
    step, steps = pl.program_id(0), pl.num_programs(0)
    slots, hidden = gu_ref.shape[2], gu_ref.shape[3] // 2

    @pl.when(step == 0)
    def _():
        dlog_all[...] = jnp.zeros_like(dlog_all)
        acc[...] = jnp.zeros_like(acc)

    place = lax.broadcasted_iota(jnp.int32, (slots, 1), 0)
    puts, dxs = [], []
    for i in range(pair):
        e = step * pair + i
        here = place == own_row(slot_ref, e)
        pick = jnp.where(here, 1.0, 0.0).astype(low)
        gate_row = own_row(gates_ref, e)
        gate = jnp.sum(jnp.where(here, gate_row, 0.0), axis=1, keepdims=True)
        d = pick_rows(pick, tok_ref, more_ref)
        d_ref[i, 0] = d
        join_down(few, wd_ref.at[i], down.at[i])
        d_act = nt(d, down[i])
        g, u = gu_ref[i, 0, :, :hidden].astype(full), gu_ref[i, 0, :, hidden:].astype(full)
        sig = jax.nn.sigmoid(g)
        silu = g * sig
        act = silu * u
        d_gate = jnp.sum(d_act * act, axis=1, keepdims=True)
        d_gate = jnp.sum(jnp.where(here, d_gate, 0.0), axis=0, keepdims=True)
        dlog_all[pl.ds(e, 1), :] = gate_row * (d_gate - mix_ref[...])
        act_ref[i, 0] = (act * gate).astype(low)
        d_act = d_act * gate
        d_g = (d_act * u * (sig + silu * (1.0 - sig))).astype(low)
        d_u = (d_act * silu).astype(low)
        dgu_ref[i, 0, :, :hidden] = d_g
        dgu_ref[i, 0, :, hidden:] = d_u
        dxs.append(nt(dgu_ref[i, 0], wgu_ref[i]).astype(low))
        puts.append(pick)
    acc[...] += tn(jnp.concatenate(puts), jnp.concatenate(dxs))

    @pl.when(step == steps - 1)
    def _():
        dlog = dlog_all[...].astype(low)
        dlog_ref[...] = dlog
        part_ref[0] = (acc[...] + tn(dlog, router_ref[...])).astype(low)


def by_expert(*shape):
    return pl.BlockSpec((1,) + shape, lambda e, at: (e, 0, 0))


def in_turn(pair, turn, *shape):
    return pl.BlockSpec((pair, 1) + shape, lambda e, at: (e, turn, 0, 0))


def same(*shape):
    return pl.BlockSpec(shape, lambda e, at: (0, 0))


def in_place(*shape):
    return pl.BlockSpec((1,) + shape, lambda e, at: (at[0], 0, 0))


def shard_call(kernel, name, at, inputs, in_specs, out_specs, out_shape, buffers, scratch, experts):
    first = len(inputs) + 1
    aliases = {first + i: i for i in range(len(buffers))}
    return pl.pallas_call(
        kernel,
        grid_spec=pltpu.PrefetchScalarGridSpec(
            num_scalar_prefetch=1,
            grid=(experts,),
            in_specs=in_specs + [pl.BlockSpec(memory_space=pl.ANY)] * len(buffers),
            out_specs=out_specs,
            scratch_shapes=scratch,
        ),
        out_shape=out_shape,
        input_output_aliases=aliases,
        compiler_params=vmem(48),
        name=name,
    )(at, *inputs, *buffers)


def weight_specs(pair, width, hidden):
    return [
        pl.BlockSpec((pair, width, 2 * hidden), lambda e, at: (e, 0, 0)),
        pl.BlockSpec((pair, width, hidden), lambda e, at: (e, 0, 2)),
    ]


def experts_forward(turn, devs, at, tokens, slot_of, member, router, weights, few, slots, buffers):
    experts, width, columns = weights.shape
    hidden = columns // 3
    pair = 1 + (experts + 1) % 2
    count = 2 * tokens[0].shape[0]
    total_experts = member.shape[0]
    return shard_call(
        functools.partial(experts_kernel, few, pair),
        "experts_forward",
        at,
        [*tokens, slot_of, member, router, weights, weights],
        [
            *(same(*half.shape) for half in tokens),
            same(experts, count),
            same(total_experts, count),
            same(total_experts, width),
            *weight_specs(pair, width, hidden),
        ],
        [
            in_place(count, width),
            in_turn(pair, turn, slots, width),
            in_turn(pair, turn, slots, 2 * hidden),
            same(experts, count),
        ],
        [
            jax.ShapeDtypeStruct((devs, count, width), low),
            jax.ShapeDtypeStruct((experts, devs, slots, width), low),
            jax.ShapeDtypeStruct((experts, devs, slots, 2 * hidden), low),
            jax.ShapeDtypeStruct((experts, count), full),
        ],
        buffers,
        [
            pltpu.VMEM((count, width), full),
            pltpu.VMEM((total_experts, count), full),
            pltpu.VMEM((pair, hidden, width), low),
        ],
        experts // pair,
    )


def experts_backward(
    turn, devs, at, d_tokens, slot_of, gates, mix_dot, router, gu, weights, few, buffers
):
    experts, width, columns = weights.shape
    hidden = columns // 3
    pair = 1 + (experts + 1) % 2
    count = 2 * d_tokens[0].shape[0]
    slots = gu.shape[2]
    lines = router.shape[0]
    return shard_call(
        functools.partial(back_kernel, few, pair),
        "experts_backward",
        at,
        [*d_tokens, slot_of, gates, mix_dot, router, gu, weights, weights],
        [
            *(same(*half.shape) for half in d_tokens),
            same(experts, count),
            same(experts, count),
            same(1, count),
            same(lines, width),
            in_turn(pair, turn, slots, 2 * hidden),
            *weight_specs(pair, width, hidden),
        ],
        [
            in_place(count, width),
            in_turn(pair, turn, slots, width),
            in_turn(pair, turn, slots, 2 * hidden),
            in_turn(pair, turn, slots, hidden),
            same(lines, count),
        ],
        [
            jax.ShapeDtypeStruct((devs, count, width), low),
            jax.ShapeDtypeStruct((experts, devs, slots, width), low),
            jax.ShapeDtypeStruct((experts, devs, slots, 2 * hidden), low),
            jax.ShapeDtypeStruct((experts, devs, slots, hidden), low),
            jax.ShapeDtypeStruct((lines, count), low),
        ],
        buffers,
        [
            pltpu.VMEM((count, width), full),
            pltpu.VMEM((lines, count), full),
            pltpu.VMEM((pair, hidden, width), low),
        ],
        experts // pair,
    )


def halving_masks(bits):
    masks = [0]
    for bit in reversed(bits):
        masks = masks + [mask ^ bit for mask in masks]
    return masks


def out_kernel(bits_a, bits_b, me_ref, rows_ref, d_ref, *refs):
    outs, acc = refs[:4], refs[4]
    half = outs[0].shape[2]
    for part, bits in enumerate((bits_a, bits_b)):
        keep, send = outs[2 * part], outs[2 * part + 1]
        rows = keep.shape[1]
        acc[...] = nn(rows_ref[...], d_ref[:, part * half : (part + 1) * half])
        for place, mask in enumerate(halving_masks(bits)):
            out = keep if place < keep.shape[0] else send
            start = pl.multiple_of((me_ref[0] ^ mask) * rows, rows)
            out[place % keep.shape[0]] = acc[pl.ds(start, rows), :].astype(low)


def out_grads(me, rows, d_proj, bits_a, bits_b):
    (height, count), width = rows.shape, d_proj.shape[1]
    devs = 2 ** len(bits_a)
    shape = (devs // 2, height // devs, width // 2)
    outs = pl.pallas_call(
        functools.partial(out_kernel, bits_a, bits_b),
        grid_spec=pltpu.PrefetchScalarGridSpec(
            num_scalar_prefetch=1,
            grid=(1,),
            in_specs=[same(height, count), same(count, width)],
            out_specs=[pl.BlockSpec(shape, lambda e, me: (0, 0, 0))] * 4,
            scratch_shapes=[pltpu.VMEM((height, width // 2), full)],
        ),
        out_shape=[jax.ShapeDtypeStruct(shape, low)] * 4,
        compiler_params=vmem(48),
        name="out_grads",
    )(me, rows, d_proj)
    return (outs[0], outs[1]), (outs[2], outs[3])


def grads_kernel(few, x_ref, dgu_ref, act_ref, d_ref, *refs):
    out_ref, down = refs[-2], refs[-1]
    hidden, width = down.shape
    out_ref[0, :, : 2 * hidden] = tn(x_ref[0], dgu_ref[0]).astype(low)
    down[...] = tn(act_ref[0], d_ref[0]).astype(low)
    chunks = width // hidden
    for dev in range(hidden // few):
        for chunk in range(chunks):
            start = (dev * chunks + chunk) * few
            out_ref[0, start : start + few, 2 * hidden :] = down[
                dev * few : (dev + 1) * few, chunk * hidden : (chunk + 1) * hidden
            ]


def weight_grads(rows, d_gu, act, d_rows, few, first, stop, buffers):
    experts, count, width = rows.shape
    hidden = act.shape[2]

    def part(*block):
        return pl.BlockSpec((1,) + block, lambda e: (first + e, 0, 0))

    return pl.pallas_call(
        functools.partial(grads_kernel, few),
        grid=(stop - first,),
        in_specs=[part(count, width), part(count, 2 * hidden), part(count, hidden), part(count, width)]
        + [pl.BlockSpec(memory_space=pl.ANY)] * len(buffers),
        out_specs=part(width, 3 * hidden),
        out_shape=jax.ShapeDtypeStruct((experts, width, 3 * hidden), low),
        scratch_shapes=[pltpu.VMEM((hidden, width), low)],
        input_output_aliases={4 + i: i for i in range(len(buffers))},
        compiler_params=vmem(56),
        name="weight_grads",
    )(rows, d_gu, act, d_rows, *buffers)


def shards(
    inputs,
    teacher,
    routes,
    valid_mask,
    block_lengths,
    gain_one,
    w_qkv,
    w_out,
    gain_two,
    w_router,
    w_gate,
    w_up,
    w_down,
):
    n = lax.axis_size("seq")
    me = lax.axis_index("seq")
    mine = lax.axis_index("fsdp")
    seqs_here, shard_len, width = inputs.shape
    assert seqs_here == 1
    seq_len = shard_len * n
    tokens_all = lax.axis_size("fsdp") * seq_len
    kv_here = KV_HEADS // n
    heads_w = kv_here * GROUP * HEAD_DIM
    group_w = kv_here * (GROUP + 2) * HEAD_DIM
    experts_here = w_gate.shape[0]
    expert_total = experts_here * n
    top_count = routes.shape[2]
    capacity = 3 * shard_len * top_count // (2 * expert_total)
    slots = -(-capacity // 16) * 16
    slot_rows = n * slots
    order_a, order_b = fsdp_bits()
    order = jnp.array(arrival_order(n), jnp.int32)[me]
    x_low = inputs.reshape(shard_len, width)

    own_qkv = lax.dynamic_slice_in_dim(w_qkv, me * group_w, group_w, 1)
    small = jnp.concatenate([gain_one[:, None], gain_two[:, None], w_router], axis=1)
    small = jnp.pad(small, ((0, 0), (0, -small.shape[1] % 128)))
    first = lax.all_gather(
        jnp.concatenate([own_qkv, small, w_out], axis=1), "fsdp", axis=0, tiled=True
    )
    full_qkv = first[:, :group_w]
    small = first[:, group_w : group_w + 2 + expert_total]
    full_out = first[:, -width:]
    full_g1 = small[:, 0].astype(full)
    full_g2 = small[:, 1].astype(full)
    router = small[:, 2:].T
    own_router = lax.dynamic_slice_in_dim(router, me * experts_here, experts_here, 0)
    own_router = jnp.pad(own_router, ((0, -experts_here % 16), (0, 0)))
    valid_rows = valid_mask.reshape(shard_len).astype(full)

    hidden_w = w_gate.shape[2]
    down_chunks = [
        w_down[:, :, start : start + hidden_w] for start in range(0, width, hidden_w)
    ]
    weights = lax.all_gather(
        jnp.concatenate([w_gate, w_up, jnp.concatenate(down_chunks, axis=1)], axis=2),
        "fsdp",
        axis=1,
        tiled=True,
    )

    routes_low = jnp.concatenate([routes.reshape(shard_len, top_count).T, valid_mask], axis=0)
    routes_low = jnp.pad(
        routes_low.astype(low), ((0, -routes_low.shape[0] % 16), (0, width - shard_len))
    )
    middle = shard_len // 2
    halves = (x_low[:middle], jnp.concatenate([x_low[middle:], routes_low], axis=0))
    positions = jnp.arange(seq_len, dtype=jnp.int32)
    cosine, sine_vals = rope_tables(positions.astype(full), HEAD_DIM)
    limit = block_limits(block_lengths[0], positions)[None]
    normed_one = jnp.zeros((seq_len, width), low)
    heads = jnp.zeros((n, kv_here, GROUP + 2, HEAD_DIM, shard_len), low)
    routes_all = []
    line = LineGather(halves)
    for turn in range(n):
        if turn:
            line.land(0, heads if turn > 1 else ())
            if turn < n - 1:
                line.go(0)
            line.land(1, ())
            if turn < n - 1:
                line.go(1)
        else:
            line.go(0)
            line.go(1)
        block = jnp.concatenate(line.block(turn))
        start = order[turn] * shard_len
        normed = rms_norm(block[:shard_len].astype(full), full_g1).astype(low)
        projected = dot("td,dc->ct", normed, full_qkv)
        projected = projected.reshape(kv_here, GROUP + 2, HEAD_DIM, shard_len)
        turned = rotate(
            projected[:, : GROUP + 1],
            lax.dynamic_slice_in_dim(cosine, start, shard_len, 1),
            lax.dynamic_slice_in_dim(sine_vals, start, shard_len, 1),
        ).astype(low)
        turned = jnp.concatenate(
            [
                turned[:, :GROUP] * jnp.asarray(attn_mult, low),
                turned[:, GROUP:],
                projected[:, GROUP + 1 :].astype(low),
            ],
            axis=1,
        )
        heads = lax.dynamic_update_index_in_dim(heads, turned, order[turn], 0)
        normed_one = lax.dynamic_update_slice_in_dim(normed_one, normed, start, 0)
        routes_all.append(block[shard_len : shard_len + top_count + 1, :shard_len])

    routes_all = jnp.stack(routes_all).astype(jnp.int32)
    valid_count = total(jnp.sum(routes_all[:, top_count]).astype(full).reshape(1, 1), "fsdp")[0, 0]
    expert_ids = jnp.arange(expert_total, dtype=jnp.int32)
    member = jnp.any(routes_all[:, :top_count, None, :] == expert_ids[:, None], axis=1)
    own_member = lax.dynamic_slice_in_dim(member, me * experts_here, experts_here, 1)
    earlier = jnp.arange(shard_len)[:, None] < jnp.arange(shard_len)[None, :]
    slot_of = dot("net,tu->neu", own_member.astype(low), earlier.astype(low)).astype(jnp.int32)
    slot_of = jnp.where(own_member, slot_of, -1)
    member = member.astype(full)

    key = jnp.moveaxis(heads[:, :, GROUP], 0, 2).reshape(kv_here, HEAD_DIM, seq_len)
    value = jnp.moveaxis(heads[:, :, GROUP + 1], 0, 2).reshape(kv_here, HEAD_DIM, seq_len)
    key_rows = jnp.swapaxes(key, 1, 2)
    value_rows = jnp.swapaxes(value, 1, 2)
    attended, out_heads, lse = attention_forward(heads, key_rows, value, limit)
    moved = exchange(attended)
    moved, slot_of, member, own_router = tie(moved, slot_of, member, own_router)
    attn_rows = by_place(nearest(*moved)).reshape(HEADS * HEAD_DIM, shard_len)
    projected = dot("kt,kd->td", attn_rows, full_out)
    hidden = x_low.astype(full) + resid_mult * projected
    normed_two, norm_two_pull = jax.vjp(rms_norm, hidden, full_g2)

    normed_low = normed_two.astype(low)
    line = LineGather((normed_low[:middle], normed_low[middle:]))
    buffers, gates, tokens = [], [], []
    line.go(0)
    line.go(1)
    other = ()
    for turn in range(n):
        if turn < n - 1:
            for h in (0, 1):
                other = line.land(h, other)
                if turn < n - 2:
                    line.go(h)
            line_slots = line.hold(slot_of[turn])
        else:
            line_slots = slot_of[turn]
        tokens.append(line.block(turn))
        *buffers, shard_gates = experts_forward(
            turn, n, jnp.stack([order[turn], me]), tokens[turn], line_slots, member[turn],
            router, weights, w_down.shape[1], slots, buffers,
        )
        gates.append(shard_gates)
        other = shard_gates
    mix_parts, expert_in, gate_up = buffers
    mixture, _ = line_scatter([mix_parts[:, :middle], mix_parts[:, middle:]], ())
    output_f32 = hidden + resid_mult * mixture
    activations = output_f32.astype(low).reshape(1, shard_len, width)
    error_rows = output_f32 - teacher.astype(full).reshape(shard_len, width)
    weighted = valid_rows[:, None] * error_rows
    loss_steps = total_steps(jnp.sum(weighted * error_rows).reshape(1, 1), "seq", "fsdp")
    squares = next(loss_steps)
    d_out = weighted * (tokens_all / valid_count)

    d_mix = resid_mult * d_out
    d_tokens = d_mix.astype(low)
    mix_dot = jnp.sum(d_mix * mixture, axis=1)[None]
    mix_high = mix_dot.astype(low)
    mix_rows = jnp.concatenate([mix_high, (mix_dot - mix_high.astype(full)).astype(low)])
    mix_rows = jnp.pad(mix_rows, ((0, 14), (0, width - shard_len)))
    line = LineGather((d_tokens[:middle], jnp.concatenate([d_tokens[middle:], mix_rows])))
    buffers, d_logits = [], []
    for turn in range(n):
        if turn:
            line.land(0, d_logits[-1])
            if turn < n - 1:
                line.go(0)
            line.land(1, ())
            if turn < n - 1:
                line.go(1)
        else:
            line.go(0)
            line.go(1)
        d_block = line.block(turn)
        mix_dot = d_block[1][middle : middle + 2, :shard_len].astype(full)
        mix_dot = jnp.sum(mix_dot, axis=0, keepdims=True)
        *buffers, shard_logits = experts_backward(
            turn, n, jnp.stack([order[turn], me]), d_block, slot_of[turn], gates[turn], mix_dot,
            own_router, gate_up, weights, w_down.shape[1], buffers,
        )
        d_logits.append(shard_logits)
    d_parts, d_rows, d_gate_up, act_low = buffers
    expert_in = expert_in.reshape(experts_here, slot_rows, width)
    d_rows = d_rows.reshape(experts_here, slot_rows, width)
    d_gate_up = d_gate_up.reshape(experts_here, slot_rows, -1)
    act_low = act_low.reshape(experts_here, slot_rows, -1)

    cut = (experts_here + 1) // 2

    def some_grads(first, stop):
        def make(before, grads):
            inputs, _ = tie((expert_in, d_gate_up, act_low, d_rows), before)
            return [weight_grads(*inputs, w_down.shape[1], first, stop, grads)]

        return make

    d_normed_two, grads = line_scatter(
        [d_parts], (some_grads(0, cut), some_grads(cut, experts_here))
    )
    expert_sum = lax.psum_scatter(grads[0], "fsdp", scatter_dimension=1, tiled=True)

    d_hidden_norm, gain_two_part = norm_two_pull(d_normed_two)
    d_hidden = d_out + d_hidden_norm
    d_proj = (resid_mult * d_hidden).astype(low)
    out_pairs = out_grads(mine.reshape(1), attn_rows, d_proj, order_a, order_b)
    out_sums = [Halving(*pair, bits) for pair, bits in zip(out_pairs, (order_a, order_b))]
    for each in out_sums:
        each.go()
    d_attended = dot("kd,td->kt", full_out, d_proj).astype(low)
    (d_attended,) = land(out_sums, d_attended)
    moved = exchange(d_attended.reshape(n, heads_w, shard_len))
    for each in out_sums:
        each.add()
    router_part = sum(
        dot("td,et->de", half, half_logits)
        for shard, shard_logits in zip(tokens, d_logits)
        for half, half_logits in (
            (shard[0], shard_logits[:experts_here, :middle]),
            (shard[1], shard_logits[:experts_here, middle:]),
        )
    )
    own_columns = jnp.zeros((width, expert_total), full)
    own_columns = lax.dynamic_update_slice_in_dim(own_columns, router_part, me * experts_here, 1)
    own_columns = jnp.concatenate([own_columns, gain_two_part[:, None]], axis=1).astype(low)
    moved, own_columns, squares = leave(out_sums, moved, own_columns, squares)
    squares = loss_steps.send(squares)
    for each in out_sums:
        each.go()
    query_grad, key_grad, value_grad = attention_backward(
        heads, key_rows, value_rows, key, limit, out_heads, lse, me.reshape(1), *moved
    )
    (query_grad, key_grad, value_grad), squares = land(
        out_sums, (query_grad, key_grad, value_grad), squares
    )
    squares = loss_steps.send(squares)
    for each in out_sums:
        each.add()
        each.go()
    d_turned = jnp.concatenate([query_grad, key_grad[:, None]], axis=1).astype(full)
    d_turned = rotate(d_turned, cosine, -sine_vals).astype(low)
    d_qkv = jnp.concatenate([d_turned, value_grad[:, None]], axis=1).reshape(group_w, seq_len)
    d_parts = dot("ct,dc->td", d_qkv, full_qkv).astype(low).reshape(n, shard_len, width)
    (d_parts,) = land(out_sums, d_parts)
    for each in out_sums:
        each.add()

    out_sum = jnp.concatenate([each.finish() for each in out_sums], axis=1).astype(low)
    out_rows = out_sum.shape[0] // n
    out_parts = jnp.swapaxes(out_sum.reshape(out_sum.shape[0], n, width // n), 0, 1)
    d_parts = [
        d_parts[:, :middle],
        jnp.concatenate([d_parts[:, middle:], out_parts.reshape(n, out_rows, width)], axis=1),
    ]
    sums = {}

    def first_work(before, _):
        rows, _ = tie(d_qkv, before)
        qkv_part = jnp.concatenate(
            [dot("td,ct->dc", normed_one, rows).astype(low), own_columns], axis=1
        )
        sums["qkv"] = rows_halving(qkv_part, order_a)
        sums["qkv"].go()
        return sums["qkv"].send

    def next_work(before, _):
        land([sums["qkv"]], before)
        sums["qkv"].add()
        sums["qkv"].go()
        return sums["qkv"].send

    ended, _ = line_scatter(d_parts, (first_work, next_work, next_work))
    qkv_sum = sums["qkv"]
    d_normed_one = ended[:shard_len]
    (ended,) = land([qkv_sum], ended)
    qkv_sum.add()
    out_own = ended[shard_len:].reshape(out_sum.shape[0], width // n)
    block = jnp.concatenate([qkv_sum.finish(), out_own], axis=1).astype(low)
    rights, lefts = [block], [block]
    _, norm_one_pull = jax.vjp(lambda v: rms_norm(v, full_g1), x_low.astype(full))
    input_grad = (d_hidden + norm_one_pull(d_normed_one)[0]).reshape(1, shard_len, width)
    few = w_down.shape[1]
    last_work = [
        lambda: expert_sum[:, :, : 2 * hidden_w].astype(full),
        lambda: jnp.concatenate(
            [
                expert_sum[:, start : start + few, 2 * hidden_w :].astype(full)
                for start in range(0, expert_sum.shape[1], few)
            ],
            axis=2,
        ),
    ]
    done = [input_grad]
    for k in range(1, n):
        right, left = line_move(rights[-1], lefts[-1], k)
        if k < 3:
            done.append(last_work[k - 1]())
        right, left, done[-1], squares = tie(right, left, done[-1], squares)
        squares = loss_steps.send(squares)
        rights.append(right)
        lefts.append(left)
    input_grad, gate_up_grad, down_grad = done
    gate_grad, up_grad = gate_up_grad[:, :, :hidden_w], gate_up_grad[:, :, hidden_w:]
    qkv_grad = jnp.zeros((w_qkv.shape[0], QKV_W), full)
    out_grad = jnp.zeros((w_out.shape[0], width), full)
    rest = 0.0
    for turn in range(n):
        block = arrived(rights, lefts, turn).astype(full)
        place = order[turn]
        qkv_grad = lax.dynamic_update_slice_in_dim(
            qkv_grad, block[:, :group_w], place * group_w, 1
        )
        out_grad = lax.dynamic_update_slice_in_dim(
            out_grad, block[:, -(width // n) :], place * (width // n), 1
        )
        rest = rest + block[:, group_w : -(width // n)]
    router_grad, gain_two_grad = rest[:, :expert_total], rest[:, expert_total]
    gain_one_grad = jnp.sum(qkv_grad * w_qkv.astype(full), axis=1) / gain_one.astype(full)
    for _ in range(4):
        squares = loss_steps.send(squares)
    loss_value = squares[0, 0] / (valid_count * width)
    return (
        activations,
        loss_value,
        input_grad,
        gain_one_grad,
        qkv_grad,
        out_grad,
        gain_two_grad,
        router_grad,
        gate_grad,
        up_grad,
        down_grad,
    )


def solution(mesh):
    return jax.shard_map(
        shards,
        mesh=mesh,
        in_specs=(
            P("fsdp", "seq", None),
            P("fsdp", "seq", None),
            P("fsdp", "seq", None),
            P("fsdp", "seq"),
            P("fsdp", None),
            P("fsdp"),
            P("fsdp", None),
            P("fsdp", None),
            P("fsdp"),
            P("fsdp", None),
            P("seq", "fsdp", None),
            P("seq", "fsdp", None),
            P("seq", "fsdp", None),
        ),
        out_specs=(
            P("fsdp", "seq", None),
            P(),
            P("fsdp", "seq", None),
            P("fsdp"),
            P("fsdp", None),
            P("fsdp", None),
            P("fsdp"),
            P("fsdp", None),
            P("seq", "fsdp", None),
            P("seq", "fsdp", None),
            P("seq", "fsdp", None),
        ),
        check_vma=False,
    )
```

```python
import functools

import jax
import jax.numpy as jnp
from jax import lax
from jax.experimental import pallas as pl
from jax.experimental.pallas import tpu as pltpu
from jax.sharding import PartitionSpec as P

HEADS = 24
KV_HEADS = 8
HEAD_DIM = 64
BLOCK = 256
GROUP = 3
QKV_W = 2560


epsilon = 1e-06
attn_mult = 0.015625
resid_mult = 0.22
rope_base = 10000.0
masked_score = -1e30

low = jnp.bfloat16
full = jnp.float32


def dot(spec, left, right):
    return jnp.einsum(spec, left, right, preferred_element_type=full)


def rms_norm(values, gain_vec):
    inv_rms = lax.rsqrt(jnp.mean(values * values, axis=-1, keepdims=True) + epsilon)
    return values * inv_rms * gain_vec


def rope_tables(positions, head_dim):
    half_dim = head_dim // 2
    frequency = rope_base ** (-(2.0 * jnp.arange(half_dim, dtype=full)) / head_dim)
    angles = frequency[:, None] * positions[None, :]
    return (jnp.cos(angles), jnp.sin(angles))


def rotate(values, cosine, sine_vals):
    half_dim = values.shape[-2] // 2
    front_half = values[..., :half_dim, :]
    back_half = values[..., half_dim:, :]
    return jnp.concatenate(
        [front_half * cosine - back_half * sine_vals, back_half * cosine + front_half * sine_vals],
        axis=-2,
    )


def block_limits(lengths_row, positions):
    block_ends = jnp.cumsum(lengths_row)
    open_ends = jnp.where(block_ends[None, :] > positions[:, None], block_ends[None, :], positions.shape[0])
    return jnp.min(open_ends, axis=1).astype(jnp.int32)


def tie(*groups):
    return lax.optimization_barrier(groups)


def line_move(right, left, k):
    n = lax.axis_size("seq")
    return (
        lax.ppermute(right, "seq", [(i, i + 1) for i in range(k - 1, n - 1)]),
        lax.ppermute(left, "seq", [(i, i - 1) for i in range(1, n - k + 1)]),
    )


def line_gather(block):
    n = lax.axis_size("seq")
    rights, lefts = [block], [block]
    for k in range(1, n):
        right, left = tie(*line_move(rights[-1], lefts[-1], k))
        rights.append(right)
        lefts.append(left)
    return nearest(rights, lefts)


def nearest(rights, lefts):
    n = lax.axis_size("seq")
    me = lax.axis_index("seq")
    return [rights[0]] + [jnp.where(me >= k, rights[k], lefts[n - k]) for k in range(1, n)]


def arrival_order(n):
    order = []
    for me in range(n):
        both = min(me, n - 1 - me)
        places = [me]
        for k in range(1, n):
            places += [me - k] if me >= k and (k <= both or me > n - 1 - me) else []
            places += [me + k] if me + k < n and (k <= both or me < n - 1 - me) else []
        order.append(places)
    return order


def arrivals(n, turn):
    return [dev - places[turn] for dev, places in enumerate(arrival_order(n))]


def arrived(rights, lefts, turn):
    gaps = arrivals(lax.axis_size("seq"), turn)
    block = None
    for gap in sorted(set(gaps)):
        moved = rights[gap] if gap >= 0 else lefts[-gap]
        if block is None:
            block = moved
        else:
            mine = jnp.array([each == gap for each in gaps])[lax.axis_index("seq")]
            block = jnp.where(mine, moved, block)
    return block


def at_place(placed, place):
    return lax.dynamic_index_in_dim(placed, place % lax.axis_size("seq"), 0, keepdims=False)


def line_send(to_right, to_left, right, left):
    if right is not None:
        to_right = (to_right.astype(full) + right.astype(full)).astype(low)
        to_left = (to_left.astype(full) + left.astype(full)).astype(low)
    return to_right, to_left


def line_pass(to_right, to_left, k):
    n = lax.axis_size("seq")
    return (
        lax.ppermute(to_right, "seq", [(i, i + 1) for i in range(n - k)]),
        lax.ppermute(to_left, "seq", [(i, i - 1) for i in range(k, n)]),
    )


class Doubling:
    def __init__(self, block, bits):
        self.blocks, self.order, self.bits = block[None], bits, list(bits)
        self.away = False

    def go(self):
        self.here, self.away = swap(self.blocks, "fsdp", self.bits.pop(0)), True

    def land(self, other):
        other, here = tie(other, self.here)
        self.blocks, self.away = jnp.concatenate([self.blocks, here]), False
        return other

    def rows(self):
        while self.bits or self.away:
            if not self.away:
                self.go()
            self.land(())
        mask = lax.axis_index("fsdp") ^ jnp.arange(self.blocks.shape[0])
        spot = sum(((mask // bit) % 2) << i for i, bit in enumerate(self.order))
        return self.blocks[spot].reshape(-1, self.blocks.shape[2])


class LineGather:
    def __init__(self, halves):
        self.rights, self.lefts = [[half] for half in halves], [[half] for half in halves]
        self.landed = [0, 0]

    def go(self, h):
        step = len(self.rights[h])
        right, left = line_move(self.rights[h][-1], self.lefts[h][-1], step)
        self.rights[h].append(right)
        self.lefts[h].append(left)

    def land(self, h, other):
        spot = self.landed[h] = len(self.rights[h]) - 1
        if isinstance(other, Doubling):
            self.rights[h][spot], self.lefts[h][spot] = other.land(
                (self.rights[h][spot], self.lefts[h][spot])
            )
            other = ()
        moved = [(self.rights[part][spot], self.lefts[part][spot]) for part in range(h + 1)]
        moved, other = tie(moved, other)
        for part, (right, left) in enumerate(moved):
            self.rights[part][spot], self.lefts[part][spot] = right, left
        return other

    def hold(self, other):
        came = [(self.rights[h][-1 - self.ahead(h)], self.lefts[h][-1 - self.ahead(h)]) for h in (0, 1)]
        return tie(other, came)[0]

    def ahead(self, h):
        return len(self.rights[h]) - 1 - self.landed[h]

    def choice(self, turn):
        gaps = arrivals(lax.axis_size("seq"), turn)
        places = sorted(set(gaps))
        return jnp.array([places.index(gap) for gap in gaps], jnp.int32)[lax.axis_index("seq")]

    def blocks(self, turn):
        places = sorted(set(arrivals(lax.axis_size("seq"), turn)))
        return [
            [rights[gap] if gap >= 0 else lefts[-gap] for gap in places]
            for rights, lefts in zip(self.rights, self.lefts)
        ]

    def block(self, turn):
        return [arrived(self.rights[h], self.lefts[h], turn) for h in (0, 1)]


def line_scatter(count, get, work):
    n = lax.axis_size("seq")
    flying = [(None, None)] * count
    before, given = (), []
    for k in range(n - 1, 0, -1):
        for h in range(count):
            if k < n - 1 and h:
                flying[h], before = tie(flying[h], before)
            elif k < n - 1:
                flying[h], given = tie(flying[h], given)
            before = line_send(get(h, k), get(h, -k), *flying[h])
            flying[h] = line_pass(*before, k)
        if n - 1 - k < len(work):
            given = work[n - 1 - k](before, given)
    sums = []
    flying[0], given = tie(flying[0], given)
    for h, (right, left) in enumerate(flying):
        sums.append(get(h, 0).astype(full) + (right.astype(full) + left.astype(full)))
    return jnp.concatenate(sums), given


def by_place(blocks):
    n = lax.axis_size("seq")
    me = lax.axis_index("seq")
    placed = jnp.zeros((n,) + blocks[0].shape, blocks[0].dtype)
    for k, block in enumerate(blocks):
        placed = lax.dynamic_update_index_in_dim(placed, block, (me - k) % n, 0)
    return placed


def exchange(blocks):
    n = lax.axis_size("seq")
    me = lax.axis_index("seq")
    own = at_place(blocks, me)
    rights, lefts = [own] * n, [own] * n
    for k in range(n - 1, 0, -1):
        to_right, to_left = at_place(blocks, me + k), at_place(blocks, me - k)
        rights[k] = lax.ppermute(to_right, "seq", [(i, i + k) for i in range(n - k)])
        lefts[k] = lax.ppermute(to_left, "seq", [(i, i - k) for i in range(k, n)])
    return rights, lefts


def swap(value, axis, bit):
    return lax.ppermute(value, axis, [(i, i ^ bit) for i in range(lax.axis_size(axis))])


def total(value, *axes):
    for axis in axes:
        for step in range(lax.axis_size(axis).bit_length() - 1):
            value = value + swap(value, axis, 1 << step)
    return value


def fsdp_bits():
    bits = [1 << step for step in range(lax.axis_size("fsdp").bit_length() - 1)]
    return tuple(bits), tuple(bits[:1] + bits[:0:-1])


def total_steps(value, *axes):
    for axis in axes:
        for step in range(lax.axis_size(axis).bit_length() - 1):
            here = swap(value, axis, 1 << step)
            here = yield here
            value = value + here
    while True:
        yield value


class Halving:
    def __init__(self, keep, send, bits):
        self.terms, self.send, self.bits = [keep], send, list(bits)

    def go(self):
        self.terms = self.terms + [swap(self.send, "fsdp", self.bits.pop(0))]

    def add(self):
        half = self.terms[0].shape[0] // 2
        if half:
            self.send = sum(term[half:].astype(full) for term in self.terms).astype(low)
            self.terms = [term[:half] for term in self.terms]

    def finish(self):
        while self.bits:
            self.go()
            self.add()
        return sum(term[0].astype(full) for term in self.terms)


def rows_halving(part, bits):
    devs = lax.axis_size("fsdp")
    order = lax.axis_index("fsdp") ^ jnp.array(halving_masks(bits), jnp.int32)
    blocks = part.reshape(devs, part.shape[0] // devs, part.shape[1])[order]
    return Halving(blocks[: devs // 2], blocks[devs // 2 :], bits)


def land(sums, *others):
    tied = tie([each.terms[-1] for each in sums], *others)
    for each, here in zip(sums, tied[0]):
        each.terms = each.terms[:-1] + [here]
    return tied[1:]


def leave(sums, *others):
    tied = tie([each.send for each in sums], *others)
    for each, send in zip(sums, tied[0]):
        each.send = send
    return tied[1:]


def nt(a, b):
    return lax.dot_general(a, b, (((1,), (1,)), ((), ())), preferred_element_type=full)

def nn(a, b):
    return lax.dot_general(a, b, (((1,), (0,)), ((), ())), preferred_element_type=full)

def tn(a, b):
    return lax.dot_general(a, b, (((0,), (0,)), ((), ())), preferred_element_type=full)


def beside(rows):
    return jnp.concatenate([rows[h] for h in range(GROUP)], axis=1)

def key_steps(i, seq_len, query_rows, key_rows):
    free = (i * query_rows) // key_rows
    need = ((i + 1) * query_rows + BLOCK - 1 + key_rows - 1) // key_rows
    return free, jnp.minimum(need, seq_len // key_rows)

def forward_kernel(seq_len, query_rows, key_rows, limit_ref, q_ref, k_ref, vt_ref, low_ref, out_ref, lse_ref):
    i = pl.program_id(1)
    qt = beside(q_ref[0, 0])
    width = GROUP * query_rows
    limit = jnp.concatenate([limit_ref[...]] * GROUP, axis=1)

    def step(masked, j, carry):
        peak, total, acc = carry
        start = pl.multiple_of(j * key_rows, key_rows)
        s = nn(k_ref[0, pl.ds(start, key_rows), :], qt)
        if masked:
            place = start + lax.broadcasted_iota(jnp.int32, (key_rows, 1), 0)
            s = jnp.where(place < limit, s, masked_score)
        new_peak = jnp.maximum(peak, jnp.max(s, axis=0, keepdims=True))
        shrink = jnp.exp(peak - new_peak)
        p = jnp.exp(s - new_peak)
        total = shrink * total + jnp.sum(p, axis=0, keepdims=True)
        acc = shrink * acc + nn(vt_ref[0, :, pl.ds(start, key_rows)], p.astype(low))
        return new_peak, total, acc

    free, need = key_steps(i, seq_len, query_rows, key_rows)
    carry = (
        jnp.full((1, width), masked_score, full),
        jnp.zeros((1, width), full),
        jnp.zeros((HEAD_DIM, width), full),
    )
    carry = lax.fori_loop(0, free, lambda j, c: step(False, j, c), carry)
    peak, total, acc = lax.fori_loop(free, need, lambda j, c: step(True, j, c), carry)
    out = acc / total
    lse = peak + jnp.log(total)
    for h in range(GROUP):
        cols = slice(h * query_rows, (h + 1) * query_rows)
        out_ref[0, h] = out[:, cols]
        low_ref[0, pl.ds(h * HEAD_DIM, HEAD_DIM), :] = out[:, cols].astype(low)
        lse_ref[0, h] = lse[:, cols]

def query_spec(query_rows, per):
    return pl.BlockSpec(
        (1, 1, GROUP, HEAD_DIM, query_rows), lambda g, i: (i // per, g, 0, 0, i % per)
    )


def attention_forward(heads, k_rows, vt, limit):
    kv_here, shard_len = heads.shape[1], heads.shape[4]
    seq_len = k_rows.shape[1]
    query_rows = min(256, shard_len)
    key_rows = min(512, seq_len)
    per = shard_len // query_rows
    return pl.pallas_call(
        functools.partial(forward_kernel, seq_len, query_rows, key_rows),
        grid=(kv_here, seq_len // query_rows),
        in_specs=[
            pl.BlockSpec((1, query_rows), lambda g, i: (0, i)),
            query_spec(query_rows, per),
            pl.BlockSpec((1, seq_len, HEAD_DIM), lambda g, i: (g, 0, 0)),
            pl.BlockSpec((1, HEAD_DIM, seq_len), lambda g, i: (g, 0, 0)),
        ],
        out_specs=[
            pl.BlockSpec((1, GROUP * HEAD_DIM, query_rows), lambda g, i: (i // per, g, i % per)),
            pl.BlockSpec((1, GROUP, HEAD_DIM, query_rows), lambda g, i: (g, 0, 0, i)),
            pl.BlockSpec((1, GROUP, 1, query_rows), lambda g, i: (g, 0, 0, i)),
        ],
        out_shape=[
            jax.ShapeDtypeStruct((seq_len // shard_len, kv_here * GROUP * HEAD_DIM, shard_len), low),
            jax.ShapeDtypeStruct((kv_here, GROUP, HEAD_DIM, seq_len), full),
            jax.ShapeDtypeStruct((kv_here, GROUP, 1, seq_len), full),
        ],
        compiler_params=vmem(60),
        name="attention_forward",
    )(limit, heads, k_rows, vt)

def backward_kernel(
    seq_len, query_rows, key_rows, per, me_ref, limit_ref, q_ref, k_ref, v_ref, kt_ref, out_ref, lse_ref, *refs
):
    blocks, (dq_ref, dk_ref, dv_ref, dk_acc, dv_acc, held) = refs[:-6], refs[-6:]
    i = pl.program_id(1)

    @pl.when(i == 0)
    def _():
        dk_acc[...] = jnp.zeros_like(dk_acc)
        dv_acc[...] = jnp.zeros_like(dv_acc)

    qt = beside(q_ref[0, 0])
    limit = jnp.concatenate([limit_ref[...]] * GROUP, axis=1)
    devs = (len(blocks) + 1) // 2
    gap = me_ref[0] - i // per
    for spot, block in enumerate(blocks):

        @pl.when(gap == (spot if spot < devs else devs - 1 - spot))
        def _():
            held[...] = block[...]

    dout = jnp.concatenate([held[pl.ds(h * HEAD_DIM, HEAD_DIM), :] for h in range(GROUP)], axis=1)
    delta = jnp.sum(dout.astype(full) * beside(out_ref[0]), axis=0, keepdims=True)
    lse = beside(lse_ref[0])

    def step(masked, j, dq):
        start = pl.multiple_of(j * key_rows, key_rows)
        keys = pl.ds(start, key_rows)
        s = nn(k_ref[0, keys, :], qt)
        if masked:
            place = start + lax.broadcasted_iota(jnp.int32, (key_rows, 1), 0)
            s = jnp.where(place < limit, s, masked_score)
        p = jnp.exp(s - lse)
        dp = nn(v_ref[0, keys, :], dout)
        ds = (p * (dp - delta)).astype(low)
        dk_acc[:, keys] += nt(qt, ds)
        dv_acc[:, keys] += nt(dout, p.astype(low))
        return dq + nn(kt_ref[0, :, keys], ds)

    free, need = key_steps(i, seq_len, query_rows, key_rows)
    dq = jnp.zeros((HEAD_DIM, GROUP * query_rows), full)
    dq = lax.fori_loop(0, free, lambda j, c: step(False, j, c), dq)
    dq = lax.fori_loop(free, need, lambda j, c: step(True, j, c), dq) * attn_mult
    for h in range(GROUP):
        dq_ref[0, h] = dq[:, h * query_rows : (h + 1) * query_rows].astype(low)

    @pl.when(i == pl.num_programs(1) - 1)
    def _():
        dk_ref[0] = dk_acc[...].astype(low)
        dv_ref[0] = dv_acc[...].astype(low)

def attention_backward(heads, k_rows, v_rows, kt, limit, out, lse, me, rights, lefts):
    blocks = [*rights, *lefts[1:]]
    kv_here, shard_len = heads.shape[1], heads.shape[4]
    seq_len = k_rows.shape[1]
    query_rows = min(256, shard_len)
    key_rows = min(512, seq_len)
    per = shard_len // query_rows
    quarter = lambda g, i, me: (g, 0, 0, i)
    whole = lambda g, i, me: (g, 0, 0)
    return pl.pallas_call(
        functools.partial(backward_kernel, seq_len, query_rows, key_rows, per),
        grid_spec=pltpu.PrefetchScalarGridSpec(
            num_scalar_prefetch=1,
            grid=(kv_here, seq_len // query_rows),
            in_specs=[
                pl.BlockSpec((1, query_rows), lambda g, i, me: (0, i)),
                pl.BlockSpec(
                    (1, 1, GROUP, HEAD_DIM, query_rows),
                    lambda g, i, me: (i // per, g, 0, 0, i % per),
                ),
                pl.BlockSpec((1, seq_len, HEAD_DIM), whole),
                pl.BlockSpec((1, seq_len, HEAD_DIM), whole),
                pl.BlockSpec((1, HEAD_DIM, seq_len), whole),
                pl.BlockSpec((1, GROUP, HEAD_DIM, query_rows), quarter),
                pl.BlockSpec((1, GROUP, 1, query_rows), quarter),
            ]
            + [pl.BlockSpec((GROUP * HEAD_DIM, query_rows), lambda g, i, me: (g, i % per))]
            * len(blocks),
            out_specs=[
                pl.BlockSpec((1, GROUP, HEAD_DIM, query_rows), quarter),
                pl.BlockSpec((1, HEAD_DIM, seq_len), whole),
                pl.BlockSpec((1, HEAD_DIM, seq_len), whole),
            ],
            scratch_shapes=[
                pltpu.VMEM((HEAD_DIM, seq_len), full),
                pltpu.VMEM((HEAD_DIM, seq_len), full),
                pltpu.VMEM((GROUP * HEAD_DIM, query_rows), low),
            ],
        ),
        out_shape=[
            jax.ShapeDtypeStruct((kv_here, GROUP, HEAD_DIM, seq_len), low),
            jax.ShapeDtypeStruct((kv_here, HEAD_DIM, seq_len), low),
            jax.ShapeDtypeStruct((kv_here, HEAD_DIM, seq_len), low),
        ],
        compiler_params=vmem(60),
        name="attention_backward",
    )(me, limit, heads, k_rows, v_rows, kt, out, lse, *blocks)


def vmem(mib):
    return pltpu.CompilerParams(vmem_limit_bytes=mib * 2**20)


def own_row(ref, row):
    return ref[pl.ds(row, 1), :]


def join_down(rows, block_ref, down_ref):
    hidden, width = down_ref.shape
    chunks = width // hidden
    for dev in range(hidden // rows):
        for chunk in range(chunks):
            start = (dev * chunks + chunk) * rows
            down_ref[dev * rows : (dev + 1) * rows, chunk * hidden : (chunk + 1) * hidden] = (
                block_ref[start : start + rows, :]
            )


def pick_rows(pick, tok_ref, more_ref):
    middle = tok_ref.shape[0]
    return (nn(pick[:, :middle], tok_ref[...]) + nn(pick[:, middle:], more_ref[:middle, :])).astype(low)


def take_tokens(choices, at_ref, refs, tok_ref, more_ref, sems):
    for choice in range(choices):

        @pl.when(at_ref[2] == choice)
        def _():
            copies = [
                pltpu.make_async_copy(refs[choice], tok_ref, sems.at[0]),
                pltpu.make_async_copy(refs[choices + choice], more_ref, sems.at[1]),
            ]
            for copy in copies:
                copy.start()
            for copy in copies:
                copy.wait()


def experts_kernel(
    few, pair, choices, at_ref, slot_ref, member_ref, router_ref, wgu_ref, wd_ref, *refs
):
    part_ref, x_ref, gu_ref, gates_ref, acc, gates_all, down, tok_ref, more_ref, sems = refs[-10:]
    step, steps = pl.program_id(0), pl.num_programs(0)
    slots = x_ref.shape[2]

    @pl.when(step == 0)
    def _():
        take_tokens(choices, at_ref, refs, tok_ref, more_ref, sems)
        member = member_ref[...] > 0
        logits = [nt(router_ref[...], ref[...]) for ref in (tok_ref, more_ref)]
        chosen = jnp.where(member, jnp.concatenate(logits, axis=1), masked_score)
        chosen = jnp.exp(chosen - jnp.max(chosen, axis=0, keepdims=True))
        chosen = jnp.where(member, chosen, 0.0)
        gates_all[...] = chosen / jnp.sum(chosen, axis=0, keepdims=True)
        acc[...] = jnp.zeros_like(acc)

    place = lax.broadcasted_iota(jnp.int32, (slots, 1), 0)
    puts, ys = [], []
    for i in range(pair):
        e = step * pair + i
        gate_row = own_row(gates_all, at_ref[1] * (steps * pair) + e)
        gates_ref[pl.ds(e, 1), :] = gate_row
        here = place == own_row(slot_ref, e)
        x = pick_rows(jnp.where(here, 1.0, 0.0).astype(low), tok_ref, more_ref)
        x_ref[i, 0] = x
        gu = nn(x, wgu_ref[i])
        gu_ref[i, 0] = gu.astype(low)
        hidden = gu.shape[1] // 2
        g, u = gu[:, :hidden], gu[:, hidden:]
        act = (g * jax.nn.sigmoid(g) * u).astype(low)
        join_down(few, wd_ref.at[i], down.at[i])
        ys.append(nn(act, down[i]).astype(low))
        puts.append(jnp.where(here, gate_row, 0.0).astype(low))
    acc[...] += tn(jnp.concatenate(puts), jnp.concatenate(ys))

    @pl.when(step == steps - 1)
    def _():
        part_ref[0] = acc[...].astype(low)


def back_kernel(
    few, pair, choices, at_ref, slot_ref, gates_ref, router_ref, gu_ref, wgu_ref, wd_ref, *refs
):
    part_ref, d_ref, dgu_ref, act_ref, dlog_ref, acc, dlog_all, down, tok_ref, more_ref, sems = refs[-11:]
    step, steps = pl.program_id(0), pl.num_programs(0)
    slots, hidden = gu_ref.shape[2], gu_ref.shape[3] // 2

    @pl.when(step == 0)
    def _():
        take_tokens(choices, at_ref, refs, tok_ref, more_ref, sems)
        dlog_all[...] = jnp.zeros_like(dlog_all)
        acc[...] = jnp.zeros_like(acc)

    middle, count = tok_ref.shape[0], slot_ref.shape[1]
    mix = more_ref[middle : middle + 2, :count].astype(full)
    mix = mix[0:1, :] + mix[1:2, :]
    place = lax.broadcasted_iota(jnp.int32, (slots, 1), 0)
    puts, dxs = [], []
    for i in range(pair):
        e = step * pair + i
        here = place == own_row(slot_ref, e)
        pick = jnp.where(here, 1.0, 0.0).astype(low)
        gate_row = own_row(gates_ref, e)
        gate = jnp.sum(jnp.where(here, gate_row, 0.0), axis=1, keepdims=True)
        d = pick_rows(pick, tok_ref, more_ref)
        d_ref[i, 0] = d
        join_down(few, wd_ref.at[i], down.at[i])
        d_act = nt(d, down[i])
        g, u = gu_ref[i, 0, :, :hidden].astype(full), gu_ref[i, 0, :, hidden:].astype(full)
        sig = jax.nn.sigmoid(g)
        silu = g * sig
        act = silu * u
        d_gate = jnp.sum(d_act * act, axis=1, keepdims=True)
        d_gate = jnp.sum(jnp.where(here, d_gate, 0.0), axis=0, keepdims=True)
        dlog_all[pl.ds(e, 1), :] = gate_row * (d_gate - mix)
        act_ref[i, 0] = (act * gate).astype(low)
        d_act = d_act * gate
        d_g = (d_act * u * (sig + silu * (1.0 - sig))).astype(low)
        d_u = (d_act * silu).astype(low)
        dgu_ref[i, 0, :, :hidden] = d_g
        dgu_ref[i, 0, :, hidden:] = d_u
        dxs.append(nt(dgu_ref[i, 0], wgu_ref[i]).astype(low))
        puts.append(pick)
    acc[...] += tn(jnp.concatenate(puts), jnp.concatenate(dxs))

    @pl.when(step == steps - 1)
    def _():
        dlog = dlog_all[...].astype(low)
        dlog_ref[...] = dlog
        part_ref[0] = (acc[...] + tn(dlog, router_ref[...])).astype(low)


def by_expert(*shape):
    return pl.BlockSpec((1,) + shape, lambda e, at: (e, 0, 0))


def in_turn(pair, turn, *shape):
    return pl.BlockSpec((pair, 1) + shape, lambda e, at: (e, turn, 0, 0))


def same(*shape):
    return pl.BlockSpec(shape, lambda e, at: (0, 0))


def in_place(*shape):
    return pl.BlockSpec((1,) + shape, lambda e, at: (at[0], 0, 0))


def shard_call(kernel, name, at, inputs, in_specs, out_specs, out_shape, buffers, scratch, experts):
    first = len(inputs) + 1
    aliases = {first + i: i for i in range(len(buffers))}
    return pl.pallas_call(
        kernel,
        grid_spec=pltpu.PrefetchScalarGridSpec(
            num_scalar_prefetch=1,
            grid=(experts,),
            in_specs=in_specs
            + [pl.BlockSpec(memory_space=pl.ANY)] * (len(inputs) + len(buffers) - len(in_specs)),
            out_specs=out_specs,
            scratch_shapes=scratch,
        ),
        out_shape=out_shape,
        input_output_aliases=aliases,
        compiler_params=vmem(48),
        name=name,
    )(at, *inputs, *buffers)


def weight_specs(pair, width, hidden):
    return [
        pl.BlockSpec((pair, width, 2 * hidden), lambda e, at: (e, 0, 0)),
        pl.BlockSpec((pair, width, hidden), lambda e, at: (e, 0, 2)),
    ]


def experts_forward(turn, devs, at, tokens, slot_of, member, router, weights, few, slots, buffers):
    experts, width, columns = weights.shape
    hidden = columns // 3
    pair = 1 + (experts + 1) % 2
    count = slot_of.shape[1]
    total_experts = member.shape[0]
    return shard_call(
        functools.partial(experts_kernel, few, pair, len(tokens[0])),
        "experts_forward",
        at,
        [slot_of, member, router, weights, weights, *tokens[0], *tokens[1]],
        [
            same(experts, count),
            same(total_experts, count),
            same(total_experts, width),
            *weight_specs(pair, width, hidden),
        ],
        [
            in_place(count, width),
            in_turn(pair, turn, slots, width),
            in_turn(pair, turn, slots, 2 * hidden),
            same(experts, count),
        ],
        [
            jax.ShapeDtypeStruct((devs, count, width), low),
            jax.ShapeDtypeStruct((experts, devs, slots, width), low),
            jax.ShapeDtypeStruct((experts, devs, slots, 2 * hidden), low),
            jax.ShapeDtypeStruct((experts, count), full),
        ],
        buffers,
        [
            pltpu.VMEM((count, width), full),
            pltpu.VMEM((total_experts, count), full),
            pltpu.VMEM((pair, hidden, width), low),
            *(pltpu.VMEM(half[0].shape, low) for half in tokens),
            pltpu.SemaphoreType.DMA((2,)),
        ],
        experts // pair,
    )


def experts_backward(
    turn, devs, at, d_tokens, slot_of, gates, router, gu, weights, few, buffers
):
    experts, width, columns = weights.shape
    hidden = columns // 3
    pair = 1 + (experts + 1) % 2
    count = slot_of.shape[1]
    slots = gu.shape[2]
    lines = router.shape[0]
    return shard_call(
        functools.partial(back_kernel, few, pair, len(d_tokens[0])),
        "experts_backward",
        at,
        [slot_of, gates, router, gu, weights, weights, *d_tokens[0], *d_tokens[1]],
        [
            same(experts, count),
            same(experts, count),
            same(lines, width),
            in_turn(pair, turn, slots, 2 * hidden),
            *weight_specs(pair, width, hidden),
        ],
        [
            in_place(count, width),
            in_turn(pair, turn, slots, width),
            in_turn(pair, turn, slots, 2 * hidden),
            in_turn(pair, turn, slots, hidden),
            same(lines, count),
        ],
        [
            jax.ShapeDtypeStruct((devs, count, width), low),
            jax.ShapeDtypeStruct((experts, devs, slots, width), low),
            jax.ShapeDtypeStruct((experts, devs, slots, 2 * hidden), low),
            jax.ShapeDtypeStruct((experts, devs, slots, hidden), low),
            jax.ShapeDtypeStruct((lines, count), low),
        ],
        buffers,
        [
            pltpu.VMEM((count, width), full),
            pltpu.VMEM((lines, count), full),
            pltpu.VMEM((pair, hidden, width), low),
            *(pltpu.VMEM(half[0].shape, low) for half in d_tokens),
            pltpu.SemaphoreType.DMA((2,)),
        ],
        experts // pair,
    )


def halving_masks(bits):
    masks = [0]
    for bit in reversed(bits):
        masks = masks + [mask ^ bit for mask in masks]
    return masks


def out_kernel(bits_a, bits_b, me_ref, rows_ref, d_ref, *refs):
    outs, acc = refs[:4], refs[4]
    half = outs[0].shape[2]
    for part, bits in enumerate((bits_a, bits_b)):
        keep, send = outs[2 * part], outs[2 * part + 1]
        rows = keep.shape[1]
        acc[...] = nn(rows_ref[...], d_ref[:, part * half : (part + 1) * half])
        for place, mask in enumerate(halving_masks(bits)):
            out = keep if place < keep.shape[0] else send
            start = pl.multiple_of((me_ref[0] ^ mask) * rows, rows)
            out[place % keep.shape[0]] = acc[pl.ds(start, rows), :].astype(low)


def out_grads(me, rows, d_proj, bits_a, bits_b):
    (height, count), width = rows.shape, d_proj.shape[1]
    devs = 2 ** len(bits_a)
    shape = (devs // 2, height // devs, width // 2)
    outs = pl.pallas_call(
        functools.partial(out_kernel, bits_a, bits_b),
        grid_spec=pltpu.PrefetchScalarGridSpec(
            num_scalar_prefetch=1,
            grid=(1,),
            in_specs=[same(height, count), same(count, width)],
            out_specs=[pl.BlockSpec(shape, lambda e, me: (0, 0, 0))] * 4,
            scratch_shapes=[pltpu.VMEM((height, width // 2), full)],
        ),
        out_shape=[jax.ShapeDtypeStruct(shape, low)] * 4,
        compiler_params=vmem(48),
        name="out_grads",
    )(me, rows, d_proj)
    return (outs[0], outs[1]), (outs[2], outs[3])


def grads_kernel(few, x_ref, dgu_ref, act_ref, d_ref, *refs):
    out_ref, down = refs[-2], refs[-1]
    hidden, width = down.shape
    out_ref[0, :, : 2 * hidden] = tn(x_ref[0], dgu_ref[0]).astype(low)
    down[...] = tn(act_ref[0], d_ref[0]).astype(low)
    chunks = width // hidden
    for dev in range(hidden // few):
        for chunk in range(chunks):
            start = (dev * chunks + chunk) * few
            out_ref[0, start : start + few, 2 * hidden :] = down[
                dev * few : (dev + 1) * few, chunk * hidden : (chunk + 1) * hidden
            ]


def weight_grads(rows, d_gu, act, d_rows, few, first, stop, buffers):
    experts, count, width = rows.shape
    hidden = act.shape[2]

    def part(*block):
        return pl.BlockSpec((1,) + block, lambda e: (first + e, 0, 0))

    return pl.pallas_call(
        functools.partial(grads_kernel, few),
        grid=(stop - first,),
        in_specs=[part(count, width), part(count, 2 * hidden), part(count, hidden), part(count, width)]
        + [pl.BlockSpec(memory_space=pl.ANY)] * len(buffers),
        out_specs=part(width, 3 * hidden),
        out_shape=jax.ShapeDtypeStruct((experts, width, 3 * hidden), low),
        scratch_shapes=[pltpu.VMEM((hidden, width), low)],
        input_output_aliases={4 + i: i for i in range(len(buffers))},
        compiler_params=vmem(56),
        name="weight_grads",
    )(rows, d_gu, act, d_rows, *buffers)


def shards(
    inputs,
    teacher,
    routes,
    valid_mask,
    block_lengths,
    gain_one,
    w_qkv,
    w_out,
    gain_two,
    w_router,
    w_gate,
    w_up,
    w_down,
):
    n = lax.axis_size("seq")
    me = lax.axis_index("seq")
    mine = lax.axis_index("fsdp")
    seqs_here, shard_len, width = inputs.shape
    assert seqs_here == 1
    seq_len = shard_len * n
    tokens_all = lax.axis_size("fsdp") * seq_len
    kv_here = KV_HEADS // n
    heads_w = kv_here * GROUP * HEAD_DIM
    group_w = kv_here * (GROUP + 2) * HEAD_DIM
    experts_here = w_gate.shape[0]
    expert_total = experts_here * n
    top_count = routes.shape[2]
    capacity = 3 * shard_len * top_count // (2 * expert_total)
    slots = -(-capacity // 16) * 16
    slot_rows = n * slots
    order_a, order_b = fsdp_bits()
    order = jnp.array(arrival_order(n), jnp.int32)[me]
    x_low = inputs.reshape(shard_len, width)

    own_qkv = lax.dynamic_slice_in_dim(w_qkv, me * group_w, group_w, 1)
    small = jnp.concatenate([gain_one[:, None], gain_two[:, None], w_router], axis=1)
    small = jnp.pad(small, ((0, 0), (0, -small.shape[1] % 128)))
    first = lax.all_gather(
        jnp.concatenate([own_qkv, small], axis=1), "fsdp", axis=0, tiled=True
    )
    out = Doubling(w_out, order_a[1:] + order_a[:1])
    full_qkv = first[:, :group_w]
    small = first[:, group_w : group_w + 2 + expert_total]
    full_g1 = small[:, 0].astype(full)
    full_g2 = small[:, 1].astype(full)
    router = small[:, 2:].T
    own_router = lax.dynamic_slice_in_dim(router, me * experts_here, experts_here, 0)
    own_router = jnp.pad(own_router, ((0, -experts_here % 16), (0, 0)))
    valid_rows = valid_mask.reshape(shard_len).astype(full)

    hidden_w = w_gate.shape[2]

    routes_low = jnp.concatenate([routes.reshape(shard_len, top_count).T, valid_mask], axis=0)
    routes_low = jnp.pad(
        routes_low.astype(low), ((0, -routes_low.shape[0] % 16), (0, width - shard_len))
    )
    middle = shard_len // 2
    halves = (x_low[:middle], jnp.concatenate([x_low[middle:], routes_low], axis=0))
    positions = jnp.arange(seq_len, dtype=jnp.int32)
    cosine, sine_vals = rope_tables(positions.astype(full), HEAD_DIM)
    limit = block_limits(block_lengths[0], positions)[None]
    normed_one = jnp.zeros((seq_len, width), low)
    heads = jnp.zeros((n, kv_here, GROUP + 2, HEAD_DIM, shard_len), low)
    routes_all = []
    line = LineGather(halves)
    line.go(0)
    line.go(1)
    out.go()
    for turn in range(n):
        if turn:
            line.land(0, heads if turn > 1 else ())
        if 0 < turn < n - 1:
            line.go(0)
        if turn == 2:
            line.land(1, out)
            out.go()
        elif turn:
            line.land(1, ())
        if 0 < turn < n - 1:
            line.go(1)
        block = jnp.concatenate(line.block(turn))
        start = order[turn] * shard_len
        normed = rms_norm(block[:shard_len].astype(full), full_g1).astype(low)
        projected = dot("td,dc->ct", normed, full_qkv)
        projected = projected.reshape(kv_here, GROUP + 2, HEAD_DIM, shard_len)
        turned = rotate(
            projected[:, : GROUP + 1],
            lax.dynamic_slice_in_dim(cosine, start, shard_len, 1),
            lax.dynamic_slice_in_dim(sine_vals, start, shard_len, 1),
        ).astype(low)
        turned = jnp.concatenate(
            [
                turned[:, :GROUP] * jnp.asarray(attn_mult, low),
                turned[:, GROUP:],
                projected[:, GROUP + 1 :].astype(low),
            ],
            axis=1,
        )
        heads = lax.dynamic_update_index_in_dim(heads, turned, order[turn], 0)
        normed_one = lax.dynamic_update_slice_in_dim(normed_one, normed, start, 0)
        routes_all.append(block[shard_len : shard_len + top_count + 1, :shard_len])

    down_chunks = [
        w_down[:, :, start : start + hidden_w] for start in range(0, width, hidden_w)
    ]
    weights = lax.all_gather(
        jnp.concatenate([w_gate, w_up, jnp.concatenate(down_chunks, axis=1)], axis=2),
        "fsdp",
        axis=1,
        tiled=True,
    )

    routes_all = jnp.stack(routes_all).astype(jnp.int32)
    valid_count = total(jnp.sum(routes_all[:, top_count]).astype(full).reshape(1, 1), "fsdp")[0, 0]
    expert_ids = jnp.arange(expert_total, dtype=jnp.int32)
    member = jnp.any(routes_all[:, :top_count, None, :] == expert_ids[:, None], axis=1)
    own_member = lax.dynamic_slice_in_dim(member, me * experts_here, experts_here, 1)
    earlier = jnp.arange(shard_len)[:, None] < jnp.arange(shard_len)[None, :]
    slot_of = dot("net,tu->neu", own_member.astype(low), earlier.astype(low)).astype(jnp.int32)
    slot_of = jnp.where(own_member, slot_of, -1)
    member = member.astype(full)

    key = jnp.moveaxis(heads[:, :, GROUP], 0, 2).reshape(kv_here, HEAD_DIM, seq_len)
    value = jnp.moveaxis(heads[:, :, GROUP + 1], 0, 2).reshape(kv_here, HEAD_DIM, seq_len)
    key_rows = jnp.swapaxes(key, 1, 2)
    value_rows = jnp.swapaxes(value, 1, 2)
    attended, out_heads, lse = attention_forward(heads, key_rows, value, limit)
    attended = out.land(attended)
    moved = exchange(attended)
    full_out = out.rows()
    moved, slot_of, member, own_router, full_out = tie(moved, slot_of, member, own_router, full_out)
    attn_rows = by_place(nearest(*moved)).reshape(HEADS * HEAD_DIM, shard_len)
    projected = dot("kt,kd->td", attn_rows, full_out)
    hidden = x_low.astype(full) + resid_mult * projected
    normed_two, norm_two_pull = jax.vjp(rms_norm, hidden, full_g2)

    normed_low = normed_two.astype(low)
    line = LineGather((normed_low[:middle], normed_low[middle:]))
    buffers, gates, tokens = [], [], []
    line.go(0)
    line.go(1)
    other = ()
    for turn in range(n):
        if turn < n - 1:
            for h in (0, 1):
                other = line.land(h, other)
                if turn < n - 2:
                    line.go(h)
            line_slots = line.hold(slot_of[turn])
        else:
            line_slots = slot_of[turn]
        tokens.append(line.block(turn))
        *buffers, shard_gates = experts_forward(
            turn, n, jnp.stack([order[turn], me, line.choice(turn)]), line.blocks(turn), line_slots,
            member[turn], router, weights, w_down.shape[1], slots, buffers,
        )
        gates.append(shard_gates)
        other = shard_gates
    mix_parts, expert_in, gate_up = buffers
    cuts = (slice(0, middle), slice(middle, None))
    mixture, _ = line_scatter(2, lambda h, shift: at_place(mix_parts[:, cuts[h]], me + shift), ())
    output_f32 = hidden + resid_mult * mixture
    activations = output_f32.astype(low).reshape(1, shard_len, width)
    error_rows = output_f32 - teacher.astype(full).reshape(shard_len, width)
    weighted = valid_rows[:, None] * error_rows
    loss_steps = total_steps(jnp.sum(weighted * error_rows).reshape(1, 1), "seq", "fsdp")
    squares = next(loss_steps)
    d_out = weighted * (tokens_all / valid_count)

    d_mix = resid_mult * d_out
    d_tokens = d_mix.astype(low)
    mix_dot = jnp.sum(d_mix * mixture, axis=1)[None]
    mix_high = mix_dot.astype(low)
    mix_rows = jnp.concatenate([mix_high, (mix_dot - mix_high.astype(full)).astype(low)])
    mix_rows = jnp.pad(mix_rows, ((0, 14), (0, width - shard_len)))
    line = LineGather((d_tokens[:middle], jnp.concatenate([d_tokens[middle:], mix_rows])))
    buffers, d_logits = [], []
    for turn in range(n):
        if turn:
            line.land(0, d_logits[-1])
            if turn < n - 1:
                line.go(0)
            line.land(1, ())
            if turn < n - 1:
                line.go(1)
        else:
            line.go(0)
            line.go(1)
        *buffers, shard_logits = experts_backward(
            turn, n, jnp.stack([order[turn], me, line.choice(turn)]), line.blocks(turn), slot_of[turn],
            gates[turn], own_router, gate_up, weights, w_down.shape[1], buffers,
        )
        d_logits.append(shard_logits)
    d_parts, d_rows, d_gate_up, act_low = buffers
    expert_in = expert_in.reshape(experts_here, slot_rows, width)
    d_rows = d_rows.reshape(experts_here, slot_rows, width)
    d_gate_up = d_gate_up.reshape(experts_here, slot_rows, -1)
    act_low = act_low.reshape(experts_here, slot_rows, -1)

    cut = (experts_here + 1) // 2

    def some_grads(first, stop):
        def make(before, grads):
            inputs, _ = tie((expert_in, d_gate_up, act_low, d_rows), before)
            return [weight_grads(*inputs, w_down.shape[1], first, stop, grads)]

        return make

    d_normed_two, grads = line_scatter(
        1,
        lambda h, shift: at_place(d_parts, me + shift),
        (some_grads(0, cut), some_grads(cut, experts_here)),
    )
    expert_sum = lax.psum_scatter(grads[0], "fsdp", scatter_dimension=1, tiled=True)

    d_hidden_norm, gain_two_part = norm_two_pull(d_normed_two)
    d_hidden = d_out + d_hidden_norm
    d_proj = (resid_mult * d_hidden).astype(low)
    d_attended = dot("kd,td->kt", full_out, d_proj).astype(low)
    moved = exchange(d_attended.reshape(n, heads_w, shard_len))
    d_proj, _ = tie(d_proj, d_attended)
    out_pairs = out_grads(mine.reshape(1), attn_rows, d_proj, order_a, order_b)
    out_sums = [Halving(*pair, bits) for pair, bits in zip(out_pairs, (order_a, order_b))]
    for each in out_sums:
        each.go()
        each.add()
    router_part = sum(
        dot("td,et->de", half, half_logits)
        for shard, shard_logits in zip(tokens, d_logits)
        for half, half_logits in (
            (shard[0], shard_logits[:experts_here, :middle]),
            (shard[1], shard_logits[:experts_here, middle:]),
        )
    )
    own_columns = jnp.zeros((width, expert_total), full)
    own_columns = lax.dynamic_update_slice_in_dim(own_columns, router_part, me * experts_here, 1)
    own_columns = jnp.concatenate([own_columns, gain_two_part[:, None]], axis=1).astype(low)
    moved, own_columns, squares = leave(out_sums, moved, own_columns, squares)
    squares = loss_steps.send(squares)
    for each in out_sums:
        each.go()
    query_grad, key_grad, value_grad = attention_backward(
        heads, key_rows, value_rows, key, limit, out_heads, lse, me.reshape(1), *moved
    )
    (query_grad, key_grad, value_grad), squares = land(
        out_sums, (query_grad, key_grad, value_grad), squares
    )
    squares = loss_steps.send(squares)
    for each in out_sums:
        each.add()
        each.go()
    d_turned = jnp.concatenate([query_grad, key_grad[:, None]], axis=1).astype(full)
    d_turned = rotate(d_turned, cosine, -sine_vals).astype(low)
    d_qkv = jnp.concatenate([d_turned, value_grad[:, None]], axis=1).reshape(group_w, seq_len)

    def d_part(rows, shift):
        start = (me + shift) % n * shard_len
        rows = lax.dynamic_slice_in_dim(rows, start, shard_len, 1)
        return dot("ct,dc->td", rows, full_qkv).astype(low)

    d_parts = {shift: d_part(d_qkv, shift) for shift in {1, n - 1}}
    (d_parts,) = land(out_sums, d_parts)
    for each in out_sums:
        each.add()

    out_sum = jnp.concatenate([each.finish() for each in out_sums], axis=1).astype(low)
    out_rows = out_sum.shape[0] // n
    out_parts = jnp.swapaxes(out_sum.reshape(out_sum.shape[0], n, width // n), 0, 1)
    out_parts = out_parts.reshape(n, out_rows, width)

    def get(h, shift):
        part = d_parts[shift % n]
        if h == 0:
            return part[:middle]
        return jnp.concatenate([part[middle:], at_place(out_parts, me + shift)])

    sums = {}

    def first_work(before, _):
        rows, _ = tie(d_qkv, before)
        for shift in range(n):
            if shift not in d_parts:
                d_parts[shift] = d_part(rows, shift)
        qkv_part = jnp.concatenate(
            [dot("td,ct->dc", normed_one, rows).astype(low), own_columns], axis=1
        )
        sums["qkv"] = rows_halving(qkv_part, order_a)
        sums["qkv"].go()
        return sums["qkv"].send

    def next_work(before, _):
        land([sums["qkv"]], before)
        sums["qkv"].add()
        sums["qkv"].go()
        return sums["qkv"].send

    ended, _ = line_scatter(2, get, (first_work, next_work, next_work))
    qkv_sum = sums["qkv"]
    d_normed_one = ended[:shard_len]
    (ended,) = land([qkv_sum], ended)
    qkv_sum.add()
    out_own = ended[shard_len:].reshape(out_sum.shape[0], width // n)
    block = jnp.concatenate([qkv_sum.finish(), out_own], axis=1).astype(low)
    rights, lefts = [block], [block]
    _, norm_one_pull = jax.vjp(lambda v: rms_norm(v, full_g1), x_low.astype(full))
    input_grad = (d_hidden + norm_one_pull(d_normed_one)[0]).reshape(1, shard_len, width)
    few = w_down.shape[1]
    last_work = [
        lambda: expert_sum[:, :, : 2 * hidden_w].astype(full),
        lambda: jnp.concatenate(
            [
                expert_sum[:, start : start + few, 2 * hidden_w :].astype(full)
                for start in range(0, expert_sum.shape[1], few)
            ],
            axis=2,
        ),
    ]
    done = [input_grad]
    for k in range(1, n):
        right, left = line_move(rights[-1], lefts[-1], k)
        if k < 3:
            done.append(last_work[k - 1]())
        right, left, done[-1], squares = tie(right, left, done[-1], squares)
        squares = loss_steps.send(squares)
        rights.append(right)
        lefts.append(left)
    input_grad, gate_up_grad, down_grad = done
    gate_grad, up_grad = gate_up_grad[:, :, :hidden_w], gate_up_grad[:, :, hidden_w:]
    qkv_grad = jnp.zeros((w_qkv.shape[0], QKV_W), full)
    out_grad = jnp.zeros((w_out.shape[0], width), full)
    rest = gain_sum = 0.0
    for turn in range(n):
        block = arrived(rights, lefts, turn).astype(full)
        own_part, out_part = block[:, :group_w], block[:, -(width // n) :]
        start = order[turn] * group_w
        qkv_grad = lax.dynamic_update_slice_in_dim(qkv_grad, own_part, start, 1)
        out_grad = lax.dynamic_update_slice_in_dim(out_grad, out_part, order[turn] * (width // n), 1)
        own_part = own_part * lax.dynamic_slice_in_dim(w_qkv, start, group_w, 1).astype(full)
        gain_sum = gain_sum + jnp.sum(own_part, axis=1)
        rest = rest + block[:, group_w : -(width // n)]
    router_grad, gain_two_grad = rest[:, :expert_total], rest[:, expert_total]
    gain_one_grad = gain_sum / gain_one.astype(full)
    for _ in range(4):
        squares = loss_steps.send(squares)
    loss_value = squares[0, 0] / (valid_count * width)
    return (
        activations,
        loss_value,
        input_grad,
        gain_one_grad,
        qkv_grad,
        out_grad,
        gain_two_grad,
        router_grad,
        gate_grad,
        up_grad,
        down_grad,
    )


def solution(mesh):
    return jax.shard_map(
        shards,
        mesh=mesh,
        in_specs=(
            P("fsdp", "seq", None),
            P("fsdp", "seq", None),
            P("fsdp", "seq", None),
            P("fsdp", "seq"),
            P("fsdp", None),
            P("fsdp"),
            P("fsdp", None),
            P("fsdp", None),
            P("fsdp"),
            P("fsdp", None),
            P("seq", "fsdp", None),
            P("seq", "fsdp", None),
            P("seq", "fsdp", None),
        ),
        out_specs=(
            P("fsdp", "seq", None),
            P(),
            P("fsdp", "seq", None),
            P("fsdp"),
            P("fsdp", None),
            P("fsdp", None),
            P("fsdp"),
            P("fsdp", None),
            P("seq", "fsdp", None),
            P("seq", "fsdp", None),
            P("seq", "fsdp", None),
        ),
        check_vma=False,
    )
```

```python
import functools

import jax
import jax.numpy as jnp
from jax import lax
from jax.experimental import pallas as pl
from jax.experimental.pallas import tpu as pltpu
from jax.sharding import PartitionSpec as P

HEADS = 24
KV_HEADS = 8
HEAD_DIM = 64
BLOCK = 256
GROUP = 3
QKV_W = 2560


epsilon = 1e-06
attn_mult = 0.015625
resid_mult = 0.22
rope_base = 10000.0
masked_score = -1e30

low = jnp.bfloat16
full = jnp.float32


def dot(spec, left, right):
    return jnp.einsum(spec, left, right, preferred_element_type=full)


def rms_norm(values, gain_vec):
    inv_rms = lax.rsqrt(jnp.mean(values * values, axis=-1, keepdims=True) + epsilon)
    return values * inv_rms * gain_vec


def rope_tables(positions, head_dim):
    half_dim = head_dim // 2
    frequency = rope_base ** (-(2.0 * jnp.arange(half_dim, dtype=full)) / head_dim)
    angles = frequency[:, None] * positions[None, :]
    return (jnp.cos(angles), jnp.sin(angles))


def rotate(values, cosine, sine_vals):
    half_dim = values.shape[-2] // 2
    front_half = values[..., :half_dim, :]
    back_half = values[..., half_dim:, :]
    return jnp.concatenate(
        [front_half * cosine - back_half * sine_vals, back_half * cosine + front_half * sine_vals],
        axis=-2,
    )


def block_limits(lengths_row, positions):
    block_ends = jnp.cumsum(lengths_row)
    open_ends = jnp.where(block_ends[None, :] > positions[:, None], block_ends[None, :], positions.shape[0])
    return jnp.min(open_ends, axis=1).astype(jnp.int32)


def tie(*groups):
    return lax.optimization_barrier(groups)


def line_move(right, left, k):
    n = lax.axis_size("seq")
    return (
        lax.ppermute(right, "seq", [(i, i + 1) for i in range(k - 1, n - 1)]),
        lax.ppermute(left, "seq", [(i, i - 1) for i in range(1, n - k + 1)]),
    )


def line_gather(block):
    n = lax.axis_size("seq")
    rights, lefts = [block], [block]
    for k in range(1, n):
        right, left = tie(*line_move(rights[-1], lefts[-1], k))
        rights.append(right)
        lefts.append(left)
    return nearest(rights, lefts)


def nearest(rights, lefts):
    n = lax.axis_size("seq")
    me = lax.axis_index("seq")
    return [rights[0]] + [jnp.where(me >= k, rights[k], lefts[n - k]) for k in range(1, n)]


def arrival_order(n):
    order = []
    for me in range(n):
        both = min(me, n - 1 - me)
        places = [me]
        for k in range(1, n):
            places += [me - k] if me >= k and (k <= both or me > n - 1 - me) else []
            places += [me + k] if me + k < n and (k <= both or me < n - 1 - me) else []
        order.append(places)
    return order


def arrived(rights, lefts, turn):
    n = lax.axis_size("seq")
    me = lax.axis_index("seq")
    sources = {}
    for dev, places in enumerate(arrival_order(n)):
        gap = dev - places[turn]
        sources.setdefault(gap, []).append(dev)
    block = None
    for gap, devs in sources.items():
        moved = rights[gap] if gap >= 0 else lefts[-gap]
        if block is None:
            block = moved
        else:
            mine = jnp.array([dev in devs for dev in range(n)])[me]
            block = jnp.where(mine, moved, block)
    return block


def at_place(placed, place):
    return lax.dynamic_index_in_dim(placed, place % lax.axis_size("seq"), 0, keepdims=False)


def line_send(to_right, to_left, right, left):
    if right is not None:
        to_right = (to_right.astype(full) + right.astype(full)).astype(low)
        to_left = (to_left.astype(full) + left.astype(full)).astype(low)
    return to_right, to_left


def line_pass(to_right, to_left, k):
    n = lax.axis_size("seq")
    return (
        lax.ppermute(to_right, "seq", [(i, i + 1) for i in range(n - k)]),
        lax.ppermute(to_left, "seq", [(i, i - 1) for i in range(k, n)]),
    )


class LineGather:
    def __init__(self, halves):
        self.rights, self.lefts = [[half] for half in halves], [[half] for half in halves]
        self.landed = [0, 0]

    def go(self, h):
        step = len(self.rights[h])
        right, left = line_move(self.rights[h][-1], self.lefts[h][-1], step)
        self.rights[h].append(right)
        self.lefts[h].append(left)

    def land(self, h, other):
        spot = self.landed[h] = len(self.rights[h]) - 1
        moved = [(self.rights[part][spot], self.lefts[part][spot]) for part in range(h + 1)]
        moved, other = tie(moved, other)
        for part, (right, left) in enumerate(moved):
            self.rights[part][spot], self.lefts[part][spot] = right, left
        return other

    def hold(self, other):
        came = [(self.rights[h][-1 - self.ahead(h)], self.lefts[h][-1 - self.ahead(h)]) for h in (0, 1)]
        return tie(other, came)[0]

    def ahead(self, h):
        return len(self.rights[h]) - 1 - self.landed[h]

    def block(self, turn):
        return [arrived(self.rights[h], self.lefts[h], turn) for h in (0, 1)]


def line_scatter(count, get, work):
    n = lax.axis_size("seq")
    flying = [(None, None)] * count
    before, given = (), []
    for k in range(n - 1, 0, -1):
        for h in range(count):
            if k < n - 1 and h:
                flying[h], before = tie(flying[h], before)
            elif k < n - 1:
                flying[h], given = tie(flying[h], given)
            before = line_send(get(h, k), get(h, -k), *flying[h])
            flying[h] = line_pass(*before, k)
        if n - 1 - k < len(work):
            given = work[n - 1 - k](before, given)
    sums = []
    flying[0], given = tie(flying[0], given)
    for h, (right, left) in enumerate(flying):
        sums.append(get(h, 0).astype(full) + (right.astype(full) + left.astype(full)))
    return jnp.concatenate(sums), given


def by_place(blocks):
    n = lax.axis_size("seq")
    me = lax.axis_index("seq")
    placed = jnp.zeros((n,) + blocks[0].shape, blocks[0].dtype)
    for k, block in enumerate(blocks):
        placed = lax.dynamic_update_index_in_dim(placed, block, (me - k) % n, 0)
    return placed


def exchange(blocks):
    n = lax.axis_size("seq")
    me = lax.axis_index("seq")
    own = at_place(blocks, me)
    rights, lefts = [own] * n, [own] * n
    for k in range(n - 1, 0, -1):
        to_right, to_left = at_place(blocks, me + k), at_place(blocks, me - k)
        rights[k] = lax.ppermute(to_right, "seq", [(i, i + k) for i in range(n - k)])
        lefts[k] = lax.ppermute(to_left, "seq", [(i, i - k) for i in range(k, n)])
    return rights, lefts


def swap(value, axis, bit):
    return lax.ppermute(value, axis, [(i, i ^ bit) for i in range(lax.axis_size(axis))])


def total(value, *axes):
    for axis in axes:
        for step in range(lax.axis_size(axis).bit_length() - 1):
            value = value + swap(value, axis, 1 << step)
    return value


def fsdp_bits():
    bits = [1 << step for step in range(lax.axis_size("fsdp").bit_length() - 1)]
    return tuple(bits), tuple(bits[:1] + bits[:0:-1])


def total_steps(value, *axes):
    for axis in axes:
        for step in range(lax.axis_size(axis).bit_length() - 1):
            here = swap(value, axis, 1 << step)
            here = yield here
            value = value + here
    while True:
        yield value


class Halving:
    def __init__(self, keep, send, bits):
        self.terms, self.send, self.bits = [keep], send, list(bits)

    def go(self):
        self.terms = self.terms + [swap(self.send, "fsdp", self.bits.pop(0))]

    def add(self):
        half = self.terms[0].shape[0] // 2
        if half:
            self.send = sum(term[half:].astype(full) for term in self.terms).astype(low)
            self.terms = [term[:half] for term in self.terms]

    def finish(self):
        while self.bits:
            self.go()
            self.add()
        return sum(term[0].astype(full) for term in self.terms)


def rows_halving(part, bits):
    devs = lax.axis_size("fsdp")
    order = lax.axis_index("fsdp") ^ jnp.array(halving_masks(bits), jnp.int32)
    blocks = part.reshape(devs, part.shape[0] // devs, part.shape[1])[order]
    return Halving(blocks[: devs // 2], blocks[devs // 2 :], bits)


def land(sums, *others):
    tied = tie([each.terms[-1] for each in sums], *others)
    for each, here in zip(sums, tied[0]):
        each.terms = each.terms[:-1] + [here]
    return tied[1:]


def leave(sums, *others):
    tied = tie([each.send for each in sums], *others)
    for each, send in zip(sums, tied[0]):
        each.send = send
    return tied[1:]


def nt(a, b):
    return lax.dot_general(a, b, (((1,), (1,)), ((), ())), preferred_element_type=full)

def nn(a, b):
    return lax.dot_general(a, b, (((1,), (0,)), ((), ())), preferred_element_type=full)

def tn(a, b):
    return lax.dot_general(a, b, (((0,), (0,)), ((), ())), preferred_element_type=full)


def beside(rows):
    return jnp.concatenate([rows[h] for h in range(GROUP)], axis=1)

def key_steps(i, seq_len, query_rows, key_rows):
    free = (i * query_rows) // key_rows
    need = ((i + 1) * query_rows + BLOCK - 1 + key_rows - 1) // key_rows
    return free, jnp.minimum(need, seq_len // key_rows)

def forward_kernel(seq_len, query_rows, key_rows, limit_ref, q_ref, k_ref, vt_ref, low_ref, out_ref, lse_ref):
    i = pl.program_id(1)
    qt = beside(q_ref[0, 0])
    width = GROUP * query_rows
    limit = jnp.concatenate([limit_ref[...]] * GROUP, axis=1)

    def step(masked, j, carry):
        peak, total, acc = carry
        start = pl.multiple_of(j * key_rows, key_rows)
        s = nn(k_ref[0, pl.ds(start, key_rows), :], qt)
        if masked:
            place = start + lax.broadcasted_iota(jnp.int32, (key_rows, 1), 0)
            s = jnp.where(place < limit, s, masked_score)
        new_peak = jnp.maximum(peak, jnp.max(s, axis=0, keepdims=True))
        shrink = jnp.exp(peak - new_peak)
        p = jnp.exp(s - new_peak)
        total = shrink * total + jnp.sum(p, axis=0, keepdims=True)
        acc = shrink * acc + nn(vt_ref[0, :, pl.ds(start, key_rows)], p.astype(low))
        return new_peak, total, acc

    free, need = key_steps(i, seq_len, query_rows, key_rows)
    carry = (
        jnp.full((1, width), masked_score, full),
        jnp.zeros((1, width), full),
        jnp.zeros((HEAD_DIM, width), full),
    )
    carry = lax.fori_loop(0, free, lambda j, c: step(False, j, c), carry)
    peak, total, acc = lax.fori_loop(free, need, lambda j, c: step(True, j, c), carry)
    out = acc / total
    lse = peak + jnp.log(total)
    for h in range(GROUP):
        cols = slice(h * query_rows, (h + 1) * query_rows)
        out_ref[0, h] = out[:, cols]
        low_ref[0, pl.ds(h * HEAD_DIM, HEAD_DIM), :] = out[:, cols].astype(low)
        lse_ref[0, h] = lse[:, cols]

def query_spec(query_rows, per):
    return pl.BlockSpec(
        (1, 1, GROUP, HEAD_DIM, query_rows), lambda g, i: (i // per, g, 0, 0, i % per)
    )


def attention_forward(heads, k_rows, vt, limit):
    kv_here, shard_len = heads.shape[1], heads.shape[4]
    seq_len = k_rows.shape[1]
    query_rows = min(256, shard_len)
    key_rows = min(512, seq_len)
    per = shard_len // query_rows
    return pl.pallas_call(
        functools.partial(forward_kernel, seq_len, query_rows, key_rows),
        grid=(kv_here, seq_len // query_rows),
        in_specs=[
            pl.BlockSpec((1, query_rows), lambda g, i: (0, i)),
            query_spec(query_rows, per),
            pl.BlockSpec((1, seq_len, HEAD_DIM), lambda g, i: (g, 0, 0)),
            pl.BlockSpec((1, HEAD_DIM, seq_len), lambda g, i: (g, 0, 0)),
        ],
        out_specs=[
            pl.BlockSpec((1, GROUP * HEAD_DIM, query_rows), lambda g, i: (i // per, g, i % per)),
            pl.BlockSpec((1, GROUP, HEAD_DIM, query_rows), lambda g, i: (g, 0, 0, i)),
            pl.BlockSpec((1, GROUP, 1, query_rows), lambda g, i: (g, 0, 0, i)),
        ],
        out_shape=[
            jax.ShapeDtypeStruct((seq_len // shard_len, kv_here * GROUP * HEAD_DIM, shard_len), low),
            jax.ShapeDtypeStruct((kv_here, GROUP, HEAD_DIM, seq_len), full),
            jax.ShapeDtypeStruct((kv_here, GROUP, 1, seq_len), full),
        ],
        compiler_params=vmem(60),
        name="attention_forward",
    )(limit, heads, k_rows, vt)

def backward_kernel(
    seq_len, query_rows, key_rows, per, me_ref, limit_ref, q_ref, k_ref, v_ref, kt_ref, out_ref, lse_ref, *refs
):
    blocks, (dq_ref, dk_ref, dv_ref, dk_acc, dv_acc, held) = refs[:-6], refs[-6:]
    i = pl.program_id(1)

    @pl.when(i == 0)
    def _():
        dk_acc[...] = jnp.zeros_like(dk_acc)
        dv_acc[...] = jnp.zeros_like(dv_acc)

    qt = beside(q_ref[0, 0])
    limit = jnp.concatenate([limit_ref[...]] * GROUP, axis=1)
    devs = (len(blocks) + 1) // 2
    gap = me_ref[0] - i // per
    for spot, block in enumerate(blocks):

        @pl.when(gap == (spot if spot < devs else devs - 1 - spot))
        def _():
            held[...] = block[...]

    dout = jnp.concatenate([held[pl.ds(h * HEAD_DIM, HEAD_DIM), :] for h in range(GROUP)], axis=1)
    delta = jnp.sum(dout.astype(full) * beside(out_ref[0]), axis=0, keepdims=True)
    lse = beside(lse_ref[0])

    def step(masked, j, dq):
        start = pl.multiple_of(j * key_rows, key_rows)
        keys = pl.ds(start, key_rows)
        s = nn(k_ref[0, keys, :], qt)
        if masked:
            place = start + lax.broadcasted_iota(jnp.int32, (key_rows, 1), 0)
            s = jnp.where(place < limit, s, masked_score)
        p = jnp.exp(s - lse)
        dp = nn(v_ref[0, keys, :], dout)
        ds = (p * (dp - delta)).astype(low)
        dk_acc[:, keys] += nt(qt, ds)
        dv_acc[:, keys] += nt(dout, p.astype(low))
        return dq + nn(kt_ref[0, :, keys], ds)

    free, need = key_steps(i, seq_len, query_rows, key_rows)
    dq = jnp.zeros((HEAD_DIM, GROUP * query_rows), full)
    dq = lax.fori_loop(0, free, lambda j, c: step(False, j, c), dq)
    dq = lax.fori_loop(free, need, lambda j, c: step(True, j, c), dq) * attn_mult
    for h in range(GROUP):
        dq_ref[0, h] = dq[:, h * query_rows : (h + 1) * query_rows].astype(low)

    @pl.when(i == pl.num_programs(1) - 1)
    def _():
        dk_ref[0] = dk_acc[...].astype(low)
        dv_ref[0] = dv_acc[...].astype(low)

def attention_backward(heads, k_rows, v_rows, kt, limit, out, lse, me, rights, lefts):
    blocks = [*rights, *lefts[1:]]
    kv_here, shard_len = heads.shape[1], heads.shape[4]
    seq_len = k_rows.shape[1]
    query_rows = min(256, shard_len)
    key_rows = min(512, seq_len)
    per = shard_len // query_rows
    quarter = lambda g, i, me: (g, 0, 0, i)
    whole = lambda g, i, me: (g, 0, 0)
    return pl.pallas_call(
        functools.partial(backward_kernel, seq_len, query_rows, key_rows, per),
        grid_spec=pltpu.PrefetchScalarGridSpec(
            num_scalar_prefetch=1,
            grid=(kv_here, seq_len // query_rows),
            in_specs=[
                pl.BlockSpec((1, query_rows), lambda g, i, me: (0, i)),
                pl.BlockSpec(
                    (1, 1, GROUP, HEAD_DIM, query_rows),
                    lambda g, i, me: (i // per, g, 0, 0, i % per),
                ),
                pl.BlockSpec((1, seq_len, HEAD_DIM), whole),
                pl.BlockSpec((1, seq_len, HEAD_DIM), whole),
                pl.BlockSpec((1, HEAD_DIM, seq_len), whole),
                pl.BlockSpec((1, GROUP, HEAD_DIM, query_rows), quarter),
                pl.BlockSpec((1, GROUP, 1, query_rows), quarter),
            ]
            + [pl.BlockSpec((GROUP * HEAD_DIM, query_rows), lambda g, i, me: (g, i % per))]
            * len(blocks),
            out_specs=[
                pl.BlockSpec((1, GROUP, HEAD_DIM, query_rows), quarter),
                pl.BlockSpec((1, HEAD_DIM, seq_len), whole),
                pl.BlockSpec((1, HEAD_DIM, seq_len), whole),
            ],
            scratch_shapes=[
                pltpu.VMEM((HEAD_DIM, seq_len), full),
                pltpu.VMEM((HEAD_DIM, seq_len), full),
                pltpu.VMEM((GROUP * HEAD_DIM, query_rows), low),
            ],
        ),
        out_shape=[
            jax.ShapeDtypeStruct((kv_here, GROUP, HEAD_DIM, seq_len), low),
            jax.ShapeDtypeStruct((kv_here, HEAD_DIM, seq_len), low),
            jax.ShapeDtypeStruct((kv_here, HEAD_DIM, seq_len), low),
        ],
        compiler_params=vmem(60),
        name="attention_backward",
    )(me, limit, heads, k_rows, v_rows, kt, out, lse, *blocks)


def vmem(mib):
    return pltpu.CompilerParams(vmem_limit_bytes=mib * 2**20)


def own_row(ref, row):
    return ref[pl.ds(row, 1), :]


def join_down(rows, block_ref, down_ref):
    hidden, width = down_ref.shape
    chunks = width // hidden
    for dev in range(hidden // rows):
        for chunk in range(chunks):
            start = (dev * chunks + chunk) * rows
            down_ref[dev * rows : (dev + 1) * rows, chunk * hidden : (chunk + 1) * hidden] = (
                block_ref[start : start + rows, :]
            )


def pick_rows(pick, tok_ref, more_ref):
    middle = tok_ref.shape[0]
    return (nn(pick[:, :middle], tok_ref[...]) + nn(pick[:, middle:], more_ref[:middle, :])).astype(low)


def experts_kernel(
    few, pair, at_ref, tok_ref, more_ref, slot_ref, member_ref, router_ref, wgu_ref, wd_ref, *refs
):
    part_ref, x_ref, gu_ref, gates_ref, acc, gates_all, down = refs[-7:]
    step, steps = pl.program_id(0), pl.num_programs(0)
    slots = x_ref.shape[2]

    @pl.when(step == 0)
    def _():
        member = member_ref[...] > 0
        logits = [nt(router_ref[...], ref[...]) for ref in (tok_ref, more_ref)]
        chosen = jnp.where(member, jnp.concatenate(logits, axis=1), masked_score)
        chosen = jnp.exp(chosen - jnp.max(chosen, axis=0, keepdims=True))
        chosen = jnp.where(member, chosen, 0.0)
        gates_all[...] = chosen / jnp.sum(chosen, axis=0, keepdims=True)
        acc[...] = jnp.zeros_like(acc)

    place = lax.broadcasted_iota(jnp.int32, (slots, 1), 0)
    puts, ys = [], []
    for i in range(pair):
        e = step * pair + i
        gate_row = own_row(gates_all, at_ref[1] * (steps * pair) + e)
        gates_ref[pl.ds(e, 1), :] = gate_row
        here = place == own_row(slot_ref, e)
        x = pick_rows(jnp.where(here, 1.0, 0.0).astype(low), tok_ref, more_ref)
        x_ref[i, 0] = x
        gu = nn(x, wgu_ref[i])
        gu_ref[i, 0] = gu.astype(low)
        hidden = gu.shape[1] // 2
        g, u = gu[:, :hidden], gu[:, hidden:]
        act = (g * jax.nn.sigmoid(g) * u).astype(low)
        join_down(few, wd_ref.at[i], down.at[i])
        ys.append(nn(act, down[i]).astype(low))
        puts.append(jnp.where(here, gate_row, 0.0).astype(low))
    acc[...] += tn(jnp.concatenate(puts), jnp.concatenate(ys))

    @pl.when(step == steps - 1)
    def _():
        part_ref[0] = acc[...].astype(low)


def back_kernel(
    few, pair, at_ref, tok_ref, more_ref, slot_ref, gates_ref, mix_ref, router_ref, gu_ref, wgu_ref, wd_ref, *refs
):
    part_ref, d_ref, dgu_ref, act_ref, dlog_ref, acc, dlog_all, down = refs[-8:]
    step, steps = pl.program_id(0), pl.num_programs(0)
    slots, hidden = gu_ref.shape[2], gu_ref.shape[3] // 2

    @pl.when(step == 0)
    def _():
        dlog_all[...] = jnp.zeros_like(dlog_all)
        acc[...] = jnp.zeros_like(acc)

    place = lax.broadcasted_iota(jnp.int32, (slots, 1), 0)
    puts, dxs = [], []
    for i in range(pair):
        e = step * pair + i
        here = place == own_row(slot_ref, e)
        pick = jnp.where(here, 1.0, 0.0).astype(low)
        gate_row = own_row(gates_ref, e)
        gate = jnp.sum(jnp.where(here, gate_row, 0.0), axis=1, keepdims=True)
        d = pick_rows(pick, tok_ref, more_ref)
        d_ref[i, 0] = d
        join_down(few, wd_ref.at[i], down.at[i])
        d_act = nt(d, down[i])
        g, u = gu_ref[i, 0, :, :hidden].astype(full), gu_ref[i, 0, :, hidden:].astype(full)
        sig = jax.nn.sigmoid(g)
        silu = g * sig
        act = silu * u
        d_gate = jnp.sum(d_act * act, axis=1, keepdims=True)
        d_gate = jnp.sum(jnp.where(here, d_gate, 0.0), axis=0, keepdims=True)
        dlog_all[pl.ds(e, 1), :] = gate_row * (d_gate - mix_ref[...])
        act_ref[i, 0] = (act * gate).astype(low)
        d_act = d_act * gate
        d_g = (d_act * u * (sig + silu * (1.0 - sig))).astype(low)
        d_u = (d_act * silu).astype(low)
        dgu_ref[i, 0, :, :hidden] = d_g
        dgu_ref[i, 0, :, hidden:] = d_u
        dxs.append(nt(dgu_ref[i, 0], wgu_ref[i]).astype(low))
        puts.append(pick)
    acc[...] += tn(jnp.concatenate(puts), jnp.concatenate(dxs))

    @pl.when(step == steps - 1)
    def _():
        dlog = dlog_all[...].astype(low)
        dlog_ref[...] = dlog
        part_ref[0] = (acc[...] + tn(dlog, router_ref[...])).astype(low)


def by_expert(*shape):
    return pl.BlockSpec((1,) + shape, lambda e, at: (e, 0, 0))


def in_turn(pair, turn, *shape):
    return pl.BlockSpec((pair, 1) + shape, lambda e, at: (e, turn, 0, 0))


def same(*shape):
    return pl.BlockSpec(shape, lambda e, at: (0, 0))


def in_place(*shape):
    return pl.BlockSpec((1,) + shape, lambda e, at: (at[0], 0, 0))


def shard_call(kernel, name, at, inputs, in_specs, out_specs, out_shape, buffers, scratch, experts):
    first = len(inputs) + 1
    aliases = {first + i: i for i in range(len(buffers))}
    return pl.pallas_call(
        kernel,
        grid_spec=pltpu.PrefetchScalarGridSpec(
            num_scalar_prefetch=1,
            grid=(experts,),
            in_specs=in_specs + [pl.BlockSpec(memory_space=pl.ANY)] * len(buffers),
            out_specs=out_specs,
            scratch_shapes=scratch,
        ),
        out_shape=out_shape,
        input_output_aliases=aliases,
        compiler_params=vmem(48),
        name=name,
    )(at, *inputs, *buffers)


def weight_specs(pair, width, hidden):
    return [
        pl.BlockSpec((pair, width, 2 * hidden), lambda e, at: (e, 0, 0)),
        pl.BlockSpec((pair, width, hidden), lambda e, at: (e, 0, 2)),
    ]


def experts_forward(turn, devs, at, tokens, slot_of, member, router, weights, few, slots, buffers):
    experts, width, columns = weights.shape
    hidden = columns // 3
    pair = 1 + (experts + 1) % 2
    count = 2 * tokens[0].shape[0]
    total_experts = member.shape[0]
    return shard_call(
        functools.partial(experts_kernel, few, pair),
        "experts_forward",
        at,
        [*tokens, slot_of, member, router, weights, weights],
        [
            *(same(*half.shape) for half in tokens),
            same(experts, count),
            same(total_experts, count),
            same(total_experts, width),
            *weight_specs(pair, width, hidden),
        ],
        [
            in_place(count, width),
            in_turn(pair, turn, slots, width),
            in_turn(pair, turn, slots, 2 * hidden),
            same(experts, count),
        ],
        [
            jax.ShapeDtypeStruct((devs, count, width), low),
            jax.ShapeDtypeStruct((experts, devs, slots, width), low),
            jax.ShapeDtypeStruct((experts, devs, slots, 2 * hidden), low),
            jax.ShapeDtypeStruct((experts, count), full),
        ],
        buffers,
        [
            pltpu.VMEM((count, width), full),
            pltpu.VMEM((total_experts, count), full),
            pltpu.VMEM((pair, hidden, width), low),
        ],
        experts // pair,
    )


def experts_backward(
    turn, devs, at, d_tokens, slot_of, gates, mix_dot, router, gu, weights, few, buffers
):
    experts, width, columns = weights.shape
    hidden = columns // 3
    pair = 1 + (experts + 1) % 2
    count = 2 * d_tokens[0].shape[0]
    slots = gu.shape[2]
    lines = router.shape[0]
    return shard_call(
        functools.partial(back_kernel, few, pair),
        "experts_backward",
        at,
        [*d_tokens, slot_of, gates, mix_dot, router, gu, weights, weights],
        [
            *(same(*half.shape) for half in d_tokens),
            same(experts, count),
            same(experts, count),
            same(1, count),
            same(lines, width),
            in_turn(pair, turn, slots, 2 * hidden),
            *weight_specs(pair, width, hidden),
        ],
        [
            in_place(count, width),
            in_turn(pair, turn, slots, width),
            in_turn(pair, turn, slots, 2 * hidden),
            in_turn(pair, turn, slots, hidden),
            same(lines, count),
        ],
        [
            jax.ShapeDtypeStruct((devs, count, width), low),
            jax.ShapeDtypeStruct((experts, devs, slots, width), low),
            jax.ShapeDtypeStruct((experts, devs, slots, 2 * hidden), low),
            jax.ShapeDtypeStruct((experts, devs, slots, hidden), low),
            jax.ShapeDtypeStruct((lines, count), low),
        ],
        buffers,
        [
            pltpu.VMEM((count, width), full),
            pltpu.VMEM((lines, count), full),
            pltpu.VMEM((pair, hidden, width), low),
        ],
        experts // pair,
    )


def halving_masks(bits):
    masks = [0]
    for bit in reversed(bits):
        masks = masks + [mask ^ bit for mask in masks]
    return masks


def out_kernel(bits_a, bits_b, me_ref, rows_ref, d_ref, *refs):
    outs, acc = refs[:4], refs[4]
    half = outs[0].shape[2]
    for part, bits in enumerate((bits_a, bits_b)):
        keep, send = outs[2 * part], outs[2 * part + 1]
        rows = keep.shape[1]
        acc[...] = nn(rows_ref[...], d_ref[:, part * half : (part + 1) * half])
        for place, mask in enumerate(halving_masks(bits)):
            out = keep if place < keep.shape[0] else send
            start = pl.multiple_of((me_ref[0] ^ mask) * rows, rows)
            out[place % keep.shape[0]] = acc[pl.ds(start, rows), :].astype(low)


def out_grads(me, rows, d_proj, bits_a, bits_b):
    (height, count), width = rows.shape, d_proj.shape[1]
    devs = 2 ** len(bits_a)
    shape = (devs // 2, height // devs, width // 2)
    outs = pl.pallas_call(
        functools.partial(out_kernel, bits_a, bits_b),
        grid_spec=pltpu.PrefetchScalarGridSpec(
            num_scalar_prefetch=1,
            grid=(1,),
            in_specs=[same(height, count), same(count, width)],
            out_specs=[pl.BlockSpec(shape, lambda e, me: (0, 0, 0))] * 4,
            scratch_shapes=[pltpu.VMEM((height, width // 2), full)],
        ),
        out_shape=[jax.ShapeDtypeStruct(shape, low)] * 4,
        compiler_params=vmem(48),
        name="out_grads",
    )(me, rows, d_proj)
    return (outs[0], outs[1]), (outs[2], outs[3])


def grads_kernel(few, x_ref, dgu_ref, act_ref, d_ref, *refs):
    out_ref, down = refs[-2], refs[-1]
    hidden, width = down.shape
    out_ref[0, :, : 2 * hidden] = tn(x_ref[0], dgu_ref[0]).astype(low)
    down[...] = tn(act_ref[0], d_ref[0]).astype(low)
    chunks = width // hidden
    for dev in range(hidden // few):
        for chunk in range(chunks):
            start = (dev * chunks + chunk) * few
            out_ref[0, start : start + few, 2 * hidden :] = down[
                dev * few : (dev + 1) * few, chunk * hidden : (chunk + 1) * hidden
            ]


def weight_grads(rows, d_gu, act, d_rows, few, first, stop, buffers):
    experts, count, width = rows.shape
    hidden = act.shape[2]

    def part(*block):
        return pl.BlockSpec((1,) + block, lambda e: (first + e, 0, 0))

    return pl.pallas_call(
        functools.partial(grads_kernel, few),
        grid=(stop - first,),
        in_specs=[part(count, width), part(count, 2 * hidden), part(count, hidden), part(count, width)]
        + [pl.BlockSpec(memory_space=pl.ANY)] * len(buffers),
        out_specs=part(width, 3 * hidden),
        out_shape=jax.ShapeDtypeStruct((experts, width, 3 * hidden), low),
        scratch_shapes=[pltpu.VMEM((hidden, width), low)],
        input_output_aliases={4 + i: i for i in range(len(buffers))},
        compiler_params=vmem(56),
        name="weight_grads",
    )(rows, d_gu, act, d_rows, *buffers)


def shards(
    inputs,
    teacher,
    routes,
    valid_mask,
    block_lengths,
    gain_one,
    w_qkv,
    w_out,
    gain_two,
    w_router,
    w_gate,
    w_up,
    w_down,
):
    n = lax.axis_size("seq")
    me = lax.axis_index("seq")
    mine = lax.axis_index("fsdp")
    seqs_here, shard_len, width = inputs.shape
    assert seqs_here == 1
    seq_len = shard_len * n
    tokens_all = lax.axis_size("fsdp") * seq_len
    kv_here = KV_HEADS // n
    heads_w = kv_here * GROUP * HEAD_DIM
    group_w = kv_here * (GROUP + 2) * HEAD_DIM
    experts_here = w_gate.shape[0]
    expert_total = experts_here * n
    top_count = routes.shape[2]
    capacity = 3 * shard_len * top_count // (2 * expert_total)
    slots = -(-capacity // 16) * 16
    slot_rows = n * slots
    order_a, order_b = fsdp_bits()
    order = jnp.array(arrival_order(n), jnp.int32)[me]
    x_low = inputs.reshape(shard_len, width)

    own_qkv = lax.dynamic_slice_in_dim(w_qkv, me * group_w, group_w, 1)
    small = jnp.concatenate([gain_one[:, None], gain_two[:, None], w_router], axis=1)
    small = jnp.pad(small, ((0, 0), (0, -small.shape[1] % 128)))
    first = lax.all_gather(
        jnp.concatenate([own_qkv, small, w_out], axis=1), "fsdp", axis=0, tiled=True
    )
    full_qkv = first[:, :group_w]
    small = first[:, group_w : group_w + 2 + expert_total]
    full_out = first[:, -width:]
    full_g1 = small[:, 0].astype(full)
    full_g2 = small[:, 1].astype(full)
    router = small[:, 2:].T
    own_router = lax.dynamic_slice_in_dim(router, me * experts_here, experts_here, 0)
    own_router = jnp.pad(own_router, ((0, -experts_here % 16), (0, 0)))
    valid_rows = valid_mask.reshape(shard_len).astype(full)

    hidden_w = w_gate.shape[2]
    down_chunks = [
        w_down[:, :, start : start + hidden_w] for start in range(0, width, hidden_w)
    ]
    weights = lax.all_gather(
        jnp.concatenate([w_gate, w_up, jnp.concatenate(down_chunks, axis=1)], axis=2),
        "fsdp",
        axis=1,
        tiled=True,
    )

    routes_low = jnp.concatenate([routes.reshape(shard_len, top_count).T, valid_mask], axis=0)
    routes_low = jnp.pad(
        routes_low.astype(low), ((0, -routes_low.shape[0] % 16), (0, width - shard_len))
    )
    middle = shard_len // 2
    halves = (x_low[:middle], jnp.concatenate([x_low[middle:], routes_low], axis=0))
    positions = jnp.arange(seq_len, dtype=jnp.int32)
    cosine, sine_vals = rope_tables(positions.astype(full), HEAD_DIM)
    limit = block_limits(block_lengths[0], positions)[None]
    normed_one = jnp.zeros((seq_len, width), low)
    heads = jnp.zeros((n, kv_here, GROUP + 2, HEAD_DIM, shard_len), low)
    routes_all = []
    line = LineGather(halves)
    for turn in range(n):
        if turn:
            line.land(0, heads if turn > 1 else ())
            if turn < n - 1:
                line.go(0)
            line.land(1, ())
            if turn < n - 1:
                line.go(1)
        else:
            line.go(0)
            line.go(1)
        block = jnp.concatenate(line.block(turn))
        start = order[turn] * shard_len
        normed = rms_norm(block[:shard_len].astype(full), full_g1).astype(low)
        projected = dot("td,dc->ct", normed, full_qkv)
        projected = projected.reshape(kv_here, GROUP + 2, HEAD_DIM, shard_len)
        turned = rotate(
            projected[:, : GROUP + 1],
            lax.dynamic_slice_in_dim(cosine, start, shard_len, 1),
            lax.dynamic_slice_in_dim(sine_vals, start, shard_len, 1),
        ).astype(low)
        turned = jnp.concatenate(
            [
                turned[:, :GROUP] * jnp.asarray(attn_mult, low),
                turned[:, GROUP:],
                projected[:, GROUP + 1 :].astype(low),
            ],
            axis=1,
        )
        heads = lax.dynamic_update_index_in_dim(heads, turned, order[turn], 0)
        normed_one = lax.dynamic_update_slice_in_dim(normed_one, normed, start, 0)
        routes_all.append(block[shard_len : shard_len + top_count + 1, :shard_len])

    routes_all = jnp.stack(routes_all).astype(jnp.int32)
    valid_count = total(jnp.sum(routes_all[:, top_count]).astype(full).reshape(1, 1), "fsdp")[0, 0]
    expert_ids = jnp.arange(expert_total, dtype=jnp.int32)
    member = jnp.any(routes_all[:, :top_count, None, :] == expert_ids[:, None], axis=1)
    own_member = lax.dynamic_slice_in_dim(member, me * experts_here, experts_here, 1)
    earlier = jnp.arange(shard_len)[:, None] < jnp.arange(shard_len)[None, :]
    slot_of = dot("net,tu->neu", own_member.astype(low), earlier.astype(low)).astype(jnp.int32)
    slot_of = jnp.where(own_member, slot_of, -1)
    member = member.astype(full)

    key = jnp.moveaxis(heads[:, :, GROUP], 0, 2).reshape(kv_here, HEAD_DIM, seq_len)
    value = jnp.moveaxis(heads[:, :, GROUP + 1], 0, 2).reshape(kv_here, HEAD_DIM, seq_len)
    key_rows = jnp.swapaxes(key, 1, 2)
    value_rows = jnp.swapaxes(value, 1, 2)
    attended, out_heads, lse = attention_forward(heads, key_rows, value, limit)
    moved = exchange(attended)
    moved, slot_of, member, own_router = tie(moved, slot_of, member, own_router)
    attn_rows = by_place(nearest(*moved)).reshape(HEADS * HEAD_DIM, shard_len)
    projected = dot("kt,kd->td", attn_rows, full_out)
    hidden = x_low.astype(full) + resid_mult * projected
    normed_two, norm_two_pull = jax.vjp(rms_norm, hidden, full_g2)

    normed_low = normed_two.astype(low)
    line = LineGather((normed_low[:middle], normed_low[middle:]))
    buffers, gates, tokens = [], [], []
    line.go(0)
    line.go(1)
    other = ()
    for turn in range(n):
        if turn < n - 1:
            for h in (0, 1):
                other = line.land(h, other)
                if turn < n - 2:
                    line.go(h)
            line_slots = line.hold(slot_of[turn])
        else:
            line_slots = slot_of[turn]
        tokens.append(line.block(turn))
        *buffers, shard_gates = experts_forward(
            turn, n, jnp.stack([order[turn], me]), tokens[turn], line_slots, member[turn],
            router, weights, w_down.shape[1], slots, buffers,
        )
        gates.append(shard_gates)
        other = shard_gates
    mix_parts, expert_in, gate_up = buffers
    cuts = (slice(0, middle), slice(middle, None))
    mixture, _ = line_scatter(2, lambda h, shift: at_place(mix_parts[:, cuts[h]], me + shift), ())
    output_f32 = hidden + resid_mult * mixture
    activations = output_f32.astype(low).reshape(1, shard_len, width)
    error_rows = output_f32 - teacher.astype(full).reshape(shard_len, width)
    weighted = valid_rows[:, None] * error_rows
    loss_steps = total_steps(jnp.sum(weighted * error_rows).reshape(1, 1), "seq", "fsdp")
    squares = next(loss_steps)
    d_out = weighted * (tokens_all / valid_count)

    d_mix = resid_mult * d_out
    d_tokens = d_mix.astype(low)
    mix_dot = jnp.sum(d_mix * mixture, axis=1)[None]
    mix_high = mix_dot.astype(low)
    mix_rows = jnp.concatenate([mix_high, (mix_dot - mix_high.astype(full)).astype(low)])
    mix_rows = jnp.pad(mix_rows, ((0, 14), (0, width - shard_len)))
    line = LineGather((d_tokens[:middle], jnp.concatenate([d_tokens[middle:], mix_rows])))
    buffers, d_logits = [], []
    for turn in range(n):
        if turn:
            line.land(0, d_logits[-1])
            if turn < n - 1:
                line.go(0)
            line.land(1, ())
            if turn < n - 1:
                line.go(1)
        else:
            line.go(0)
            line.go(1)
        d_block = line.block(turn)
        mix_dot = d_block[1][middle : middle + 2, :shard_len].astype(full)
        mix_dot = jnp.sum(mix_dot, axis=0, keepdims=True)
        *buffers, shard_logits = experts_backward(
            turn, n, jnp.stack([order[turn], me]), d_block, slot_of[turn], gates[turn], mix_dot,
            own_router, gate_up, weights, w_down.shape[1], buffers,
        )
        d_logits.append(shard_logits)
    d_parts, d_rows, d_gate_up, act_low = buffers
    expert_in = expert_in.reshape(experts_here, slot_rows, width)
    d_rows = d_rows.reshape(experts_here, slot_rows, width)
    d_gate_up = d_gate_up.reshape(experts_here, slot_rows, -1)
    act_low = act_low.reshape(experts_here, slot_rows, -1)

    cut = (experts_here + 1) // 2

    def some_grads(first, stop):
        def make(before, grads):
            inputs, _ = tie((expert_in, d_gate_up, act_low, d_rows), before)
            return [weight_grads(*inputs, w_down.shape[1], first, stop, grads)]

        return make

    d_normed_two, grads = line_scatter(
        1,
        lambda h, shift: at_place(d_parts, me + shift),
        (some_grads(0, cut), some_grads(cut, experts_here)),
    )
    expert_sum = lax.psum_scatter(grads[0], "fsdp", scatter_dimension=1, tiled=True)

    d_hidden_norm, gain_two_part = norm_two_pull(d_normed_two)
    d_hidden = d_out + d_hidden_norm
    d_proj = (resid_mult * d_hidden).astype(low)
    d_attended = dot("kd,td->kt", full_out, d_proj).astype(low)
    moved = exchange(d_attended.reshape(n, heads_w, shard_len))
    moved[0][1], d_proj, d_logits = tie(moved[0][1], d_proj, d_logits)
    out_pairs = out_grads(mine.reshape(1), attn_rows, d_proj, order_a, order_b)
    out_sums = [Halving(*pair, bits) for pair, bits in zip(out_pairs, (order_a, order_b))]
    for each in out_sums:
        each.go()
        each.add()
    router_part = sum(
        dot("td,et->de", half, half_logits)
        for shard, shard_logits in zip(tokens, d_logits)
        for half, half_logits in (
            (shard[0], shard_logits[:experts_here, :middle]),
            (shard[1], shard_logits[:experts_here, middle:]),
        )
    )
    own_columns = jnp.zeros((width, expert_total), full)
    own_columns = lax.dynamic_update_slice_in_dim(own_columns, router_part, me * experts_here, 1)
    own_columns = jnp.concatenate([own_columns, gain_two_part[:, None]], axis=1).astype(low)
    moved, own_columns, squares = leave(out_sums, moved, own_columns, squares)
    squares = loss_steps.send(squares)
    for each in out_sums:
        each.go()
    query_grad, key_grad, value_grad = attention_backward(
        heads, key_rows, value_rows, key, limit, out_heads, lse, me.reshape(1), *moved
    )
    (query_grad, key_grad, value_grad), squares = land(
        out_sums, (query_grad, key_grad, value_grad), squares
    )
    squares = loss_steps.send(squares)
    for each in out_sums:
        each.add()
        each.go()
    d_turned = jnp.concatenate([query_grad, key_grad[:, None]], axis=1).astype(full)
    d_turned = rotate(d_turned, cosine, -sine_vals).astype(low)
    d_qkv = jnp.concatenate([d_turned, value_grad[:, None]], axis=1).reshape(group_w, seq_len)

    def d_part(rows, shift):
        start = (me + shift) % n * shard_len
        rows = lax.dynamic_slice_in_dim(rows, start, shard_len, 1)
        return dot("ct,dc->td", rows, full_qkv).astype(low)

    d_parts = {shift: d_part(d_qkv, shift) for shift in {1, n - 1}}
    (d_parts,) = land(out_sums, d_parts)
    for each in out_sums:
        each.add()

    out_sum = jnp.concatenate([each.finish() for each in out_sums], axis=1).astype(low)
    out_rows = out_sum.shape[0] // n
    out_parts = jnp.swapaxes(out_sum.reshape(out_sum.shape[0], n, width // n), 0, 1)
    out_parts = out_parts.reshape(n, out_rows, width)

    def get(h, shift):
        part = d_parts[shift % n]
        if h == 0:
            return part[:middle]
        return jnp.concatenate([part[middle:], at_place(out_parts, me + shift)])

    sums = {}

    def first_work(before, _):
        rows, _ = tie(d_qkv, before)
        for shift in range(n):
            if shift not in d_parts:
                d_parts[shift] = d_part(rows, shift)
        qkv_part = jnp.concatenate(
            [dot("td,ct->dc", normed_one, rows).astype(low), own_columns], axis=1
        )
        sums["qkv"] = rows_halving(qkv_part, order_a)
        sums["qkv"].go()
        return sums["qkv"].send

    def next_work(before, _):
        land([sums["qkv"]], before)
        sums["qkv"].add()
        sums["qkv"].go()
        return sums["qkv"].send

    ended, _ = line_scatter(2, get, (first_work, next_work, next_work))
    qkv_sum = sums["qkv"]
    d_normed_one = ended[:shard_len]
    (ended,) = land([qkv_sum], ended)
    qkv_sum.add()
    out_own = ended[shard_len:].reshape(out_sum.shape[0], width // n)
    block = jnp.concatenate([qkv_sum.finish(), out_own], axis=1).astype(low)
    rights, lefts = [block], [block]
    _, norm_one_pull = jax.vjp(lambda v: rms_norm(v, full_g1), x_low.astype(full))
    input_grad = (d_hidden + norm_one_pull(d_normed_one)[0]).reshape(1, shard_len, width)
    few = w_down.shape[1]
    last_work = [
        lambda: expert_sum[:, :, : 2 * hidden_w].astype(full),
        lambda: jnp.concatenate(
            [
                expert_sum[:, start : start + few, 2 * hidden_w :].astype(full)
                for start in range(0, expert_sum.shape[1], few)
            ],
            axis=2,
        ),
    ]
    done = [input_grad]
    for k in range(1, n):
        right, left = line_move(rights[-1], lefts[-1], k)
        if k < 3:
            done.append(last_work[k - 1]())
        right, left, done[-1], squares = tie(right, left, done[-1], squares)
        squares = loss_steps.send(squares)
        rights.append(right)
        lefts.append(left)
    input_grad, gate_up_grad, down_grad = done
    gate_grad, up_grad = gate_up_grad[:, :, :hidden_w], gate_up_grad[:, :, hidden_w:]
    qkv_grad = jnp.zeros((w_qkv.shape[0], QKV_W), full)
    out_grad = jnp.zeros((w_out.shape[0], width), full)
    rest = 0.0
    for turn in range(n):
        block = arrived(rights, lefts, turn).astype(full)
        place = order[turn]
        qkv_grad = lax.dynamic_update_slice_in_dim(
            qkv_grad, block[:, :group_w], place * group_w, 1
        )
        out_grad = lax.dynamic_update_slice_in_dim(
            out_grad, block[:, -(width // n) :], place * (width // n), 1
        )
        rest = rest + block[:, group_w : -(width // n)]
    router_grad, gain_two_grad = rest[:, :expert_total], rest[:, expert_total]
    gain_one_grad = jnp.sum(qkv_grad * w_qkv.astype(full), axis=1) / gain_one.astype(full)
    for _ in range(4):
        squares = loss_steps.send(squares)
    loss_value = squares[0, 0] / (valid_count * width)
    return (
        activations,
        loss_value,
        input_grad,
        gain_one_grad,
        qkv_grad,
        out_grad,
        gain_two_grad,
        router_grad,
        gate_grad,
        up_grad,
        down_grad,
    )


def solution(mesh):
    return jax.shard_map(
        shards,
        mesh=mesh,
        in_specs=(
            P("fsdp", "seq", None),
            P("fsdp", "seq", None),
            P("fsdp", "seq", None),
            P("fsdp", "seq"),
            P("fsdp", None),
            P("fsdp"),
            P("fsdp", None),
            P("fsdp", None),
            P("fsdp"),
            P("fsdp", None),
            P("seq", "fsdp", None),
            P("seq", "fsdp", None),
            P("seq", "fsdp", None),
        ),
        out_specs=(
            P("fsdp", "seq", None),
            P(),
            P("fsdp", "seq", None),
            P("fsdp"),
            P("fsdp", None),
            P("fsdp", None),
            P("fsdp"),
            P("fsdp", None),
            P("seq", "fsdp", None),
            P("seq", "fsdp", None),
            P("seq", "fsdp", None),
        ),
        check_vma=False,
    )
```

```python
import functools

import jax
import jax.numpy as jnp
from jax import lax
from jax.experimental import pallas as pl
from jax.experimental.pallas import tpu as pltpu
from jax.sharding import PartitionSpec as P

HEADS = 24
KV_HEADS = 8
HEAD_DIM = 64
BLOCK = 256
GROUP = 3
QKV_W = 2560


epsilon = 1e-06
attn_mult = 0.015625
resid_mult = 0.22
rope_base = 10000.0
masked_score = -1e30

low = jnp.bfloat16
full = jnp.float32


def dot(spec, left, right):
    return jnp.einsum(spec, left, right, preferred_element_type=full)


def rms_norm(values, gain_vec):
    inv_rms = lax.rsqrt(jnp.mean(values * values, axis=-1, keepdims=True) + epsilon)
    return values * inv_rms * gain_vec


def rope_tables(positions, head_dim):
    half_dim = head_dim // 2
    frequency = rope_base ** (-(2.0 * jnp.arange(half_dim, dtype=full)) / head_dim)
    angles = frequency[:, None] * positions[None, :]
    return (jnp.cos(angles), jnp.sin(angles))


def rotate(values, cosine, sine_vals):
    half_dim = values.shape[-2] // 2
    front_half = values[..., :half_dim, :]
    back_half = values[..., half_dim:, :]
    return jnp.concatenate(
        [front_half * cosine - back_half * sine_vals, back_half * cosine + front_half * sine_vals],
        axis=-2,
    )


def block_limits(lengths_row, positions):
    block_ends = jnp.cumsum(lengths_row)
    open_ends = jnp.where(block_ends[None, :] > positions[:, None], block_ends[None, :], positions.shape[0])
    return jnp.min(open_ends, axis=1).astype(jnp.int32)


def tie(*groups):
    return lax.optimization_barrier(groups)


def line_move(right, left, k):
    n = lax.axis_size("seq")
    return (
        lax.ppermute(right, "seq", [(i, i + 1) for i in range(k - 1, n - 1)]),
        lax.ppermute(left, "seq", [(i, i - 1) for i in range(1, n - k + 1)]),
    )


def line_gather(block):
    n = lax.axis_size("seq")
    rights, lefts = [block], [block]
    for k in range(1, n):
        right, left = tie(*line_move(rights[-1], lefts[-1], k))
        rights.append(right)
        lefts.append(left)
    return nearest(rights, lefts)


def nearest(rights, lefts):
    n = lax.axis_size("seq")
    me = lax.axis_index("seq")
    return [rights[0]] + [jnp.where(me >= k, rights[k], lefts[n - k]) for k in range(1, n)]


def arrival_order(n):
    order = []
    for me in range(n):
        both = min(me, n - 1 - me)
        places = [me]
        for k in range(1, n):
            places += [me - k] if me >= k and (k <= both or me > n - 1 - me) else []
            places += [me + k] if me + k < n and (k <= both or me < n - 1 - me) else []
        order.append(places)
    return order


def arrived(rights, lefts, turn):
    n = lax.axis_size("seq")
    me = lax.axis_index("seq")
    sources = {}
    for dev, places in enumerate(arrival_order(n)):
        gap = dev - places[turn]
        sources.setdefault(gap, []).append(dev)
    block = None
    for gap, devs in sources.items():
        moved = rights[gap] if gap >= 0 else lefts[-gap]
        if block is None:
            block = moved
        else:
            mine = jnp.array([dev in devs for dev in range(n)])[me]
            block = jnp.where(mine, moved, block)
    return block


def at_place(placed, place):
    return lax.dynamic_index_in_dim(placed, place % lax.axis_size("seq"), 0, keepdims=False)


def line_send(to_right, to_left, right, left):
    if right is not None:
        to_right = (to_right.astype(full) + right.astype(full)).astype(low)
        to_left = (to_left.astype(full) + left.astype(full)).astype(low)
    return to_right, to_left


def line_pass(to_right, to_left, k):
    n = lax.axis_size("seq")
    return (
        lax.ppermute(to_right, "seq", [(i, i + 1) for i in range(n - k)]),
        lax.ppermute(to_left, "seq", [(i, i - 1) for i in range(k, n)]),
    )


class LineGather:
    def __init__(self, halves):
        self.rights, self.lefts = [[half] for half in halves], [[half] for half in halves]
        self.landed = [0, 0]

    def go(self, h):
        step = len(self.rights[h])
        right, left = line_move(self.rights[h][-1], self.lefts[h][-1], step)
        self.rights[h].append(right)
        self.lefts[h].append(left)

    def land(self, h, other):
        spot = self.landed[h] = len(self.rights[h]) - 1
        moved = [(self.rights[part][spot], self.lefts[part][spot]) for part in range(h + 1)]
        moved, other = tie(moved, other)
        for part, (right, left) in enumerate(moved):
            self.rights[part][spot], self.lefts[part][spot] = right, left
        return other

    def hold(self, other):
        came = [(self.rights[h][-1 - self.ahead(h)], self.lefts[h][-1 - self.ahead(h)]) for h in (0, 1)]
        return tie(other, came)[0]

    def ahead(self, h):
        return len(self.rights[h]) - 1 - self.landed[h]

    def block(self, turn):
        return [arrived(self.rights[h], self.lefts[h], turn) for h in (0, 1)]


def line_scatter(count, get, work):
    n = lax.axis_size("seq")
    flying = [(None, None)] * count
    before, given = (), []
    for k in range(n - 1, 0, -1):
        for h in range(count):
            if k < n - 1 and h:
                flying[h], before = tie(flying[h], before)
            elif k < n - 1:
                flying[h], given = tie(flying[h], given)
            before = line_send(get(h, k), get(h, -k), *flying[h])
            flying[h] = line_pass(*before, k)
        if n - 1 - k < len(work):
            given = work[n - 1 - k](before, given)
    sums = []
    flying[0], given = tie(flying[0], given)
    for h, (right, left) in enumerate(flying):
        sums.append(get(h, 0).astype(full) + (right.astype(full) + left.astype(full)))
    return jnp.concatenate(sums), given


def by_place(blocks):
    n = lax.axis_size("seq")
    me = lax.axis_index("seq")
    placed = jnp.zeros((n,) + blocks[0].shape, blocks[0].dtype)
    for k, block in enumerate(blocks):
        placed = lax.dynamic_update_index_in_dim(placed, block, (me - k) % n, 0)
    return placed


def exchange(blocks):
    n = lax.axis_size("seq")
    me = lax.axis_index("seq")
    own = at_place(blocks, me)
    rights, lefts = [own] * n, [own] * n
    for k in range(n - 1, 0, -1):
        to_right, to_left = at_place(blocks, me + k), at_place(blocks, me - k)
        rights[k] = lax.ppermute(to_right, "seq", [(i, i + k) for i in range(n - k)])
        lefts[k] = lax.ppermute(to_left, "seq", [(i, i - k) for i in range(k, n)])
    return rights, lefts


def swap(value, axis, bit):
    return lax.ppermute(value, axis, [(i, i ^ bit) for i in range(lax.axis_size(axis))])


def total(value, *axes):
    for axis in axes:
        for step in range(lax.axis_size(axis).bit_length() - 1):
            value = value + swap(value, axis, 1 << step)
    return value


def fsdp_bits():
    bits = [1 << step for step in range(lax.axis_size("fsdp").bit_length() - 1)]
    return tuple(bits), tuple(bits[:1] + bits[:0:-1])


def total_steps(value, *axes):
    for axis in axes:
        for step in range(lax.axis_size(axis).bit_length() - 1):
            here = swap(value, axis, 1 << step)
            here = yield here
            value = value + here
    while True:
        yield value


class Halving:
    def __init__(self, keep, send, bits):
        self.terms, self.send, self.bits = [keep], send, list(bits)

    def go(self):
        self.terms = self.terms + [swap(self.send, "fsdp", self.bits.pop(0))]

    def add(self):
        half = self.terms[0].shape[0] // 2
        if half:
            self.send = sum(term[half:].astype(full) for term in self.terms).astype(low)
            self.terms = [term[:half] for term in self.terms]

    def finish(self):
        while self.bits:
            self.go()
            self.add()
        return sum(term[0].astype(full) for term in self.terms)


def rows_halving(part, bits):
    devs = lax.axis_size("fsdp")
    order = lax.axis_index("fsdp") ^ jnp.array(halving_masks(bits), jnp.int32)
    blocks = part.reshape(devs, part.shape[0] // devs, part.shape[1])[order]
    return Halving(blocks[: devs // 2], blocks[devs // 2 :], bits)


def land(sums, *others):
    tied = tie([each.terms[-1] for each in sums], *others)
    for each, here in zip(sums, tied[0]):
        each.terms = each.terms[:-1] + [here]
    return tied[1:]


def leave(sums, *others):
    tied = tie([each.send for each in sums], *others)
    for each, send in zip(sums, tied[0]):
        each.send = send
    return tied[1:]


def nt(a, b):
    return lax.dot_general(a, b, (((1,), (1,)), ((), ())), preferred_element_type=full)

def nn(a, b):
    return lax.dot_general(a, b, (((1,), (0,)), ((), ())), preferred_element_type=full)

def tn(a, b):
    return lax.dot_general(a, b, (((0,), (0,)), ((), ())), preferred_element_type=full)


def beside(rows):
    return jnp.concatenate([rows[h] for h in range(GROUP)], axis=1)

def key_steps(i, seq_len, query_rows, key_rows):
    free = (i * query_rows) // key_rows
    need = ((i + 1) * query_rows + BLOCK - 1 + key_rows - 1) // key_rows
    return free, jnp.minimum(need, seq_len // key_rows)

def forward_kernel(seq_len, query_rows, key_rows, limit_ref, q_ref, k_ref, vt_ref, low_ref, out_ref, lse_ref):
    i = pl.program_id(1)
    qt = beside(q_ref[0, 0])
    width = GROUP * query_rows
    limit = jnp.concatenate([limit_ref[...]] * GROUP, axis=1)

    def step(masked, j, carry):
        peak, total, acc = carry
        start = pl.multiple_of(j * key_rows, key_rows)
        s = nn(k_ref[0, pl.ds(start, key_rows), :], qt)
        if masked:
            place = start + lax.broadcasted_iota(jnp.int32, (key_rows, 1), 0)
            s = jnp.where(place < limit, s, masked_score)
        new_peak = jnp.maximum(peak, jnp.max(s, axis=0, keepdims=True))
        shrink = jnp.exp(peak - new_peak)
        p = jnp.exp(s - new_peak)
        total = shrink * total + jnp.sum(p, axis=0, keepdims=True)
        acc = shrink * acc + nn(vt_ref[0, :, pl.ds(start, key_rows)], p.astype(low))
        return new_peak, total, acc

    free, need = key_steps(i, seq_len, query_rows, key_rows)
    carry = (
        jnp.full((1, width), masked_score, full),
        jnp.zeros((1, width), full),
        jnp.zeros((HEAD_DIM, width), full),
    )
    carry = lax.fori_loop(0, free, lambda j, c: step(False, j, c), carry)
    peak, total, acc = lax.fori_loop(free, need, lambda j, c: step(True, j, c), carry)
    out = acc / total
    lse = peak + jnp.log(total)
    for h in range(GROUP):
        cols = slice(h * query_rows, (h + 1) * query_rows)
        out_ref[0, h] = out[:, cols]
        low_ref[0, pl.ds(h * HEAD_DIM, HEAD_DIM), :] = out[:, cols].astype(low)
        lse_ref[0, h] = lse[:, cols]

def query_spec(query_rows, per):
    return pl.BlockSpec(
        (1, 1, GROUP, HEAD_DIM, query_rows), lambda g, i: (i // per, g, 0, 0, i % per)
    )


def attention_forward(heads, k_rows, vt, limit):
    kv_here, shard_len = heads.shape[1], heads.shape[4]
    seq_len = k_rows.shape[1]
    query_rows = min(256, shard_len)
    key_rows = min(512, seq_len)
    per = shard_len // query_rows
    return pl.pallas_call(
        functools.partial(forward_kernel, seq_len, query_rows, key_rows),
        grid=(kv_here, seq_len // query_rows),
        in_specs=[
            pl.BlockSpec((1, query_rows), lambda g, i: (0, i)),
            query_spec(query_rows, per),
            pl.BlockSpec((1, seq_len, HEAD_DIM), lambda g, i: (g, 0, 0)),
            pl.BlockSpec((1, HEAD_DIM, seq_len), lambda g, i: (g, 0, 0)),
        ],
        out_specs=[
            pl.BlockSpec((1, GROUP * HEAD_DIM, query_rows), lambda g, i: (i // per, g, i % per)),
            pl.BlockSpec((1, GROUP, HEAD_DIM, query_rows), lambda g, i: (g, 0, 0, i)),
            pl.BlockSpec((1, GROUP, 1, query_rows), lambda g, i: (g, 0, 0, i)),
        ],
        out_shape=[
            jax.ShapeDtypeStruct((seq_len // shard_len, kv_here * GROUP * HEAD_DIM, shard_len), low),
            jax.ShapeDtypeStruct((kv_here, GROUP, HEAD_DIM, seq_len), full),
            jax.ShapeDtypeStruct((kv_here, GROUP, 1, seq_len), full),
        ],
        compiler_params=vmem(60),
        name="attention_forward",
    )(limit, heads, k_rows, vt)

def backward_kernel(
    seq_len, query_rows, key_rows, per, me_ref, limit_ref, q_ref, k_ref, v_ref, kt_ref, out_ref, lse_ref, *refs
):
    blocks, (dq_ref, dk_ref, dv_ref, dk_acc, dv_acc, held) = refs[:-6], refs[-6:]
    i = pl.program_id(1)

    @pl.when(i == 0)
    def _():
        dk_acc[...] = jnp.zeros_like(dk_acc)
        dv_acc[...] = jnp.zeros_like(dv_acc)

    qt = beside(q_ref[0, 0])
    limit = jnp.concatenate([limit_ref[...]] * GROUP, axis=1)
    devs = (len(blocks) + 1) // 2
    gap = me_ref[0] - i // per
    for spot, block in enumerate(blocks):

        @pl.when(gap == (spot if spot < devs else devs - 1 - spot))
        def _():
            held[...] = block[...]

    dout = jnp.concatenate([held[pl.ds(h * HEAD_DIM, HEAD_DIM), :] for h in range(GROUP)], axis=1)
    delta = jnp.sum(dout.astype(full) * beside(out_ref[0]), axis=0, keepdims=True)
    lse = beside(lse_ref[0])

    def step(masked, j, dq):
        start = pl.multiple_of(j * key_rows, key_rows)
        keys = pl.ds(start, key_rows)
        s = nn(k_ref[0, keys, :], qt)
        if masked:
            place = start + lax.broadcasted_iota(jnp.int32, (key_rows, 1), 0)
            s = jnp.where(place < limit, s, masked_score)
        p = jnp.exp(s - lse)
        dp = nn(v_ref[0, keys, :], dout)
        ds = (p * (dp - delta)).astype(low)
        dk_acc[:, keys] += nt(qt, ds)
        dv_acc[:, keys] += nt(dout, p.astype(low))
        return dq + nn(kt_ref[0, :, keys], ds)

    free, need = key_steps(i, seq_len, query_rows, key_rows)
    dq = jnp.zeros((HEAD_DIM, GROUP * query_rows), full)
    dq = lax.fori_loop(0, free, lambda j, c: step(False, j, c), dq)
    dq = lax.fori_loop(free, need, lambda j, c: step(True, j, c), dq) * attn_mult
    for h in range(GROUP):
        dq_ref[0, h] = dq[:, h * query_rows : (h + 1) * query_rows].astype(low)

    @pl.when(i == pl.num_programs(1) - 1)
    def _():
        dk_ref[0] = dk_acc[...].astype(low)
        dv_ref[0] = dv_acc[...].astype(low)

def attention_backward(heads, k_rows, v_rows, kt, limit, out, lse, me, rights, lefts):
    blocks = [*rights, *lefts[1:]]
    kv_here, shard_len = heads.shape[1], heads.shape[4]
    seq_len = k_rows.shape[1]
    query_rows = min(256, shard_len)
    key_rows = min(512, seq_len)
    per = shard_len // query_rows
    quarter = lambda g, i, me: (g, 0, 0, i)
    whole = lambda g, i, me: (g, 0, 0)
    return pl.pallas_call(
        functools.partial(backward_kernel, seq_len, query_rows, key_rows, per),
        grid_spec=pltpu.PrefetchScalarGridSpec(
            num_scalar_prefetch=1,
            grid=(kv_here, seq_len // query_rows),
            in_specs=[
                pl.BlockSpec((1, query_rows), lambda g, i, me: (0, i)),
                pl.BlockSpec(
                    (1, 1, GROUP, HEAD_DIM, query_rows),
                    lambda g, i, me: (i // per, g, 0, 0, i % per),
                ),
                pl.BlockSpec((1, seq_len, HEAD_DIM), whole),
                pl.BlockSpec((1, seq_len, HEAD_DIM), whole),
                pl.BlockSpec((1, HEAD_DIM, seq_len), whole),
                pl.BlockSpec((1, GROUP, HEAD_DIM, query_rows), quarter),
                pl.BlockSpec((1, GROUP, 1, query_rows), quarter),
            ]
            + [pl.BlockSpec((GROUP * HEAD_DIM, query_rows), lambda g, i, me: (g, i % per))]
            * len(blocks),
            out_specs=[
                pl.BlockSpec((1, GROUP, HEAD_DIM, query_rows), quarter),
                pl.BlockSpec((1, HEAD_DIM, seq_len), whole),
                pl.BlockSpec((1, HEAD_DIM, seq_len), whole),
            ],
            scratch_shapes=[
                pltpu.VMEM((HEAD_DIM, seq_len), full),
                pltpu.VMEM((HEAD_DIM, seq_len), full),
                pltpu.VMEM((GROUP * HEAD_DIM, query_rows), low),
            ],
        ),
        out_shape=[
            jax.ShapeDtypeStruct((kv_here, GROUP, HEAD_DIM, seq_len), low),
            jax.ShapeDtypeStruct((kv_here, HEAD_DIM, seq_len), low),
            jax.ShapeDtypeStruct((kv_here, HEAD_DIM, seq_len), low),
        ],
        compiler_params=vmem(60),
        name="attention_backward",
    )(me, limit, heads, k_rows, v_rows, kt, out, lse, *blocks)


def vmem(mib):
    return pltpu.CompilerParams(vmem_limit_bytes=mib * 2**20)


def own_row(ref, row):
    return ref[pl.ds(row, 1), :]


def join_down(rows, block_ref, down_ref):
    hidden, width = down_ref.shape
    chunks = width // hidden
    for dev in range(hidden // rows):
        for chunk in range(chunks):
            start = (dev * chunks + chunk) * rows
            down_ref[dev * rows : (dev + 1) * rows, chunk * hidden : (chunk + 1) * hidden] = (
                block_ref[start : start + rows, :]
            )


def pick_rows(pick, tok_ref, more_ref):
    middle = tok_ref.shape[0]
    return (nn(pick[:, :middle], tok_ref[...]) + nn(pick[:, middle:], more_ref[:middle, :])).astype(low)


def experts_kernel(
    few, pair, at_ref, tok_ref, more_ref, slot_ref, member_ref, router_ref, wgu_ref, wd_ref, *refs
):
    part_ref, x_ref, gu_ref, gates_ref, acc, gates_all, down = refs[-7:]
    step, steps = pl.program_id(0), pl.num_programs(0)
    slots = x_ref.shape[2]

    @pl.when(step == 0)
    def _():
        member = member_ref[...] > 0
        logits = [nt(router_ref[...], ref[...]) for ref in (tok_ref, more_ref)]
        chosen = jnp.where(member, jnp.concatenate(logits, axis=1), masked_score)
        chosen = jnp.exp(chosen - jnp.max(chosen, axis=0, keepdims=True))
        chosen = jnp.where(member, chosen, 0.0)
        gates_all[...] = chosen / jnp.sum(chosen, axis=0, keepdims=True)
        acc[...] = jnp.zeros_like(acc)

    place = lax.broadcasted_iota(jnp.int32, (slots, 1), 0)
    puts, ys = [], []
    for i in range(pair):
        e = step * pair + i
        gate_row = own_row(gates_all, at_ref[1] * (steps * pair) + e)
        gates_ref[pl.ds(e, 1), :] = gate_row
        here = place == own_row(slot_ref, e)
        x = pick_rows(jnp.where(here, 1.0, 0.0).astype(low), tok_ref, more_ref)
        x_ref[i, 0] = x
        gu = nn(x, wgu_ref[i])
        gu_ref[i, 0] = gu.astype(low)
        hidden = gu.shape[1] // 2
        g, u = gu[:, :hidden], gu[:, hidden:]
        act = (g * jax.nn.sigmoid(g) * u).astype(low)
        join_down(few, wd_ref.at[i], down.at[i])
        ys.append(nn(act, down[i]).astype(low))
        puts.append(jnp.where(here, gate_row, 0.0).astype(low))
    acc[...] += tn(jnp.concatenate(puts), jnp.concatenate(ys))

    @pl.when(step == steps - 1)
    def _():
        part_ref[0] = acc[...].astype(low)


def back_kernel(
    few, pair, at_ref, tok_ref, more_ref, slot_ref, gates_ref, mix_ref, router_ref, gu_ref, wgu_ref, wd_ref, *refs
):
    part_ref, d_ref, dgu_ref, act_ref, dlog_ref, acc, dlog_all, down = refs[-8:]
    step, steps = pl.program_id(0), pl.num_programs(0)
    slots, hidden = gu_ref.shape[2], gu_ref.shape[3] // 2

    @pl.when(step == 0)
    def _():
        dlog_all[...] = jnp.zeros_like(dlog_all)
        acc[...] = jnp.zeros_like(acc)

    place = lax.broadcasted_iota(jnp.int32, (slots, 1), 0)
    puts, dxs = [], []
    for i in range(pair):
        e = step * pair + i
        here = place == own_row(slot_ref, e)
        pick = jnp.where(here, 1.0, 0.0).astype(low)
        gate_row = own_row(gates_ref, e)
        gate = jnp.sum(jnp.where(here, gate_row, 0.0), axis=1, keepdims=True)
        d = pick_rows(pick, tok_ref, more_ref)
        d_ref[i, 0] = d
        join_down(few, wd_ref.at[i], down.at[i])
        d_act = nt(d, down[i])
        g, u = gu_ref[i, 0, :, :hidden].astype(full), gu_ref[i, 0, :, hidden:].astype(full)
        sig = jax.nn.sigmoid(g)
        silu = g * sig
        act = silu * u
        d_gate = jnp.sum(d_act * act, axis=1, keepdims=True)
        d_gate = jnp.sum(jnp.where(here, d_gate, 0.0), axis=0, keepdims=True)
        dlog_all[pl.ds(e, 1), :] = gate_row * (d_gate - mix_ref[...])
        act_ref[i, 0] = (act * gate).astype(low)
        d_act = d_act * gate
        d_g = (d_act * u * (sig + silu * (1.0 - sig))).astype(low)
        d_u = (d_act * silu).astype(low)
        dgu_ref[i, 0, :, :hidden] = d_g
        dgu_ref[i, 0, :, hidden:] = d_u
        dxs.append(nt(dgu_ref[i, 0], wgu_ref[i]).astype(low))
        puts.append(pick)
    acc[...] += tn(jnp.concatenate(puts), jnp.concatenate(dxs))

    @pl.when(step == steps - 1)
    def _():
        dlog = dlog_all[...].astype(low)
        dlog_ref[...] = dlog
        part_ref[0] = (acc[...] + tn(dlog, router_ref[...])).astype(low)


def by_expert(*shape):
    return pl.BlockSpec((1,) + shape, lambda e, at: (e, 0, 0))


def in_turn(pair, turn, *shape):
    return pl.BlockSpec((pair, 1) + shape, lambda e, at: (e, turn, 0, 0))


def same(*shape):
    return pl.BlockSpec(shape, lambda e, at: (0, 0))


def in_place(*shape):
    return pl.BlockSpec((1,) + shape, lambda e, at: (at[0], 0, 0))


def shard_call(kernel, name, at, inputs, in_specs, out_specs, out_shape, buffers, scratch, experts):
    first = len(inputs) + 1
    aliases = {first + i: i for i in range(len(buffers))}
    return pl.pallas_call(
        kernel,
        grid_spec=pltpu.PrefetchScalarGridSpec(
            num_scalar_prefetch=1,
            grid=(experts,),
            in_specs=in_specs + [pl.BlockSpec(memory_space=pl.ANY)] * len(buffers),
            out_specs=out_specs,
            scratch_shapes=scratch,
        ),
        out_shape=out_shape,
        input_output_aliases=aliases,
        compiler_params=vmem(48),
        name=name,
    )(at, *inputs, *buffers)


def weight_specs(pair, width, hidden):
    return [
        pl.BlockSpec((pair, width, 2 * hidden), lambda e, at: (e, 0, 0)),
        pl.BlockSpec((pair, width, hidden), lambda e, at: (e, 0, 2)),
    ]


def experts_forward(turn, devs, at, tokens, slot_of, member, router, weights, few, slots, buffers):
    experts, width, columns = weights.shape
    hidden = columns // 3
    pair = 1 + (experts + 1) % 2
    count = 2 * tokens[0].shape[0]
    total_experts = member.shape[0]
    return shard_call(
        functools.partial(experts_kernel, few, pair),
        "experts_forward",
        at,
        [*tokens, slot_of, member, router, weights, weights],
        [
            *(same(*half.shape) for half in tokens),
            same(experts, count),
            same(total_experts, count),
            same(total_experts, width),
            *weight_specs(pair, width, hidden),
        ],
        [
            in_place(count, width),
            in_turn(pair, turn, slots, width),
            in_turn(pair, turn, slots, 2 * hidden),
            same(experts, count),
        ],
        [
            jax.ShapeDtypeStruct((devs, count, width), low),
            jax.ShapeDtypeStruct((experts, devs, slots, width), low),
            jax.ShapeDtypeStruct((experts, devs, slots, 2 * hidden), low),
            jax.ShapeDtypeStruct((experts, count), full),
        ],
        buffers,
        [
            pltpu.VMEM((count, width), full),
            pltpu.VMEM((total_experts, count), full),
            pltpu.VMEM((pair, hidden, width), low),
        ],
        experts // pair,
    )


def experts_backward(
    turn, devs, at, d_tokens, slot_of, gates, mix_dot, router, gu, weights, few, buffers
):
    experts, width, columns = weights.shape
    hidden = columns // 3
    pair = 1 + (experts + 1) % 2
    count = 2 * d_tokens[0].shape[0]
    slots = gu.shape[2]
    lines = router.shape[0]
    return shard_call(
        functools.partial(back_kernel, few, pair),
        "experts_backward",
        at,
        [*d_tokens, slot_of, gates, mix_dot, router, gu, weights, weights],
        [
            *(same(*half.shape) for half in d_tokens),
            same(experts, count),
            same(experts, count),
            same(1, count),
            same(lines, width),
            in_turn(pair, turn, slots, 2 * hidden),
            *weight_specs(pair, width, hidden),
        ],
        [
            in_place(count, width),
            in_turn(pair, turn, slots, width),
            in_turn(pair, turn, slots, 2 * hidden),
            in_turn(pair, turn, slots, hidden),
            same(lines, count),
        ],
        [
            jax.ShapeDtypeStruct((devs, count, width), low),
            jax.ShapeDtypeStruct((experts, devs, slots, width), low),
            jax.ShapeDtypeStruct((experts, devs, slots, 2 * hidden), low),
            jax.ShapeDtypeStruct((experts, devs, slots, hidden), low),
            jax.ShapeDtypeStruct((lines, count), low),
        ],
        buffers,
        [
            pltpu.VMEM((count, width), full),
            pltpu.VMEM((lines, count), full),
            pltpu.VMEM((pair, hidden, width), low),
        ],
        experts // pair,
    )


def halving_masks(bits):
    masks = [0]
    for bit in reversed(bits):
        masks = masks + [mask ^ bit for mask in masks]
    return masks


def out_kernel(bits_a, bits_b, me_ref, rows_ref, d_ref, *refs):
    outs, acc = refs[:4], refs[4]
    half = outs[0].shape[2]
    for part, bits in enumerate((bits_a, bits_b)):
        keep, send = outs[2 * part], outs[2 * part + 1]
        rows = keep.shape[1]
        acc[...] = nn(rows_ref[...], d_ref[:, part * half : (part + 1) * half])
        for place, mask in enumerate(halving_masks(bits)):
            out = keep if place < keep.shape[0] else send
            start = pl.multiple_of((me_ref[0] ^ mask) * rows, rows)
            out[place % keep.shape[0]] = acc[pl.ds(start, rows), :].astype(low)


def out_grads(me, rows, d_proj, bits_a, bits_b):
    (height, count), width = rows.shape, d_proj.shape[1]
    devs = 2 ** len(bits_a)
    shape = (devs // 2, height // devs, width // 2)
    outs = pl.pallas_call(
        functools.partial(out_kernel, bits_a, bits_b),
        grid_spec=pltpu.PrefetchScalarGridSpec(
            num_scalar_prefetch=1,
            grid=(1,),
            in_specs=[same(height, count), same(count, width)],
            out_specs=[pl.BlockSpec(shape, lambda e, me: (0, 0, 0))] * 4,
            scratch_shapes=[pltpu.VMEM((height, width // 2), full)],
        ),
        out_shape=[jax.ShapeDtypeStruct(shape, low)] * 4,
        compiler_params=vmem(48),
        name="out_grads",
    )(me, rows, d_proj)
    return (outs[0], outs[1]), (outs[2], outs[3])


def grads_kernel(few, x_ref, dgu_ref, act_ref, d_ref, *refs):
    out_ref, down = refs[-2], refs[-1]
    hidden, width = down.shape
    out_ref[0, :, : 2 * hidden] = tn(x_ref[0], dgu_ref[0]).astype(low)
    down[...] = tn(act_ref[0], d_ref[0]).astype(low)
    chunks = width // hidden
    for dev in range(hidden // few):
        for chunk in range(chunks):
            start = (dev * chunks + chunk) * few
            out_ref[0, start : start + few, 2 * hidden :] = down[
                dev * few : (dev + 1) * few, chunk * hidden : (chunk + 1) * hidden
            ]


def weight_grads(rows, d_gu, act, d_rows, few, first, stop, buffers):
    experts, count, width = rows.shape
    hidden = act.shape[2]

    def part(*block):
        return pl.BlockSpec((1,) + block, lambda e: (first + e, 0, 0))

    return pl.pallas_call(
        functools.partial(grads_kernel, few),
        grid=(stop - first,),
        in_specs=[part(count, width), part(count, 2 * hidden), part(count, hidden), part(count, width)]
        + [pl.BlockSpec(memory_space=pl.ANY)] * len(buffers),
        out_specs=part(width, 3 * hidden),
        out_shape=jax.ShapeDtypeStruct((experts, width, 3 * hidden), low),
        scratch_shapes=[pltpu.VMEM((hidden, width), low)],
        input_output_aliases={4 + i: i for i in range(len(buffers))},
        compiler_params=vmem(56),
        name="weight_grads",
    )(rows, d_gu, act, d_rows, *buffers)


def shards(
    inputs,
    teacher,
    routes,
    valid_mask,
    block_lengths,
    gain_one,
    w_qkv,
    w_out,
    gain_two,
    w_router,
    w_gate,
    w_up,
    w_down,
):
    n = lax.axis_size("seq")
    me = lax.axis_index("seq")
    mine = lax.axis_index("fsdp")
    seqs_here, shard_len, width = inputs.shape
    assert seqs_here == 1
    seq_len = shard_len * n
    tokens_all = lax.axis_size("fsdp") * seq_len
    kv_here = KV_HEADS // n
    heads_w = kv_here * GROUP * HEAD_DIM
    group_w = kv_here * (GROUP + 2) * HEAD_DIM
    experts_here = w_gate.shape[0]
    expert_total = experts_here * n
    top_count = routes.shape[2]
    capacity = 3 * shard_len * top_count // (2 * expert_total)
    slots = -(-capacity // 16) * 16
    slot_rows = n * slots
    order_a, order_b = fsdp_bits()
    order = jnp.array(arrival_order(n), jnp.int32)[me]
    x_low = inputs.reshape(shard_len, width)

    own_qkv = lax.dynamic_slice_in_dim(w_qkv, me * group_w, group_w, 1)
    small = jnp.concatenate([gain_one[:, None], gain_two[:, None], w_router], axis=1)
    small = jnp.pad(small, ((0, 0), (0, -small.shape[1] % 128)))
    first = lax.all_gather(
        jnp.concatenate([own_qkv, small, w_out], axis=1), "fsdp", axis=0, tiled=True
    )
    full_qkv = first[:, :group_w]
    small = first[:, group_w : group_w + 2 + expert_total]
    full_out = first[:, -width:]
    full_g1 = small[:, 0].astype(full)
    full_g2 = small[:, 1].astype(full)
    router = small[:, 2:].T
    own_router = lax.dynamic_slice_in_dim(router, me * experts_here, experts_here, 0)
    own_router = jnp.pad(own_router, ((0, -experts_here % 16), (0, 0)))
    valid_rows = valid_mask.reshape(shard_len).astype(full)

    hidden_w = w_gate.shape[2]
    down_chunks = [
        w_down[:, :, start : start + hidden_w] for start in range(0, width, hidden_w)
    ]
    weights = lax.all_gather(
        jnp.concatenate([w_gate, w_up, jnp.concatenate(down_chunks, axis=1)], axis=2),
        "fsdp",
        axis=1,
        tiled=True,
    )

    routes_low = jnp.concatenate([routes.reshape(shard_len, top_count).T, valid_mask], axis=0)
    routes_low = jnp.pad(
        routes_low.astype(low), ((0, -routes_low.shape[0] % 16), (0, width - shard_len))
    )
    middle = shard_len // 2
    halves = (x_low[:middle], jnp.concatenate([x_low[middle:], routes_low], axis=0))
    positions = jnp.arange(seq_len, dtype=jnp.int32)
    cosine, sine_vals = rope_tables(positions.astype(full), HEAD_DIM)
    limit = block_limits(block_lengths[0], positions)[None]
    normed_one = jnp.zeros((seq_len, width), low)
    heads = jnp.zeros((n, kv_here, GROUP + 2, HEAD_DIM, shard_len), low)
    routes_all = []
    line = LineGather(halves)
    for turn in range(n):
        if turn:
            line.land(0, heads if turn > 1 else ())
            if turn < n - 1:
                line.go(0)
            line.land(1, ())
            if turn < n - 1:
                line.go(1)
        else:
            line.go(0)
            line.go(1)
        block = jnp.concatenate(line.block(turn))
        start = order[turn] * shard_len
        normed = rms_norm(block[:shard_len].astype(full), full_g1).astype(low)
        projected = dot("td,dc->ct", normed, full_qkv)
        projected = projected.reshape(kv_here, GROUP + 2, HEAD_DIM, shard_len)
        turned = rotate(
            projected[:, : GROUP + 1],
            lax.dynamic_slice_in_dim(cosine, start, shard_len, 1),
            lax.dynamic_slice_in_dim(sine_vals, start, shard_len, 1),
        ).astype(low)
        turned = jnp.concatenate(
            [
                turned[:, :GROUP] * jnp.asarray(attn_mult, low),
                turned[:, GROUP:],
                projected[:, GROUP + 1 :].astype(low),
            ],
            axis=1,
        )
        heads = lax.dynamic_update_index_in_dim(heads, turned, order[turn], 0)
        normed_one = lax.dynamic_update_slice_in_dim(normed_one, normed, start, 0)
        routes_all.append(block[shard_len : shard_len + top_count + 1, :shard_len])

    routes_all = jnp.stack(routes_all).astype(jnp.int32)
    valid_count = total(jnp.sum(routes_all[:, top_count]).astype(full).reshape(1, 1), "fsdp")[0, 0]
    expert_ids = jnp.arange(expert_total, dtype=jnp.int32)
    member = jnp.any(routes_all[:, :top_count, None, :] == expert_ids[:, None], axis=1)
    own_member = lax.dynamic_slice_in_dim(member, me * experts_here, experts_here, 1)
    earlier = jnp.arange(shard_len)[:, None] < jnp.arange(shard_len)[None, :]
    slot_of = dot("net,tu->neu", own_member.astype(low), earlier.astype(low)).astype(jnp.int32)
    slot_of = jnp.where(own_member, slot_of, -1)
    member = member.astype(full)

    key = jnp.moveaxis(heads[:, :, GROUP], 0, 2).reshape(kv_here, HEAD_DIM, seq_len)
    value = jnp.moveaxis(heads[:, :, GROUP + 1], 0, 2).reshape(kv_here, HEAD_DIM, seq_len)
    key_rows = jnp.swapaxes(key, 1, 2)
    value_rows = jnp.swapaxes(value, 1, 2)
    attended, out_heads, lse = attention_forward(heads, key_rows, value, limit)
    moved = exchange(attended)
    moved, slot_of, member, own_router = tie(moved, slot_of, member, own_router)
    attn_rows = by_place(nearest(*moved)).reshape(HEADS * HEAD_DIM, shard_len)
    projected = dot("kt,kd->td", attn_rows, full_out)
    hidden = x_low.astype(full) + resid_mult * projected
    normed_two, norm_two_pull = jax.vjp(rms_norm, hidden, full_g2)

    normed_low = normed_two.astype(low)
    line = LineGather((normed_low[:middle], normed_low[middle:]))
    buffers, gates, tokens = [], [], []
    line.go(0)
    line.go(1)
    other = ()
    for turn in range(n):
        if turn < n - 1:
            for h in (0, 1):
                other = line.land(h, other)
                if turn < n - 2:
                    line.go(h)
            line_slots = line.hold(slot_of[turn])
        else:
            line_slots = slot_of[turn]
        tokens.append(line.block(turn))
        *buffers, shard_gates = experts_forward(
            turn, n, jnp.stack([order[turn], me]), tokens[turn], line_slots, member[turn],
            router, weights, w_down.shape[1], slots, buffers,
        )
        gates.append(shard_gates)
        other = shard_gates
    mix_parts, expert_in, gate_up = buffers
    cuts = (slice(0, middle), slice(middle, None))
    mixture, _ = line_scatter(2, lambda h, shift: at_place(mix_parts[:, cuts[h]], me + shift), ())
    output_f32 = hidden + resid_mult * mixture
    activations = output_f32.astype(low).reshape(1, shard_len, width)
    error_rows = output_f32 - teacher.astype(full).reshape(shard_len, width)
    weighted = valid_rows[:, None] * error_rows
    loss_steps = total_steps(jnp.sum(weighted * error_rows).reshape(1, 1), "seq", "fsdp")
    squares = next(loss_steps)
    d_out = weighted * (tokens_all / valid_count)

    d_mix = resid_mult * d_out
    d_tokens = d_mix.astype(low)
    mix_dot = jnp.sum(d_mix * mixture, axis=1)[None]
    mix_high = mix_dot.astype(low)
    mix_rows = jnp.concatenate([mix_high, (mix_dot - mix_high.astype(full)).astype(low)])
    mix_rows = jnp.pad(mix_rows, ((0, 14), (0, width - shard_len)))
    line = LineGather((d_tokens[:middle], jnp.concatenate([d_tokens[middle:], mix_rows])))
    buffers, d_logits = [], []
    for turn in range(n):
        if turn:
            line.land(0, d_logits[-1])
            if turn < n - 1:
                line.go(0)
            line.land(1, ())
            if turn < n - 1:
                line.go(1)
        else:
            line.go(0)
            line.go(1)
        d_block = line.block(turn)
        mix_dot = d_block[1][middle : middle + 2, :shard_len].astype(full)
        mix_dot = jnp.sum(mix_dot, axis=0, keepdims=True)
        *buffers, shard_logits = experts_backward(
            turn, n, jnp.stack([order[turn], me]), d_block, slot_of[turn], gates[turn], mix_dot,
            own_router, gate_up, weights, w_down.shape[1], buffers,
        )
        d_logits.append(shard_logits)
    d_parts, d_rows, d_gate_up, act_low = buffers
    expert_in = expert_in.reshape(experts_here, slot_rows, width)
    d_rows = d_rows.reshape(experts_here, slot_rows, width)
    d_gate_up = d_gate_up.reshape(experts_here, slot_rows, -1)
    act_low = act_low.reshape(experts_here, slot_rows, -1)

    cut = (experts_here + 1) // 2

    def some_grads(first, stop):
        def make(before, grads):
            inputs, _ = tie((expert_in, d_gate_up, act_low, d_rows), before)
            return [weight_grads(*inputs, w_down.shape[1], first, stop, grads)]

        return make

    d_normed_two, grads = line_scatter(
        1,
        lambda h, shift: at_place(d_parts, me + shift),
        (some_grads(0, cut), some_grads(cut, experts_here)),
    )
    expert_sum = lax.psum_scatter(grads[0], "fsdp", scatter_dimension=1, tiled=True)

    d_hidden_norm, gain_two_part = norm_two_pull(d_normed_two)
    d_hidden = d_out + d_hidden_norm
    d_proj = (resid_mult * d_hidden).astype(low)
    out_pairs = out_grads(mine.reshape(1), attn_rows, d_proj, order_a, order_b)
    out_sums = [Halving(*pair, bits) for pair, bits in zip(out_pairs, (order_a, order_b))]
    for each in out_sums:
        each.go()
    d_attended = dot("kd,td->kt", full_out, d_proj).astype(low)
    (d_attended,) = land(out_sums, d_attended)
    moved = exchange(d_attended.reshape(n, heads_w, shard_len))
    for each in out_sums:
        each.add()
    router_part = sum(
        dot("td,et->de", half, half_logits)
        for shard, shard_logits in zip(tokens, d_logits)
        for half, half_logits in (
            (shard[0], shard_logits[:experts_here, :middle]),
            (shard[1], shard_logits[:experts_here, middle:]),
        )
    )
    own_columns = jnp.where(
        expert_ids // experts_here == me, jnp.concatenate([router_part] * n, axis=1), 0.0
    )
    own_columns = jnp.concatenate([own_columns, gain_two_part[:, None]], axis=1).astype(low)
    moved, own_columns, squares = leave(out_sums, moved, own_columns, squares)
    squares = loss_steps.send(squares)
    for each in out_sums:
        each.go()
    query_grad, key_grad, value_grad = attention_backward(
        heads, key_rows, value_rows, key, limit, out_heads, lse, me.reshape(1), *moved
    )
    (query_grad, key_grad, value_grad), squares = land(
        out_sums, (query_grad, key_grad, value_grad), squares
    )
    squares = loss_steps.send(squares)
    for each in out_sums:
        each.add()
        each.go()
    d_turned = jnp.concatenate([query_grad, key_grad[:, None]], axis=1).astype(full)
    d_turned = rotate(d_turned, cosine, -sine_vals).astype(low)
    d_qkv = jnp.concatenate([d_turned, value_grad[:, None]], axis=1).reshape(group_w, seq_len)

    def d_part(rows, shift):
        start = (me + shift) % n * shard_len
        rows = lax.dynamic_slice_in_dim(rows, start, shard_len, 1)
        return dot("ct,dc->td", rows, full_qkv).astype(low)

    d_parts = {shift: d_part(d_qkv, shift) for shift in {1, n - 1}}
    (d_parts,) = land(out_sums, d_parts)
    for each in out_sums:
        each.add()

    out_sum = jnp.concatenate([each.finish() for each in out_sums], axis=1).astype(low)
    out_rows = out_sum.shape[0] // n
    out_parts = jnp.swapaxes(out_sum.reshape(out_sum.shape[0], n, width // n), 0, 1)
    out_parts = out_parts.reshape(n, out_rows, width)

    def get(h, shift):
        part = d_parts[shift % n]
        if h == 0:
            return part[:middle]
        return jnp.concatenate([part[middle:], at_place(out_parts, me + shift)])

    sums = {}

    def first_work(before, _):
        rows, _ = tie(d_qkv, before)
        for shift in range(n):
            if shift not in d_parts:
                d_parts[shift] = d_part(rows, shift)
        qkv_part = jnp.concatenate(
            [dot("td,ct->dc", normed_one, rows).astype(low), own_columns], axis=1
        )
        sums["qkv"] = rows_halving(qkv_part, order_a)
        sums["qkv"].go()
        return sums["qkv"].send

    def next_work(before, _):
        land([sums["qkv"]], before)
        sums["qkv"].add()
        sums["qkv"].go()
        return sums["qkv"].send

    ended, _ = line_scatter(2, get, (first_work, next_work, next_work))
    qkv_sum = sums["qkv"]
    d_normed_one = ended[:shard_len]
    (ended,) = land([qkv_sum], ended)
    qkv_sum.add()
    out_own = ended[shard_len:].reshape(out_sum.shape[0], width // n)
    block = jnp.concatenate([qkv_sum.finish(), out_own], axis=1).astype(low)
    rights, lefts = [block], [block]
    _, norm_one_pull = jax.vjp(lambda v: rms_norm(v, full_g1), x_low.astype(full))
    input_grad = (d_hidden + norm_one_pull(d_normed_one)[0]).reshape(1, shard_len, width)
    few = w_down.shape[1]
    last_work = [
        lambda: expert_sum[:, :, : 2 * hidden_w].astype(full),
        lambda: jnp.concatenate(
            [
                expert_sum[:, start : start + few, 2 * hidden_w :].astype(full)
                for start in range(0, expert_sum.shape[1], few)
            ],
            axis=2,
        ),
    ]
    done = [input_grad]
    grads = [
        jnp.zeros((w_qkv.shape[0], QKV_W), full),
        jnp.zeros((w_out.shape[0], width), full),
        jnp.zeros((w_qkv.shape[0], block.shape[1] - group_w - width // n), full),
        jnp.zeros((w_qkv.shape[0],), full),
    ]

    def write(grads, turn):
        qkv_grad, out_grad, rest, gain_sum = grads
        came = arrived(rights, lefts, turn).astype(full)
        own_part, start = came[:, :group_w], order[turn] * group_w
        own_qkv = lax.dynamic_slice_in_dim(w_qkv, start, group_w, 1).astype(full)
        return [
            lax.dynamic_update_slice_in_dim(qkv_grad, own_part, start, 1),
            lax.dynamic_update_slice_in_dim(
                out_grad, came[:, -(width // n) :], order[turn] * (width // n), 1
            ),
            rest + came[:, group_w : -(width // n)],
            gain_sum + jnp.sum(own_part * own_qkv, axis=1),
        ]

    for k in range(1, n):
        right, left = line_move(rights[-1], lefts[-1], k)
        grads = write(grads, k - 1)
        if k < 3:
            done.append(last_work[k - 1]())
        right, left, done[-1], squares, grads = tie(right, left, done[-1], squares, grads)
        squares = loss_steps.send(squares)
        rights.append(right)
        lefts.append(left)
    qkv_grad, out_grad, rest, gain_sum = write(grads, n - 1)
    input_grad, gate_up_grad, down_grad = done
    gate_grad, up_grad = gate_up_grad[:, :, :hidden_w], gate_up_grad[:, :, hidden_w:]
    router_grad, gain_two_grad = rest[:, :expert_total], rest[:, expert_total]
    gain_one_grad = gain_sum / gain_one.astype(full)
    for _ in range(4):
        squares = loss_steps.send(squares)
    loss_value = squares[0, 0] / (valid_count * width)
    return (
        activations,
        loss_value,
        input_grad,
        gain_one_grad,
        qkv_grad,
        out_grad,
        gain_two_grad,
        router_grad,
        gate_grad,
        up_grad,
        down_grad,
    )


def solution(mesh):
    return jax.shard_map(
        shards,
        mesh=mesh,
        in_specs=(
            P("fsdp", "seq", None),
            P("fsdp", "seq", None),
            P("fsdp", "seq", None),
            P("fsdp", "seq"),
            P("fsdp", None),
            P("fsdp"),
            P("fsdp", None),
            P("fsdp", None),
            P("fsdp"),
            P("fsdp", None),
            P("seq", "fsdp", None),
            P("seq", "fsdp", None),
            P("seq", "fsdp", None),
        ),
        out_specs=(
            P("fsdp", "seq", None),
            P(),
            P("fsdp", "seq", None),
            P("fsdp"),
            P("fsdp", None),
            P("fsdp", None),
            P("fsdp"),
            P("fsdp", None),
            P("seq", "fsdp", None),
            P("seq", "fsdp", None),
            P("seq", "fsdp", None),
        ),
        check_vma=False,
    )
```

```python
import functools

import jax
import jax.numpy as jnp
from jax import lax
from jax.experimental import pallas as pl
from jax.experimental.pallas import tpu as pltpu
from jax.sharding import PartitionSpec as P

HEADS = 24
KV_HEADS = 8
HEAD_DIM = 64
BLOCK = 256
GROUP = 3
QKV_W = 2560


epsilon = 1e-06
attn_mult = 0.015625
resid_mult = 0.22
rope_base = 10000.0
masked_score = -1e30

low = jnp.bfloat16
full = jnp.float32


def dot(spec, left, right):
    return jnp.einsum(spec, left, right, preferred_element_type=full)


def rms_norm(values, gain_vec):
    inv_rms = lax.rsqrt(jnp.mean(values * values, axis=-1, keepdims=True) + epsilon)
    return values * inv_rms * gain_vec


def rope_tables(positions, head_dim):
    half_dim = head_dim // 2
    frequency = rope_base ** (-(2.0 * jnp.arange(half_dim, dtype=full)) / head_dim)
    angles = frequency[:, None] * positions[None, :]
    return (jnp.cos(angles), jnp.sin(angles))


def rotate(values, cosine, sine_vals):
    half_dim = values.shape[-2] // 2
    front_half = values[..., :half_dim, :]
    back_half = values[..., half_dim:, :]
    return jnp.concatenate(
        [front_half * cosine - back_half * sine_vals, back_half * cosine + front_half * sine_vals],
        axis=-2,
    )


def block_limits(lengths_row, positions):
    block_ends = jnp.cumsum(lengths_row)
    open_ends = jnp.where(block_ends[None, :] > positions[:, None], block_ends[None, :], positions.shape[0])
    return jnp.min(open_ends, axis=1).astype(jnp.int32)


def tie(*groups):
    return lax.optimization_barrier(groups)


def line_move(right, left, k):
    n = lax.axis_size("seq")
    return (
        lax.ppermute(right, "seq", [(i, i + 1) for i in range(k - 1, n - 1)]),
        lax.ppermute(left, "seq", [(i, i - 1) for i in range(1, n - k + 1)]),
    )


def line_gather(block):
    n = lax.axis_size("seq")
    rights, lefts = [block], [block]
    for k in range(1, n):
        right, left = tie(*line_move(rights[-1], lefts[-1], k))
        rights.append(right)
        lefts.append(left)
    return nearest(rights, lefts)


def nearest(rights, lefts):
    n = lax.axis_size("seq")
    me = lax.axis_index("seq")
    return [rights[0]] + [jnp.where(me >= k, rights[k], lefts[n - k]) for k in range(1, n)]


def arrival_order(n):
    order = []
    for me in range(n):
        both = min(me, n - 1 - me)
        places = [me]
        for k in range(1, n):
            places += [me - k] if me >= k and (k <= both or me > n - 1 - me) else []
            places += [me + k] if me + k < n and (k <= both or me < n - 1 - me) else []
        order.append(places)
    return order


def arrived(rights, lefts, turn):
    n = lax.axis_size("seq")
    me = lax.axis_index("seq")
    sources = {}
    for dev, places in enumerate(arrival_order(n)):
        gap = dev - places[turn]
        sources.setdefault(gap, []).append(dev)
    block = None
    for gap, devs in sources.items():
        moved = rights[gap] if gap >= 0 else lefts[-gap]
        if block is None:
            block = moved
        else:
            mine = jnp.array([dev in devs for dev in range(n)])[me]
            block = jnp.where(mine, moved, block)
    return block


def at_place(placed, place):
    return lax.dynamic_index_in_dim(placed, place % lax.axis_size("seq"), 0, keepdims=False)


def line_send(to_right, to_left, right, left):
    if right is not None:
        to_right = (to_right.astype(full) + right.astype(full)).astype(low)
        to_left = (to_left.astype(full) + left.astype(full)).astype(low)
    return to_right, to_left


def line_pass(to_right, to_left, k):
    n = lax.axis_size("seq")
    return (
        lax.ppermute(to_right, "seq", [(i, i + 1) for i in range(n - k)]),
        lax.ppermute(to_left, "seq", [(i, i - 1) for i in range(k, n)]),
    )


class LineGather:
    def __init__(self, halves):
        self.rights, self.lefts = [[half] for half in halves], [[half] for half in halves]
        self.landed = [0, 0]

    def go(self, h):
        step = len(self.rights[h])
        right, left = line_move(self.rights[h][-1], self.lefts[h][-1], step)
        self.rights[h].append(right)
        self.lefts[h].append(left)

    def land(self, h, other):
        spot = self.landed[h] = len(self.rights[h]) - 1
        moved = [(self.rights[part][spot], self.lefts[part][spot]) for part in range(h + 1)]
        moved, other = tie(moved, other)
        for part, (right, left) in enumerate(moved):
            self.rights[part][spot], self.lefts[part][spot] = right, left
        return other

    def hold(self, other):
        came = [(self.rights[h][-1 - self.ahead(h)], self.lefts[h][-1 - self.ahead(h)]) for h in (0, 1)]
        return tie(other, came)[0]

    def ahead(self, h):
        return len(self.rights[h]) - 1 - self.landed[h]

    def block(self, turn):
        return [arrived(self.rights[h], self.lefts[h], turn) for h in (0, 1)]


def line_scatter(count, get, work):
    n = lax.axis_size("seq")
    flying = [(None, None)] * count
    before, given = (), []
    for k in range(n - 1, 0, -1):
        for h in range(count):
            if k < n - 1 and h:
                flying[h], before = tie(flying[h], before)
            elif k < n - 1:
                flying[h], given = tie(flying[h], given)
            before = line_send(get(h, k), get(h, -k), *flying[h])
            flying[h] = line_pass(*before, k)
        if n - 1 - k < len(work):
            given = work[n - 1 - k](before, given)
    sums = []
    flying[0], given = tie(flying[0], given)
    for h, (right, left) in enumerate(flying):
        sums.append(get(h, 0).astype(full) + (right.astype(full) + left.astype(full)))
    return jnp.concatenate(sums), given


def by_place(blocks):
    n = lax.axis_size("seq")
    me = lax.axis_index("seq")
    placed = jnp.zeros((n,) + blocks[0].shape, blocks[0].dtype)
    for k, block in enumerate(blocks):
        placed = lax.dynamic_update_index_in_dim(placed, block, (me - k) % n, 0)
    return placed


def exchange(blocks):
    n = lax.axis_size("seq")
    me = lax.axis_index("seq")
    own = at_place(blocks, me)
    rights, lefts = [own] * n, [own] * n
    for k in range(n - 1, 0, -1):
        to_right, to_left = at_place(blocks, me + k), at_place(blocks, me - k)
        rights[k] = lax.ppermute(to_right, "seq", [(i, i + k) for i in range(n - k)])
        lefts[k] = lax.ppermute(to_left, "seq", [(i, i - k) for i in range(k, n)])
    return rights, lefts


def swap(value, axis, bit):
    return lax.ppermute(value, axis, [(i, i ^ bit) for i in range(lax.axis_size(axis))])


def total(value, *axes):
    for axis in axes:
        for step in range(lax.axis_size(axis).bit_length() - 1):
            value = value + swap(value, axis, 1 << step)
    return value


def fsdp_bits():
    bits = [1 << step for step in range(lax.axis_size("fsdp").bit_length() - 1)]
    return tuple(bits), tuple(bits[:1] + bits[:0:-1])


def total_steps(value, *axes):
    for axis in axes:
        for step in range(lax.axis_size(axis).bit_length() - 1):
            here = swap(value, axis, 1 << step)
            here = yield here
            value = value + here
    while True:
        yield value


class Halving:
    def __init__(self, keep, send, bits):
        self.terms, self.send, self.bits = [keep], send, list(bits)

    def go(self):
        self.terms = self.terms + [swap(self.send, "fsdp", self.bits.pop(0))]

    def add(self):
        half = self.terms[0].shape[0] // 2
        if half:
            self.send = sum(term[half:].astype(full) for term in self.terms).astype(low)
            self.terms = [term[:half] for term in self.terms]

    def finish(self):
        while self.bits:
            self.go()
            self.add()
        return sum(term[0].astype(full) for term in self.terms)


def rows_halving(part, bits):
    devs = lax.axis_size("fsdp")
    order = lax.axis_index("fsdp") ^ jnp.array(halving_masks(bits), jnp.int32)
    blocks = part.reshape(devs, part.shape[0] // devs, part.shape[1])[order]
    return Halving(blocks[: devs // 2], blocks[devs // 2 :], bits)


def land(sums, *others):
    tied = tie([each.terms[-1] for each in sums], *others)
    for each, here in zip(sums, tied[0]):
        each.terms = each.terms[:-1] + [here]
    return tied[1:]


def leave(sums, *others):
    tied = tie([each.send for each in sums], *others)
    for each, send in zip(sums, tied[0]):
        each.send = send
    return tied[1:]


def nt(a, b):
    return lax.dot_general(a, b, (((1,), (1,)), ((), ())), preferred_element_type=full)

def nn(a, b):
    return lax.dot_general(a, b, (((1,), (0,)), ((), ())), preferred_element_type=full)

def tn(a, b):
    return lax.dot_general(a, b, (((0,), (0,)), ((), ())), preferred_element_type=full)


def beside(rows):
    return jnp.concatenate([rows[h] for h in range(GROUP)], axis=1)

def key_steps(i, seq_len, query_rows, key_rows):
    free = (i * query_rows) // key_rows
    need = ((i + 1) * query_rows + BLOCK - 1 + key_rows - 1) // key_rows
    return free, jnp.minimum(need, seq_len // key_rows)

def forward_kernel(seq_len, query_rows, key_rows, limit_ref, q_ref, k_ref, vt_ref, low_ref, out_ref, lse_ref):
    i = pl.program_id(1)
    qt = beside(q_ref[0, 0])
    width = GROUP * query_rows
    limit = jnp.concatenate([limit_ref[...]] * GROUP, axis=1)

    def step(masked, j, carry):
        peak, total, acc = carry
        start = pl.multiple_of(j * key_rows, key_rows)
        s = nn(k_ref[0, pl.ds(start, key_rows), :], qt)
        if masked:
            place = start + lax.broadcasted_iota(jnp.int32, (key_rows, 1), 0)
            s = jnp.where(place < limit, s, masked_score)
        new_peak = jnp.maximum(peak, jnp.max(s, axis=0, keepdims=True))
        shrink = jnp.exp(peak - new_peak)
        p = jnp.exp(s - new_peak)
        total = shrink * total + jnp.sum(p, axis=0, keepdims=True)
        acc = shrink * acc + nn(vt_ref[0, :, pl.ds(start, key_rows)], p.astype(low))
        return new_peak, total, acc

    free, need = key_steps(i, seq_len, query_rows, key_rows)
    carry = (
        jnp.full((1, width), masked_score, full),
        jnp.zeros((1, width), full),
        jnp.zeros((HEAD_DIM, width), full),
    )
    carry = lax.fori_loop(0, free, lambda j, c: step(False, j, c), carry)
    peak, total, acc = lax.fori_loop(free, need, lambda j, c: step(True, j, c), carry)
    out = acc / total
    lse = peak + jnp.log(total)
    for h in range(GROUP):
        cols = slice(h * query_rows, (h + 1) * query_rows)
        out_ref[0, h] = out[:, cols]
        low_ref[0, pl.ds(h * HEAD_DIM, HEAD_DIM), :] = out[:, cols].astype(low)
        lse_ref[0, h] = lse[:, cols]

def query_spec(query_rows, per):
    return pl.BlockSpec(
        (1, 1, GROUP, HEAD_DIM, query_rows), lambda g, i: (i // per, g, 0, 0, i % per)
    )


def attention_forward(heads, k_rows, vt, limit):
    kv_here, shard_len = heads.shape[1], heads.shape[4]
    seq_len = k_rows.shape[1]
    query_rows = min(256, shard_len)
    key_rows = min(512, seq_len)
    per = shard_len // query_rows
    return pl.pallas_call(
        functools.partial(forward_kernel, seq_len, query_rows, key_rows),
        grid=(kv_here, seq_len // query_rows),
        in_specs=[
            pl.BlockSpec((1, query_rows), lambda g, i: (0, i)),
            query_spec(query_rows, per),
            pl.BlockSpec((1, seq_len, HEAD_DIM), lambda g, i: (g, 0, 0)),
            pl.BlockSpec((1, HEAD_DIM, seq_len), lambda g, i: (g, 0, 0)),
        ],
        out_specs=[
            pl.BlockSpec((1, GROUP * HEAD_DIM, query_rows), lambda g, i: (i // per, g, i % per)),
            pl.BlockSpec((1, GROUP, HEAD_DIM, query_rows), lambda g, i: (g, 0, 0, i)),
            pl.BlockSpec((1, GROUP, 1, query_rows), lambda g, i: (g, 0, 0, i)),
        ],
        out_shape=[
            jax.ShapeDtypeStruct((seq_len // shard_len, kv_here * GROUP * HEAD_DIM, shard_len), low),
            jax.ShapeDtypeStruct((kv_here, GROUP, HEAD_DIM, seq_len), full),
            jax.ShapeDtypeStruct((kv_here, GROUP, 1, seq_len), full),
        ],
        compiler_params=vmem(60),
        name="attention_forward",
    )(limit, heads, k_rows, vt)

def backward_kernel(
    seq_len, query_rows, key_rows, per, me_ref, limit_ref, q_ref, k_ref, v_ref, kt_ref, out_ref, lse_ref, *refs
):
    blocks, (dq_ref, dk_ref, dv_ref, dk_acc, dv_acc, held) = refs[:-6], refs[-6:]
    i = pl.program_id(1)

    @pl.when(i == 0)
    def _():
        dk_acc[...] = jnp.zeros_like(dk_acc)
        dv_acc[...] = jnp.zeros_like(dv_acc)

    qt = beside(q_ref[0, 0])
    limit = jnp.concatenate([limit_ref[...]] * GROUP, axis=1)
    devs = (len(blocks) + 1) // 2
    gap = me_ref[0] - i // per
    for spot, block in enumerate(blocks):

        @pl.when(gap == (spot if spot < devs else devs - 1 - spot))
        def _():
            held[...] = block[...]

    dout = jnp.concatenate([held[pl.ds(h * HEAD_DIM, HEAD_DIM), :] for h in range(GROUP)], axis=1)
    delta = jnp.sum(dout.astype(full) * beside(out_ref[0]), axis=0, keepdims=True)
    lse = beside(lse_ref[0])

    def step(masked, j, dq):
        start = pl.multiple_of(j * key_rows, key_rows)
        keys = pl.ds(start, key_rows)
        s = nn(k_ref[0, keys, :], qt)
        if masked:
            place = start + lax.broadcasted_iota(jnp.int32, (key_rows, 1), 0)
            s = jnp.where(place < limit, s, masked_score)
        p = jnp.exp(s - lse)
        dp = nn(v_ref[0, keys, :], dout)
        ds = (p * (dp - delta)).astype(low)
        dk_acc[:, keys] += nt(qt, ds)
        dv_acc[:, keys] += nt(dout, p.astype(low))
        return dq + nn(kt_ref[0, :, keys], ds)

    free, need = key_steps(i, seq_len, query_rows, key_rows)
    dq = jnp.zeros((HEAD_DIM, GROUP * query_rows), full)
    dq = lax.fori_loop(0, free, lambda j, c: step(False, j, c), dq)
    dq = lax.fori_loop(free, need, lambda j, c: step(True, j, c), dq) * attn_mult
    for h in range(GROUP):
        dq_ref[0, h] = dq[:, h * query_rows : (h + 1) * query_rows].astype(low)

    @pl.when(i == pl.num_programs(1) - 1)
    def _():
        dk_ref[0] = dk_acc[...].astype(low)
        dv_ref[0] = dv_acc[...].astype(low)

def attention_backward(heads, k_rows, v_rows, kt, limit, out, lse, me, rights, lefts):
    blocks = [*rights, *lefts[1:]]
    kv_here, shard_len = heads.shape[1], heads.shape[4]
    seq_len = k_rows.shape[1]
    query_rows = min(256, shard_len)
    key_rows = min(512, seq_len)
    per = shard_len // query_rows
    quarter = lambda g, i, me: (g, 0, 0, i)
    whole = lambda g, i, me: (g, 0, 0)
    return pl.pallas_call(
        functools.partial(backward_kernel, seq_len, query_rows, key_rows, per),
        grid_spec=pltpu.PrefetchScalarGridSpec(
            num_scalar_prefetch=1,
            grid=(kv_here, seq_len // query_rows),
            in_specs=[
                pl.BlockSpec((1, query_rows), lambda g, i, me: (0, i)),
                pl.BlockSpec(
                    (1, 1, GROUP, HEAD_DIM, query_rows),
                    lambda g, i, me: (i // per, g, 0, 0, i % per),
                ),
                pl.BlockSpec((1, seq_len, HEAD_DIM), whole),
                pl.BlockSpec((1, seq_len, HEAD_DIM), whole),
                pl.BlockSpec((1, HEAD_DIM, seq_len), whole),
                pl.BlockSpec((1, GROUP, HEAD_DIM, query_rows), quarter),
                pl.BlockSpec((1, GROUP, 1, query_rows), quarter),
            ]
            + [pl.BlockSpec((GROUP * HEAD_DIM, query_rows), lambda g, i, me: (g, i % per))]
            * len(blocks),
            out_specs=[
                pl.BlockSpec((1, GROUP, HEAD_DIM, query_rows), quarter),
                pl.BlockSpec((1, HEAD_DIM, seq_len), whole),
                pl.BlockSpec((1, HEAD_DIM, seq_len), whole),
            ],
            scratch_shapes=[
                pltpu.VMEM((HEAD_DIM, seq_len), full),
                pltpu.VMEM((HEAD_DIM, seq_len), full),
                pltpu.VMEM((GROUP * HEAD_DIM, query_rows), low),
            ],
        ),
        out_shape=[
            jax.ShapeDtypeStruct((kv_here, GROUP, HEAD_DIM, seq_len), low),
            jax.ShapeDtypeStruct((kv_here, HEAD_DIM, seq_len), low),
            jax.ShapeDtypeStruct((kv_here, HEAD_DIM, seq_len), low),
        ],
        compiler_params=vmem(60),
        name="attention_backward",
    )(me, limit, heads, k_rows, v_rows, kt, out, lse, *blocks)


def vmem(mib):
    return pltpu.CompilerParams(vmem_limit_bytes=mib * 2**20)


def own_row(ref, row):
    return ref[pl.ds(row, 1), :]


def join_down(rows, block_ref, down_ref):
    hidden, width = down_ref.shape
    chunks = width // hidden
    for dev in range(hidden // rows):
        for chunk in range(chunks):
            start = (dev * chunks + chunk) * rows
            down_ref[dev * rows : (dev + 1) * rows, chunk * hidden : (chunk + 1) * hidden] = (
                block_ref[start : start + rows, :]
            )


def pick_rows(pick, tok_ref, more_ref):
    middle = tok_ref.shape[0]
    return (nn(pick[:, :middle], tok_ref[...]) + nn(pick[:, middle:], more_ref[:middle, :])).astype(low)


def experts_kernel(
    few, pair, at_ref, tok_ref, more_ref, slot_ref, member_ref, router_ref, wgu_ref, wd_ref, *refs
):
    part_ref, x_ref, gu_ref, gates_ref, acc, gates_all, down = refs[-7:]
    step, steps = pl.program_id(0), pl.num_programs(0)
    slots = x_ref.shape[2]

    @pl.when(step == 0)
    def _():
        member = member_ref[...] > 0
        logits = [nt(router_ref[...], ref[...]) for ref in (tok_ref, more_ref)]
        chosen = jnp.where(member, jnp.concatenate(logits, axis=1), masked_score)
        chosen = jnp.exp(chosen - jnp.max(chosen, axis=0, keepdims=True))
        chosen = jnp.where(member, chosen, 0.0)
        gates_all[...] = chosen / jnp.sum(chosen, axis=0, keepdims=True)
        acc[...] = jnp.zeros_like(acc)

    place = lax.broadcasted_iota(jnp.int32, (slots, 1), 0)
    puts, ys = [], []
    for i in range(pair):
        e = step * pair + i
        gate_row = own_row(gates_all, at_ref[1] * (steps * pair) + e)
        gates_ref[pl.ds(e, 1), :] = gate_row
        here = place == own_row(slot_ref, e)
        x = pick_rows(jnp.where(here, 1.0, 0.0).astype(low), tok_ref, more_ref)
        x_ref[i, 0] = x
        gu = nn(x, wgu_ref[i])
        gu_ref[i, 0] = gu.astype(low)
        hidden = gu.shape[1] // 2
        g, u = gu[:, :hidden], gu[:, hidden:]
        act = (g * jax.nn.sigmoid(g) * u).astype(low)
        join_down(few, wd_ref.at[i], down.at[i])
        ys.append(nn(act, down[i]).astype(low))
        puts.append(jnp.where(here, gate_row, 0.0).astype(low))
    acc[...] += tn(jnp.concatenate(puts), jnp.concatenate(ys))

    @pl.when(step == steps - 1)
    def _():
        part_ref[0] = acc[...].astype(low)


def back_kernel(
    few, pair, at_ref, tok_ref, more_ref, slot_ref, gates_ref, mix_ref, router_ref, gu_ref, wgu_ref, wd_ref, *refs
):
    part_ref, d_ref, dgu_ref, act_ref, dlog_ref, acc, dlog_all, down = refs[-8:]
    step, steps = pl.program_id(0), pl.num_programs(0)
    slots, hidden = gu_ref.shape[2], gu_ref.shape[3] // 2

    @pl.when(step == 0)
    def _():
        dlog_all[...] = jnp.zeros_like(dlog_all)
        acc[...] = jnp.zeros_like(acc)

    place = lax.broadcasted_iota(jnp.int32, (slots, 1), 0)
    puts, dxs = [], []
    for i in range(pair):
        e = step * pair + i
        here = place == own_row(slot_ref, e)
        pick = jnp.where(here, 1.0, 0.0).astype(low)
        gate_row = own_row(gates_ref, e)
        gate = jnp.sum(jnp.where(here, gate_row, 0.0), axis=1, keepdims=True)
        d = pick_rows(pick, tok_ref, more_ref)
        d_ref[i, 0] = d
        join_down(few, wd_ref.at[i], down.at[i])
        d_act = nt(d, down[i])
        g, u = gu_ref[i, 0, :, :hidden].astype(full), gu_ref[i, 0, :, hidden:].astype(full)
        sig = jax.nn.sigmoid(g)
        silu = g * sig
        act = silu * u
        d_gate = jnp.sum(d_act * act, axis=1, keepdims=True)
        d_gate = jnp.sum(jnp.where(here, d_gate, 0.0), axis=0, keepdims=True)
        dlog_all[pl.ds(e, 1), :] = gate_row * (d_gate - mix_ref[...])
        act_ref[i, 0] = (act * gate).astype(low)
        d_act = d_act * gate
        d_g = (d_act * u * (sig + silu * (1.0 - sig))).astype(low)
        d_u = (d_act * silu).astype(low)
        dgu_ref[i, 0, :, :hidden] = d_g
        dgu_ref[i, 0, :, hidden:] = d_u
        dxs.append(nt(dgu_ref[i, 0], wgu_ref[i]).astype(low))
        puts.append(pick)
    acc[...] += tn(jnp.concatenate(puts), jnp.concatenate(dxs))

    @pl.when(step == steps - 1)
    def _():
        dlog = dlog_all[...].astype(low)
        dlog_ref[...] = dlog
        part_ref[0] = (acc[...] + tn(dlog, router_ref[...])).astype(low)


def by_expert(*shape):
    return pl.BlockSpec((1,) + shape, lambda e, at: (e, 0, 0))


def in_turn(pair, turn, *shape):
    return pl.BlockSpec((pair, 1) + shape, lambda e, at: (e, turn, 0, 0))


def same(*shape):
    return pl.BlockSpec(shape, lambda e, at: (0, 0))


def in_place(*shape):
    return pl.BlockSpec((1,) + shape, lambda e, at: (at[0], 0, 0))


def shard_call(kernel, name, at, inputs, in_specs, out_specs, out_shape, buffers, scratch, experts):
    first = len(inputs) + 1
    aliases = {first + i: i for i in range(len(buffers))}
    return pl.pallas_call(
        kernel,
        grid_spec=pltpu.PrefetchScalarGridSpec(
            num_scalar_prefetch=1,
            grid=(experts,),
            in_specs=in_specs + [pl.BlockSpec(memory_space=pl.ANY)] * len(buffers),
            out_specs=out_specs,
            scratch_shapes=scratch,
        ),
        out_shape=out_shape,
        input_output_aliases=aliases,
        compiler_params=vmem(48),
        name=name,
    )(at, *inputs, *buffers)


def weight_specs(pair, width, hidden):
    return [
        pl.BlockSpec((pair, width, 2 * hidden), lambda e, at: (e, 0, 0)),
        pl.BlockSpec((pair, width, hidden), lambda e, at: (e, 0, 2)),
    ]


def experts_forward(turn, devs, at, tokens, slot_of, member, router, weights, few, slots, buffers):
    experts, width, columns = weights.shape
    hidden = columns // 3
    pair = 1 + (experts + 1) % 2
    count = 2 * tokens[0].shape[0]
    total_experts = member.shape[0]
    return shard_call(
        functools.partial(experts_kernel, few, pair),
        "experts_forward",
        at,
        [*tokens, slot_of, member, router, weights, weights],
        [
            *(same(*half.shape) for half in tokens),
            same(experts, count),
            same(total_experts, count),
            same(total_experts, width),
            *weight_specs(pair, width, hidden),
        ],
        [
            in_place(count, width),
            in_turn(pair, turn, slots, width),
            in_turn(pair, turn, slots, 2 * hidden),
            same(experts, count),
        ],
        [
            jax.ShapeDtypeStruct((devs, count, width), low),
            jax.ShapeDtypeStruct((experts, devs, slots, width), low),
            jax.ShapeDtypeStruct((experts, devs, slots, 2 * hidden), low),
            jax.ShapeDtypeStruct((experts, count), full),
        ],
        buffers,
        [
            pltpu.VMEM((count, width), full),
            pltpu.VMEM((total_experts, count), full),
            pltpu.VMEM((pair, hidden, width), low),
        ],
        experts // pair,
    )


def experts_backward(
    turn, devs, at, d_tokens, slot_of, gates, mix_dot, router, gu, weights, few, buffers
):
    experts, width, columns = weights.shape
    hidden = columns // 3
    pair = 1 + (experts + 1) % 2
    count = 2 * d_tokens[0].shape[0]
    slots = gu.shape[2]
    lines = router.shape[0]
    return shard_call(
        functools.partial(back_kernel, few, pair),
        "experts_backward",
        at,
        [*d_tokens, slot_of, gates, mix_dot, router, gu, weights, weights],
        [
            *(same(*half.shape) for half in d_tokens),
            same(experts, count),
            same(experts, count),
            same(1, count),
            same(lines, width),
            in_turn(pair, turn, slots, 2 * hidden),
            *weight_specs(pair, width, hidden),
        ],
        [
            in_place(count, width),
            in_turn(pair, turn, slots, width),
            in_turn(pair, turn, slots, 2 * hidden),
            in_turn(pair, turn, slots, hidden),
            same(lines, count),
        ],
        [
            jax.ShapeDtypeStruct((devs, count, width), low),
            jax.ShapeDtypeStruct((experts, devs, slots, width), low),
            jax.ShapeDtypeStruct((experts, devs, slots, 2 * hidden), low),
            jax.ShapeDtypeStruct((experts, devs, slots, hidden), low),
            jax.ShapeDtypeStruct((lines, count), low),
        ],
        buffers,
        [
            pltpu.VMEM((count, width), full),
            pltpu.VMEM((lines, count), full),
            pltpu.VMEM((pair, hidden, width), low),
        ],
        experts // pair,
    )


def halving_masks(bits):
    masks = [0]
    for bit in reversed(bits):
        masks = masks + [mask ^ bit for mask in masks]
    return masks


def out_kernel(bits_a, bits_b, me_ref, rows_ref, d_ref, *refs):
    outs, acc = refs[:4], refs[4]
    half = outs[0].shape[2]
    for part, bits in enumerate((bits_a, bits_b)):
        keep, send = outs[2 * part], outs[2 * part + 1]
        rows = keep.shape[1]
        acc[...] = nn(rows_ref[...], d_ref[:, part * half : (part + 1) * half])
        for place, mask in enumerate(halving_masks(bits)):
            out = keep if place < keep.shape[0] else send
            start = pl.multiple_of((me_ref[0] ^ mask) * rows, rows)
            out[place % keep.shape[0]] = acc[pl.ds(start, rows), :].astype(low)


def out_grads(me, rows, d_proj, bits_a, bits_b):
    (height, count), width = rows.shape, d_proj.shape[1]
    devs = 2 ** len(bits_a)
    shape = (devs // 2, height // devs, width // 2)
    outs = pl.pallas_call(
        functools.partial(out_kernel, bits_a, bits_b),
        grid_spec=pltpu.PrefetchScalarGridSpec(
            num_scalar_prefetch=1,
            grid=(1,),
            in_specs=[same(height, count), same(count, width)],
            out_specs=[pl.BlockSpec(shape, lambda e, me: (0, 0, 0))] * 4,
            scratch_shapes=[pltpu.VMEM((height, width // 2), full)],
        ),
        out_shape=[jax.ShapeDtypeStruct(shape, low)] * 4,
        compiler_params=vmem(48),
        name="out_grads",
    )(me, rows, d_proj)
    return (outs[0], outs[1]), (outs[2], outs[3])


def grads_kernel(few, x_ref, dgu_ref, act_ref, d_ref, *refs):
    out_ref, down = refs[-2], refs[-1]
    hidden, width = down.shape
    out_ref[0, :, : 2 * hidden] = tn(x_ref[0], dgu_ref[0]).astype(low)
    down[...] = tn(act_ref[0], d_ref[0]).astype(low)
    chunks = width // hidden
    for dev in range(hidden // few):
        for chunk in range(chunks):
            start = (dev * chunks + chunk) * few
            out_ref[0, start : start + few, 2 * hidden :] = down[
                dev * few : (dev + 1) * few, chunk * hidden : (chunk + 1) * hidden
            ]


def weight_grads(rows, d_gu, act, d_rows, few, first, stop, buffers):
    experts, count, width = rows.shape
    hidden = act.shape[2]

    def part(*block):
        return pl.BlockSpec((1,) + block, lambda e: (first + e, 0, 0))

    return pl.pallas_call(
        functools.partial(grads_kernel, few),
        grid=(stop - first,),
        in_specs=[part(count, width), part(count, 2 * hidden), part(count, hidden), part(count, width)]
        + [pl.BlockSpec(memory_space=pl.ANY)] * len(buffers),
        out_specs=part(width, 3 * hidden),
        out_shape=jax.ShapeDtypeStruct((experts, width, 3 * hidden), low),
        scratch_shapes=[pltpu.VMEM((hidden, width), low)],
        input_output_aliases={4 + i: i for i in range(len(buffers))},
        compiler_params=vmem(56),
        name="weight_grads",
    )(rows, d_gu, act, d_rows, *buffers)


def shards(
    inputs,
    teacher,
    routes,
    valid_mask,
    block_lengths,
    gain_one,
    w_qkv,
    w_out,
    gain_two,
    w_router,
    w_gate,
    w_up,
    w_down,
):
    n = lax.axis_size("seq")
    me = lax.axis_index("seq")
    mine = lax.axis_index("fsdp")
    seqs_here, shard_len, width = inputs.shape
    assert seqs_here == 1
    seq_len = shard_len * n
    tokens_all = lax.axis_size("fsdp") * seq_len
    kv_here = KV_HEADS // n
    heads_w = kv_here * GROUP * HEAD_DIM
    group_w = kv_here * (GROUP + 2) * HEAD_DIM
    experts_here = w_gate.shape[0]
    expert_total = experts_here * n
    top_count = routes.shape[2]
    capacity = 3 * shard_len * top_count // (2 * expert_total)
    slots = -(-capacity // 16) * 16
    slot_rows = n * slots
    order_a, order_b = fsdp_bits()
    order = jnp.array(arrival_order(n), jnp.int32)[me]
    x_low = inputs.reshape(shard_len, width)

    own_qkv = lax.dynamic_slice_in_dim(w_qkv, me * group_w, group_w, 1)
    small = jnp.concatenate([gain_one[:, None], gain_two[:, None], w_router], axis=1)
    small = jnp.pad(small, ((0, 0), (0, -small.shape[1] % 128)))
    first = lax.all_gather(
        jnp.concatenate([own_qkv, small, w_out], axis=1), "fsdp", axis=0, tiled=True
    )
    full_qkv = first[:, :group_w]
    small = first[:, group_w : group_w + 2 + expert_total]
    full_out = first[:, -width:]
    full_g1 = small[:, 0].astype(full)
    full_g2 = small[:, 1].astype(full)
    router = small[:, 2:].T
    own_router = lax.dynamic_slice_in_dim(router, me * experts_here, experts_here, 0)
    own_router = jnp.pad(own_router, ((0, -experts_here % 16), (0, 0)))
    valid_rows = valid_mask.reshape(shard_len).astype(full)

    hidden_w = w_gate.shape[2]
    down_chunks = [
        w_down[:, :, start : start + hidden_w] for start in range(0, width, hidden_w)
    ]
    weights = lax.all_gather(
        jnp.concatenate([w_gate, w_up, jnp.concatenate(down_chunks, axis=1)], axis=2),
        "fsdp",
        axis=1,
        tiled=True,
    )

    routes_low = jnp.concatenate([routes.reshape(shard_len, top_count).T, valid_mask], axis=0)
    routes_low = jnp.pad(
        routes_low.astype(low), ((0, -routes_low.shape[0] % 16), (0, width - shard_len))
    )
    middle = shard_len // 2
    halves = (x_low[:middle], jnp.concatenate([x_low[middle:], routes_low], axis=0))
    positions = jnp.arange(seq_len, dtype=jnp.int32)
    cosine, sine_vals = rope_tables(positions.astype(full), HEAD_DIM)
    limit = block_limits(block_lengths[0], positions)[None]
    normed_one = jnp.zeros((seq_len, width), low)
    heads = jnp.zeros((n, kv_here, GROUP + 2, HEAD_DIM, shard_len), low)
    routes_all = []
    line = LineGather(halves)
    for turn in range(n):
        if turn:
            line.land(0, heads if turn > 1 else ())
            if turn < n - 1:
                line.go(0)
            line.land(1, ())
            if turn < n - 1:
                line.go(1)
        else:
            line.go(0)
            line.go(1)
        block = jnp.concatenate(line.block(turn))
        start = order[turn] * shard_len
        normed = rms_norm(block[:shard_len].astype(full), full_g1).astype(low)
        projected = dot("td,dc->ct", normed, full_qkv)
        projected = projected.reshape(kv_here, GROUP + 2, HEAD_DIM, shard_len)
        turned = rotate(
            projected[:, : GROUP + 1],
            lax.dynamic_slice_in_dim(cosine, start, shard_len, 1),
            lax.dynamic_slice_in_dim(sine_vals, start, shard_len, 1),
        ).astype(low)
        turned = jnp.concatenate(
            [
                turned[:, :GROUP] * jnp.asarray(attn_mult, low),
                turned[:, GROUP:],
                projected[:, GROUP + 1 :].astype(low),
            ],
            axis=1,
        )
        heads = lax.dynamic_update_index_in_dim(heads, turned, order[turn], 0)
        normed_one = lax.dynamic_update_slice_in_dim(normed_one, normed, start, 0)
        routes_all.append(block[shard_len : shard_len + top_count + 1, :shard_len])

    routes_all = jnp.stack(routes_all).astype(jnp.int32)
    valid_count = total(jnp.sum(routes_all[:, top_count]).astype(full).reshape(1, 1), "fsdp")[0, 0]
    expert_ids = jnp.arange(expert_total, dtype=jnp.int32)
    member = jnp.any(routes_all[:, :top_count, None, :] == expert_ids[:, None], axis=1)
    own_member = lax.dynamic_slice_in_dim(member, me * experts_here, experts_here, 1)
    earlier = jnp.arange(shard_len)[:, None] < jnp.arange(shard_len)[None, :]
    slot_of = dot("net,tu->neu", own_member.astype(low), earlier.astype(low)).astype(jnp.int32)
    slot_of = jnp.where(own_member, slot_of, -1)
    member = member.astype(full)

    key = jnp.moveaxis(heads[:, :, GROUP], 0, 2).reshape(kv_here, HEAD_DIM, seq_len)
    value = jnp.moveaxis(heads[:, :, GROUP + 1], 0, 2).reshape(kv_here, HEAD_DIM, seq_len)
    key_rows = jnp.swapaxes(key, 1, 2)
    value_rows = jnp.swapaxes(value, 1, 2)
    attended, out_heads, lse = attention_forward(heads, key_rows, value, limit)
    moved = exchange(attended)
    moved, slot_of, member, own_router = tie(moved, slot_of, member, own_router)
    attn_rows = by_place(nearest(*moved)).reshape(HEADS * HEAD_DIM, shard_len)
    projected = dot("kt,kd->td", attn_rows, full_out)
    hidden = x_low.astype(full) + resid_mult * projected
    normed_two, norm_two_pull = jax.vjp(rms_norm, hidden, full_g2)

    normed_low = normed_two.astype(low)
    line = LineGather((normed_low[:middle], normed_low[middle:]))
    buffers, gates, tokens = [], [], []
    line.go(0)
    line.go(1)
    other = ()
    for turn in range(n):
        if turn < n - 1:
            for h in (0, 1):
                other = line.land(h, other)
                if turn < n - 2:
                    line.go(h)
            line_slots = line.hold(slot_of[turn])
        else:
            line_slots = slot_of[turn]
        tokens.append(line.block(turn))
        *buffers, shard_gates = experts_forward(
            turn, n, jnp.stack([order[turn], me]), tokens[turn], line_slots, member[turn],
            router, weights, w_down.shape[1], slots, buffers,
        )
        gates.append(shard_gates)
        other = shard_gates
    mix_parts, expert_in, gate_up = buffers
    cuts = (slice(0, middle), slice(middle, None))
    mixture, _ = line_scatter(2, lambda h, shift: at_place(mix_parts[:, cuts[h]], me + shift), ())
    output_f32 = hidden + resid_mult * mixture
    activations = output_f32.astype(low).reshape(1, shard_len, width)
    error_rows = output_f32 - teacher.astype(full).reshape(shard_len, width)
    weighted = valid_rows[:, None] * error_rows
    loss_steps = total_steps(jnp.sum(weighted * error_rows).reshape(1, 1), "seq", "fsdp")
    squares = next(loss_steps)
    d_out = weighted * (tokens_all / valid_count)

    d_mix = resid_mult * d_out
    d_tokens = d_mix.astype(low)
    mix_dot = jnp.sum(d_mix * mixture, axis=1)[None]
    mix_high = mix_dot.astype(low)
    mix_rows = jnp.concatenate([mix_high, (mix_dot - mix_high.astype(full)).astype(low)])
    mix_rows = jnp.pad(mix_rows, ((0, 14), (0, width - shard_len)))
    line = LineGather((d_tokens[:middle], jnp.concatenate([d_tokens[middle:], mix_rows])))
    buffers, d_logits = [], []
    for turn in range(n):
        if turn:
            line.land(0, d_logits[-1])
            if turn < n - 1:
                line.go(0)
            line.land(1, ())
            if turn < n - 1:
                line.go(1)
        else:
            line.go(0)
            line.go(1)
        d_block = line.block(turn)
        mix_dot = d_block[1][middle : middle + 2, :shard_len].astype(full)
        mix_dot = jnp.sum(mix_dot, axis=0, keepdims=True)
        *buffers, shard_logits = experts_backward(
            turn, n, jnp.stack([order[turn], me]), d_block, slot_of[turn], gates[turn], mix_dot,
            own_router, gate_up, weights, w_down.shape[1], buffers,
        )
        d_logits.append(shard_logits)
    d_parts, d_rows, d_gate_up, act_low = buffers
    expert_in = expert_in.reshape(experts_here, slot_rows, width)
    d_rows = d_rows.reshape(experts_here, slot_rows, width)
    d_gate_up = d_gate_up.reshape(experts_here, slot_rows, -1)
    act_low = act_low.reshape(experts_here, slot_rows, -1)

    cut = (experts_here + 1) // 2

    def some_grads(first, stop):
        def make(before, grads):
            inputs, _ = tie((expert_in, d_gate_up, act_low, d_rows), before)
            return [weight_grads(*inputs, w_down.shape[1], first, stop, grads)]

        return make

    d_normed_two, grads = line_scatter(
        1,
        lambda h, shift: at_place(d_parts, me + shift),
        (some_grads(0, cut), some_grads(cut, experts_here)),
    )
    expert_sum = lax.psum_scatter(grads[0], "fsdp", scatter_dimension=1, tiled=True)

    d_hidden_norm, gain_two_part = norm_two_pull(d_normed_two)
    d_hidden = d_out + d_hidden_norm
    d_proj = (resid_mult * d_hidden).astype(low)
    out_pairs = out_grads(mine.reshape(1), attn_rows, d_proj, order_a, order_b)
    out_sums = [Halving(*pair, bits) for pair, bits in zip(out_pairs, (order_a, order_b))]
    for each in out_sums:
        each.go()
    d_attended = dot("kd,td->kt", full_out, d_proj).astype(low)
    (d_attended,) = land(out_sums, d_attended)
    moved = exchange(d_attended.reshape(n, heads_w, shard_len))
    for each in out_sums:
        each.add()
    router_part = sum(
        dot("td,et->de", half, half_logits)
        for shard, shard_logits in zip(tokens, d_logits)
        for half, half_logits in (
            (shard[0], shard_logits[:experts_here, :middle]),
            (shard[1], shard_logits[:experts_here, middle:]),
        )
    )
    own_columns = jnp.where(
        expert_ids // experts_here == me, jnp.concatenate([router_part] * n, axis=1), 0.0
    )
    own_columns = jnp.concatenate([own_columns, gain_two_part[:, None]], axis=1).astype(low)
    moved, own_columns, squares = leave(out_sums, moved, own_columns, squares)
    squares = loss_steps.send(squares)
    for each in out_sums:
        each.go()
    query_grad, key_grad, value_grad = attention_backward(
        heads, key_rows, value_rows, key, limit, out_heads, lse, me.reshape(1), *moved
    )
    (query_grad, key_grad, value_grad), squares = land(
        out_sums, (query_grad, key_grad, value_grad), squares
    )
    squares = loss_steps.send(squares)
    for each in out_sums:
        each.add()
        each.go()
    d_turned = jnp.concatenate([query_grad, key_grad[:, None]], axis=1).astype(full)
    d_turned = rotate(d_turned, cosine, -sine_vals).astype(low)
    d_qkv = jnp.concatenate([d_turned, value_grad[:, None]], axis=1).reshape(group_w, seq_len)

    def d_part(rows, shift):
        start = (me + shift) % n * shard_len
        rows = lax.dynamic_slice_in_dim(rows, start, shard_len, 1)
        return dot("ct,dc->td", rows, full_qkv).astype(low)

    d_parts = {shift: d_part(d_qkv, shift) for shift in {1, n - 1}}
    (d_parts,) = land(out_sums, d_parts)
    for each in out_sums:
        each.add()

    out_sum = jnp.concatenate([each.finish() for each in out_sums], axis=1).astype(low)
    out_rows = out_sum.shape[0] // n
    out_parts = jnp.swapaxes(out_sum.reshape(out_sum.shape[0], n, width // n), 0, 1)
    out_parts = out_parts.reshape(n, out_rows, width)

    def get(h, shift):
        part = d_parts[shift % n]
        if h == 0:
            return part[:middle]
        return jnp.concatenate([part[middle:], at_place(out_parts, me + shift)])

    sums = {}

    def first_work(before, _):
        rows, _ = tie(d_qkv, before)
        for shift in range(n):
            if shift not in d_parts:
                d_parts[shift] = d_part(rows, shift)
        qkv_part = jnp.concatenate(
            [dot("td,ct->dc", normed_one, rows).astype(low), own_columns], axis=1
        )
        sums["qkv"] = rows_halving(qkv_part, order_a)
        sums["qkv"].go()
        return sums["qkv"].send

    def next_work(before, _):
        land([sums["qkv"]], before)
        sums["qkv"].add()
        sums["qkv"].go()
        return sums["qkv"].send

    ended, _ = line_scatter(2, get, (first_work, next_work, next_work))
    qkv_sum = sums["qkv"]
    d_normed_one = ended[:shard_len]
    (ended,) = land([qkv_sum], ended)
    qkv_sum.add()
    out_own = ended[shard_len:].reshape(out_sum.shape[0], width // n)
    block = jnp.concatenate([qkv_sum.finish(), out_own], axis=1).astype(low)
    block, expert_sum, squares = tie(block, expert_sum, squares)
    blocks = lax.all_gather(block, "seq", axis=0)
    _, norm_one_pull = jax.vjp(lambda v: rms_norm(v, full_g1), x_low.astype(full))
    input_grad = (d_hidden + norm_one_pull(d_normed_one)[0]).reshape(1, shard_len, width)
    few = w_down.shape[1]
    gate_grad = expert_sum[:, :, :hidden_w].astype(full)
    up_grad = expert_sum[:, :, hidden_w : 2 * hidden_w].astype(full)
    down_grad = jnp.concatenate(
        [
            expert_sum[:, start : start + few, 2 * hidden_w :].astype(full)
            for start in range(0, expert_sum.shape[1], few)
        ],
        axis=2,
    )
    qkv_grad = jnp.concatenate([came[:, :group_w] for came in blocks], axis=1).astype(full)
    out_grad = jnp.concatenate([came[:, -(width // n) :] for came in blocks], axis=1).astype(full)
    rest = jnp.sum(blocks[:, :, group_w : -(width // n)].astype(full), axis=0)
    router_grad, gain_two_grad = rest[:, :expert_total], rest[:, expert_total]
    gain_one_grad = jnp.sum(qkv_grad * w_qkv.astype(full), axis=1) / gain_one.astype(full)
    for _ in range(4):
        squares = loss_steps.send(squares)
    loss_value = squares[0, 0] / (valid_count * width)
    return (
        activations,
        loss_value,
        input_grad,
        gain_one_grad,
        qkv_grad,
        out_grad,
        gain_two_grad,
        router_grad,
        gate_grad,
        up_grad,
        down_grad,
    )


def solution(mesh):
    return jax.shard_map(
        shards,
        mesh=mesh,
        in_specs=(
            P("fsdp", "seq", None),
            P("fsdp", "seq", None),
            P("fsdp", "seq", None),
            P("fsdp", "seq"),
            P("fsdp", None),
            P("fsdp"),
            P("fsdp", None),
            P("fsdp", None),
            P("fsdp"),
            P("fsdp", None),
            P("seq", "fsdp", None),
            P("seq", "fsdp", None),
            P("seq", "fsdp", None),
        ),
        out_specs=(
            P("fsdp", "seq", None),
            P(),
            P("fsdp", "seq", None),
            P("fsdp"),
            P("fsdp", None),
            P("fsdp", None),
            P("fsdp"),
            P("fsdp", None),
            P("seq", "fsdp", None),
            P("seq", "fsdp", None),
            P("seq", "fsdp", None),
        ),
        check_vma=False,
    )
```

```python
import functools

import jax
import jax.numpy as jnp
from jax import lax
from jax.experimental import pallas as pl
from jax.experimental.pallas import tpu as pltpu
from jax.sharding import PartitionSpec as P

HEADS = 24
KV_HEADS = 8
HEAD_DIM = 64
BLOCK = 256
GROUP = 3
QKV_W = 2560


epsilon = 1e-06
attn_mult = 0.015625
resid_mult = 0.22
rope_base = 10000.0
masked_score = -1e30

low = jnp.bfloat16
full = jnp.float32


def dot(spec, left, right):
    return jnp.einsum(spec, left, right, preferred_element_type=full)


def rms_norm(values, gain_vec):
    inv_rms = lax.rsqrt(jnp.mean(values * values, axis=-1, keepdims=True) + epsilon)
    return values * inv_rms * gain_vec


def rope_tables(positions, head_dim):
    half_dim = head_dim // 2
    frequency = rope_base ** (-(2.0 * jnp.arange(half_dim, dtype=full)) / head_dim)
    angles = frequency[:, None] * positions[None, :]
    return (jnp.cos(angles), jnp.sin(angles))


def rotate(values, cosine, sine_vals):
    half_dim = values.shape[-2] // 2
    front_half = values[..., :half_dim, :]
    back_half = values[..., half_dim:, :]
    return jnp.concatenate(
        [front_half * cosine - back_half * sine_vals, back_half * cosine + front_half * sine_vals],
        axis=-2,
    )


def block_limits(lengths_row, positions):
    block_ends = jnp.cumsum(lengths_row)
    open_ends = jnp.where(block_ends[None, :] > positions[:, None], block_ends[None, :], positions.shape[0])
    return jnp.min(open_ends, axis=1).astype(jnp.int32)


def tie(*groups):
    return lax.optimization_barrier(groups)


def line_move(right, left, k):
    n = lax.axis_size("seq")
    return (
        lax.ppermute(right, "seq", [(i, i + 1) for i in range(k - 1, n - 1)]),
        lax.ppermute(left, "seq", [(i, i - 1) for i in range(1, n - k + 1)]),
    )


def line_gather(block):
    n = lax.axis_size("seq")
    rights, lefts = [block], [block]
    for k in range(1, n):
        right, left = tie(*line_move(rights[-1], lefts[-1], k))
        rights.append(right)
        lefts.append(left)
    return nearest(rights, lefts)


def nearest(rights, lefts):
    n = lax.axis_size("seq")
    me = lax.axis_index("seq")
    return [rights[0]] + [jnp.where(me >= k, rights[k], lefts[n - k]) for k in range(1, n)]


def arrival_order(n):
    order = []
    for me in range(n):
        both = min(me, n - 1 - me)
        places = [me]
        for k in range(1, n):
            places += [me - k] if me >= k and (k <= both or me > n - 1 - me) else []
            places += [me + k] if me + k < n and (k <= both or me < n - 1 - me) else []
        order.append(places)
    return order


def arrivals(n, turn):
    return [dev - places[turn] for dev, places in enumerate(arrival_order(n))]


def arrived(rights, lefts, turn):
    gaps = arrivals(lax.axis_size("seq"), turn)
    block = None
    for gap in sorted(set(gaps)):
        moved = rights[gap] if gap >= 0 else lefts[-gap]
        if block is None:
            block = moved
        else:
            mine = jnp.array([each == gap for each in gaps])[lax.axis_index("seq")]
            block = jnp.where(mine, moved, block)
    return block


def at_place(placed, place):
    return lax.dynamic_index_in_dim(placed, place % lax.axis_size("seq"), 0, keepdims=False)


def line_send(to_right, to_left, right, left):
    if right is not None:
        to_right = (to_right.astype(full) + right.astype(full)).astype(low)
        to_left = (to_left.astype(full) + left.astype(full)).astype(low)
    return to_right, to_left


def line_pass(to_right, to_left, k):
    n = lax.axis_size("seq")
    return (
        lax.ppermute(to_right, "seq", [(i, i + 1) for i in range(n - k)]),
        lax.ppermute(to_left, "seq", [(i, i - 1) for i in range(k, n)]),
    )


class LineGather:
    def __init__(self, halves):
        self.rights, self.lefts = [[half] for half in halves], [[half] for half in halves]
        self.landed = [0, 0]

    def go(self, h):
        step = len(self.rights[h])
        right, left = line_move(self.rights[h][-1], self.lefts[h][-1], step)
        self.rights[h].append(right)
        self.lefts[h].append(left)

    def land(self, h, other):
        spot = self.landed[h] = len(self.rights[h]) - 1
        moved = [(self.rights[part][spot], self.lefts[part][spot]) for part in range(h + 1)]
        moved, other = tie(moved, other)
        for part, (right, left) in enumerate(moved):
            self.rights[part][spot], self.lefts[part][spot] = right, left
        return other

    def hold(self, other):
        came = [(self.rights[h][-1 - self.ahead(h)], self.lefts[h][-1 - self.ahead(h)]) for h in (0, 1)]
        return tie(other, came)[0]

    def ahead(self, h):
        return len(self.rights[h]) - 1 - self.landed[h]

    def choice(self, turn):
        gaps = arrivals(lax.axis_size("seq"), turn)
        places = sorted(set(gaps))
        return jnp.array([places.index(gap) for gap in gaps], jnp.int32)[lax.axis_index("seq")]

    def blocks(self, turn):
        places = sorted(set(arrivals(lax.axis_size("seq"), turn)))
        return [
            [rights[gap] if gap >= 0 else lefts[-gap] for gap in places]
            for rights, lefts in zip(self.rights, self.lefts)
        ]

    def block(self, turn):
        return [arrived(self.rights[h], self.lefts[h], turn) for h in (0, 1)]


def line_scatter(count, get, work):
    n = lax.axis_size("seq")
    flying = [(None, None)] * count
    before, given = (), []
    for k in range(n - 1, 0, -1):
        for h in range(count):
            if k < n - 1 and h:
                flying[h], before = tie(flying[h], before)
            elif k < n - 1:
                flying[h], given = tie(flying[h], given)
            before = line_send(get(h, k), get(h, -k), *flying[h])
            flying[h] = line_pass(*before, k)
        if n - 1 - k < len(work):
            given = work[n - 1 - k](before, given)
    sums = []
    flying[0], given = tie(flying[0], given)
    for h, (right, left) in enumerate(flying):
        sums.append(get(h, 0).astype(full) + (right.astype(full) + left.astype(full)))
    return jnp.concatenate(sums), given


def by_place(blocks):
    n = lax.axis_size("seq")
    me = lax.axis_index("seq")
    placed = jnp.zeros((n,) + blocks[0].shape, blocks[0].dtype)
    for k, block in enumerate(blocks):
        placed = lax.dynamic_update_index_in_dim(placed, block, (me - k) % n, 0)
    return placed


def exchange(blocks):
    n = lax.axis_size("seq")
    me = lax.axis_index("seq")
    own = at_place(blocks, me)
    rights, lefts = [own] * n, [own] * n
    for k in range(n - 1, 0, -1):
        to_right, to_left = at_place(blocks, me + k), at_place(blocks, me - k)
        rights[k] = lax.ppermute(to_right, "seq", [(i, i + k) for i in range(n - k)])
        lefts[k] = lax.ppermute(to_left, "seq", [(i, i - k) for i in range(k, n)])
    return rights, lefts


def swap(value, axis, bit):
    return lax.ppermute(value, axis, [(i, i ^ bit) for i in range(lax.axis_size(axis))])


def total(value, *axes):
    for axis in axes:
        for step in range(lax.axis_size(axis).bit_length() - 1):
            value = value + swap(value, axis, 1 << step)
    return value


def fsdp_bits():
    bits = [1 << step for step in range(lax.axis_size("fsdp").bit_length() - 1)]
    return tuple(bits), tuple(bits[:1] + bits[:0:-1])


def total_steps(value, *axes):
    for axis in axes:
        for step in range(lax.axis_size(axis).bit_length() - 1):
            here = swap(value, axis, 1 << step)
            here = yield here
            value = value + here
    while True:
        yield value


class Halving:
    def __init__(self, keep, send, bits):
        self.terms, self.send, self.bits = [keep], send, list(bits)

    def go(self):
        self.terms = self.terms + [swap(self.send, "fsdp", self.bits.pop(0))]

    def add(self):
        half = self.terms[0].shape[0] // 2
        if half:
            self.send = sum(term[half:].astype(full) for term in self.terms).astype(low)
            self.terms = [term[:half] for term in self.terms]

    def finish(self):
        while self.bits:
            self.go()
            self.add()
        return sum(term[0].astype(full) for term in self.terms)


def rows_halving(part, bits):
    devs = lax.axis_size("fsdp")
    order = lax.axis_index("fsdp") ^ jnp.array(halving_masks(bits), jnp.int32)
    blocks = part.reshape(devs, part.shape[0] // devs, part.shape[1])[order]
    return Halving(blocks[: devs // 2], blocks[devs // 2 :], bits)


def land(sums, *others):
    tied = tie([each.terms[-1] for each in sums], *others)
    for each, here in zip(sums, tied[0]):
        each.terms = each.terms[:-1] + [here]
    return tied[1:]


def leave(sums, *others):
    tied = tie([each.send for each in sums], *others)
    for each, send in zip(sums, tied[0]):
        each.send = send
    return tied[1:]


def nt(a, b):
    return lax.dot_general(a, b, (((1,), (1,)), ((), ())), preferred_element_type=full)

def nn(a, b):
    return lax.dot_general(a, b, (((1,), (0,)), ((), ())), preferred_element_type=full)

def tn(a, b):
    return lax.dot_general(a, b, (((0,), (0,)), ((), ())), preferred_element_type=full)


def beside(rows):
    return jnp.concatenate([rows[h] for h in range(GROUP)], axis=1)

def key_steps(i, seq_len, query_rows, key_rows):
    free = (i * query_rows) // key_rows
    need = ((i + 1) * query_rows + BLOCK - 1 + key_rows - 1) // key_rows
    return free, jnp.minimum(need, seq_len // key_rows)

def forward_kernel(seq_len, query_rows, key_rows, limit_ref, q_ref, k_ref, vt_ref, low_ref, out_ref, lse_ref):
    i = pl.program_id(1)
    qt = beside(q_ref[0, 0])
    width = GROUP * query_rows
    limit = jnp.concatenate([limit_ref[...]] * GROUP, axis=1)

    def step(masked, j, carry):
        peak, total, acc = carry
        start = pl.multiple_of(j * key_rows, key_rows)
        s = nn(k_ref[0, pl.ds(start, key_rows), :], qt)
        if masked:
            place = start + lax.broadcasted_iota(jnp.int32, (key_rows, 1), 0)
            s = jnp.where(place < limit, s, masked_score)
        new_peak = jnp.maximum(peak, jnp.max(s, axis=0, keepdims=True))
        shrink = jnp.exp(peak - new_peak)
        p = jnp.exp(s - new_peak)
        total = shrink * total + jnp.sum(p, axis=0, keepdims=True)
        acc = shrink * acc + nn(vt_ref[0, :, pl.ds(start, key_rows)], p.astype(low))
        return new_peak, total, acc

    free, need = key_steps(i, seq_len, query_rows, key_rows)
    carry = (
        jnp.full((1, width), masked_score, full),
        jnp.zeros((1, width), full),
        jnp.zeros((HEAD_DIM, width), full),
    )
    carry = lax.fori_loop(0, free, lambda j, c: step(False, j, c), carry)
    peak, total, acc = lax.fori_loop(free, need, lambda j, c: step(True, j, c), carry)
    out = acc / total
    lse = peak + jnp.log(total)
    for h in range(GROUP):
        cols = slice(h * query_rows, (h + 1) * query_rows)
        out_ref[0, h] = out[:, cols]
        low_ref[0, pl.ds(h * HEAD_DIM, HEAD_DIM), :] = out[:, cols].astype(low)
        lse_ref[0, h] = lse[:, cols]

def query_spec(query_rows, per):
    return pl.BlockSpec(
        (1, 1, GROUP, HEAD_DIM, query_rows), lambda g, i: (i // per, g, 0, 0, i % per)
    )


def attention_forward(heads, k_rows, vt, limit):
    kv_here, shard_len = heads.shape[1], heads.shape[4]
    seq_len = k_rows.shape[1]
    query_rows = min(256, shard_len)
    key_rows = min(512, seq_len)
    per = shard_len // query_rows
    return pl.pallas_call(
        functools.partial(forward_kernel, seq_len, query_rows, key_rows),
        grid=(kv_here, seq_len // query_rows),
        in_specs=[
            pl.BlockSpec((1, query_rows), lambda g, i: (0, i)),
            query_spec(query_rows, per),
            pl.BlockSpec((1, seq_len, HEAD_DIM), lambda g, i: (g, 0, 0)),
            pl.BlockSpec((1, HEAD_DIM, seq_len), lambda g, i: (g, 0, 0)),
        ],
        out_specs=[
            pl.BlockSpec((1, GROUP * HEAD_DIM, query_rows), lambda g, i: (i // per, g, i % per)),
            pl.BlockSpec((1, GROUP, HEAD_DIM, query_rows), lambda g, i: (g, 0, 0, i)),
            pl.BlockSpec((1, GROUP, 1, query_rows), lambda g, i: (g, 0, 0, i)),
        ],
        out_shape=[
            jax.ShapeDtypeStruct((seq_len // shard_len, kv_here * GROUP * HEAD_DIM, shard_len), low),
            jax.ShapeDtypeStruct((kv_here, GROUP, HEAD_DIM, seq_len), full),
            jax.ShapeDtypeStruct((kv_here, GROUP, 1, seq_len), full),
        ],
        compiler_params=vmem(60),
        name="attention_forward",
    )(limit, heads, k_rows, vt)

def backward_kernel(
    seq_len, query_rows, key_rows, per, me_ref, limit_ref, q_ref, k_ref, v_ref, kt_ref, out_ref, lse_ref, *refs
):
    blocks, (dq_ref, dk_ref, dv_ref, dk_acc, dv_acc, held) = refs[:-6], refs[-6:]
    i = pl.program_id(1)

    @pl.when(i == 0)
    def _():
        dk_acc[...] = jnp.zeros_like(dk_acc)
        dv_acc[...] = jnp.zeros_like(dv_acc)

    qt = beside(q_ref[0, 0])
    limit = jnp.concatenate([limit_ref[...]] * GROUP, axis=1)
    devs = (len(blocks) + 1) // 2
    gap = me_ref[0] - i // per
    for spot, block in enumerate(blocks):

        @pl.when(gap == (spot if spot < devs else devs - 1 - spot))
        def _():
            held[...] = block[...]

    dout = jnp.concatenate([held[pl.ds(h * HEAD_DIM, HEAD_DIM), :] for h in range(GROUP)], axis=1)
    delta = jnp.sum(dout.astype(full) * beside(out_ref[0]), axis=0, keepdims=True)
    lse = beside(lse_ref[0])

    def step(masked, j, dq):
        start = pl.multiple_of(j * key_rows, key_rows)
        keys = pl.ds(start, key_rows)
        s = nn(k_ref[0, keys, :], qt)
        if masked:
            place = start + lax.broadcasted_iota(jnp.int32, (key_rows, 1), 0)
            s = jnp.where(place < limit, s, masked_score)
        p = jnp.exp(s - lse)
        dp = nn(v_ref[0, keys, :], dout)
        ds = (p * (dp - delta)).astype(low)
        dk_acc[:, keys] += nt(qt, ds)
        dv_acc[:, keys] += nt(dout, p.astype(low))
        return dq + nn(kt_ref[0, :, keys], ds)

    free, need = key_steps(i, seq_len, query_rows, key_rows)
    dq = jnp.zeros((HEAD_DIM, GROUP * query_rows), full)
    dq = lax.fori_loop(0, free, lambda j, c: step(False, j, c), dq)
    dq = lax.fori_loop(free, need, lambda j, c: step(True, j, c), dq) * attn_mult
    for h in range(GROUP):
        dq_ref[0, h] = dq[:, h * query_rows : (h + 1) * query_rows].astype(low)

    @pl.when(i == pl.num_programs(1) - 1)
    def _():
        dk_ref[0] = dk_acc[...].astype(low)
        dv_ref[0] = dv_acc[...].astype(low)

def attention_backward(heads, k_rows, v_rows, kt, limit, out, lse, me, rights, lefts):
    blocks = [*rights, *lefts[1:]]
    kv_here, shard_len = heads.shape[1], heads.shape[4]
    seq_len = k_rows.shape[1]
    query_rows = min(256, shard_len)
    key_rows = min(512, seq_len)
    per = shard_len // query_rows
    quarter = lambda g, i, me: (g, 0, 0, i)
    whole = lambda g, i, me: (g, 0, 0)
    return pl.pallas_call(
        functools.partial(backward_kernel, seq_len, query_rows, key_rows, per),
        grid_spec=pltpu.PrefetchScalarGridSpec(
            num_scalar_prefetch=1,
            grid=(kv_here, seq_len // query_rows),
            in_specs=[
                pl.BlockSpec((1, query_rows), lambda g, i, me: (0, i)),
                pl.BlockSpec(
                    (1, 1, GROUP, HEAD_DIM, query_rows),
                    lambda g, i, me: (i // per, g, 0, 0, i % per),
                ),
                pl.BlockSpec((1, seq_len, HEAD_DIM), whole),
                pl.BlockSpec((1, seq_len, HEAD_DIM), whole),
                pl.BlockSpec((1, HEAD_DIM, seq_len), whole),
                pl.BlockSpec((1, GROUP, HEAD_DIM, query_rows), quarter),
                pl.BlockSpec((1, GROUP, 1, query_rows), quarter),
            ]
            + [pl.BlockSpec((GROUP * HEAD_DIM, query_rows), lambda g, i, me: (g, i % per))]
            * len(blocks),
            out_specs=[
                pl.BlockSpec((1, GROUP, HEAD_DIM, query_rows), quarter),
                pl.BlockSpec((1, HEAD_DIM, seq_len), whole),
                pl.BlockSpec((1, HEAD_DIM, seq_len), whole),
            ],
            scratch_shapes=[
                pltpu.VMEM((HEAD_DIM, seq_len), full),
                pltpu.VMEM((HEAD_DIM, seq_len), full),
                pltpu.VMEM((GROUP * HEAD_DIM, query_rows), low),
            ],
        ),
        out_shape=[
            jax.ShapeDtypeStruct((kv_here, GROUP, HEAD_DIM, seq_len), low),
            jax.ShapeDtypeStruct((kv_here, HEAD_DIM, seq_len), low),
            jax.ShapeDtypeStruct((kv_here, HEAD_DIM, seq_len), low),
        ],
        compiler_params=vmem(60),
        name="attention_backward",
    )(me, limit, heads, k_rows, v_rows, kt, out, lse, *blocks)


def vmem(mib):
    return pltpu.CompilerParams(vmem_limit_bytes=mib * 2**20)


def own_row(ref, row):
    return ref[pl.ds(row, 1), :]


def join_down(rows, block_ref, down_ref):
    hidden, width = down_ref.shape
    chunks = width // hidden
    for dev in range(hidden // rows):
        for chunk in range(chunks):
            start = (dev * chunks + chunk) * rows
            down_ref[dev * rows : (dev + 1) * rows, chunk * hidden : (chunk + 1) * hidden] = (
                block_ref[start : start + rows, :]
            )


def pick_rows(pick, tok_ref, more_ref):
    middle = tok_ref.shape[0]
    return (nn(pick[:, :middle], tok_ref[...]) + nn(pick[:, middle:], more_ref[:middle, :])).astype(low)


def take_tokens(choices, at_ref, refs, tok_ref, more_ref, sems):
    for choice in range(choices):

        @pl.when(at_ref[2] == choice)
        def _():
            copies = [
                pltpu.make_async_copy(refs[choice], tok_ref, sems.at[0]),
                pltpu.make_async_copy(refs[choices + choice], more_ref, sems.at[1]),
            ]
            for copy in copies:
                copy.start()
            for copy in copies:
                copy.wait()


def experts_kernel(
    few, pair, choices, at_ref, slot_ref, member_ref, router_ref, wgu_ref, wd_ref, *refs
):
    part_ref, x_ref, gu_ref, gates_ref, acc, gates_all, down, tok_ref, more_ref, sems = refs[-10:]
    step, steps = pl.program_id(0), pl.num_programs(0)
    slots = x_ref.shape[2]

    @pl.when(step == 0)
    def _():
        take_tokens(choices, at_ref, refs, tok_ref, more_ref, sems)
        member = member_ref[...] > 0
        logits = [nt(router_ref[...], ref[...]) for ref in (tok_ref, more_ref)]
        chosen = jnp.where(member, jnp.concatenate(logits, axis=1), masked_score)
        chosen = jnp.exp(chosen - jnp.max(chosen, axis=0, keepdims=True))
        chosen = jnp.where(member, chosen, 0.0)
        gates_all[...] = chosen / jnp.sum(chosen, axis=0, keepdims=True)
        acc[...] = jnp.zeros_like(acc)

    place = lax.broadcasted_iota(jnp.int32, (slots, 1), 0)
    puts, ys = [], []
    for i in range(pair):
        e = step * pair + i
        gate_row = own_row(gates_all, at_ref[1] * (steps * pair) + e)
        gates_ref[pl.ds(e, 1), :] = gate_row
        here = place == own_row(slot_ref, e)
        x = pick_rows(jnp.where(here, 1.0, 0.0).astype(low), tok_ref, more_ref)
        x_ref[i, 0] = x
        gu = nn(x, wgu_ref[i])
        gu_ref[i, 0] = gu.astype(low)
        hidden = gu.shape[1] // 2
        g, u = gu[:, :hidden], gu[:, hidden:]
        act = (g * jax.nn.sigmoid(g) * u).astype(low)
        join_down(few, wd_ref.at[i], down.at[i])
        ys.append(nn(act, down[i]).astype(low))
        puts.append(jnp.where(here, gate_row, 0.0).astype(low))
    acc[...] += tn(jnp.concatenate(puts), jnp.concatenate(ys))

    @pl.when(step == steps - 1)
    def _():
        part_ref[0] = acc[...].astype(low)


def back_kernel(
    few, pair, choices, at_ref, slot_ref, gates_ref, router_ref, gu_ref, wgu_ref, wd_ref, *refs
):
    part_ref, d_ref, dgu_ref, act_ref, dlog_ref, acc, dlog_all, down, tok_ref, more_ref, sems = refs[-11:]
    step, steps = pl.program_id(0), pl.num_programs(0)
    slots, hidden = gu_ref.shape[2], gu_ref.shape[3] // 2

    @pl.when(step == 0)
    def _():
        take_tokens(choices, at_ref, refs, tok_ref, more_ref, sems)
        dlog_all[...] = jnp.zeros_like(dlog_all)
        acc[...] = jnp.zeros_like(acc)

    middle, count = tok_ref.shape[0], slot_ref.shape[1]
    mix = more_ref[middle : middle + 2, :count].astype(full)
    mix = mix[0:1, :] + mix[1:2, :]
    place = lax.broadcasted_iota(jnp.int32, (slots, 1), 0)
    puts, dxs = [], []
    for i in range(pair):
        e = step * pair + i
        here = place == own_row(slot_ref, e)
        pick = jnp.where(here, 1.0, 0.0).astype(low)
        gate_row = own_row(gates_ref, e)
        gate = jnp.sum(jnp.where(here, gate_row, 0.0), axis=1, keepdims=True)
        d = pick_rows(pick, tok_ref, more_ref)
        d_ref[i, 0] = d
        join_down(few, wd_ref.at[i], down.at[i])
        d_act = nt(d, down[i])
        g, u = gu_ref[i, 0, :, :hidden].astype(full), gu_ref[i, 0, :, hidden:].astype(full)
        sig = jax.nn.sigmoid(g)
        silu = g * sig
        act = silu * u
        d_gate = jnp.sum(d_act * act, axis=1, keepdims=True)
        d_gate = jnp.sum(jnp.where(here, d_gate, 0.0), axis=0, keepdims=True)
        dlog_all[pl.ds(e, 1), :] = gate_row * (d_gate - mix)
        act_ref[i, 0] = (act * gate).astype(low)
        d_act = d_act * gate
        d_g = (d_act * u * (sig + silu * (1.0 - sig))).astype(low)
        d_u = (d_act * silu).astype(low)
        dgu_ref[i, 0, :, :hidden] = d_g
        dgu_ref[i, 0, :, hidden:] = d_u
        dxs.append(nt(dgu_ref[i, 0], wgu_ref[i]).astype(low))
        puts.append(pick)
    acc[...] += tn(jnp.concatenate(puts), jnp.concatenate(dxs))

    @pl.when(step == steps - 1)
    def _():
        dlog = dlog_all[...].astype(low)
        dlog_ref[...] = dlog
        part_ref[0] = (acc[...] + tn(dlog, router_ref[...])).astype(low)


def by_expert(*shape):
    return pl.BlockSpec((1,) + shape, lambda e, at: (e, 0, 0))


def in_turn(pair, turn, *shape):
    return pl.BlockSpec((pair, 1) + shape, lambda e, at: (e, turn, 0, 0))


def same(*shape):
    return pl.BlockSpec(shape, lambda e, at: (0, 0))


def in_place(*shape):
    return pl.BlockSpec((1,) + shape, lambda e, at: (at[0], 0, 0))


def shard_call(kernel, name, at, inputs, in_specs, out_specs, out_shape, buffers, scratch, experts):
    first = len(inputs) + 1
    aliases = {first + i: i for i in range(len(buffers))}
    return pl.pallas_call(
        kernel,
        grid_spec=pltpu.PrefetchScalarGridSpec(
            num_scalar_prefetch=1,
            grid=(experts,),
            in_specs=in_specs
            + [pl.BlockSpec(memory_space=pl.ANY)] * (len(inputs) + len(buffers) - len(in_specs)),
            out_specs=out_specs,
            scratch_shapes=scratch,
        ),
        out_shape=out_shape,
        input_output_aliases=aliases,
        compiler_params=vmem(48),
        name=name,
    )(at, *inputs, *buffers)


def weight_specs(pair, width, hidden):
    return [
        pl.BlockSpec((pair, width, 2 * hidden), lambda e, at: (e, 0, 0)),
        pl.BlockSpec((pair, width, hidden), lambda e, at: (e, 0, 2)),
    ]


def experts_forward(turn, devs, at, tokens, slot_of, member, router, weights, few, slots, buffers):
    experts, width, columns = weights.shape
    hidden = columns // 3
    pair = 1 + (experts + 1) % 2
    count = slot_of.shape[1]
    total_experts = member.shape[0]
    return shard_call(
        functools.partial(experts_kernel, few, pair, len(tokens[0])),
        "experts_forward",
        at,
        [slot_of, member, router, weights, weights, *tokens[0], *tokens[1]],
        [
            same(experts, count),
            same(total_experts, count),
            same(total_experts, width),
            *weight_specs(pair, width, hidden),
        ],
        [
            in_place(count, width),
            in_turn(pair, turn, slots, width),
            in_turn(pair, turn, slots, 2 * hidden),
            same(experts, count),
        ],
        [
            jax.ShapeDtypeStruct((devs, count, width), low),
            jax.ShapeDtypeStruct((experts, devs, slots, width), low),
            jax.ShapeDtypeStruct((experts, devs, slots, 2 * hidden), low),
            jax.ShapeDtypeStruct((experts, count), full),
        ],
        buffers,
        [
            pltpu.VMEM((count, width), full),
            pltpu.VMEM((total_experts, count), full),
            pltpu.VMEM((pair, hidden, width), low),
            *(pltpu.VMEM(half[0].shape, low) for half in tokens),
            pltpu.SemaphoreType.DMA((2,)),
        ],
        experts // pair,
    )


def experts_backward(
    turn, devs, at, d_tokens, slot_of, gates, router, gu, weights, few, buffers
):
    experts, width, columns = weights.shape
    hidden = columns // 3
    pair = 1 + (experts + 1) % 2
    count = slot_of.shape[1]
    slots = gu.shape[2]
    lines = router.shape[0]
    return shard_call(
        functools.partial(back_kernel, few, pair, len(d_tokens[0])),
        "experts_backward",
        at,
        [slot_of, gates, router, gu, weights, weights, *d_tokens[0], *d_tokens[1]],
        [
            same(experts, count),
            same(experts, count),
            same(lines, width),
            in_turn(pair, turn, slots, 2 * hidden),
            *weight_specs(pair, width, hidden),
        ],
        [
            in_place(count, width),
            in_turn(pair, turn, slots, width),
            in_turn(pair, turn, slots, 2 * hidden),
            in_turn(pair, turn, slots, hidden),
            same(lines, count),
        ],
        [
            jax.ShapeDtypeStruct((devs, count, width), low),
            jax.ShapeDtypeStruct((experts, devs, slots, width), low),
            jax.ShapeDtypeStruct((experts, devs, slots, 2 * hidden), low),
            jax.ShapeDtypeStruct((experts, devs, slots, hidden), low),
            jax.ShapeDtypeStruct((lines, count), low),
        ],
        buffers,
        [
            pltpu.VMEM((count, width), full),
            pltpu.VMEM((lines, count), full),
            pltpu.VMEM((pair, hidden, width), low),
            *(pltpu.VMEM(half[0].shape, low) for half in d_tokens),
            pltpu.SemaphoreType.DMA((2,)),
        ],
        experts // pair,
    )


def halving_masks(bits):
    masks = [0]
    for bit in reversed(bits):
        masks = masks + [mask ^ bit for mask in masks]
    return masks


def out_kernel(bits_a, bits_b, me_ref, rows_ref, d_ref, *refs):
    outs, acc = refs[:4], refs[4]
    half = outs[0].shape[2]
    for part, bits in enumerate((bits_a, bits_b)):
        keep, send = outs[2 * part], outs[2 * part + 1]
        rows = keep.shape[1]
        acc[...] = nn(rows_ref[...], d_ref[:, part * half : (part + 1) * half])
        for place, mask in enumerate(halving_masks(bits)):
            out = keep if place < keep.shape[0] else send
            start = pl.multiple_of((me_ref[0] ^ mask) * rows, rows)
            out[place % keep.shape[0]] = acc[pl.ds(start, rows), :].astype(low)


def out_grads(me, rows, d_proj, bits_a, bits_b):
    (height, count), width = rows.shape, d_proj.shape[1]
    devs = 2 ** len(bits_a)
    shape = (devs // 2, height // devs, width // 2)
    outs = pl.pallas_call(
        functools.partial(out_kernel, bits_a, bits_b),
        grid_spec=pltpu.PrefetchScalarGridSpec(
            num_scalar_prefetch=1,
            grid=(1,),
            in_specs=[same(height, count), same(count, width)],
            out_specs=[pl.BlockSpec(shape, lambda e, me: (0, 0, 0))] * 4,
            scratch_shapes=[pltpu.VMEM((height, width // 2), full)],
        ),
        out_shape=[jax.ShapeDtypeStruct(shape, low)] * 4,
        compiler_params=vmem(48),
        name="out_grads",
    )(me, rows, d_proj)
    return (outs[0], outs[1]), (outs[2], outs[3])


def grads_kernel(few, x_ref, dgu_ref, act_ref, d_ref, *refs):
    out_ref, down = refs[-2], refs[-1]
    hidden, width = down.shape
    out_ref[0, :, : 2 * hidden] = tn(x_ref[0], dgu_ref[0]).astype(low)
    down[...] = tn(act_ref[0], d_ref[0]).astype(low)
    chunks = width // hidden
    for dev in range(hidden // few):
        for chunk in range(chunks):
            start = (dev * chunks + chunk) * few
            out_ref[0, start : start + few, 2 * hidden :] = down[
                dev * few : (dev + 1) * few, chunk * hidden : (chunk + 1) * hidden
            ]


def weight_grads(rows, d_gu, act, d_rows, few, first, stop, buffers):
    experts, count, width = rows.shape
    hidden = act.shape[2]

    def part(*block):
        return pl.BlockSpec((1,) + block, lambda e: (first + e, 0, 0))

    return pl.pallas_call(
        functools.partial(grads_kernel, few),
        grid=(stop - first,),
        in_specs=[part(count, width), part(count, 2 * hidden), part(count, hidden), part(count, width)]
        + [pl.BlockSpec(memory_space=pl.ANY)] * len(buffers),
        out_specs=part(width, 3 * hidden),
        out_shape=jax.ShapeDtypeStruct((experts, width, 3 * hidden), low),
        scratch_shapes=[pltpu.VMEM((hidden, width), low)],
        input_output_aliases={4 + i: i for i in range(len(buffers))},
        compiler_params=vmem(56),
        name="weight_grads",
    )(rows, d_gu, act, d_rows, *buffers)


def shards(
    inputs,
    teacher,
    routes,
    valid_mask,
    block_lengths,
    gain_one,
    w_qkv,
    w_out,
    gain_two,
    w_router,
    w_gate,
    w_up,
    w_down,
):
    n = lax.axis_size("seq")
    me = lax.axis_index("seq")
    mine = lax.axis_index("fsdp")
    seqs_here, shard_len, width = inputs.shape
    assert seqs_here == 1
    seq_len = shard_len * n
    tokens_all = lax.axis_size("fsdp") * seq_len
    kv_here = KV_HEADS // n
    heads_w = kv_here * GROUP * HEAD_DIM
    group_w = kv_here * (GROUP + 2) * HEAD_DIM
    experts_here = w_gate.shape[0]
    expert_total = experts_here * n
    top_count = routes.shape[2]
    capacity = 3 * shard_len * top_count // (2 * expert_total)
    slots = -(-capacity // 16) * 16
    slot_rows = n * slots
    order_a, order_b = fsdp_bits()
    order = jnp.array(arrival_order(n), jnp.int32)[me]
    x_low = inputs.reshape(shard_len, width)

    own_qkv = lax.dynamic_slice_in_dim(w_qkv, me * group_w, group_w, 1)
    small = jnp.concatenate([gain_one[:, None], gain_two[:, None], w_router], axis=1)
    small = jnp.pad(small, ((0, 0), (0, -small.shape[1] % 128)))
    first = lax.all_gather(
        jnp.concatenate([own_qkv, small, w_out], axis=1), "fsdp", axis=0, tiled=True
    )
    full_qkv = first[:, :group_w]
    small = first[:, group_w : group_w + 2 + expert_total]
    full_out = first[:, -width:]
    full_g1 = small[:, 0].astype(full)
    full_g2 = small[:, 1].astype(full)
    router = small[:, 2:].T
    own_router = lax.dynamic_slice_in_dim(router, me * experts_here, experts_here, 0)
    own_router = jnp.pad(own_router, ((0, -experts_here % 16), (0, 0)))
    valid_rows = valid_mask.reshape(shard_len).astype(full)

    hidden_w = w_gate.shape[2]
    down_chunks = [
        w_down[:, :, start : start + hidden_w] for start in range(0, width, hidden_w)
    ]
    weights = lax.all_gather(
        jnp.concatenate([w_gate, w_up, jnp.concatenate(down_chunks, axis=1)], axis=2),
        "fsdp",
        axis=1,
        tiled=True,
    )

    routes_low = jnp.concatenate([routes.reshape(shard_len, top_count).T, valid_mask], axis=0)
    routes_low = jnp.pad(
        routes_low.astype(low), ((0, -routes_low.shape[0] % 16), (0, width - shard_len))
    )
    middle = shard_len // 2
    halves = (x_low[:middle], jnp.concatenate([x_low[middle:], routes_low], axis=0))
    positions = jnp.arange(seq_len, dtype=jnp.int32)
    cosine, sine_vals = rope_tables(positions.astype(full), HEAD_DIM)
    limit = block_limits(block_lengths[0], positions)[None]
    normed_one = jnp.zeros((seq_len, width), low)
    heads = jnp.zeros((n, kv_here, GROUP + 2, HEAD_DIM, shard_len), low)
    routes_all = []
    line = LineGather(halves)
    for turn in range(n):
        if turn:
            line.land(0, heads if turn > 1 else ())
            if turn < n - 1:
                line.go(0)
            line.land(1, ())
            if turn < n - 1:
                line.go(1)
        else:
            line.go(0)
            line.go(1)
        block = jnp.concatenate(line.block(turn))
        start = order[turn] * shard_len
        normed = rms_norm(block[:shard_len].astype(full), full_g1).astype(low)
        projected = dot("td,dc->ct", normed, full_qkv)
        projected = projected.reshape(kv_here, GROUP + 2, HEAD_DIM, shard_len)
        turned = rotate(
            projected[:, : GROUP + 1],
            lax.dynamic_slice_in_dim(cosine, start, shard_len, 1),
            lax.dynamic_slice_in_dim(sine_vals, start, shard_len, 1),
        ).astype(low)
        turned = jnp.concatenate(
            [
                turned[:, :GROUP] * jnp.asarray(attn_mult, low),
                turned[:, GROUP:],
                projected[:, GROUP + 1 :].astype(low),
            ],
            axis=1,
        )
        heads = lax.dynamic_update_index_in_dim(heads, turned, order[turn], 0)
        normed_one = lax.dynamic_update_slice_in_dim(normed_one, normed, start, 0)
        routes_all.append(block[shard_len : shard_len + top_count + 1, :shard_len])

    routes_all = jnp.stack(routes_all).astype(jnp.int32)
    valid_count = total(jnp.sum(routes_all[:, top_count]).astype(full).reshape(1, 1), "fsdp")[0, 0]
    expert_ids = jnp.arange(expert_total, dtype=jnp.int32)
    member = jnp.any(routes_all[:, :top_count, None, :] == expert_ids[:, None], axis=1)
    own_member = lax.dynamic_slice_in_dim(member, me * experts_here, experts_here, 1)
    earlier = jnp.arange(shard_len)[:, None] < jnp.arange(shard_len)[None, :]
    slot_of = dot("net,tu->neu", own_member.astype(low), earlier.astype(low)).astype(jnp.int32)
    slot_of = jnp.where(own_member, slot_of, -1)
    member = member.astype(full)

    key = jnp.moveaxis(heads[:, :, GROUP], 0, 2).reshape(kv_here, HEAD_DIM, seq_len)
    value = jnp.moveaxis(heads[:, :, GROUP + 1], 0, 2).reshape(kv_here, HEAD_DIM, seq_len)
    key_rows = jnp.swapaxes(key, 1, 2)
    value_rows = jnp.swapaxes(value, 1, 2)
    attended, out_heads, lse = attention_forward(heads, key_rows, value, limit)
    moved = exchange(attended)
    moved, slot_of, member, own_router = tie(moved, slot_of, member, own_router)
    attn_rows = by_place(nearest(*moved)).reshape(HEADS * HEAD_DIM, shard_len)
    projected = dot("kt,kd->td", attn_rows, full_out)
    hidden = x_low.astype(full) + resid_mult * projected
    normed_two, norm_two_pull = jax.vjp(rms_norm, hidden, full_g2)

    normed_low = normed_two.astype(low)
    line = LineGather((normed_low[:middle], normed_low[middle:]))
    buffers, gates = [], []
    line.go(0)
    line.go(1)
    other = ()
    for turn in range(n):
        if turn < n - 1:
            for h in (0, 1):
                other = line.land(h, other)
                if turn < n - 2:
                    line.go(h)
            line_slots = line.hold(slot_of[turn])
        else:
            line_slots = slot_of[turn]
        *buffers, shard_gates = experts_forward(
            turn, n, jnp.stack([order[turn], me, line.choice(turn)]), line.blocks(turn), line_slots,
            member[turn], router, weights, w_down.shape[1], slots, buffers,
        )
        gates.append(shard_gates)
        other = shard_gates
    mix_parts, expert_in, gate_up = buffers
    token_line = line
    cuts = (slice(0, middle), slice(middle, None))
    mixture, tokens = line_scatter(
        2,
        lambda h, shift: at_place(mix_parts[:, cuts[h]], me + shift),
        (lambda before, given: [token_line.block(turn) for turn in range(n)],),
    )
    output_f32 = hidden + resid_mult * mixture
    activations = output_f32.astype(low).reshape(1, shard_len, width)
    error_rows = output_f32 - teacher.astype(full).reshape(shard_len, width)
    weighted = valid_rows[:, None] * error_rows
    loss_steps = total_steps(jnp.sum(weighted * error_rows).reshape(1, 1), "seq", "fsdp")
    squares = next(loss_steps)
    d_out = weighted * (tokens_all / valid_count)

    d_mix = resid_mult * d_out
    d_tokens = d_mix.astype(low)
    mix_dot = jnp.sum(d_mix * mixture, axis=1)[None]
    mix_high = mix_dot.astype(low)
    mix_rows = jnp.concatenate([mix_high, (mix_dot - mix_high.astype(full)).astype(low)])
    mix_rows = jnp.pad(mix_rows, ((0, 14), (0, width - shard_len)))
    line = LineGather((d_tokens[:middle], jnp.concatenate([d_tokens[middle:], mix_rows])))
    buffers, d_logits = [], []
    for turn in range(n):
        if turn:
            line.land(0, d_logits[-1])
            if turn < n - 1:
                line.go(0)
            line.land(1, ())
            if turn < n - 1:
                line.go(1)
        else:
            line.go(0)
            line.go(1)
        *buffers, shard_logits = experts_backward(
            turn, n, jnp.stack([order[turn], me, line.choice(turn)]), line.blocks(turn), slot_of[turn],
            gates[turn], own_router, gate_up, weights, w_down.shape[1], buffers,
        )
        d_logits.append(shard_logits)
    d_parts, d_rows, d_gate_up, act_low = buffers
    expert_in = expert_in.reshape(experts_here, slot_rows, width)
    d_rows = d_rows.reshape(experts_here, slot_rows, width)
    d_gate_up = d_gate_up.reshape(experts_here, slot_rows, -1)
    act_low = act_low.reshape(experts_here, slot_rows, -1)

    cut = (experts_here + 1) // 2

    def some_grads(first, stop):
        def make(before, grads):
            inputs, _ = tie((expert_in, d_gate_up, act_low, d_rows), before)
            return [weight_grads(*inputs, w_down.shape[1], first, stop, grads)]

        return make

    d_normed_two, grads = line_scatter(
        1,
        lambda h, shift: at_place(d_parts, me + shift),
        (some_grads(0, cut), some_grads(cut, experts_here)),
    )
    expert_sum = lax.psum_scatter(grads[0], "fsdp", scatter_dimension=1, tiled=True)

    d_hidden_norm, gain_two_part = norm_two_pull(d_normed_two)
    d_hidden = d_out + d_hidden_norm
    d_proj = (resid_mult * d_hidden).astype(low)
    out_pairs = out_grads(mine.reshape(1), attn_rows, d_proj, order_a, order_b)
    out_sums = [Halving(*pair, bits) for pair, bits in zip(out_pairs, (order_a, order_b))]
    for each in out_sums:
        each.go()
    d_attended = dot("kd,td->kt", full_out, d_proj).astype(low)
    (d_attended,) = land(out_sums, d_attended)
    moved = exchange(d_attended.reshape(n, heads_w, shard_len))
    for each in out_sums:
        each.add()
    router_part = sum(
        dot("td,et->de", half, half_logits)
        for shard, shard_logits in zip(tokens, d_logits)
        for half, half_logits in (
            (shard[0], shard_logits[:experts_here, :middle]),
            (shard[1], shard_logits[:experts_here, middle:]),
        )
    )
    own_columns = jnp.where(
        expert_ids // experts_here == me, jnp.concatenate([router_part] * n, axis=1), 0.0
    )
    own_columns = jnp.concatenate([own_columns, gain_two_part[:, None]], axis=1).astype(low)
    moved, own_columns, squares = leave(out_sums, moved, own_columns, squares)
    squares = loss_steps.send(squares)
    for each in out_sums:
        each.go()
    query_grad, key_grad, value_grad = attention_backward(
        heads, key_rows, value_rows, key, limit, out_heads, lse, me.reshape(1), *moved
    )
    (query_grad, key_grad, value_grad), squares = land(
        out_sums, (query_grad, key_grad, value_grad), squares
    )
    squares = loss_steps.send(squares)
    for each in out_sums:
        each.add()
        each.go()
    d_turned = jnp.concatenate([query_grad, key_grad[:, None]], axis=1).astype(full)
    d_turned = rotate(d_turned, cosine, -sine_vals).astype(low)
    d_qkv = jnp.concatenate([d_turned, value_grad[:, None]], axis=1).reshape(group_w, seq_len)

    def d_part(rows, shift):
        start = (me + shift) % n * shard_len
        rows = lax.dynamic_slice_in_dim(rows, start, shard_len, 1)
        return dot("ct,dc->td", rows, full_qkv).astype(low)

    d_parts = {shift: d_part(d_qkv, shift) for shift in {1, n - 1}}
    (d_parts,) = land(out_sums, d_parts)
    for each in out_sums:
        each.add()

    out_sum = jnp.concatenate([each.finish() for each in out_sums], axis=1).astype(low)
    out_rows = out_sum.shape[0] // n
    out_parts = jnp.swapaxes(out_sum.reshape(out_sum.shape[0], n, width // n), 0, 1)
    out_parts = out_parts.reshape(n, out_rows, width)

    def get(h, shift):
        part = d_parts[shift % n]
        if h == 0:
            return part[:middle]
        return jnp.concatenate([part[middle:], at_place(out_parts, me + shift)])

    sums = {}

    def first_work(before, _):
        rows, _ = tie(d_qkv, before)
        for shift in range(n):
            if shift not in d_parts:
                d_parts[shift] = d_part(rows, shift)
        qkv_part = jnp.concatenate(
            [dot("td,ct->dc", normed_one, rows).astype(low), own_columns], axis=1
        )
        sums["qkv"] = rows_halving(qkv_part, order_a)
        sums["qkv"].go()
        return sums["qkv"].send

    def next_work(before, _):
        land([sums["qkv"]], before)
        sums["qkv"].add()
        sums["qkv"].go()
        return sums["qkv"].send

    ended, _ = line_scatter(2, get, (first_work, next_work, next_work))
    qkv_sum = sums["qkv"]
    d_normed_one = ended[:shard_len]
    (ended,) = land([qkv_sum], ended)
    qkv_sum.add()
    out_own = ended[shard_len:].reshape(out_sum.shape[0], width // n)
    block = jnp.concatenate([qkv_sum.finish(), out_own], axis=1).astype(low)
    block, expert_sum, squares = tie(block, expert_sum, squares)
    blocks = lax.all_gather(block, "seq", axis=0)
    _, norm_one_pull = jax.vjp(lambda v: rms_norm(v, full_g1), x_low.astype(full))
    input_grad = (d_hidden + norm_one_pull(d_normed_one)[0]).reshape(1, shard_len, width)
    few = w_down.shape[1]
    gate_grad = expert_sum[:, :, :hidden_w].astype(full)
    up_grad = expert_sum[:, :, hidden_w : 2 * hidden_w].astype(full)
    down_grad = jnp.concatenate(
        [
            expert_sum[:, start : start + few, 2 * hidden_w :].astype(full)
            for start in range(0, expert_sum.shape[1], few)
        ],
        axis=2,
    )
    qkv_grad = jnp.concatenate([came[:, :group_w] for came in blocks], axis=1).astype(full)
    out_grad = jnp.concatenate([came[:, -(width // n) :] for came in blocks], axis=1).astype(full)
    rest = jnp.sum(blocks[:, :, group_w : -(width // n)].astype(full), axis=0)
    router_grad, gain_two_grad = rest[:, :expert_total], rest[:, expert_total]
    gain_one_grad = jnp.sum(qkv_grad * w_qkv.astype(full), axis=1) / gain_one.astype(full)
    for _ in range(4):
        squares = loss_steps.send(squares)
    loss_value = squares[0, 0] / (valid_count * width)
    return (
        activations,
        loss_value,
        input_grad,
        gain_one_grad,
        qkv_grad,
        out_grad,
        gain_two_grad,
        router_grad,
        gate_grad,
        up_grad,
        down_grad,
    )


def solution(mesh):
    return jax.shard_map(
        shards,
        mesh=mesh,
        in_specs=(
            P("fsdp", "seq", None),
            P("fsdp", "seq", None),
            P("fsdp", "seq", None),
            P("fsdp", "seq"),
            P("fsdp", None),
            P("fsdp"),
            P("fsdp", None),
            P("fsdp", None),
            P("fsdp"),
            P("fsdp", None),
            P("seq", "fsdp", None),
            P("seq", "fsdp", None),
            P("seq", "fsdp", None),
        ),
        out_specs=(
            P("fsdp", "seq", None),
            P(),
            P("fsdp", "seq", None),
            P("fsdp"),
            P("fsdp", None),
            P("fsdp", None),
            P("fsdp"),
            P("fsdp", None),
            P("seq", "fsdp", None),
            P("seq", "fsdp", None),
            P("seq", "fsdp", None),
        ),
        check_vma=False,
    )
```
